32 devices in a mesh: samp: 8 (over z, y), tok: 4 (over x, core).
Axes of the slice: x: 2, y: 2, z: 4, core: 2. Of those that a mesh axis runs over, the one named last changes fastest.
Arguments:
- atom_feats: bfloat16 [32, 5120, 128], P('samp', 'tok'), may hold values from -6 to 6
- atom_counts: int32 [4, 64], P('tok'), may hold values from 1 to 24, 1280 in all within a row
- atom_mask: int32 [5120], replicated, may hold values 0 or 1
- token_single: bfloat16 [256, 768], P('tok'), may hold values from -6 to 6
- pair: bfloat16 [256, 256, 128], P('tok', 'samp'), may hold values from -6 to 6
- pair_gain: float32 [128], replicated, may hold values from 0.5 to 2
- w_bias: bfloat16 [128, 16], replicated
- w_atom_qkv: bfloat16 [128, 384], replicated
- w_atom_out: bfloat16 [128, 128], replicated, may hold values from -0.5 to 0.5
- w_embed: bfloat16 [128, 768], replicated, may hold values from -0.5 to 0.5
- w_qkv: bfloat16 [768, 2304], replicated, may hold values from -0.21875 to 0.21875
- w_out: bfloat16 [768, 768], replicated, may hold values from -0.21875 to 0.21875
- w_gate: bfloat16 [768, 1536], replicated, may hold values from -0.21875 to 0.21875
- w_up: bfloat16 [768, 1536], replicated, may hold values from -0.21875 to 0.21875
- w_down: bfloat16 [1536, 768], replicated, may hold values from -0.15625 to 0.15625
- cotangent: bfloat16 [32, 256, 768], P('samp', 'tok'), may hold values from -6 to 6
Outputs:
- token_out: bfloat16 [32, 256, 768], P('samp', 'tok')
- pair_grad: float32 [256, 256, 128], P('tok', 'samp')
The draws below stay inside these ranges and needn't reach their ends.
Inputs may be any that keep to these rules, and one draw needn't show every extreme that they name: `atom_counts`: each row sums to 1280.
All inputs are finite; a program needn't handle non-finite values.
Results may differ from the reference program's by a relative error of at most 0.015.
The reference program's roundings to bfloat16 on the way count: a program that leaves them out, or rounds other values in their place, can miss the bound.
Values may be sent and summed in bfloat16 or wider, within the bound.
No kernel may reach another device: no remote copies, remote signals or barrier semaphores. Data moves between devices by JAX's collectives and lax.ppermute only.
A program may use at most 192 MiB of HBM per device.

```python
import math
import jax
import jax.numpy as jnp
import numpy as np
from jax import lax

C_ATOM = 128
ATOM_HEADS = 4
C_TOK = 768
HEADS = 16
CZ = 128
TRANSITION = 1536
TOK_DEV = 64
MOST_ATOMS = 24
ATOM_HD = 32
HD = 48
ATOM_DEV = 1280
NTOK = 256
ATOMS = 5120
SAMPLES = 32
N_TOK = 4


def draw_w_bias(key, part):
    key = jax.random.fold_in(key, 21)
    base_key = jax.random.fold_in(key, 0)
    values = jax.random.normal(base_key, (CZ, HEADS), jnp.float32) * CZ ** (-0.5)
    return values.astype(jnp.bfloat16)


def draw_w_atom_qkv(key, part):
    key = jax.random.fold_in(key, 37)
    base_key = jax.random.fold_in(key, 0)
    values = jax.random.normal(base_key, (C_ATOM, 3 * C_ATOM), jnp.float32) * C_ATOM ** (-0.5)
    return values.astype(jnp.bfloat16)


def with_ends(values, key, smallest, high):
    place = [jax.random.randint(jax.random.fold_in(key, axis), (), 0, length) for axis, length in enumerate(values.shape)]
    longest = values.shape.index(max(values.shape))
    next_to = place[:longest] + [(place[longest] + 1) % values.shape[longest]] + place[longest + 1:]
    return values.at[tuple(place)].set(smallest).at[tuple(next_to)].set(high)


def level_of(rng, extent, cuts, smallest, top_value):
    level = 1.0
    for axis_at, blocks in cuts:
        steps = jax.random.uniform(jax.random.fold_in(jax.random.fold_in(rng, 6), axis_at), (blocks,), jnp.float32, smallest / len(cuts), top_value / len(cuts))
        level = level * jnp.repeat(jnp.exp(steps), extent[axis_at] // blocks).reshape((-1,) + (1,) * (len(extent) - 1 - axis_at))
    return level


def length_profile(amount, total, most, lean):
    weights = [(1 << 20) // math.isqrt(rank ** lean) + 1 for rank in range(2, amount + 1)]
    surplus, holding = total - most - (amount - 1), [1] * (amount - 1)
    while surplus > 0:
        free = [i for i in range(amount - 1) if holding[i] < most]
        pool, budget = sum([weights[i] for i in free]), surplus
        for i in free:
            addition = min(most - holding[i], max(1, budget * weights[i] // pool), surplus)
            holding[i] = holding[i] + addition
            surplus = surplus - addition
    return np.array([most] + holding)


def ragged_sizes(key, number_of, total, most, lean):
    if number_of == 2:
        one = jax.random.randint(key, (), max(1, total - most), min(most, total - 1) + 1)
        return jnp.stack([one, total - one])
    tallies = jnp.asarray(length_profile(number_of, total, most, lean), jnp.int32)
    twos = (number_of - 1) // 2
    giver, receiver = tallies[1:1 + 2 * twos:2], tallies[2:2 + 2 * twos:2]
    margin = jnp.minimum(giver - 1, most - receiver)
    moved = jax.random.randint(jax.random.fold_in(key, 1), (twos,), 0, 1 << 20) % (margin + 1)
    tallies = tallies.at[1:1 + 2 * twos:2].set(giver - moved).at[2:2 + 2 * twos:2].set(receiver + moved)
    return tallies[jax.random.permutation(jax.random.fold_in(key, 2), number_of)]


def gaussian(rng, extent, deviation, reach, cuts=(), held_as=jnp.bfloat16):
    factor_of = level_of(rng, extent, cuts, -0.22, 0.18) if cuts else 1.0
    result = jax.random.normal(rng, extent, jnp.float32) * deviation * factor_of
    return jnp.minimum(jnp.maximum(result, -reach), reach).astype(held_as)


def setup_inputs(seed: int = 0) -> dict:
    key_list = jax.random.split(jax.random.key(seed), 17)
    return {
        "atom_feats": gaussian(key_list[0], (SAMPLES, ATOMS, C_ATOM), 1.0, 6.0, ((0, 8), (1, 4))),
        "atom_counts": jax.vmap(lambda own: ragged_sizes(own, TOK_DEV, ATOM_DEV, MOST_ATOMS, 1))(jax.random.split(key_list[1], N_TOK)).reshape((N_TOK, TOK_DEV)).astype(jnp.int32),
        "atom_mask": with_ends((jax.random.randint(key_list[2], (ATOMS,), 0, 8) < 7).astype(jnp.int32), jax.random.fold_in(key_list[2], 1), 0, 1),
        "token_single": gaussian(key_list[3], (NTOK, C_TOK), 1.0, 6.0, ((0, 4),)),
        "pair": gaussian(key_list[4], (NTOK, NTOK, CZ), 1.0, 6.0, ((0, 4), (1, 8))),
        "pair_gain": jnp.clip(jnp.exp(jax.random.uniform(key_list[5], (CZ,), jnp.float32, math.log(0.5), math.log(2.0))), 0.5, 2.0),
        "w_bias": draw_w_bias(jax.random.fold_in(key_list[16], 71), 0),
        "w_atom_qkv": draw_w_atom_qkv(jax.random.fold_in(key_list[16], 71), 0),
        "w_atom_out": gaussian(key_list[8], (C_ATOM, C_ATOM), C_ATOM ** -0.5, 0.5),
        "w_embed": gaussian(key_list[9], (C_ATOM, C_TOK), C_ATOM ** -0.5, 0.5),
        "w_qkv": gaussian(key_list[10], (C_TOK, 3 * C_TOK), C_TOK ** -0.5, 0.21875),
        "w_out": gaussian(key_list[11], (C_TOK, C_TOK), C_TOK ** -0.5, 0.21875),
        "w_gate": gaussian(key_list[12], (C_TOK, TRANSITION), C_TOK ** -0.5, 0.21875),
        "w_up": gaussian(key_list[13], (C_TOK, TRANSITION), C_TOK ** -0.5, 0.21875),
        "w_down": gaussian(key_list[14], (TRANSITION, C_TOK), TRANSITION ** -0.5, 0.15625),
        "cotangent": gaussian(key_list[15], (SAMPLES, NTOK, C_TOK), 1.0, 6.0, ((0, 8), (1, 4))),
    }


epsilon = 1e-05
highest = lax.Precision.HIGHEST

def norm_rows(values):
    center = values - lax.optimization_barrier(jnp.mean(values, axis=-1, keepdims=True))
    scale_inv = lax.rsqrt(lax.optimization_barrier(jnp.mean(center * center, axis=-1, keepdims=True)) + epsilon)
    return (center * scale_inv, scale_inv)

def norm_back(grads, normed, scale_inv):
    first = lax.optimization_barrier(jnp.mean(grads, axis=-1, keepdims=True))
    second = lax.optimization_barrier(jnp.mean(grads * normed, axis=-1, keepdims=True))
    return scale_inv * (grads - first - normed * second)

def softmax_rows(scores):
    peak = lax.optimization_barrier(jnp.max(scores, axis=-1, keepdims=True))
    expo = jnp.exp(scores - peak)
    return expo / lax.optimization_barrier(jnp.sum(expo, axis=-1, keepdims=True))

def atom_windows(padded):
    windows = (padded.shape[0] - 96) // 32
    pieces = [padded[32 * r:32 * r + 32 * windows].reshape(windows, 32, padded.shape[1]) for r in range(4)]
    return jnp.concatenate(pieces, axis=1)

def atom_attend(queries, keyvals, atom_mask):
    total_atoms = queries.shape[0]
    windows = total_atoms // 32
    padded = jnp.pad(keyvals, ((48, 48), (0, 0)))
    window_keys = atom_windows(padded)
    query_win = queries.reshape(windows, 32, ATOM_HEADS, ATOM_HD).astype(jnp.float32)
    key_win = window_keys[:, :, :C_ATOM].reshape(windows, 128, ATOM_HEADS, ATOM_HD).astype(jnp.float32)
    value_win = window_keys[:, :, C_ATOM:].reshape(windows, 128, ATOM_HEADS, ATOM_HD).astype(jnp.float32)
    scores = jnp.einsum('wqhd,wkhd->whqk', query_win, key_win) * ATOM_HD ** (-0.5)
    window_ids = jnp.arange(windows, dtype=jnp.int32)
    query_pos = 32 * window_ids[:, None] + jnp.arange(32, dtype=jnp.int32)[None, :]
    key_pos = 32 * window_ids[:, None] - 48 + jnp.arange(128, dtype=jnp.int32)[None, :]
    inside = (key_pos >= 0) & (key_pos < total_atoms)
    flags = jnp.take(atom_mask, jnp.clip(key_pos, 0, total_atoms - 1)) == 1
    valid = inside[:, None, :] & (flags[:, None, :] | (key_pos[:, None, :] == query_pos[:, :, None]))
    scores = jnp.where(valid[:, None], scores, -1e+30)
    weights = softmax_rows(scores).astype(jnp.bfloat16).astype(jnp.float32)
    mixed = jnp.einsum('whqk,wkhd->wqhd', weights, value_win)
    return mixed.astype(jnp.bfloat16).reshape(total_atoms, C_ATOM)

def reference(atom_feats, atom_counts, atom_mask, token_single, pair, pair_gain, w_bias, w_atom_qkv, w_atom_out, w_embed, w_qkv, w_out, w_gate, w_up, w_down, cotangent):
    total_tokens = token_single.shape[0]
    total_atoms = atom_mask.shape[0]
    pair_hat, pair_rstd = norm_rows(pair.astype(jnp.float32))
    scaled = (pair_hat * pair_gain).astype(jnp.bfloat16).astype(jnp.float32)
    bias = jnp.einsum('ijc,ch->hij', scaled, w_bias.astype(jnp.float32)).astype(jnp.bfloat16).astype(jnp.float32)
    counts = atom_counts.reshape(-1)
    bounds = jnp.cumsum(counts)
    owners = jnp.searchsorted(bounds, jnp.arange(total_atoms, dtype=jnp.int32), side='right').astype(jnp.int32)

    def one_sample(d_total, inputs):
        feats, cot = inputs
        normed, unused = norm_rows(feats.astype(jnp.float32))
        atom_qkv = jnp.dot(normed.astype(jnp.bfloat16), w_atom_qkv, preferred_element_type=jnp.float32).astype(jnp.bfloat16)
        mixed = atom_attend(atom_qkv[:, :C_ATOM], atom_qkv[:, C_ATOM:], atom_mask)
        updated = (feats.astype(jnp.float32) + jnp.dot(mixed, w_atom_out, preferred_element_type=jnp.float32)).astype(jnp.bfloat16)
        embedded = jax.nn.relu(jnp.dot(updated, w_embed, preferred_element_type=jnp.float32))
        pooled = jax.ops.segment_sum(embedded, owners, num_segments=total_tokens) / counts.astype(jnp.float32)[:, None]
        tokens = pooled + token_single.astype(jnp.float32)
        normed_tok, unused = norm_rows(tokens)
        tok_qkv = jnp.dot(normed_tok.astype(jnp.bfloat16), w_qkv, preferred_element_type=jnp.float32).astype(jnp.bfloat16)
        queries = tok_qkv[:, :C_TOK].reshape(total_tokens, HEADS, HD).astype(jnp.float32)
        keys = tok_qkv[:, C_TOK:2 * C_TOK].reshape(total_tokens, HEADS, HD).astype(jnp.float32)
        values = tok_qkv[:, 2 * C_TOK:].reshape(total_tokens, HEADS, HD).astype(jnp.float32)
        scores = jnp.einsum('ihd,jhd->hij', queries, keys) * HD ** (-0.5) + bias
        probs = softmax_rows(scores)
        weights = probs.astype(jnp.bfloat16).astype(jnp.float32)
        attended = jnp.einsum('hij,jhd->ihd', weights, values).astype(jnp.bfloat16).reshape(total_tokens, C_TOK)
        resid = tokens + jnp.dot(attended, w_out, preferred_element_type=jnp.float32)
        resid_hat, resid_rstd = norm_rows(resid)
        shaped = resid_hat.astype(jnp.bfloat16)
        gate = jnp.dot(shaped, w_gate, preferred_element_type=jnp.float32)
        upward = jnp.dot(shaped, w_up, preferred_element_type=jnp.float32)
        hidden = (jax.nn.silu(gate) * upward).astype(jnp.bfloat16)
        output = (resid + jnp.dot(hidden, w_down, preferred_element_type=jnp.float32)).astype(jnp.bfloat16)
        d_hidden = jnp.dot(cot, w_down.T, preferred_element_type=jnp.float32)
        sigmoid_gate = jax.nn.sigmoid(gate)
        d_gate = (d_hidden * upward * sigmoid_gate * (1.0 + gate * (1.0 - sigmoid_gate))).astype(jnp.bfloat16)
        d_upward = (d_hidden * jax.nn.silu(gate)).astype(jnp.bfloat16)
        d_normed = jnp.dot(d_gate, w_gate.T, preferred_element_type=jnp.float32) + jnp.dot(d_upward, w_up.T, preferred_element_type=jnp.float32)
        d_resid = cot.astype(jnp.float32) + norm_back(d_normed, resid_hat, resid_rstd)
        d_attended = jnp.dot(d_resid.astype(jnp.bfloat16), w_out.T, preferred_element_type=jnp.float32).astype(jnp.bfloat16)
        d_attended = d_attended.reshape(total_tokens, HEADS, HD).astype(jnp.float32)
        d_probs = jnp.einsum('ihd,jhd->hij', d_attended, values)
        delta = lax.optimization_barrier(jnp.sum(probs * d_probs, axis=-1, keepdims=True))
        d_scores = probs * (d_probs - delta)
        return (d_total + d_scores, output)
    d_init = jnp.zeros((HEADS, total_tokens, total_tokens), jnp.float32)
    d_bias, token_out = lax.scan(one_sample, d_init, (atom_feats, cotangent))
    d_scaled = jnp.einsum('hij,ch->ijc', d_bias, w_bias.astype(jnp.float32), precision=highest) * pair_gain
    pair_grad = norm_back(d_scaled, pair_hat, pair_rstd)
    return (token_out, pair_grad)
```

```python
import functools

import jax
import jax.numpy as jnp
from jax import lax
from jax.experimental import pallas as pl
from jax.experimental.pallas import tpu as pltpu
from jax.sharding import PartitionSpec as P

C_ATOM = 128
ATOM_HEADS = 4
C_TOK = 768
HEADS = 16
ATOM_HD = 32
HD = 48
CZ = 128
HALO = 48
PAIRS = HEADS // 2

epsilon = 1e-05
f32 = jnp.float32
bf16 = jnp.bfloat16

WINDOWS = ((0, 128), (0, 256), (128, 384), (256, 384))


def nn(a, b):
    return lax.dot_general(a, b, (((1,), (0,)), ((), ())), preferred_element_type=f32)


def nt(a, b):
    return lax.dot_general(a, b, (((1,), (1,)), ((), ())), preferred_element_type=f32)


def tn(a, b):
    return lax.dot_general(a, b, (((0,), (0,)), ((), ())), preferred_element_type=f32)


def norm_rows(values):
    center = values - jnp.mean(values, axis=-1, keepdims=True)
    scale_inv = lax.rsqrt(jnp.mean(center * center, axis=-1, keepdims=True) + epsilon)
    return (center * scale_inv, scale_inv)


def iota(shape, dim):
    return lax.broadcasted_iota(jnp.int32, shape, dim)


def split_heads(w_bias):
    row, col = iota((PAIRS, HEADS), 0), iota((PAIRS, HEADS), 1)
    even = (col == 2 * row).astype(f32).astype(bf16)
    odd = (col == 2 * row + 1).astype(f32).astype(bf16)
    return nt(even, w_bias).astype(bf16), nt(odd, w_bias).astype(bf16)


def bias_kernel(pair_ref, gain_ref, w_bias_ref, out_ref, scaled_ref, stage_ref):
    rows, keys = pair_ref.shape[0], pair_ref.shape[1]
    gain = gain_ref[...]

    def norm_step(i, carry):
        block = pair_ref[pl.ds(i * 8, 8)].astype(f32).reshape(8 * keys, CZ)
        hat, unused = norm_rows(block)
        scaled_ref[pl.ds(pl.multiple_of(i * 8 * keys, 8 * keys), 8 * keys), :] = hat * gain
        return carry

    lax.fori_loop(0, rows // 8, norm_step, 0)
    even, odd = split_heads(w_bias_ref[...])
    weights = jnp.concatenate([even, odd], axis=1)
    blank = jnp.zeros((rows, CZ), bf16)
    for j in range(keys):
        block = scaled_ref[pl.ds(j, rows, stride=keys), :].astype(bf16)
        both = jnp.concatenate(
            [jnp.concatenate([block, blank], axis=1), jnp.concatenate([blank, block], axis=1)],
            axis=0,
        )
        stage_ref[pl.ds(j * PAIRS, PAIRS), :] = nt(weights, both)
    out_ref[...] = stage_ref[...].astype(bf16)


def pair_bias(pair, pair_gain, w_bias):
    rows, keys = pair.shape[0], pair.shape[1]
    return pl.pallas_call(
        bias_kernel,
        out_shape=jax.ShapeDtypeStruct((keys * PAIRS, 2 * rows), bf16),
        scratch_shapes=[
            pltpu.VMEM((rows * keys, CZ), f32),
            pltpu.VMEM((keys * PAIRS, 2 * rows), f32),
        ],
        compiler_params=pltpu.CompilerParams(vmem_limit_bytes=16 << 20),
        cost_estimate=pl.CostEstimate(flops=10**7, bytes_accessed=10**7, transcendentals=0),
        name="pair_bias",
    )(pair, pair_gain.reshape(1, CZ), w_bias)


def atom_kernel(
    feats_ref, left_ref, right_ref, flags_ref, counts_ref, single_ref, w_qkv_ref, w_out_ref,
    w_embed_ref, tokens_ref, normed_ref, xn_ref, qkv_ref, keybias_ref, onehot_ref, pooled_ref,
    counts_col_ref,
):
    atoms = feats_ref.shape[1]
    padded = atoms + 2 * HALO
    tok_rows = single_ref.shape[0]

    @pl.when(pl.program_id(0) == 0)
    def prepare():
        eye = iota((128, 128), 0) == iota((128, 128), 1)
        for b in range(flags_ref.shape[0]):
            row = jnp.broadcast_to(flags_ref[b : b + 1, :], (128, 128))
            col = jnp.sum(jnp.where(eye, row, 0.0), axis=1, keepdims=True)
            keybias_ref[b * 128 : (b + 1) * 128, :] = jnp.broadcast_to(
                (col - 1.0) * 1e30, (128, 128)
            )
        counts = jnp.broadcast_to(counts_ref[...].astype(f32), (tok_rows, tok_rows))
        sub, lane = iota((tok_rows, tok_rows), 0), iota((tok_rows, tok_rows), 1)
        start = jnp.sum(jnp.where(lane < sub, counts, 0.0), axis=1, keepdims=True)
        own = jnp.sum(jnp.where(lane == sub, counts, 0.0), axis=1, keepdims=True)
        counts_col_ref[...] = jnp.broadcast_to(own, (tok_rows, 128))
        pos = iota((tok_rows, 128), 1).astype(f32)
        for g in range(atoms // 128):
            at = pos + float(g * 128)
            hit = jnp.where((at >= start) & (at < start + own), 1.0, 0.0).astype(bf16)
            onehot_ref[g] = jnp.concatenate([hit, hit], axis=1)

    xn_ref[0:HALO, :] = norm_rows(left_ref[0].astype(f32))[0].astype(bf16)
    xn_ref[atoms + HALO : padded, :] = norm_rows(right_ref[0].astype(f32))[0].astype(bf16)

    def norm_step(i, carry):
        at = pl.multiple_of(i * 256, 256)
        block = feats_ref[0, pl.ds(at, 256), :].astype(f32)
        xn_ref[pl.ds(HALO + at, 256), :] = norm_rows(block)[0].astype(bf16)
        return carry

    lax.fori_loop(0, atoms // 256, norm_step, 0)

    chunk = padded // 4
    w_qkv = w_qkv_ref[...]

    def qkv_step(i, carry):
        at = pl.multiple_of(i * chunk, 8)
        qkv_ref[pl.ds(at, chunk), :] = nn(xn_ref[pl.ds(at, chunk), :], w_qkv).astype(bf16)
        return carry

    for i in range(4):
        qkv_ref[i * chunk : (i + 1) * chunk, :] = nn(
            xn_ref[i * chunk : (i + 1) * chunk, :], w_qkv
        ).astype(bf16)

    pooled_ref[...] = jnp.zeros_like(pooled_ref)
    lane = iota((32, 128), 1)
    head_of = lane // ATOM_HD
    head_mask = [(head_of == h).astype(f32).astype(bf16) for h in range(ATOM_HEADS)]
    own_atom = (lane % 32) == iota((32, 128), 0)
    factor = ATOM_HD ** (-0.5)

    def group_step(g, carry):
        base = pl.multiple_of(g * 128, 128)
        queries = qkv_ref[pl.ds(base + HALO, 128), 0:C_ATOM]
        mixed = []
        for w in range(4):
            query = queries[32 * w : 32 * w + 32]
            spread = jnp.concatenate([query * head_mask[h] for h in range(ATOM_HEADS)], axis=0)
            keys = qkv_ref[pl.ds(base + 32 * w, 128), C_ATOM : 2 * C_ATOM]
            values = qkv_ref[pl.ds(base + 32 * w, 128), 2 * C_ATOM : 3 * C_ATOM]
            scores = nt(keys, spread) * factor
            keybias = keybias_ref[pl.ds(base + 32 * w, 128), :]
            keybias = jnp.concatenate(
                [keybias[0:48], jnp.where(own_atom, 0.0, keybias[48:80]), keybias[80:128]], axis=0
            )
            scores = scores + keybias
            expo = jnp.exp(scores - jnp.max(scores, axis=0, keepdims=True))
            weights = expo * (1.0 / jnp.sum(expo, axis=0, keepdims=True))
            part = tn(weights.astype(bf16), values)
            mix = part[0:32]
            for h in range(1, ATOM_HEADS):
                mix = jnp.where(head_of == h, part[32 * h : 32 * h + 32], mix)
            mixed.append(mix.astype(bf16))
        mixed = jnp.concatenate(mixed, axis=0)
        feats = feats_ref[0, pl.ds(base, 128), :].astype(f32)
        updated = (feats + nn(mixed, w_out_ref[...])).astype(bf16)
        embedded = jnp.maximum(nn(updated, w_embed_ref[...]), 0.0)
        high = embedded.astype(bf16)
        low = (embedded - high.astype(f32)).astype(bf16)
        pooled_ref[...] += nn(onehot_ref[g], jnp.concatenate([high, low], axis=0))
        return carry

    lax.fori_loop(0, atoms // 128, group_step, 0)
    counts = counts_col_ref[:, 0:1]
    tokens = pooled_ref[...] / counts + single_ref[...].astype(f32)
    tokens_ref[0] = tokens
    normed_ref[0] = norm_rows(tokens)[0].astype(bf16)


def atom_stage(feats, left, right, flags, counts, single, w_qkv, w_out, w_embed):
    batch, atoms, _ = feats.shape
    tok_rows = single.shape[0]
    padded = atoms + 2 * HALO
    by_sample = lambda rows, cols: pl.BlockSpec((1, rows, cols), lambda s: (s, 0, 0))
    whole = lambda a: pl.BlockSpec(a.shape, lambda s: (0,) * a.ndim)
    return pl.pallas_call(
        atom_kernel,
        grid=(batch,),
        in_specs=[
            by_sample(atoms, C_ATOM), by_sample(HALO, C_ATOM), by_sample(HALO, C_ATOM),
            whole(flags), whole(counts), whole(single), whole(w_qkv), whole(w_out), whole(w_embed),
        ],
        out_specs=[by_sample(tok_rows, C_TOK), by_sample(tok_rows, C_TOK)],
        out_shape=[
            jax.ShapeDtypeStruct((batch, tok_rows, C_TOK), f32),
            jax.ShapeDtypeStruct((batch, tok_rows, C_TOK), bf16),
        ],
        scratch_shapes=[
            pltpu.VMEM((padded, C_ATOM), bf16),
            pltpu.VMEM((padded, 3 * C_ATOM), bf16),
            pltpu.VMEM((flags.shape[0] * 128, 128), f32),
            pltpu.VMEM((atoms // 128, tok_rows, 256), bf16),
            pltpu.VMEM((tok_rows, C_TOK), f32),
            pltpu.VMEM((tok_rows, 128), f32),
        ],
        compiler_params=pltpu.CompilerParams(vmem_limit_bytes=24 << 20),
        cost_estimate=pl.CostEstimate(
            flops=6 * 10**9, bytes_accessed=4 * 10**6, transcendentals=3 * 10**6
        ),
        name="atoms",
    )(feats, left, right, flags, counts, single, w_qkv, w_out, w_embed)


def head_masks(rows):
    masks = []
    for pair in range(4):
        low, high = WINDOWS[pair]
        lane = iota((rows, high - low), 1) + low
        first = 2 * pair * HD
        masks.append(
            [(lane >= first + HD * k) & (lane < first + HD * (k + 1)) for k in range(2)]
        )
    return masks


def token_kernel(
    local_ref, all_ref, tokens_ref, bias_ref, cot_ref, w_qkv_hbm, w_out_hbm, w_gate_hbm, w_up_hbm,
    w_down_hbm, resid_ref, hidden_ref, d_bias_ref, w_qkv_ref, w_out_ref, w_gate_ref, w_up_ref,
    w_down_ref, sems, q_ref, kv_ref, biasf_ref, probs_ref, att_ref, d_gate_ref, d_up_ref, hat_ref,
    d_bias_f_ref,
):
    batch, keys_all = all_ref.shape[0], all_ref.shape[1]
    tok_rows = tokens_ref.shape[1]
    rows = batch * tok_rows
    copies = [
        pltpu.make_async_copy(src, dst, sems.at[i])
        for i, (src, dst) in enumerate(
            [
                (w_qkv_hbm, w_qkv_ref), (w_out_hbm, w_out_ref), (w_gate_hbm, w_gate_ref),
                (w_up_hbm, w_up_ref), (w_down_hbm, w_down_ref),
            ]
        )
    ]
    for copy in copies:
        copy.start()
    biasf_ref[...] = bias_ref[...].astype(f32)
    copies[0].wait()

    def q_step(n, carry):
        at = pl.multiple_of(n * 256, 256)
        q_ref[:, pl.ds(at, 256)] = nn(
            local_ref[...].reshape(rows, C_TOK), w_qkv_ref[:, pl.ds(at, 256)]
        ).astype(bf16)
        return carry

    lax.fori_loop(0, C_TOK // 256, q_step, 0)

    def kv_step(i, carry):
        s, n = i // 3, i % 3
        at = pl.multiple_of(n * 512, 512)
        kv_ref[s, :, pl.ds(at, 512)] = nn(
            all_ref[s], w_qkv_ref[:, pl.ds(pl.multiple_of(C_TOK + at, 256), 512)]
        ).astype(bf16)
        return carry

    lax.fori_loop(0, batch * 3, kv_step, 0)

    masks = head_masks(tok_rows)
    factor = HD ** (-0.5)

    def two_heads(block, pair):
        first, second = masks[pair % 4]
        blank = jnp.zeros_like(block)
        return jnp.concatenate([jnp.where(first, block, blank), jnp.where(second, block, blank)], 0)

    def attend_step(s, carry):
        at = pl.multiple_of(s * tok_rows, 64)
        for half in range(2):
            lanes = [jnp.zeros((tok_rows, 128), f32) for _ in range(3)]
            for sub in range(4):
                pair = half * 4 + sub
                low, high = (384 * half + v for v in WINDOWS[sub])
                queries = two_heads(q_ref[pl.ds(at, tok_rows), low:high], pair)
                scores = nt(kv_ref[s, :, low:high], queries) * factor
                scores = scores + biasf_ref[pl.ds(pair, keys_all, stride=PAIRS), :]
                expo = jnp.exp(scores - jnp.max(scores, axis=0, keepdims=True))
                probs = expo * (1.0 / jnp.sum(expo, axis=0, keepdims=True))
                probs_ref[s, pair] = probs
                part = tn(probs.astype(bf16), kv_ref[s, :, C_TOK + low : C_TOK + high])
                first, second = masks[sub]
                mix = jnp.where(first, part[0:tok_rows], 0.0)
                mix = jnp.where(second, part[tok_rows : 2 * tok_rows], mix)
                for t in range((high - low) // 128):
                    tile = WINDOWS[sub][0] // 128 + t
                    lanes[tile] = lanes[tile] + mix[:, 128 * t : 128 * t + 128]
            att_ref[pl.ds(at, tok_rows), 384 * half : 384 * half + 384] = jnp.concatenate(
                lanes, axis=1
            ).astype(bf16)
        return carry

    lax.fori_loop(0, batch, attend_step, 0)

    copies[1].wait()
    resid = tokens_ref[...].reshape(rows, C_TOK) + nn(att_ref[...], w_out_ref[...])
    resid_ref[...] = resid
    hat, rstd = norm_rows(resid)
    hat_ref[...] = hat
    shaped = hat.astype(bf16)
    att_ref[...] = shaped
    copies[2].wait()
    copies[3].wait()
    copies[4].wait()

    def transition_step(n, carry):
        at = pl.multiple_of(n * 256, 256)
        shaped = att_ref[...]
        gate = nn(shaped, w_gate_ref[:, pl.ds(at, 256)])
        up = nn(shaped, w_up_ref[:, pl.ds(at, 256)])
        d_hidden = nt(cot_ref[...].reshape(rows, C_TOK), w_down_ref[pl.ds(at, 256), :])
        sig = 1.0 / (1.0 + jnp.exp(-gate))
        act = gate * sig
        hidden_ref[:, pl.ds(at, 256)] = (act * up).astype(bf16)
        d_gate_ref[:, pl.ds(at, 256)] = (
            d_hidden * up * sig * (1.0 + gate * (1.0 - sig))
        ).astype(bf16)
        d_up_ref[:, pl.ds(at, 256)] = (d_hidden * act).astype(bf16)
        return carry

    lax.fori_loop(0, w_gate_ref.shape[1] // 256, transition_step, 0)
    parts = []
    for n in range(C_TOK // 256):
        parts.append(
            nt(d_gate_ref[...], w_gate_ref[256 * n : 256 * n + 256, :])
            + nt(d_up_ref[...], w_up_ref[256 * n : 256 * n + 256, :])
        )
    d_normed = jnp.concatenate(parts, axis=1)
    hat = hat_ref[...]
    first = jnp.mean(d_normed, axis=-1, keepdims=True)
    second = jnp.mean(d_normed * hat, axis=-1, keepdims=True)
    d_resid = cot_ref[...].reshape(rows, C_TOK).astype(f32) + rstd * (
        d_normed - first - hat * second
    )
    q_ref[...] = nt(d_resid.astype(bf16), w_out_ref[...]).astype(bf16)

    for pair in range(PAIRS):
        half, sub = pair // 4, pair % 4
        low, high = (384 * half + v for v in WINDOWS[sub])

        def back_step(s, total):
            at = pl.multiple_of(s * tok_rows, 64)
            grads = two_heads(q_ref[pl.ds(at, tok_rows), low:high], pair)
            d_probs = nt(kv_ref[s, :, C_TOK + low : C_TOK + high], grads)
            probs = probs_ref[s, pair]
            delta = jnp.sum(probs * d_probs, axis=0, keepdims=True)
            return total + probs * (d_probs - delta)

        total = back_step(0, jnp.zeros((keys_all, 2 * tok_rows), f32))
        for s in range(1, batch):
            total = back_step(s, total)
        d_bias_f_ref[pl.ds(pair, keys_all, stride=PAIRS), :] = total
    d_bias_ref[...] = d_bias_f_ref[...].astype(bf16)


def token_stage(local, every, tokens, bias, cot, w_qkv, w_out, w_gate, w_up, w_down):
    batch, tok_rows, _ = tokens.shape
    keys_all = every.shape[1]
    rows = batch * tok_rows
    hidden = w_gate.shape[1]
    vmem = pl.BlockSpec(memory_space=pltpu.VMEM)
    hbm = pl.BlockSpec(memory_space=pl.ANY)
    return pl.pallas_call(
        token_kernel,
        in_specs=[vmem] * 5 + [hbm] * 5,
        out_specs=[vmem] * 3,
        out_shape=[
            jax.ShapeDtypeStruct((rows, C_TOK), f32),
            jax.ShapeDtypeStruct((rows, hidden), bf16),
            jax.ShapeDtypeStruct((keys_all * PAIRS, 2 * tok_rows), bf16),
        ],
        scratch_shapes=[
            pltpu.VMEM(w_qkv.shape, bf16),
            pltpu.VMEM(w_out.shape, bf16),
            pltpu.VMEM(w_gate.shape, bf16),
            pltpu.VMEM(w_up.shape, bf16),
            pltpu.VMEM(w_down.shape, bf16),
            pltpu.SemaphoreType.DMA((5,)),
            pltpu.VMEM((rows, C_TOK), bf16),
            pltpu.VMEM((batch, keys_all, 2 * C_TOK), bf16),
            pltpu.VMEM((keys_all * PAIRS, 2 * tok_rows), f32),
            pltpu.VMEM((batch, PAIRS, keys_all, 2 * tok_rows), f32),
            pltpu.VMEM((rows, C_TOK), bf16),
            pltpu.VMEM((rows, hidden), bf16),
            pltpu.VMEM((rows, hidden), bf16),
            pltpu.VMEM((rows, C_TOK), f32),
            pltpu.VMEM((keys_all * PAIRS, 2 * tok_rows), f32),
        ],
        compiler_params=pltpu.CompilerParams(vmem_limit_bytes=52 << 20),
        cost_estimate=pl.CostEstimate(
            flops=8 * 10**9, bytes_accessed=2 * 10**7, transcendentals=2 * 10**6
        ),
        name="tokens",
    )(local, every, tokens, bias, cot, w_qkv, w_out, w_gate, w_up, w_down)


def output_kernel(resid_ref, hidden_ref, w_down_ref, out_ref):
    out_ref[...] = (resid_ref[...] + nn(hidden_ref[...], w_down_ref[...])).astype(bf16)


def output_stage(resid, hidden, w_down):
    return pl.pallas_call(
        output_kernel,
        out_shape=jax.ShapeDtypeStruct(resid.shape, bf16),
        compiler_params=pltpu.CompilerParams(vmem_limit_bytes=16 << 20),
        cost_estimate=pl.CostEstimate(
            flops=6 * 10**8, bytes_accessed=5 * 10**6, transcendentals=0
        ),
        name="output",
    )(resid, hidden, w_down)


def grad_kernel(parts_ref, pair_ref, gain_ref, w_bias_ref, out_ref, pairf_ref):
    rows, keys = pair_ref.shape[0], pair_ref.shape[1]
    gain = gain_ref[...]
    for i in range(rows // 8):
        pairf_ref[8 * keys * i : 8 * keys * (i + 1), :] = (
            pair_ref[8 * i : 8 * i + 8].astype(f32).reshape(8 * keys, CZ)
        )
    even, odd = split_heads(w_bias_ref[...])
    weights = jnp.concatenate([even, odd], axis=1).astype(f32)
    weights = jnp.concatenate([weights, weights, weights], axis=0).astype(bf16)
    for j in range(keys):
        total = parts_ref[0, PAIRS * j : PAIRS * (j + 1), :].astype(f32)
        for k in range(1, parts_ref.shape[0]):
            total = total + parts_ref[k, PAIRS * j : PAIRS * (j + 1), :].astype(f32)
        high = total.astype(bf16).astype(f32)
        rest = total - high
        middle = rest.astype(bf16).astype(f32)
        stack = jnp.concatenate([high, middle, rest - middle], axis=0)
        both = nn(stack.T.astype(bf16), weights)
        scaled = (both[0:rows, 0:CZ] + both[rows : 2 * rows, CZ : 2 * CZ]) * gain
        hat, rstd = norm_rows(pairf_ref[pl.ds(j, rows, stride=keys), :])
        first = jnp.mean(scaled, axis=-1, keepdims=True)
        second = jnp.mean(scaled * hat, axis=-1, keepdims=True)
        out_ref[pl.ds(j, rows, stride=keys), :] = rstd * (scaled - first - hat * second)


def pair_back(parts, pair, pair_gain, w_bias):
    rows, keys = pair.shape[0], pair.shape[1]
    out = pl.pallas_call(
        grad_kernel,
        out_shape=jax.ShapeDtypeStruct((rows * keys, CZ), f32),
        scratch_shapes=[pltpu.VMEM((rows * keys, CZ), f32)],
        compiler_params=pltpu.CompilerParams(vmem_limit_bytes=24 << 20),
        cost_estimate=pl.CostEstimate(flops=10**8, bytes_accessed=3 * 10**6, transcendentals=0),
        name="pair_grad",
    )(parts, pair, pair_gain.reshape(1, CZ), w_bias)
    return out.reshape(rows, keys, CZ)


def body(
    atom_feats, atom_counts, atom_mask, token_single, pair, pair_gain, w_bias, w_atom_qkv,
    w_atom_out, w_embed, w_qkv, w_out, w_gate, w_up, w_down, cotangent,
):
    batch, atom_rows, _ = atom_feats.shape
    tok_rows = token_single.shape[0]
    shard, shards = lax.axis_index("tok"), lax.axis_size("tok")
    groups = lax.axis_size("samp")

    steps = [(i, i + 1) for i in range(shards - 1)]
    left = lax.ppermute(atom_feats[:, atom_rows - HALO :], "tok", steps)
    right = lax.ppermute(atom_feats[:, :HALO], "tok", [(j, i) for i, j in steps])

    local_bias = pair_bias(pair, pair_gain, w_bias)
    bias = lax.all_gather(local_bias, "samp", axis=0, tiled=True)

    reach = -(-(atom_rows + 2 * HALO) // 128) * 128
    flags = jnp.pad(atom_mask.astype(f32), (HALO, reach - atom_rows - HALO))
    flags = lax.dynamic_slice(flags, (shard * atom_rows,), (reach,)).reshape(reach // 128, 128)

    tokens, normed = atom_stage(
        atom_feats, left, right, flags, atom_counts, token_single, w_atom_qkv, w_atom_out, w_embed
    )
    every = lax.all_gather(normed, "tok", axis=1, tiled=True)
    resid, hidden, d_bias = token_stage(
        normed, every, tokens, bias, cotangent, w_qkv, w_out, w_gate, w_up, w_down
    )
    parts = d_bias.reshape(groups, -1, 2 * tok_rows)
    parts = lax.all_to_all(parts, "samp", 0, 0)
    token_out = output_stage(resid, hidden, w_down).reshape(batch, tok_rows, C_TOK)
    pair_grad = pair_back(parts, pair, pair_gain, w_bias)
    return (token_out, pair_grad)


def solution(mesh):
    in_specs = (
        P("samp", "tok", None),
        P("tok", None),
        P(),
        P("tok", None),
        P("tok", "samp", None),
        P(), P(), P(), P(), P(), P(), P(), P(), P(), P(),
        P("samp", "tok", None),
    )
    out_specs = (P("samp", "tok", None), P("tok", "samp", None))
    return jax.shard_map(body, mesh=mesh, in_specs=in_specs, out_specs=out_specs, check_vma=False)
```

```python
import functools

import jax
import jax.numpy as jnp
from jax import lax
from jax.experimental import pallas as pl
from jax.experimental.pallas import tpu as pltpu
from jax.sharding import PartitionSpec as P

C_ATOM = 128
ATOM_HEADS = 4
C_TOK = 768
HEADS = 16
ATOM_HD = 32
HD = 48
CZ = 128
HALO = 48
PAIRS = HEADS // 2
GRANT = 60 << 20
LOG2E = 1.4426950408889634

epsilon = 1e-05
f32 = jnp.float32
bf16 = jnp.bfloat16

WINDOWS = ((0, 128), (0, 256), (128, 384), (256, 384))


def nn(a, b):
    return lax.dot_general(a, b, (((1,), (0,)), ((), ())), preferred_element_type=f32)


def nt(a, b):
    return lax.dot_general(a, b, (((1,), (1,)), ((), ())), preferred_element_type=f32)


def tn(a, b):
    return lax.dot_general(a, b, (((0,), (0,)), ((), ())), preferred_element_type=f32)


def norm_rows(values):
    center = values - jnp.mean(values, axis=-1, keepdims=True)
    scale_inv = lax.rsqrt(jnp.mean(center * center, axis=-1, keepdims=True) + epsilon)
    return (center * scale_inv, scale_inv)


def iota(shape, dim):
    return lax.broadcasted_iota(jnp.int32, shape, dim)


def split_heads(w_bias):
    row, col = iota((PAIRS, HEADS), 0), iota((PAIRS, HEADS), 1)
    even = (col == 2 * row).astype(f32).astype(bf16)
    odd = (col == 2 * row + 1).astype(f32).astype(bf16)
    return nt(even, w_bias).astype(bf16), nt(odd, w_bias).astype(bf16)


def bias_kernel(pair_ref, gain_ref, w_bias_ref, out_ref, scaled_ref, stage_ref):
    rows, keys = pair_ref.shape[0], pair_ref.shape[1]
    gain = gain_ref[...]

    def norm_step(i, carry):
        block = pair_ref[pl.ds(i * 8, 8)].astype(f32).reshape(8 * keys, CZ)
        hat, unused = norm_rows(block)
        scaled_ref[pl.ds(pl.multiple_of(i * 8 * keys, 8 * keys), 8 * keys), :] = hat * gain
        return carry

    lax.fori_loop(0, rows // 8, norm_step, 0)
    even, odd = split_heads(w_bias_ref[...])
    weights = jnp.concatenate([even, odd], axis=1)
    blank = jnp.zeros((rows, CZ), bf16)
    for j in range(keys):
        block = scaled_ref[pl.ds(j, rows, stride=keys), :].astype(bf16)
        both = jnp.concatenate(
            [jnp.concatenate([block, blank], axis=1), jnp.concatenate([blank, block], axis=1)],
            axis=0,
        )
        stage_ref[pl.ds(j * PAIRS, PAIRS), :] = nt(weights, both)
    for k in range(out_ref.shape[0]):
        out_ref[k] = stage_ref[...].astype(bf16)


def pair_bias(pair, pair_gain, w_bias, copies):
    rows, keys = pair.shape[0], pair.shape[1]
    return pl.pallas_call(
        bias_kernel,
        out_shape=jax.ShapeDtypeStruct((copies, keys * PAIRS, 2 * rows), bf16),
        scratch_shapes=[
            pltpu.VMEM((rows * keys, CZ), f32),
            pltpu.VMEM((keys * PAIRS, 2 * rows), f32),
        ],
        compiler_params=pltpu.CompilerParams(vmem_limit_bytes=GRANT),
        cost_estimate=pl.CostEstimate(flops=10**7, bytes_accessed=10**7, transcendentals=0),
        name="pair_bias",
    )(pair, pair_gain.reshape(1, CZ), w_bias)


def atom_kernel(
    feats_ref, left_ref, right_ref, flags_ref, counts_ref, single_ref, w_qkv_ref, w_out_ref,
    w_embed_ref, tokens_ref, normed_ref, xn_ref, qkv_ref, scores_ref, probs_ref, mixed_ref,
    keybias_ref, onehot_ref, pooled_ref, counts_col_ref,
):
    atoms = feats_ref.shape[1]
    padded = atoms + 2 * HALO
    tok_rows = single_ref.shape[0]

    @pl.when(pl.program_id(0) == 0)
    def prepare():
        eye = iota((128, 128), 0) == iota((128, 128), 1)
        for b in range(flags_ref.shape[0]):
            row = jnp.broadcast_to(flags_ref[b : b + 1, :], (128, 128))
            col = jnp.sum(jnp.where(eye, row, 0.0), axis=1, keepdims=True)
            keybias_ref[b * 128 : (b + 1) * 128, :] = jnp.broadcast_to(
                (col - 1.0) * 1e30, (128, 128)
            )
        counts = jnp.broadcast_to(counts_ref[...].astype(f32), (tok_rows, tok_rows))
        sub, lane = iota((tok_rows, tok_rows), 0), iota((tok_rows, tok_rows), 1)
        start = jnp.sum(jnp.where(lane < sub, counts, 0.0), axis=1, keepdims=True)
        own = jnp.sum(jnp.where(lane == sub, counts, 0.0), axis=1, keepdims=True)
        counts_col_ref[...] = jnp.broadcast_to(own, (tok_rows, 128))
        pos = iota((tok_rows, 256), 1).astype(f32)
        for g in range(atoms // 256):
            at = pos + float(g * 256)
            hit = jnp.where((at >= start) & (at < start + own), 1.0, 0.0).astype(bf16)
            onehot_ref[g] = jnp.concatenate([hit, hit], axis=1)
        probs_ref[...] = jnp.zeros_like(probs_ref)

    xn_ref[0:HALO, :] = norm_rows(left_ref[0].astype(f32))[0].astype(bf16)
    xn_ref[atoms + HALO : padded, :] = norm_rows(right_ref[0].astype(f32))[0].astype(bf16)

    def norm_step(i, carry):
        at = pl.multiple_of(i * 256, 256)
        block = feats_ref[0, pl.ds(at, 256), :].astype(f32)
        xn_ref[pl.ds(HALO + at, 256), :] = norm_rows(block)[0].astype(bf16)
        return carry

    lax.fori_loop(0, atoms // 256, norm_step, 0)

    chunk = padded // 4
    w_qkv = w_qkv_ref[...]
    for i in range(4):
        qkv_ref[i * chunk : (i + 1) * chunk, :] = nn(
            xn_ref[i * chunk : (i + 1) * chunk, :], w_qkv
        ).astype(bf16)

    lane = iota((32, 128), 1)
    head_of = lane // ATOM_HD
    head_mask = [(head_of == h).astype(f32).astype(bf16) for h in range(ATOM_HEADS)]
    own_atom = (lane % 32) == iota((32, 128), 0)
    factor = ATOM_HD ** (-0.5) * LOG2E
    pairs = atoms // 64
    per = 4

    def score_step(i, carry):
        for k in range(per):
            pair = i * per + k
            base = pl.multiple_of(pair * 64, 64)
            queries = qkv_ref[pl.ds(base + HALO, 64), 0:C_ATOM]
            spread = jnp.concatenate(
                [
                    queries[32 * w : 32 * w + 32] * head_mask[h]
                    for w in range(2)
                    for h in range(ATOM_HEADS)
                ],
                axis=0,
            )
            scores_ref[pair] = nt(qkv_ref[pl.ds(base, 160), C_ATOM : 2 * C_ATOM], spread)
        return carry

    lax.fori_loop(0, pairs // per, score_step, 0)

    def softmax_step(i, carry):
        for k in range(2):
            pair = i * 2 + k
            base = pl.multiple_of(pair * 64, 64)
            for w in range(2):
                keybias = keybias_ref[pl.ds(base + 32 * w, 128), :]
                keybias = jnp.concatenate(
                    [keybias[0:48], jnp.where(own_atom, 0.0, keybias[48:80]), keybias[80:128]],
                    axis=0,
                )
                scores = scores_ref[pair, 32 * w : 32 * w + 128, 128 * w : 128 * w + 128] + keybias
                expo = jnp.exp2((scores - jnp.max(scores, axis=0, keepdims=True)) * factor)
                weights = expo * (1.0 / jnp.sum(expo, axis=0, keepdims=True))
                probs_ref[pair, 32 * w : 32 * w + 128, 128 * w : 128 * w + 128] = weights.astype(
                    bf16
                )
        return carry

    lax.fori_loop(0, pairs // 2, softmax_step, 0)

    def value_step(i, carry):
        for k in range(per):
            pair = i * per + k
            base = pl.multiple_of(pair * 64, 64)
            part = tn(probs_ref[pair], qkv_ref[pl.ds(base, 160), 2 * C_ATOM : 3 * C_ATOM])
            mixes = []
            for w in range(2):
                mix = part[128 * w : 128 * w + 32]
                for h in range(1, ATOM_HEADS):
                    low = 128 * w + 32 * h
                    mix = jnp.where(head_of == h, part[low : low + 32], mix)
                mixes.append(mix.astype(bf16))
            mixed_ref[pl.ds(base, 64), :] = jnp.concatenate(mixes, axis=0)
        return carry

    lax.fori_loop(0, pairs // per, value_step, 0)

    pooled_ref[...] = jnp.zeros_like(pooled_ref)

    def embed_step(g, carry):
        base = pl.multiple_of(g * 256, 256)
        feats = feats_ref[0, pl.ds(base, 256), :].astype(f32)
        updated = (feats + nn(mixed_ref[pl.ds(base, 256), :], w_out_ref[...])).astype(bf16)
        embedded = jnp.maximum(nn(updated, w_embed_ref[...]), 0.0)
        high = embedded.astype(bf16)
        low = (embedded - high.astype(f32)).astype(bf16)
        pooled_ref[...] += nn(onehot_ref[g], jnp.concatenate([high, low], axis=0))
        return carry

    lax.fori_loop(0, atoms // 256, embed_step, 0)
    counts = counts_col_ref[:, 0:1]
    tokens = pooled_ref[...] / counts + single_ref[...].astype(f32)
    tokens_ref[0] = tokens
    normed_ref[0] = norm_rows(tokens)[0].astype(bf16)


def atom_stage(first, batch, feats, left, right, flags, counts, single, w_qkv, w_out, w_embed):
    atoms = feats.shape[1]
    tok_rows = single.shape[0]
    padded = atoms + 2 * HALO
    pairs = atoms // 64
    of_sample = lambda rows, cols: pl.BlockSpec((1, rows, cols), lambda s: (s + first, 0, 0))
    by_sample = lambda rows, cols: pl.BlockSpec((1, rows, cols), lambda s: (s, 0, 0))
    whole = lambda a: pl.BlockSpec(a.shape, lambda s: (0,) * a.ndim)
    return pl.pallas_call(
        atom_kernel,
        grid=(batch,),
        in_specs=[
            of_sample(atoms, C_ATOM), of_sample(HALO, C_ATOM), of_sample(HALO, C_ATOM),
            whole(flags), whole(counts), whole(single), whole(w_qkv), whole(w_out), whole(w_embed),
        ],
        out_specs=[by_sample(tok_rows, C_TOK), by_sample(tok_rows, C_TOK)],
        out_shape=[
            jax.ShapeDtypeStruct((batch, tok_rows, C_TOK), f32),
            jax.ShapeDtypeStruct((batch, tok_rows, C_TOK), bf16),
        ],
        scratch_shapes=[
            pltpu.VMEM((padded, C_ATOM), bf16),
            pltpu.VMEM((padded, 3 * C_ATOM), bf16),
            pltpu.VMEM((pairs, 160, 256), f32),
            pltpu.VMEM((pairs, 160, 256), bf16),
            pltpu.VMEM((atoms, C_ATOM), bf16),
            pltpu.VMEM((flags.shape[0] * 128, 128), f32),
            pltpu.VMEM((atoms // 256, tok_rows, 512), bf16),
            pltpu.VMEM((tok_rows, C_TOK), f32),
            pltpu.VMEM((tok_rows, 128), f32),
        ],
        compiler_params=pltpu.CompilerParams(vmem_limit_bytes=GRANT),
        cost_estimate=pl.CostEstimate(
            flops=10**10, bytes_accessed=4 * 10**6, transcendentals=3 * 10**6
        ),
        name="atoms",
    )(feats, left, right, flags, counts, single, w_qkv, w_out, w_embed)


def head_masks(rows):
    masks = []
    for pair in range(4):
        low, high = WINDOWS[pair]
        lane = iota((rows, high - low), 1) + low
        first = 2 * pair * HD
        masks.append(
            [(lane >= first + HD * k) & (lane < first + HD * (k + 1)) for k in range(2)]
        )
    return masks


def two_heads(block, masks):
    blank = jnp.zeros_like(block)
    return jnp.concatenate([jnp.where(mask, block, blank) for mask in masks], axis=0)


def attend_kernel(
    *refs, sources,
):
    piece_refs = refs[: len(sources)]
    bias_ref, w_qkv_hbm, att_ref, probs_ref, values_ref = refs[len(sources) : len(sources) + 5]
    w_qkv_ref, sems, all_ref, qk_ref, biasf_ref = refs[len(sources) + 5 :]
    batch, tok_rows = piece_refs[0].shape[0], piece_refs[0].shape[1]
    keys_all = tok_rows * len(sources)
    copies = [
        pltpu.make_async_copy(
            w_qkv_hbm.at[:, pl.ds(C_TOK * i, C_TOK)], w_qkv_ref.at[i], sems.at[i]
        )
        for i in range(3)
    ]
    for copy in copies:
        copy.start()
    here = lax.axis_index("tok")
    count = len(sources)
    for piece, (shift, flip) in zip(piece_refs, sources):
        owner = lax.rem(here + shift, count)
        if flip:
            owner = owner + 1 - 2 * lax.rem(owner, 2)
        at = pl.multiple_of(owner * tok_rows, tok_rows)
        for s in range(batch):
            all_ref[s, pl.ds(at, tok_rows), :] = piece[s]
    biasf_ref[...] = bias_ref[...].astype(f32)
    copies[0].wait()
    own = piece_refs[0][...].reshape(batch * tok_rows, C_TOK)
    queries_ref = att_ref
    for n in range(3):
        queries_ref[:, 256 * n : 256 * n + 256] = nn(
            own, w_qkv_ref[0, :, 256 * n : 256 * n + 256]
        ).astype(bf16)
    copies[1].wait()
    copies[2].wait()

    def project_step(n, carry):
        at = pl.multiple_of(n * 256, 256)
        for s in range(batch):
            qk_ref[s, :, pl.ds(at, 256)] = nn(
                all_ref[s], w_qkv_ref[1, :, pl.ds(at, 256)]
            ).astype(bf16)
            values_ref[s, :, pl.ds(at, 256)] = nn(
                all_ref[s], w_qkv_ref[2, :, pl.ds(at, 256)]
            ).astype(bf16)
        return carry

    lax.fori_loop(0, C_TOK // 256, project_step, 0)
    masks = head_masks(tok_rows)
    factor = HD ** (-0.5)

    def attend_step(s, carry):
        at = pl.multiple_of(s * tok_rows, 64)
        for half in range(2):
            lanes = [jnp.zeros((tok_rows, 128), f32) for _ in range(3)]
            for sub in range(4):
                pair = half * 4 + sub
                low, high = (384 * half + v for v in WINDOWS[sub])
                queries = two_heads(queries_ref[pl.ds(at, tok_rows), low:high], masks[sub])
                scores = nt(qk_ref[s, :, low:high], queries) * factor
                scores = scores + biasf_ref[pl.ds(pair, keys_all, stride=PAIRS), :]
                expo = jnp.exp(scores - jnp.max(scores, axis=0, keepdims=True))
                probs = expo * (1.0 / jnp.sum(expo, axis=0, keepdims=True))
                probs_ref[s, pair] = probs
                part = tn(probs.astype(bf16), values_ref[s, :, low:high])
                first, second = masks[sub]
                mix = jnp.where(first, part[0:tok_rows], 0.0)
                mix = jnp.where(second, part[tok_rows : 2 * tok_rows], mix)
                for t in range((high - low) // 128):
                    tile = WINDOWS[sub][0] // 128 + t
                    lanes[tile] = lanes[tile] + mix[:, 128 * t : 128 * t + 128]
            att_ref[pl.ds(at, tok_rows), 384 * half : 384 * half + 384] = jnp.concatenate(
                lanes, axis=1
            ).astype(bf16)
        return carry

    lax.fori_loop(0, batch, attend_step, 0)


def attend_stage(pieces, sources, bias, w_qkv):
    batch, tok_rows, _ = pieces[0].shape
    keys_all = tok_rows * len(pieces)
    vmem = pl.BlockSpec(memory_space=pltpu.VMEM)
    hbm = pl.BlockSpec(memory_space=pl.ANY)
    return pl.pallas_call(
        functools.partial(attend_kernel, sources=sources),
        in_specs=[vmem] * (len(pieces) + 1) + [hbm],
        out_specs=[vmem] * 3,
        out_shape=[
            jax.ShapeDtypeStruct((batch * tok_rows, C_TOK), bf16),
            jax.ShapeDtypeStruct((batch, PAIRS, keys_all, 2 * tok_rows), f32),
            jax.ShapeDtypeStruct((batch, keys_all, C_TOK), bf16),
        ],
        scratch_shapes=[
            pltpu.VMEM((3, C_TOK, C_TOK), bf16),
            pltpu.SemaphoreType.DMA((3,)),
            pltpu.VMEM((batch, keys_all, C_TOK), bf16),
            pltpu.VMEM((batch, keys_all, C_TOK), bf16),
            pltpu.VMEM((keys_all * PAIRS, 2 * tok_rows), f32),
        ],
        compiler_params=pltpu.CompilerParams(vmem_limit_bytes=GRANT),
        cost_estimate=pl.CostEstimate(
            flops=4 * 10**9, bytes_accessed=10**7, transcendentals=10**6
        ),
        name="attend",
    )(*pieces, bias, w_qkv)


def token_kernel(*refs, halves):
    tokens_refs, att_refs = refs[0:halves], refs[halves : 2 * halves]
    probs_hbm, values_hbm = refs[2 * halves : 3 * halves], refs[3 * halves : 4 * halves]
    cot_ref, w_out_hbm, w_gate_hbm, w_up_hbm, w_down_hbm = refs[4 * halves : 4 * halves + 5]
    resid_ref, hidden_ref, d_bias_ref = refs[4 * halves + 5 : 4 * halves + 8]
    (
        w_out_ref, w_gate_ref, w_up_ref, w_down_ref, probs_ref, values_ref, sems, grads_ref,
        d_gate_ref, d_up_ref, hat_ref, d_bias_f_ref,
    ) = refs[4 * halves + 8 :]
    batch, tok_rows = cot_ref.shape[0], cot_ref.shape[1]
    keys_all = values_ref.shape[1]
    rows = batch * tok_rows
    each = batch // halves
    moves = [
        (w_out_hbm, w_out_ref), (w_gate_hbm, w_gate_ref), (w_up_hbm, w_up_ref),
        (w_down_hbm, w_down_ref),
    ]
    for i in range(halves):
        moves.append((values_hbm[i], values_ref.at[pl.ds(i * each, each)]))
        moves.append((probs_hbm[i], probs_ref.at[pl.ds(i * each, each)]))
    copies = [pltpu.make_async_copy(s, d, sems.at[i]) for i, (s, d) in enumerate(moves)]
    for copy in copies:
        copy.start()
    cot = cot_ref[...].reshape(rows, C_TOK)
    copies[0].wait()
    for i in range(halves):
        part = slice(i * each * tok_rows, (i + 1) * each * tok_rows)
        resid_ref[part, :] = tokens_refs[i][...].reshape(each * tok_rows, C_TOK) + nn(
            att_refs[i][...], w_out_ref[...]
        )
    hat, rstd = norm_rows(resid_ref[...])
    hat_ref[...] = hat
    grads_ref[...] = hat.astype(bf16)
    copies[1].wait()
    copies[2].wait()
    copies[3].wait()

    def transition_step(n, carry):
        at = pl.multiple_of(n * 256, 256)
        shaped = grads_ref[...]
        gate = nn(shaped, w_gate_ref[:, pl.ds(at, 256)])
        up = nn(shaped, w_up_ref[:, pl.ds(at, 256)])
        d_hidden = nt(cot_ref[...].reshape(rows, C_TOK), w_down_ref[pl.ds(at, 256), :])
        sig = 1.0 / (1.0 + jnp.exp(-gate))
        act = gate * sig
        hidden_ref[:, pl.ds(at, 256)] = (act * up).astype(bf16)
        d_gate_ref[:, pl.ds(at, 256)] = (
            d_hidden * up * sig * (1.0 + gate * (1.0 - sig))
        ).astype(bf16)
        d_up_ref[:, pl.ds(at, 256)] = (d_hidden * act).astype(bf16)
        return carry

    lax.fori_loop(0, w_gate_ref.shape[1] // 256, transition_step, 0)
    parts = []
    for n in range(C_TOK // 256):
        parts.append(
            nt(d_gate_ref[...], w_gate_ref[256 * n : 256 * n + 256, :])
            + nt(d_up_ref[...], w_up_ref[256 * n : 256 * n + 256, :])
        )
    d_normed = jnp.concatenate(parts, axis=1)
    hat = hat_ref[...]
    first = jnp.mean(d_normed, axis=-1, keepdims=True)
    second = jnp.mean(d_normed * hat, axis=-1, keepdims=True)
    d_resid = cot.astype(f32) + rstd * (d_normed - first - hat * second)
    grads_ref[...] = nt(d_resid.astype(bf16), w_out_ref[...]).astype(bf16)
    for copy in copies[4:]:
        copy.wait()
    masks = head_masks(tok_rows)
    for pair in range(PAIRS):
        half, sub = pair // 4, pair % 4
        low, high = (384 * half + v for v in WINDOWS[sub])
        total = jnp.zeros((keys_all, 2 * tok_rows), f32)
        for s in range(batch):
            grads = two_heads(
                grads_ref[s * tok_rows : (s + 1) * tok_rows, low:high], masks[sub]
            )
            d_probs = nt(values_ref[s, :, low:high], grads)
            probs = probs_ref[s, pair]
            delta = jnp.sum(probs * d_probs, axis=0, keepdims=True)
            total = total + probs * (d_probs - delta)
        d_bias_f_ref[pl.ds(pair, keys_all, stride=PAIRS), :] = total
    d_bias_ref[...] = d_bias_f_ref[...].astype(bf16)


def token_stage(tokens, att, probs, values, cot, w_out, w_gate, w_up, w_down):
    halves = len(tokens)
    batch, tok_rows, _ = cot.shape
    keys_all = values[0].shape[1]
    rows = batch * tok_rows
    hidden = w_gate.shape[1]
    vmem = pl.BlockSpec(memory_space=pltpu.VMEM)
    hbm = pl.BlockSpec(memory_space=pl.ANY)
    return pl.pallas_call(
        functools.partial(token_kernel, halves=halves),
        in_specs=[vmem] * (2 * halves) + [hbm] * (2 * halves) + [vmem] + [hbm] * 4,
        out_specs=[vmem] * 3,
        out_shape=[
            jax.ShapeDtypeStruct((rows, C_TOK), f32),
            jax.ShapeDtypeStruct((rows, hidden), bf16),
            jax.ShapeDtypeStruct((keys_all * PAIRS, 2 * tok_rows), bf16),
        ],
        scratch_shapes=[
            pltpu.VMEM(w_out.shape, bf16),
            pltpu.VMEM(w_gate.shape, bf16),
            pltpu.VMEM(w_up.shape, bf16),
            pltpu.VMEM(w_down.shape, bf16),
            pltpu.VMEM((batch, PAIRS, keys_all, 2 * tok_rows), f32),
            pltpu.VMEM((batch, keys_all, C_TOK), bf16),
            pltpu.SemaphoreType.DMA((4 + 2 * halves,)),
            pltpu.VMEM((rows, C_TOK), bf16),
            pltpu.VMEM((rows, hidden), bf16),
            pltpu.VMEM((rows, hidden), bf16),
            pltpu.VMEM((rows, C_TOK), f32),
            pltpu.VMEM((keys_all * PAIRS, 2 * tok_rows), f32),
        ],
        compiler_params=pltpu.CompilerParams(vmem_limit_bytes=GRANT),
        cost_estimate=pl.CostEstimate(
            flops=8 * 10**9, bytes_accessed=2 * 10**7, transcendentals=10**6
        ),
        name="tokens",
    )(*tokens, *att, *probs, *values, cot, w_out, w_gate, w_up, w_down)


def output_kernel(resid_ref, hidden_ref, w_down_ref, out_ref):
    out_ref[...] = (resid_ref[...] + nn(hidden_ref[...], w_down_ref[...])).astype(bf16)


def output_stage(resid, hidden, w_down):
    return pl.pallas_call(
        output_kernel,
        out_shape=jax.ShapeDtypeStruct(resid.shape, bf16),
        compiler_params=pltpu.CompilerParams(vmem_limit_bytes=GRANT),
        cost_estimate=pl.CostEstimate(
            flops=6 * 10**8, bytes_accessed=5 * 10**6, transcendentals=0
        ),
        name="output",
    )(resid, hidden, w_down)


def grad_kernel(parts_ref, pair_ref, gain_ref, w_bias_ref, out_ref, pairf_ref):
    rows, keys = pair_ref.shape[0], pair_ref.shape[1]
    gain = gain_ref[...]
    for i in range(rows // 8):
        pairf_ref[8 * keys * i : 8 * keys * (i + 1), :] = (
            pair_ref[8 * i : 8 * i + 8].astype(f32).reshape(8 * keys, CZ)
        )
    even, odd = split_heads(w_bias_ref[...])
    weights = jnp.concatenate([even, odd], axis=1).astype(f32)
    weights = jnp.concatenate([weights, weights, weights], axis=0).astype(bf16)
    for j in range(keys):
        total = parts_ref[0, PAIRS * j : PAIRS * (j + 1), :].astype(f32)
        for k in range(1, parts_ref.shape[0]):
            total = total + parts_ref[k, PAIRS * j : PAIRS * (j + 1), :].astype(f32)
        high = total.astype(bf16).astype(f32)
        rest = total - high
        middle = rest.astype(bf16).astype(f32)
        stack = jnp.concatenate([high, middle, rest - middle], axis=0)
        both = nn(stack.T.astype(bf16), weights)
        scaled = (both[0:rows, 0:CZ] + both[rows : 2 * rows, CZ : 2 * CZ]) * gain
        hat, rstd = norm_rows(pairf_ref[pl.ds(j, rows, stride=keys), :])
        first = jnp.mean(scaled, axis=-1, keepdims=True)
        second = jnp.mean(scaled * hat, axis=-1, keepdims=True)
        out_ref[pl.ds(j, rows, stride=keys), :] = rstd * (scaled - first - hat * second)


def pair_back(parts, pair, pair_gain, w_bias):
    rows, keys = pair.shape[0], pair.shape[1]
    out = pl.pallas_call(
        grad_kernel,
        out_shape=jax.ShapeDtypeStruct((rows * keys, CZ), f32),
        scratch_shapes=[pltpu.VMEM((rows * keys, CZ), f32)],
        compiler_params=pltpu.CompilerParams(vmem_limit_bytes=GRANT),
        cost_estimate=pl.CostEstimate(flops=10**8, bytes_accessed=3 * 10**6, transcendentals=0),
        name="pair_grad",
    )(parts, pair, pair_gain.reshape(1, CZ), w_bias)
    return out.reshape(rows, keys, CZ)


def gather_tokens(normed):
    count = lax.axis_size("tok")
    swap = [(i, i ^ 1) for i in range(count)]
    pieces, sources = [normed], [(0, False)]
    for k in range(1, count // 2):
        steps = [(i, (i + 2 * k) % count) for i in range(count)]
        pieces.append(lax.ppermute(normed, "tok", steps))
        sources.append((count - 2 * k, False))
    for piece, (shift, _) in list(zip(pieces, sources)):
        pieces.append(lax.ppermute(piece, "tok", swap))
        sources.append((shift, True))
    return pieces, tuple(sources)


def body(
    atom_feats, atom_counts, atom_mask, token_single, pair, pair_gain, w_bias, w_atom_qkv,
    w_atom_out, w_embed, w_qkv, w_out, w_gate, w_up, w_down, cotangent,
):
    batch, atom_rows, _ = atom_feats.shape
    tok_rows = token_single.shape[0]
    shard, shards = lax.axis_index("tok"), lax.axis_size("tok")
    groups = lax.axis_size("samp")

    steps = [(i, i + 1) for i in range(shards - 1)]
    left = lax.ppermute(atom_feats[:, atom_rows - HALO :], "tok", steps)
    right = lax.ppermute(atom_feats[:, :HALO], "tok", [(j, i) for i, j in steps])

    local_bias = pair_bias(pair, pair_gain, w_bias, groups)
    bias = lax.all_to_all(local_bias, "samp", 0, 0).reshape(-1, 2 * tok_rows)

    reach = -(-(atom_rows + 2 * HALO) // 128) * 128
    flags = jnp.pad(atom_mask.astype(f32), (HALO, reach - atom_rows - HALO))
    flags = lax.dynamic_slice(flags, (shard * atom_rows,), (reach,)).reshape(reach // 128, 128)
    flags, local_bias = lax.optimization_barrier((flags, local_bias))

    halves = 2
    each = batch // halves
    tokens, att, probs, values = [], [], [], []
    gathered = []
    for i in range(halves):
        tok, normed = atom_stage(
            i * each, each, atom_feats, left, right, flags, atom_counts, token_single, w_atom_qkv,
            w_atom_out, w_embed,
        )
        tokens.append(tok)
        gathered.append(gather_tokens(normed))
    for pieces, sources in gathered:
        for kept, new in zip((att, probs, values), attend_stage(pieces, sources, bias, w_qkv)):
            kept.append(new)
    resid, hidden, d_bias = token_stage(
        tokens, att, probs, values, cotangent, w_out, w_gate, w_up, w_down
    )
    parts = d_bias.reshape(groups, -1, 2 * tok_rows)
    parts = lax.all_to_all(parts, "samp", 0, 0)
    token_out = output_stage(resid, hidden, w_down).reshape(batch, tok_rows, C_TOK)
    pair_grad = pair_back(parts, pair, pair_gain, w_bias)
    return (token_out, pair_grad)


def solution(mesh):
    in_specs = (
        P("samp", "tok", None),
        P("tok", None),
        P(),
        P("tok", None),
        P("tok", "samp", None),
        P(), P(), P(), P(), P(), P(), P(), P(), P(), P(),
        P("samp", "tok", None),
    )
    out_specs = (P("samp", "tok", None), P("tok", "samp", None))
    return jax.shard_map(body, mesh=mesh, in_specs=in_specs, out_specs=out_specs, check_vma=False)
```

```python
import functools

import jax
import jax.numpy as jnp
from jax import lax
from jax.experimental import pallas as pl
from jax.experimental.pallas import tpu as pltpu
from jax.sharding import PartitionSpec as P

C_ATOM = 128
ATOM_HEADS = 4
C_TOK = 768
HEADS = 16
ATOM_HD = 32
HD = 48
CZ = 128
HALO = 48
PAIRS = HEADS // 2
GRANT = 60 << 20
LOG2E = 1.4426950408889634

epsilon = 1e-05
f32 = jnp.float32
bf16 = jnp.bfloat16

WINDOWS = ((0, 128), (0, 256), (128, 384), (256, 384))


def nn(a, b):
    return lax.dot_general(a, b, (((1,), (0,)), ((), ())), preferred_element_type=f32)


def nt(a, b):
    return lax.dot_general(a, b, (((1,), (1,)), ((), ())), preferred_element_type=f32)


def tn(a, b):
    return lax.dot_general(a, b, (((0,), (0,)), ((), ())), preferred_element_type=f32)


def norm_rows(values):
    center = values - jnp.mean(values, axis=-1, keepdims=True)
    scale_inv = lax.rsqrt(jnp.mean(center * center, axis=-1, keepdims=True) + epsilon)
    return (center * scale_inv, scale_inv)


def iota(shape, dim):
    return lax.broadcasted_iota(jnp.int32, shape, dim)


def pick_heads(parity):
    row, col = iota((PAIRS, HEADS), 0), iota((PAIRS, HEADS), 1)
    return (col == 2 * row + parity).astype(f32).astype(bf16)


def split_heads(w_bias_t):
    return [nn(pick_heads(parity), w_bias_t) for parity in range(2)]


def bias_kernel(pair_ref, gain_ref, w_bias_ref, out_ref, scaled_ref, stage_ref):
    rows, keys = pair_ref.shape[0], pair_ref.shape[1]
    gain = gain_ref[...]

    def norm_step(i, carry):
        block = pair_ref[pl.ds(i * 8, 8)].astype(f32).reshape(8 * keys, CZ)
        hat, unused = norm_rows(block)
        scaled_ref[pl.ds(pl.multiple_of(i * 8 * keys, 8 * keys), 8 * keys), :] = hat * gain
        return carry

    lax.fori_loop(0, rows // 8, norm_step, 0)
    weights = jnp.concatenate(split_heads(w_bias_ref[...]), axis=1).astype(bf16)
    blank = jnp.zeros((rows, CZ), bf16)
    for j in range(keys):
        block = scaled_ref[pl.ds(j, rows, stride=keys), :].astype(bf16)
        both = jnp.concatenate(
            [jnp.concatenate([block, blank], axis=1), jnp.concatenate([blank, block], axis=1)],
            axis=0,
        )
        stage_ref[pl.ds(j * PAIRS, PAIRS), :] = nt(weights, both)
    out_ref[...] = stage_ref[...].astype(bf16)


def pair_bias(pair, pair_gain, w_bias_t):
    rows, keys = pair.shape[0], pair.shape[1]
    return pl.pallas_call(
        bias_kernel,
        out_shape=jax.ShapeDtypeStruct((keys * PAIRS, 2 * rows), bf16),
        scratch_shapes=[
            pltpu.VMEM((rows * keys, CZ), f32),
            pltpu.VMEM((keys * PAIRS, 2 * rows), f32),
        ],
        compiler_params=pltpu.CompilerParams(vmem_limit_bytes=GRANT),
        cost_estimate=pl.CostEstimate(flops=10**7, bytes_accessed=10**7, transcendentals=0),
        name="pair_bias",
    )(pair, pair_gain.reshape(1, CZ), w_bias_t)


def atom_kernel(
    feats_ref, left_ref, right_ref, flags_ref, counts_ref, single_ref, w_qkv_ref, w_out_ref,
    w_embed_ref, tokens_ref, normed_ref, xn_ref, qkv_ref, scores_a, scores_b, probs_a, probs_b,
    mixed_ref, updated_ref, split_ref, keybias_ref, onehot_ref, counts_col_ref,
):
    atoms = feats_ref.shape[1]
    padded = atoms + 2 * HALO
    tok_rows = single_ref.shape[0]

    @pl.when(pl.program_id(0) == 0)
    def prepare():
        eye = iota((128, 128), 0) == iota((128, 128), 1)
        for b in range(flags_ref.shape[0]):
            row = jnp.broadcast_to(flags_ref[b : b + 1, :], (128, 128))
            col = jnp.sum(jnp.where(eye, row, 0.0), axis=1, keepdims=True)
            keybias_ref[b * 128 : (b + 1) * 128, :] = jnp.broadcast_to(
                (col - 1.0) * 1e30, (128, 128)
            )
        counts = jnp.broadcast_to(counts_ref[...].astype(f32), (tok_rows, tok_rows))
        sub, lane = iota((tok_rows, tok_rows), 0), iota((tok_rows, tok_rows), 1)
        start = jnp.sum(jnp.where(lane < sub, counts, 0.0), axis=1, keepdims=True)
        own = jnp.sum(jnp.where(lane == sub, counts, 0.0), axis=1, keepdims=True)
        counts_col_ref[...] = jnp.broadcast_to(own, (tok_rows, 128))
        pos = iota((tok_rows, 256), 1).astype(f32)
        for g in range(atoms // 256):
            at = pos + float(g * 256)
            hit = jnp.where((at >= start) & (at < start + own), 1.0, 0.0).astype(bf16)
            onehot_ref[g] = jnp.concatenate([hit, hit], axis=1)
        probs_a[...] = jnp.zeros_like(probs_a)
        probs_b[...] = jnp.zeros_like(probs_b)

    xn_ref[0:HALO, :] = norm_rows(left_ref[0].astype(f32))[0].astype(bf16)
    xn_ref[atoms + HALO : padded, :] = norm_rows(right_ref[0].astype(f32))[0].astype(bf16)

    for i in range(atoms // 256):
        block = feats_ref[0, 256 * i : 256 * i + 256, :].astype(f32)
        xn_ref[HALO + 256 * i : HALO + 256 * i + 256, :] = norm_rows(block)[0].astype(bf16)
    chunk = padded // 4
    w_qkv = w_qkv_ref[...]
    for i in range(4):
        qkv_ref[i * chunk : (i + 1) * chunk, :] = nn(
            xn_ref[i * chunk : (i + 1) * chunk, :], w_qkv
        ).astype(bf16)

    head_of = iota((32, 128), 1) // ATOM_HD
    head_mask = [(head_of == h).astype(f32).astype(bf16) for h in range(ATOM_HEADS)]
    own_atom = (iota((32, 128), 1) % 32) == iota((32, 128), 0)
    factor = ATOM_HD ** (-0.5) * LOG2E
    groups = atoms // 128

    def score_step(group, to_ref):
        for k in range(2):
            base = pl.multiple_of(group * 128 + 64 * k, 64)
            queries = qkv_ref[pl.ds(base + HALO, 64), 0:C_ATOM]
            spread = jnp.concatenate(
                [
                    queries[32 * w : 32 * w + 32] * head_mask[h]
                    for w in range(2)
                    for h in range(ATOM_HEADS)
                ],
                axis=0,
            )
            to_ref[k] = nt(qkv_ref[pl.ds(base, 160), C_ATOM : 2 * C_ATOM], spread)

    def softmax_step(group, from_ref, to_ref):
        for k in range(2):
            base = pl.multiple_of(group * 128 + 64 * k, 64)
            for w in range(2):
                keybias = keybias_ref[pl.ds(base + 32 * w, 128), :]
                keybias = jnp.concatenate(
                    [keybias[0:48], jnp.where(own_atom, 0.0, keybias[48:80]), keybias[80:128]],
                    axis=0,
                )
                scores = from_ref[k, 32 * w : 32 * w + 128, 128 * w : 128 * w + 128] + keybias
                expo = jnp.exp2((scores - jnp.max(scores, axis=0, keepdims=True)) * factor)
                weights = expo * (1.0 / jnp.sum(expo, axis=0, keepdims=True))
                to_ref[k, 32 * w : 32 * w + 128, 128 * w : 128 * w + 128] = weights.astype(bf16)

    def value_step(group, from_ref):
        for k in range(2):
            base = pl.multiple_of(group * 128 + 64 * k, 64)
            part = tn(from_ref[k], qkv_ref[pl.ds(base, 160), 2 * C_ATOM : 3 * C_ATOM])
            mixes = []
            for w in range(2):
                mix = part[128 * w : 128 * w + 32]
                for h in range(1, ATOM_HEADS):
                    low = 128 * w + 32 * h
                    mix = jnp.where(head_of == h, part[low : low + 32], mix)
                mixes.append(mix.astype(bf16))
            mixed_ref[pl.ds(base, 64), :] = jnp.concatenate(mixes, axis=0)

    score_step(0, scores_a)

    def window_step(i, carry):
        even, odd = 2 * i, 2 * i + 1
        score_step(odd, scores_b)
        softmax_step(even, scores_a, probs_a)
        value_step(jnp.maximum(even - 1, 0), probs_b)
        score_step(jnp.minimum(odd + 1, groups - 1), scores_a)
        softmax_step(odd, scores_b, probs_b)
        value_step(even, probs_a)
        return carry

    lax.fori_loop(0, groups // 2, window_step, 0)
    value_step(groups - 1, probs_b)

    w_out = w_out_ref[...]
    for g in range(atoms // 256):
        part = slice(256 * g, 256 * g + 256)
        feats = feats_ref[0, part, :].astype(f32)
        updated_ref[part, :] = (feats + nn(mixed_ref[part, :], w_out)).astype(bf16)
    pooled = jnp.zeros((tok_rows, C_TOK), f32)
    for g in range(atoms // 256):
        embedded = jnp.maximum(
            nn(updated_ref[256 * g : 256 * g + 256, :], w_embed_ref[...]), 0.0
        )
        high = embedded.astype(bf16)
        split_ref[g, 0:256, :] = high
        split_ref[g, 256:512, :] = (embedded - high.astype(f32)).astype(bf16)
        pooled = pooled + nn(onehot_ref[g], split_ref[g])
    tokens = pooled / counts_col_ref[:, 0:1] + single_ref[...].astype(f32)
    tokens_ref[0] = tokens
    normed_ref[0] = norm_rows(tokens)[0].astype(bf16)


def atom_stage(first, batch, feats, left, right, flags, counts, single, w_qkv, w_out, w_embed):
    atoms = feats.shape[1]
    tok_rows = single.shape[0]
    padded = atoms + 2 * HALO
    of_sample = lambda rows, cols: pl.BlockSpec((1, rows, cols), lambda s: (s + first, 0, 0))
    by_sample = lambda rows, cols: pl.BlockSpec((1, rows, cols), lambda s: (s, 0, 0))
    whole = lambda a: pl.BlockSpec(a.shape, lambda s: (0,) * a.ndim)
    return pl.pallas_call(
        atom_kernel,
        grid=(batch,),
        in_specs=[
            of_sample(atoms, C_ATOM), of_sample(HALO, C_ATOM), of_sample(HALO, C_ATOM),
            whole(flags), whole(counts), whole(single), whole(w_qkv), whole(w_out), whole(w_embed),
        ],
        out_specs=[by_sample(tok_rows, C_TOK), by_sample(tok_rows, C_TOK)],
        out_shape=[
            jax.ShapeDtypeStruct((batch, tok_rows, C_TOK), f32),
            jax.ShapeDtypeStruct((batch, tok_rows, C_TOK), bf16),
        ],
        scratch_shapes=[
            pltpu.VMEM((padded, C_ATOM), bf16),
            pltpu.VMEM((padded, 3 * C_ATOM), bf16),
            pltpu.VMEM((2, 160, 256), f32),
            pltpu.VMEM((2, 160, 256), f32),
            pltpu.VMEM((2, 160, 256), bf16),
            pltpu.VMEM((2, 160, 256), bf16),
            pltpu.VMEM((atoms, C_ATOM), bf16),
            pltpu.VMEM((atoms, C_ATOM), bf16),
            pltpu.VMEM((atoms // 256, 512, C_TOK), bf16),
            pltpu.VMEM((flags.shape[0] * 128, 128), f32),
            pltpu.VMEM((atoms // 256, tok_rows, 512), bf16),
            pltpu.VMEM((tok_rows, 128), f32),
        ],
        compiler_params=pltpu.CompilerParams(vmem_limit_bytes=GRANT),
        cost_estimate=pl.CostEstimate(
            flops=10**10, bytes_accessed=4 * 10**6, transcendentals=3 * 10**6
        ),
        name="atoms",
    )(feats, left, right, flags, counts, single, w_qkv, w_out, w_embed)


def head_masks(rows):
    masks = []
    for pair in range(4):
        low, high = WINDOWS[pair]
        lane = iota((rows, high - low), 1) + low
        first = 2 * pair * HD
        masks.append(
            [(lane >= first + HD * k) & (lane < first + HD * (k + 1)) for k in range(2)]
        )
    return masks


def two_heads(block, masks):
    blank = jnp.zeros_like(block)
    return jnp.concatenate([jnp.where(mask, block, blank) for mask in masks], axis=0)


def attend_kernel(
    *refs, count, groups,
):
    piece_refs, bias_refs = refs[:count], refs[count : count + groups]
    w_qkv_hbm, att_ref, probs_ref, values_ref = refs[count + groups : count + groups + 4]
    w_qkv_ref, sems, all_ref, qk_ref, biasf_ref = refs[count + groups + 4 :]
    batch, tok_rows = piece_refs[0].shape[0], piece_refs[0].shape[1]
    keys_all = tok_rows * count
    copies = [
        pltpu.make_async_copy(
            w_qkv_hbm.at[:, pl.ds(C_TOK * i, C_TOK)], w_qkv_ref.at[i], sems.at[i]
        )
        for i in range(3)
    ]
    for copy in copies:
        copy.start()
    here = lax.axis_index("tok")
    for k, piece in enumerate(piece_refs):
        at = pl.multiple_of((here ^ k) * tok_rows, tok_rows)
        for s in range(batch):
            all_ref[s, pl.ds(at, tok_rows), :] = piece[s]
    here = lax.axis_index("samp")
    for k, piece in enumerate(bias_refs):
        size = piece.shape[0]
        biasf_ref[pl.ds(pl.multiple_of((here ^ k) * size, size), size), :] = piece[...].astype(f32)
    copies[0].wait()
    own = piece_refs[0][...].reshape(batch * tok_rows, C_TOK)
    queries_ref = att_ref
    for n in range(3):
        queries_ref[:, 256 * n : 256 * n + 256] = nn(
            own, w_qkv_ref[0, :, 256 * n : 256 * n + 256]
        ).astype(bf16)
    copies[1].wait()
    copies[2].wait()

    def project_step(n, carry):
        at = pl.multiple_of(n * 256, 256)
        for s in range(batch):
            qk_ref[s, :, pl.ds(at, 256)] = nn(
                all_ref[s], w_qkv_ref[1, :, pl.ds(at, 256)]
            ).astype(bf16)
            values_ref[s, :, pl.ds(at, 256)] = nn(
                all_ref[s], w_qkv_ref[2, :, pl.ds(at, 256)]
            ).astype(bf16)
        return carry

    lax.fori_loop(0, C_TOK // 256, project_step, 0)
    masks = head_masks(tok_rows)
    factor = HD ** (-0.5)

    def attend_step(s, carry):
        at = pl.multiple_of(s * tok_rows, 64)
        for half in range(2):
            lanes = [jnp.zeros((tok_rows, 128), f32) for _ in range(3)]
            for sub in range(4):
                pair = half * 4 + sub
                low, high = (384 * half + v for v in WINDOWS[sub])
                queries = two_heads(queries_ref[pl.ds(at, tok_rows), low:high], masks[sub])
                scores = nt(qk_ref[s, :, low:high], queries) * factor
                scores = scores + biasf_ref[pl.ds(pair, keys_all, stride=PAIRS), :]
                expo = jnp.exp(scores - jnp.max(scores, axis=0, keepdims=True))
                probs = expo * (1.0 / jnp.sum(expo, axis=0, keepdims=True))
                probs_ref[s, pair] = probs
                part = tn(probs.astype(bf16), values_ref[s, :, low:high])
                first, second = masks[sub]
                mix = jnp.where(first, part[0:tok_rows], 0.0)
                mix = jnp.where(second, part[tok_rows : 2 * tok_rows], mix)
                for t in range((high - low) // 128):
                    tile = WINDOWS[sub][0] // 128 + t
                    lanes[tile] = lanes[tile] + mix[:, 128 * t : 128 * t + 128]
            att_ref[pl.ds(at, tok_rows), 384 * half : 384 * half + 384] = jnp.concatenate(
                lanes, axis=1
            ).astype(bf16)
        return carry

    lax.fori_loop(0, batch, attend_step, 0)


def attend_stage(pieces, bias, w_qkv):
    batch, tok_rows, _ = pieces[0].shape
    keys_all = tok_rows * len(pieces)
    vmem = pl.BlockSpec(memory_space=pltpu.VMEM)
    hbm = pl.BlockSpec(memory_space=pl.ANY)
    return pl.pallas_call(
        functools.partial(attend_kernel, count=len(pieces), groups=len(bias)),
        in_specs=[vmem] * (len(pieces) + len(bias)) + [hbm],
        out_specs=[vmem] * 3,
        out_shape=[
            jax.ShapeDtypeStruct((batch * tok_rows, C_TOK), bf16),
            jax.ShapeDtypeStruct((batch, PAIRS, keys_all, 2 * tok_rows), f32),
            jax.ShapeDtypeStruct((batch, keys_all, C_TOK), bf16),
        ],
        scratch_shapes=[
            pltpu.VMEM((3, C_TOK, C_TOK), bf16),
            pltpu.SemaphoreType.DMA((3,)),
            pltpu.VMEM((batch, keys_all, C_TOK), bf16),
            pltpu.VMEM((batch, keys_all, C_TOK), bf16),
            pltpu.VMEM((keys_all * PAIRS, 2 * tok_rows), f32),
        ],
        compiler_params=pltpu.CompilerParams(vmem_limit_bytes=GRANT),
        cost_estimate=pl.CostEstimate(
            flops=4 * 10**9, bytes_accessed=10**7, transcendentals=10**6
        ),
        name="attend",
    )(*pieces, *bias, w_qkv)


def token_kernel(*refs, halves, groups):
    tokens_refs, att_refs = refs[0:halves], refs[halves : 2 * halves]
    probs_hbm, values_hbm = refs[2 * halves : 3 * halves], refs[3 * halves : 4 * halves]
    cot_ref, w_out_hbm, w_gate_hbm, w_up_hbm, w_down_hbm = refs[4 * halves : 4 * halves + 5]
    resid_ref, hidden_ref = refs[4 * halves + 5 : 4 * halves + 7]
    block_refs = refs[4 * halves + 7 : 4 * halves + 7 + groups]
    (
        w_out_ref, w_gate_ref, w_up_ref, w_down_ref, probs_ref, values_ref, sems, grads_ref,
        d_gate_ref, d_up_ref, hat_ref, d_bias_f_ref,
    ) = refs[4 * halves + 7 + groups :]
    batch, tok_rows = cot_ref.shape[0], cot_ref.shape[1]
    keys_all = values_ref.shape[1]
    rows = batch * tok_rows
    each = batch // halves
    moves = [
        (w_out_hbm, w_out_ref), (w_gate_hbm, w_gate_ref), (w_up_hbm, w_up_ref),
        (w_down_hbm, w_down_ref),
    ]
    for i in range(halves):
        moves.append((values_hbm[i], values_ref.at[pl.ds(i * each, each)]))
        moves.append((probs_hbm[i], probs_ref.at[pl.ds(i * each, each)]))
    copies = [pltpu.make_async_copy(s, d, sems.at[i]) for i, (s, d) in enumerate(moves)]
    for copy in copies:
        copy.start()
    cot = cot_ref[...].reshape(rows, C_TOK)
    copies[0].wait()
    for i in range(halves):
        part = slice(i * each * tok_rows, (i + 1) * each * tok_rows)
        resid_ref[part, :] = tokens_refs[i][...].reshape(each * tok_rows, C_TOK) + nn(
            att_refs[i][...], w_out_ref[...]
        )
    hat, rstd = norm_rows(resid_ref[...])
    hat_ref[...] = hat
    grads_ref[...] = hat.astype(bf16)
    copies[1].wait()
    copies[2].wait()
    copies[3].wait()

    def transition_step(n, carry):
        at = pl.multiple_of(n * 256, 256)
        shaped = grads_ref[...]
        gate = nn(shaped, w_gate_ref[:, pl.ds(at, 256)])
        up = nn(shaped, w_up_ref[:, pl.ds(at, 256)])
        d_hidden = nt(cot_ref[...].reshape(rows, C_TOK), w_down_ref[pl.ds(at, 256), :])
        sig = 1.0 / (1.0 + jnp.exp(-gate))
        act = gate * sig
        hidden_ref[:, pl.ds(at, 256)] = (act * up).astype(bf16)
        d_gate_ref[:, pl.ds(at, 256)] = (
            d_hidden * up * sig * (1.0 + gate * (1.0 - sig))
        ).astype(bf16)
        d_up_ref[:, pl.ds(at, 256)] = (d_hidden * act).astype(bf16)
        return carry

    lax.fori_loop(0, w_gate_ref.shape[1] // 256, transition_step, 0)
    parts = []
    for n in range(C_TOK // 256):
        parts.append(
            nt(d_gate_ref[...], w_gate_ref[256 * n : 256 * n + 256, :])
            + nt(d_up_ref[...], w_up_ref[256 * n : 256 * n + 256, :])
        )
    d_normed = jnp.concatenate(parts, axis=1)
    hat = hat_ref[...]
    first = jnp.mean(d_normed, axis=-1, keepdims=True)
    second = jnp.mean(d_normed * hat, axis=-1, keepdims=True)
    d_resid = cot.astype(f32) + rstd * (d_normed - first - hat * second)
    grads_ref[...] = nt(d_resid.astype(bf16), w_out_ref[...]).astype(bf16)
    for copy in copies[4:]:
        copy.wait()
    masks = head_masks(tok_rows)
    for pair in range(PAIRS):
        half, sub = pair // 4, pair % 4
        low, high = (384 * half + v for v in WINDOWS[sub])
        total = jnp.zeros((keys_all, 2 * tok_rows), f32)
        for s in range(batch):
            grads = two_heads(
                grads_ref[s * tok_rows : (s + 1) * tok_rows, low:high], masks[sub]
            )
            d_probs = nt(values_ref[s, :, low:high], grads)
            probs = probs_ref[s, pair]
            delta = jnp.sum(probs * d_probs, axis=0, keepdims=True)
            total = total + probs * (d_probs - delta)
        d_bias_f_ref[pl.ds(pair, keys_all, stride=PAIRS), :] = total
    here = lax.axis_index("samp")
    for k, block in enumerate(block_refs):
        size = block.shape[0]
        at = pl.multiple_of((here ^ k) * size, size)
        block[...] = d_bias_f_ref[pl.ds(at, size), :].astype(bf16)


def token_stage(groups, tokens, att, probs, values, cot, w_out, w_gate, w_up, w_down):
    halves = len(tokens)
    batch, tok_rows, _ = cot.shape
    keys_all = values[0].shape[1]
    rows = batch * tok_rows
    hidden = w_gate.shape[1]
    vmem = pl.BlockSpec(memory_space=pltpu.VMEM)
    hbm = pl.BlockSpec(memory_space=pl.ANY)
    return pl.pallas_call(
        functools.partial(token_kernel, halves=halves, groups=groups),
        in_specs=[vmem] * (2 * halves) + [hbm] * (2 * halves) + [vmem] + [hbm] * 4,
        out_specs=[vmem] * (2 + groups),
        out_shape=[
            jax.ShapeDtypeStruct((rows, C_TOK), f32),
            jax.ShapeDtypeStruct((rows, hidden), bf16),
        ]
        + [jax.ShapeDtypeStruct((keys_all * PAIRS // groups, 2 * tok_rows), bf16)] * groups,
        scratch_shapes=[
            pltpu.VMEM(w_out.shape, bf16),
            pltpu.VMEM(w_gate.shape, bf16),
            pltpu.VMEM(w_up.shape, bf16),
            pltpu.VMEM(w_down.shape, bf16),
            pltpu.VMEM((batch, PAIRS, keys_all, 2 * tok_rows), f32),
            pltpu.VMEM((batch, keys_all, C_TOK), bf16),
            pltpu.SemaphoreType.DMA((4 + 2 * halves,)),
            pltpu.VMEM((rows, C_TOK), bf16),
            pltpu.VMEM((rows, hidden), bf16),
            pltpu.VMEM((rows, hidden), bf16),
            pltpu.VMEM((rows, C_TOK), f32),
            pltpu.VMEM((keys_all * PAIRS, 2 * tok_rows), f32),
        ],
        compiler_params=pltpu.CompilerParams(vmem_limit_bytes=GRANT),
        cost_estimate=pl.CostEstimate(
            flops=8 * 10**9, bytes_accessed=2 * 10**7, transcendentals=10**6
        ),
        name="tokens",
    )(*tokens, *att, *probs, *values, cot, w_out, w_gate, w_up, w_down)


def output_kernel(
    resid_ref, hidden_ref, w_down_ref, pair_ref, out_ref, hat_ref, rstd_ref, pairf_ref
):
    out_ref[...] = (resid_ref[...] + nn(hidden_ref[...], w_down_ref[...])).astype(bf16)
    rows, keys = pair_ref.shape[0], pair_ref.shape[1]
    for i in range(rows // 8):
        pairf_ref[8 * keys * i : 8 * keys * (i + 1), :] = (
            pair_ref[8 * i : 8 * i + 8].astype(f32).reshape(8 * keys, CZ)
        )

    def norm_step(j, carry):
        hat, rstd = norm_rows(pairf_ref[pl.ds(j, rows, stride=keys), :])
        at = pl.multiple_of(j * rows, rows)
        hat_ref[pl.ds(at, rows), :] = hat
        rstd_ref[pl.ds(at, rows), :] = jnp.broadcast_to(rstd, (rows, CZ))
        return carry

    lax.fori_loop(0, keys, norm_step, 0, unroll=4)


def output_stage(resid, hidden, w_down, pair):
    rows, keys = pair.shape[0], pair.shape[1]
    return pl.pallas_call(
        output_kernel,
        out_shape=[jax.ShapeDtypeStruct(resid.shape, bf16)]
        + [jax.ShapeDtypeStruct((rows * keys, CZ), f32)] * 2,
        scratch_shapes=[pltpu.VMEM((rows * keys, CZ), f32)],
        compiler_params=pltpu.CompilerParams(vmem_limit_bytes=GRANT),
        cost_estimate=pl.CostEstimate(
            flops=10**9, bytes_accessed=8 * 10**6, transcendentals=0
        ),
        name="output",
    )(resid, hidden, w_down, pair)


def grad_kernel(*refs, groups):
    part_refs = refs[:groups]
    hat_ref, rstd_ref, gain_ref, w_bias_ref, out_ref, total_ref = refs[groups:]
    keys = part_refs[0].shape[0] // PAIRS
    rows = hat_ref.shape[0] // keys
    total = part_refs[0][...].astype(f32)
    for part in part_refs[1:]:
        total = total + part[...].astype(f32)
    total_ref[...] = total
    weights = jnp.concatenate(split_heads(w_bias_ref[...]), axis=0) * gain_ref[...]
    weights = weights - jnp.mean(weights, axis=-1, keepdims=True)
    weights = jnp.concatenate([weights[0:PAIRS], weights[PAIRS:HEADS]], axis=1)
    w_high = weights.astype(bf16).astype(f32)
    w_middle = (weights - w_high).astype(bf16).astype(f32)
    w_low = weights - w_high - w_middle
    weights = jnp.concatenate([w_high, w_middle, w_low, w_high, w_middle, w_high], axis=0)
    weights = weights.astype(bf16)
    for j in range(keys):
        total = total_ref[PAIRS * j : PAIRS * (j + 1), :]
        high = total.astype(bf16).astype(f32)
        middle = (total - high).astype(bf16).astype(f32)
        low = total - high - middle
        stack = jnp.concatenate([high, high, high, middle, middle, low], axis=0)
        both = nn(stack.T.astype(bf16), weights)
        scaled = both[0:rows, 0:CZ] + both[rows : 2 * rows, CZ : 2 * CZ]
        hat = hat_ref[rows * j : rows * (j + 1), :]
        second = jnp.mean(scaled * hat, axis=-1, keepdims=True)
        out_ref[pl.ds(j, rows, stride=keys), :] = rstd_ref[rows * j : rows * (j + 1), :] * (
            scaled - hat * second
        )


def pair_back(parts, hat, rstd, pair_gain, w_bias_t):
    keys = parts[0].shape[0] // PAIRS
    rows = hat.shape[0] // keys
    out = pl.pallas_call(
        functools.partial(grad_kernel, groups=len(parts)),
        out_shape=jax.ShapeDtypeStruct((rows * keys, CZ), f32),
        scratch_shapes=[pltpu.VMEM((keys * PAIRS, 2 * rows), f32)],
        compiler_params=pltpu.CompilerParams(vmem_limit_bytes=GRANT),
        cost_estimate=pl.CostEstimate(flops=10**8, bytes_accessed=4 * 10**6, transcendentals=0),
        name="pair_grad",
    )(*parts, hat, rstd, pair_gain.reshape(1, CZ), w_bias_t)
    return out.reshape(rows, keys, CZ)


def swap(values, axis, k):
    return lax.ppermute(values, axis, [(i, i ^ k) for i in range(lax.axis_size(axis))])


def gather(values, axis):
    far = range(lax.axis_size(axis) - 1, 0, -1)
    return [values] + [swap(values, axis, k) for k in far][::-1]


def body(
    atom_feats, atom_counts, atom_mask, token_single, pair, pair_gain, w_bias, w_atom_qkv,
    w_atom_out, w_embed, w_qkv, w_out, w_gate, w_up, w_down, cotangent,
):
    batch, atom_rows, _ = atom_feats.shape
    tok_rows = token_single.shape[0]
    shard, shards = lax.axis_index("tok"), lax.axis_size("tok")
    groups = lax.axis_size("samp")

    steps = [(i, i + 1) for i in range(shards - 1)]
    left = lax.ppermute(atom_feats[:, atom_rows - HALO :], "tok", steps)
    right = lax.ppermute(atom_feats[:, :HALO], "tok", [(j, i) for i, j in steps])

    w_bias_t = w_bias.T
    bias = gather(pair_bias(pair, pair_gain, w_bias_t), "samp")

    reach = -(-(atom_rows + 2 * HALO) // 128) * 128
    flags = jnp.pad(atom_mask.astype(f32), (HALO, reach - atom_rows - HALO))
    flags = lax.dynamic_slice(flags, (shard * atom_rows,), (reach,)).reshape(reach // 128, 128)
    flags, bias[0] = lax.optimization_barrier((flags, bias[0]))

    halves = 2
    each = batch // halves
    tokens, att, probs, values = [], [], [], []
    gathered = []
    for i in range(halves):
        tok, normed = atom_stage(
            i * each, each, atom_feats, left, right, flags, atom_counts, token_single, w_atom_qkv,
            w_atom_out, w_embed,
        )
        tokens.append(tok)
        gathered.append(gather(normed, "tok"))
    for pieces in gathered:
        for kept, new in zip((att, probs, values), attend_stage(pieces, bias, w_qkv)):
            kept.append(new)
    resid, hidden, *blocks = token_stage(
        groups, tokens, att, probs, values, cotangent, w_out, w_gate, w_up, w_down
    )
    far = range(groups - 1, 0, -1)
    parts = [blocks[0]] + [swap(blocks[k], "samp", k) for k in far]
    token_out, hat, rstd = output_stage(resid, hidden, w_down, pair)
    pair_grad = pair_back(parts, hat, rstd, pair_gain, w_bias_t)
    token_out = token_out.reshape(batch, tok_rows, C_TOK)
    return (token_out, pair_grad)


def solution(mesh):
    in_specs = (
        P("samp", "tok", None),
        P("tok", None),
        P(),
        P("tok", None),
        P("tok", "samp", None),
        P(), P(), P(), P(), P(), P(), P(), P(), P(), P(),
        P("samp", "tok", None),
    )
    out_specs = (P("samp", "tok", None), P("tok", "samp", None))
    return jax.shard_map(body, mesh=mesh, in_specs=in_specs, out_specs=out_specs, check_vma=False)
```

```python
import functools

import jax
import jax.numpy as jnp
from jax import lax
from jax.experimental import pallas as pl
from jax.experimental.pallas import tpu as pltpu
from jax.sharding import PartitionSpec as P

C_ATOM = 128
ATOM_HEADS = 4
C_TOK = 768
HEADS = 16
ATOM_HD = 32
HD = 48
CZ = 128
HALO = 48
PAIRS = HEADS // 2
GRANT = 60 << 20
LOG2E = 1.4426950408889634

epsilon = 1e-05
f32 = jnp.float32
bf16 = jnp.bfloat16

WINDOWS = ((0, 128), (0, 256), (128, 384), (256, 384))


def nn(a, b):
    return lax.dot_general(a, b, (((1,), (0,)), ((), ())), preferred_element_type=f32)


def nt(a, b):
    return lax.dot_general(a, b, (((1,), (1,)), ((), ())), preferred_element_type=f32)


def tn(a, b):
    return lax.dot_general(a, b, (((0,), (0,)), ((), ())), preferred_element_type=f32)


def norm_rows(values):
    center = values - jnp.mean(values, axis=-1, keepdims=True)
    scale_inv = lax.rsqrt(jnp.mean(center * center, axis=-1, keepdims=True) + epsilon)
    return (center * scale_inv, scale_inv)


def iota(shape, dim):
    return lax.broadcasted_iota(jnp.int32, shape, dim)


def pick_heads(parity):
    row, col = iota((PAIRS, HEADS), 0), iota((PAIRS, HEADS), 1)
    return (col == 2 * row + parity).astype(f32).astype(bf16)


def split_heads(w_bias_t):
    return [nn(pick_heads(parity), w_bias_t) for parity in range(2)]


def bias_kernel(pair_ref, gain_ref, w_bias_ref, out_ref, scaled_ref, stage_ref):
    rows, keys = pair_ref.shape[0], pair_ref.shape[1]
    gain = gain_ref[...]

    def norm_step(i, carry):
        block = pair_ref[pl.ds(i * 8, 8)].astype(f32).reshape(8 * keys, CZ)
        hat, unused = norm_rows(block)
        scaled_ref[pl.ds(pl.multiple_of(i * 8 * keys, 8 * keys), 8 * keys), :] = hat * gain
        return carry

    lax.fori_loop(0, rows // 8, norm_step, 0, unroll=True)
    weights = jnp.concatenate(split_heads(w_bias_ref[...]), axis=1).astype(bf16)
    blank = jnp.zeros((rows, CZ), bf16)
    for j in range(keys):
        block = scaled_ref[pl.ds(j, rows, stride=keys), :].astype(bf16)
        both = jnp.concatenate(
            [jnp.concatenate([block, blank], axis=1), jnp.concatenate([blank, block], axis=1)],
            axis=0,
        )
        stage_ref[pl.ds(j * PAIRS, PAIRS), :] = nt(weights, both)
    for k in range(out_ref.shape[0]):
        out_ref[k] = stage_ref[...].astype(bf16)


def pair_bias(pair, pair_gain, w_bias_t, copies):
    rows, keys = pair.shape[0], pair.shape[1]
    return pl.pallas_call(
        bias_kernel,
        out_shape=jax.ShapeDtypeStruct((copies, keys * PAIRS, 2 * rows), bf16),
        scratch_shapes=[
            pltpu.VMEM((rows * keys, CZ), f32),
            pltpu.VMEM((keys * PAIRS, 2 * rows), f32),
        ],
        compiler_params=pltpu.CompilerParams(vmem_limit_bytes=GRANT),
        cost_estimate=pl.CostEstimate(flops=10**7, bytes_accessed=10**7, transcendentals=0),
        name="pair_bias",
    )(pair, pair_gain.reshape(1, CZ), w_bias_t)


def atom_kernel(
    feats_ref, left_ref, right_ref, flags_ref, counts_ref, single_ref, w_qkv_ref, w_out_ref,
    w_embed_ref, tokens_ref, normed_ref, xn_ref, qkv_ref, scores_a, scores_b, probs_a, probs_b,
    mixed_ref, updated_ref, split_ref, keybias_ref, onehot_ref, counts_col_ref,
):
    atoms = feats_ref.shape[1]
    padded = atoms + 2 * HALO
    tok_rows = single_ref.shape[0]

    @pl.when(pl.program_id(0) == 0)
    def prepare():
        eye = iota((128, 128), 0) == iota((128, 128), 1)
        for b in range(flags_ref.shape[0]):
            row = jnp.broadcast_to(flags_ref[b : b + 1, :], (128, 128))
            col = jnp.sum(jnp.where(eye, row, 0.0), axis=1, keepdims=True)
            keybias_ref[b * 128 : (b + 1) * 128, :] = jnp.broadcast_to(
                (col - 1.0) * 1e30, (128, 128)
            )
        counts = jnp.broadcast_to(counts_ref[...].astype(f32), (tok_rows, tok_rows))
        sub, lane = iota((tok_rows, tok_rows), 0), iota((tok_rows, tok_rows), 1)
        start = jnp.sum(jnp.where(lane < sub, counts, 0.0), axis=1, keepdims=True)
        own = jnp.sum(jnp.where(lane == sub, counts, 0.0), axis=1, keepdims=True)
        counts_col_ref[...] = jnp.broadcast_to(own, (tok_rows, 128))
        pos = iota((tok_rows, 256), 1).astype(f32)
        for g in range(atoms // 256):
            at = pos + float(g * 256)
            hit = jnp.where((at >= start) & (at < start + own), 1.0, 0.0).astype(bf16)
            onehot_ref[g] = jnp.concatenate([hit, hit], axis=1)
        probs_a[...] = jnp.zeros_like(probs_a)
        probs_b[...] = jnp.zeros_like(probs_b)

    xn_ref[0:HALO, :] = norm_rows(left_ref[0].astype(f32))[0].astype(bf16)
    xn_ref[atoms + HALO : padded, :] = norm_rows(right_ref[0].astype(f32))[0].astype(bf16)

    for i in range(atoms // 256):
        block = feats_ref[0, 256 * i : 256 * i + 256, :].astype(f32)
        xn_ref[HALO + 256 * i : HALO + 256 * i + 256, :] = norm_rows(block)[0].astype(bf16)
    chunk = padded // 4
    w_qkv = w_qkv_ref[...]
    for i in range(4):
        qkv_ref[i * chunk : (i + 1) * chunk, :] = nn(
            xn_ref[i * chunk : (i + 1) * chunk, :], w_qkv
        ).astype(bf16)

    head_of = iota((32, 128), 1) // ATOM_HD
    head_mask = [(head_of == h).astype(f32).astype(bf16) for h in range(ATOM_HEADS)]
    own_atom = (iota((32, 128), 1) % 32) == iota((32, 128), 0)
    factor = ATOM_HD ** (-0.5) * LOG2E
    groups = atoms // 128

    def score_step(group, to_ref):
        for k in range(2):
            base = pl.multiple_of(group * 128 + 64 * k, 64)
            queries = qkv_ref[pl.ds(base + HALO, 64), 0:C_ATOM]
            spread = jnp.concatenate(
                [
                    queries[32 * w : 32 * w + 32] * head_mask[h]
                    for w in range(2)
                    for h in range(ATOM_HEADS)
                ],
                axis=0,
            )
            to_ref[k] = nt(qkv_ref[pl.ds(base, 160), C_ATOM : 2 * C_ATOM], spread)

    def softmax_step(group, from_ref, to_ref):
        for k in range(2):
            base = pl.multiple_of(group * 128 + 64 * k, 64)
            for w in range(2):
                keybias = keybias_ref[pl.ds(base + 32 * w, 128), :]
                keybias = jnp.concatenate(
                    [keybias[0:48], jnp.where(own_atom, 0.0, keybias[48:80]), keybias[80:128]],
                    axis=0,
                )
                scores = from_ref[k, 32 * w : 32 * w + 128, 128 * w : 128 * w + 128] + keybias
                expo = jnp.exp2((scores - jnp.max(scores, axis=0, keepdims=True)) * factor)
                weights = expo * (1.0 / jnp.sum(expo, axis=0, keepdims=True))
                to_ref[k, 32 * w : 32 * w + 128, 128 * w : 128 * w + 128] = weights.astype(bf16)

    def value_step(group, from_ref):
        for k in range(2):
            base = pl.multiple_of(group * 128 + 64 * k, 64)
            part = tn(from_ref[k], qkv_ref[pl.ds(base, 160), 2 * C_ATOM : 3 * C_ATOM])
            mixes = []
            for w in range(2):
                mix = part[128 * w : 128 * w + 32]
                for h in range(1, ATOM_HEADS):
                    low = 128 * w + 32 * h
                    mix = jnp.where(head_of == h, part[low : low + 32], mix)
                mixes.append(mix.astype(bf16))
            mixed_ref[pl.ds(base, 64), :] = jnp.concatenate(mixes, axis=0)

    score_step(0, scores_a)

    def window_step(i, carry):
        even, odd = 2 * i, 2 * i + 1
        score_step(odd, scores_b)
        softmax_step(even, scores_a, probs_a)
        value_step(jnp.maximum(even - 1, 0), probs_b)
        score_step(jnp.minimum(odd + 1, groups - 1), scores_a)
        softmax_step(odd, scores_b, probs_b)
        value_step(even, probs_a)
        return carry

    lax.fori_loop(0, groups // 2, window_step, 0)
    value_step(groups - 1, probs_b)

    w_out = w_out_ref[...]
    for g in range(atoms // 256):
        part = slice(256 * g, 256 * g + 256)
        feats = feats_ref[0, part, :].astype(f32)
        updated_ref[part, :] = (feats + nn(mixed_ref[part, :], w_out)).astype(bf16)
    pooled = jnp.zeros((tok_rows, C_TOK), f32)
    for g in range(atoms // 256):
        embedded = jnp.maximum(
            nn(updated_ref[256 * g : 256 * g + 256, :], w_embed_ref[...]), 0.0
        )
        high = embedded.astype(bf16)
        split_ref[g, 0:256, :] = high
        split_ref[g, 256:512, :] = (embedded - high.astype(f32)).astype(bf16)
        pooled = pooled + nn(onehot_ref[g], split_ref[g])
    tokens = pooled / counts_col_ref[:, 0:1] + single_ref[...].astype(f32)
    tokens_ref[0] = tokens
    normed_ref[0] = norm_rows(tokens)[0].astype(bf16)


def atom_stage(first, batch, feats, left, right, flags, counts, single, w_qkv, w_out, w_embed):
    atoms = feats.shape[1]
    tok_rows = single.shape[0]
    padded = atoms + 2 * HALO
    of_sample = lambda rows, cols: pl.BlockSpec((1, rows, cols), lambda s: (s + first, 0, 0))
    by_sample = lambda rows, cols: pl.BlockSpec((1, rows, cols), lambda s: (s, 0, 0))
    whole = lambda a: pl.BlockSpec(a.shape, lambda s: (0,) * a.ndim)
    return pl.pallas_call(
        atom_kernel,
        grid=(batch,),
        in_specs=[
            of_sample(atoms, C_ATOM), of_sample(HALO, C_ATOM), of_sample(HALO, C_ATOM),
            whole(flags), whole(counts), whole(single), whole(w_qkv), whole(w_out), whole(w_embed),
        ],
        out_specs=[by_sample(tok_rows, C_TOK), by_sample(tok_rows, C_TOK)],
        out_shape=[
            jax.ShapeDtypeStruct((batch, tok_rows, C_TOK), f32),
            jax.ShapeDtypeStruct((batch, tok_rows, C_TOK), bf16),
        ],
        scratch_shapes=[
            pltpu.VMEM((padded, C_ATOM), bf16),
            pltpu.VMEM((padded, 3 * C_ATOM), bf16),
            pltpu.VMEM((2, 160, 256), f32),
            pltpu.VMEM((2, 160, 256), f32),
            pltpu.VMEM((2, 160, 256), bf16),
            pltpu.VMEM((2, 160, 256), bf16),
            pltpu.VMEM((atoms, C_ATOM), bf16),
            pltpu.VMEM((atoms, C_ATOM), bf16),
            pltpu.VMEM((atoms // 256, 512, C_TOK), bf16),
            pltpu.VMEM((flags.shape[0] * 128, 128), f32),
            pltpu.VMEM((atoms // 256, tok_rows, 512), bf16),
            pltpu.VMEM((tok_rows, 128), f32),
        ],
        compiler_params=pltpu.CompilerParams(vmem_limit_bytes=GRANT),
        cost_estimate=pl.CostEstimate(
            flops=10**10, bytes_accessed=4 * 10**6, transcendentals=3 * 10**6
        ),
        name="atoms",
    )(feats, left, right, flags, counts, single, w_qkv, w_out, w_embed)


def head_masks(rows):
    masks = []
    for pair in range(4):
        low, high = WINDOWS[pair]
        lane = iota((rows, high - low), 1) + low
        first = 2 * pair * HD
        masks.append(
            [(lane >= first + HD * k) & (lane < first + HD * (k + 1)) for k in range(2)]
        )
    return masks


def two_heads(block, masks):
    blank = jnp.zeros_like(block)
    return jnp.concatenate([jnp.where(mask, block, blank) for mask in masks], axis=0)


def project(piece_refs, w_qkv_ref, copies, all_ref, queries_ref, keys_ref, values_ref):
    batch, tok_rows = piece_refs[0].shape[0], piece_refs[0].shape[1]
    here = lax.axis_index("tok")
    for k, piece in enumerate(piece_refs):
        at = pl.multiple_of((here ^ k) * tok_rows, tok_rows)
        for s in range(batch):
            all_ref[s, pl.ds(at, tok_rows), :] = piece[s]
    own = piece_refs[0][...].reshape(batch * tok_rows, C_TOK)
    copies[0].wait()
    for n in range(0, C_TOK, 256):
        queries_ref[:, n : n + 256] = nn(own, w_qkv_ref[0, :, n : n + 256]).astype(bf16)
    for which, to_ref in ((1, keys_ref), (2, values_ref)):
        copies[which].wait()
        for n in range(0, C_TOK, 256):
            for s in range(batch):
                to_ref[s, :, n : n + 256] = nn(
                    all_ref[s], w_qkv_ref[which, :, n : n + 256]
                ).astype(bf16)


def windows(pair):
    low, high = WINDOWS[pair % 4]
    return 384 * (pair // 4) + low, 384 * (pair // 4) + high


def attend(bias_ref, queries_ref, keys_ref, values_ref, probs_ref, att_ref):
    batch, keys_all = keys_ref.shape[0], keys_ref.shape[1]
    tok_rows = queries_ref.shape[0] // batch
    masks = head_masks(tok_rows)
    factor = HD ** (-0.5)

    def sample_step(s, carry):
        at = pl.multiple_of(s * tok_rows, 64)
        for pair in range(PAIRS):
            low, high = windows(pair)
            queries = two_heads(queries_ref[pl.ds(at, tok_rows), low:high], masks[pair % 4])
            probs_ref[s, pair] = nt(keys_ref[s, :, low:high], queries)
        for pair in range(PAIRS):
            scores = probs_ref[s, pair] * factor
            scores = scores + bias_ref[pl.ds(pair, keys_all, stride=PAIRS), :]
            expo = jnp.exp(scores - jnp.max(scores, axis=0, keepdims=True))
            probs_ref[s, pair] = expo * (1.0 / jnp.sum(expo, axis=0, keepdims=True))
        lanes = [jnp.zeros((tok_rows, 128), f32) for _ in range(C_TOK // 128)]
        for pair in range(PAIRS):
            low, high = windows(pair)
            part = tn(probs_ref[s, pair].astype(bf16), values_ref[s, :, low:high])
            first, second = masks[pair % 4]
            mix = jnp.where(first, part[0:tok_rows], 0.0)
            mix = jnp.where(second, part[tok_rows : 2 * tok_rows], mix)
            for t in range((high - low) // 128):
                lanes[low // 128 + t] = lanes[low // 128 + t] + mix[:, 128 * t : 128 * t + 128]
        for t in range(C_TOK // 128):
            att_ref[pl.ds(at, tok_rows), 128 * t : 128 * t + 128] = lanes[t].astype(bf16)
        return carry

    lax.fori_loop(0, batch, sample_step, 0)


def start_all(moves, sems):
    copies = [pltpu.make_async_copy(src, dst, sems.at[i]) for i, (src, dst) in enumerate(moves)]
    for copy in copies:
        copy.start()
    return copies


def qkv_moves(w_qkv_hbm, w_qkv_ref):
    return [
        (w_qkv_hbm.at[:, pl.ds(C_TOK * i, C_TOK)], w_qkv_ref.at[i]) for i in range(3)
    ]


def attend_kernel(*refs, count):
    piece_refs = refs[:count]
    (
        bias_ref, w_qkv_hbm, att_ref, probs_ref, values_ref, w_qkv_ref, sems, all_ref, queries_ref,
        keys_ref, biasf_ref,
    ) = refs[count:]
    copies = start_all(qkv_moves(w_qkv_hbm, w_qkv_ref), sems)
    biasf_ref[...] = bias_ref[...].astype(f32)
    project(piece_refs, w_qkv_ref, copies, all_ref, queries_ref, keys_ref, values_ref)
    attend(biasf_ref, queries_ref, keys_ref, values_ref, probs_ref, att_ref)


def attend_scratch(batch, tok_rows, keys_all):
    return [
        pltpu.VMEM((batch, keys_all, C_TOK), bf16),
        pltpu.VMEM((batch * tok_rows, C_TOK), bf16),
        pltpu.VMEM((batch, keys_all, C_TOK), bf16),
        pltpu.VMEM((keys_all * PAIRS, 2 * tok_rows), f32),
    ]


def attend_stage(pieces, bias, w_qkv):
    batch, tok_rows, _ = pieces[0].shape
    keys_all = tok_rows * len(pieces)
    vmem = pl.BlockSpec(memory_space=pltpu.VMEM)
    hbm = pl.BlockSpec(memory_space=pl.ANY)
    return pl.pallas_call(
        functools.partial(attend_kernel, count=len(pieces)),
        in_specs=[vmem] * (len(pieces) + 1) + [hbm],
        out_specs=[vmem] * 3,
        out_shape=[
            jax.ShapeDtypeStruct((batch * tok_rows, C_TOK), bf16),
            jax.ShapeDtypeStruct((batch, PAIRS, keys_all, 2 * tok_rows), f32),
            jax.ShapeDtypeStruct((batch, keys_all, C_TOK), bf16),
        ],
        scratch_shapes=[
            pltpu.VMEM((3, C_TOK, C_TOK), bf16),
            pltpu.SemaphoreType.DMA((3,)),
        ]
        + attend_scratch(batch, tok_rows, keys_all),
        compiler_params=pltpu.CompilerParams(vmem_limit_bytes=GRANT),
        cost_estimate=pl.CostEstimate(
            flops=4 * 10**9, bytes_accessed=10**7, transcendentals=10**6
        ),
        name="attend",
    )(*pieces, bias, w_qkv)


def token_kernel(*refs, count):
    piece_refs = refs[:count]
    (
        bias_ref, tokens_a_ref, tokens_b_ref, att_a_ref, cot_ref, probs_a_hbm, values_a_hbm,
        w_qkv_hbm, w_out_hbm, w_gate_hbm, w_up_hbm, w_down_hbm,
        resid_ref, hidden_ref, d_bias_ref,
        w_qkv_ref, w_out_ref, w_gate_ref, w_up_ref, w_down_ref, probs_ref, values_ref, sems,
        all_ref, queries_ref, keys_ref, biasf_ref, grads_ref, d_gate_ref, d_up_ref, hat_ref,
    ) = refs[count:]
    batch, tok_rows = cot_ref.shape[0], cot_ref.shape[1]
    keys_all = values_ref.shape[1]
    rows = batch * tok_rows
    ahead = values_a_hbm.shape[0]
    lead = ahead * tok_rows
    copies = start_all(
        qkv_moves(w_qkv_hbm, w_qkv_ref)
        + [
            (w_out_hbm, w_out_ref), (w_down_hbm, w_down_ref), (w_gate_hbm, w_gate_ref),
            (w_up_hbm, w_up_ref), (values_a_hbm, values_ref.at[pl.ds(0, ahead)]),
            (probs_a_hbm, probs_ref.at[pl.ds(0, ahead)]),
        ],
        sems,
    )
    biasf_ref[...] = bias_ref[...].astype(f32)
    own_values = values_ref.at[pl.ds(ahead, batch - ahead)]
    own_probs = probs_ref.at[pl.ds(ahead, batch - ahead)]
    project(piece_refs, w_qkv_ref, copies, all_ref, queries_ref, keys_ref, own_values)
    attend(biasf_ref, queries_ref, keys_ref, own_values, own_probs, queries_ref)

    copies[3].wait()
    resid_ref[0:lead, :] = tokens_a_ref[...].reshape(lead, C_TOK) + nn(
        att_a_ref[...], w_out_ref[...]
    )
    resid_ref[lead:rows, :] = tokens_b_ref[...].reshape(rows - lead, C_TOK) + nn(
        queries_ref[...], w_out_ref[...]
    )
    hat, rstd = norm_rows(resid_ref[...])
    hat_ref[...] = hat
    grads_ref[...] = hat.astype(bf16)
    for copy in copies[4:7]:
        copy.wait()

    for n in range(0, w_gate_ref.shape[1], 256):
        shaped = grads_ref[...]
        gate = nn(shaped, w_gate_ref[:, n : n + 256])
        up = nn(shaped, w_up_ref[:, n : n + 256])
        d_hidden = nt(cot_ref[...].reshape(rows, C_TOK), w_down_ref[n : n + 256, :])
        sig = 1.0 / (1.0 + jnp.exp(-gate))
        act = gate * sig
        hidden_ref[:, n : n + 256] = (act * up).astype(bf16)
        d_gate_ref[:, n : n + 256] = (
            d_hidden * up * sig * (1.0 + gate * (1.0 - sig))
        ).astype(bf16)
        d_up_ref[:, n : n + 256] = (d_hidden * act).astype(bf16)

    parts = []
    for n in range(0, C_TOK, 256):
        parts.append(
            nt(d_gate_ref[...], w_gate_ref[n : n + 256, :])
            + nt(d_up_ref[...], w_up_ref[n : n + 256, :])
        )
    d_normed = jnp.concatenate(parts, axis=1)
    hat = hat_ref[...]
    first = jnp.mean(d_normed, axis=-1, keepdims=True)
    second = jnp.mean(d_normed * hat, axis=-1, keepdims=True)
    d_resid = cot_ref[...].reshape(rows, C_TOK).astype(f32) + rstd * (
        d_normed - first - hat * second
    )
    grads_ref[...] = nt(d_resid.astype(bf16), w_out_ref[...]).astype(bf16)
    for copy in copies[7:]:
        copy.wait()
    masks = head_masks(tok_rows)
    for pair in range(PAIRS):
        low, high = windows(pair)
        total = jnp.zeros((keys_all, 2 * tok_rows), f32)
        for s in range(batch):
            grads = two_heads(
                grads_ref[s * tok_rows : (s + 1) * tok_rows, low:high], masks[pair % 4]
            )
            d_probs = nt(values_ref[s, :, low:high], grads)
            probs = probs_ref[s, pair]
            delta = jnp.sum(probs * d_probs, axis=0, keepdims=True)
            total = total + probs * (d_probs - delta)
        biasf_ref[pl.ds(pair, keys_all, stride=PAIRS), :] = total
    d_bias_ref[...] = biasf_ref[...].astype(bf16)


def token_stage(
    pieces, bias, tokens_a, tokens_b, att_a, cot, probs_a, values_a, w_qkv, w_out, w_gate, w_up,
    w_down,
):
    batch, tok_rows, _ = cot.shape
    keys_all = tok_rows * len(pieces)
    rows = batch * tok_rows
    hidden = w_gate.shape[1]
    vmem = pl.BlockSpec(memory_space=pltpu.VMEM)
    hbm = pl.BlockSpec(memory_space=pl.ANY)
    return pl.pallas_call(
        functools.partial(token_kernel, count=len(pieces)),
        in_specs=[vmem] * (len(pieces) + 5) + [hbm] * 7,
        out_specs=[vmem] * 3,
        out_shape=[
            jax.ShapeDtypeStruct((rows, C_TOK), f32),
            jax.ShapeDtypeStruct((rows, hidden), bf16),
            jax.ShapeDtypeStruct((keys_all * PAIRS, 2 * tok_rows), bf16),
        ],
        scratch_shapes=[
            pltpu.VMEM((3, C_TOK, C_TOK), bf16),
            pltpu.VMEM(w_out.shape, bf16),
            pltpu.VMEM(w_gate.shape, bf16),
            pltpu.VMEM(w_up.shape, bf16),
            pltpu.VMEM(w_down.shape, bf16),
            pltpu.VMEM((batch, PAIRS, keys_all, 2 * tok_rows), f32),
            pltpu.VMEM((batch, keys_all, C_TOK), bf16),
            pltpu.SemaphoreType.DMA((9,)),
        ]
        + attend_scratch(pieces[0].shape[0], tok_rows, keys_all)
        + [
            pltpu.VMEM((rows, C_TOK), bf16),
            pltpu.VMEM((rows, hidden), bf16),
            pltpu.VMEM((rows, hidden), bf16),
            pltpu.VMEM((rows, C_TOK), f32),
        ],
        compiler_params=pltpu.CompilerParams(vmem_limit_bytes=GRANT),
        cost_estimate=pl.CostEstimate(
            flops=10**10, bytes_accessed=2 * 10**7, transcendentals=10**6
        ),
        name="tokens",
    )(
        *pieces, bias, tokens_a, tokens_b, att_a, cot, probs_a, values_a, w_qkv, w_out, w_gate,
        w_up, w_down,
    )


def output_kernel(
    resid_ref, hidden_ref, w_down_ref, pair_ref, out_ref, hat_ref, rstd_ref, pairf_ref
):
    out_ref[...] = (resid_ref[...] + nn(hidden_ref[...], w_down_ref[...])).astype(bf16)
    rows, keys = pair_ref.shape[0], pair_ref.shape[1]
    for i in range(rows // 8):
        pairf_ref[8 * keys * i : 8 * keys * (i + 1), :] = (
            pair_ref[8 * i : 8 * i + 8].astype(f32).reshape(8 * keys, CZ)
        )

    def norm_step(j, carry):
        hat, rstd = norm_rows(pairf_ref[pl.ds(j, rows, stride=keys), :])
        at = pl.multiple_of(j * rows, rows)
        hat_ref[pl.ds(at, rows), :] = hat
        rstd_ref[pl.ds(at, rows), :] = jnp.broadcast_to(rstd, (rows, CZ))
        return carry

    lax.fori_loop(0, keys, norm_step, 0, unroll=4)


def output_stage(resid, hidden, w_down, pair):
    rows, keys = pair.shape[0], pair.shape[1]
    return pl.pallas_call(
        output_kernel,
        out_shape=[jax.ShapeDtypeStruct(resid.shape, bf16)]
        + [jax.ShapeDtypeStruct((rows * keys, CZ), f32)] * 2,
        scratch_shapes=[pltpu.VMEM((rows * keys, CZ), f32)],
        compiler_params=pltpu.CompilerParams(vmem_limit_bytes=GRANT),
        cost_estimate=pl.CostEstimate(
            flops=10**9, bytes_accessed=8 * 10**6, transcendentals=0
        ),
        name="output",
    )(resid, hidden, w_down, pair)


def grad_kernel(parts_ref, hat_ref, rstd_ref, gain_ref, w_bias_ref, out_ref, total_ref):
    keys = parts_ref.shape[1] // PAIRS
    rows = hat_ref.shape[0] // keys
    total = parts_ref[0].astype(f32)
    for k in range(1, parts_ref.shape[0]):
        total = total + parts_ref[k].astype(f32)
    total_ref[...] = total
    weights = jnp.concatenate(split_heads(w_bias_ref[...]), axis=0) * gain_ref[...]
    weights = weights - jnp.mean(weights, axis=-1, keepdims=True)
    weights = jnp.concatenate([weights[0:PAIRS], weights[PAIRS:HEADS]], axis=1)
    w_high = weights.astype(bf16).astype(f32)
    w_middle = (weights - w_high).astype(bf16).astype(f32)
    w_low = weights - w_high - w_middle
    weights = jnp.concatenate([w_high, w_middle, w_low, w_high, w_middle, w_high], axis=0)
    weights = weights.astype(bf16)
    for j in range(keys):
        total = total_ref[PAIRS * j : PAIRS * (j + 1), :]
        high = total.astype(bf16).astype(f32)
        middle = (total - high).astype(bf16).astype(f32)
        low = total - high - middle
        stack = jnp.concatenate([high, high, high, middle, middle, low], axis=0)
        both = nn(stack.T.astype(bf16), weights)
        scaled = both[0:rows, 0:CZ] + both[rows : 2 * rows, CZ : 2 * CZ]
        hat = hat_ref[rows * j : rows * (j + 1), :]
        second = jnp.mean(scaled * hat, axis=-1, keepdims=True)
        out_ref[pl.ds(j, rows, stride=keys), :] = rstd_ref[rows * j : rows * (j + 1), :] * (
            scaled - hat * second
        )


def pair_back(parts, hat, rstd, pair_gain, w_bias_t):
    keys = parts.shape[1] // PAIRS
    rows = hat.shape[0] // keys
    out = pl.pallas_call(
        grad_kernel,
        out_shape=jax.ShapeDtypeStruct((rows * keys, CZ), f32),
        scratch_shapes=[pltpu.VMEM((keys * PAIRS, 2 * rows), f32)],
        compiler_params=pltpu.CompilerParams(vmem_limit_bytes=GRANT),
        cost_estimate=pl.CostEstimate(flops=10**8, bytes_accessed=4 * 10**6, transcendentals=0),
        name="pair_grad",
    )(parts, hat, rstd, pair_gain.reshape(1, CZ), w_bias_t)
    return out.reshape(rows, keys, CZ)


def swap(values, axis, k):
    return lax.ppermute(values, axis, [(i, i ^ k) for i in range(lax.axis_size(axis))])


def gather(values, axis):
    far = range(lax.axis_size(axis) - 1, 0, -1)
    return [values] + [swap(values, axis, k) for k in far][::-1]


def body(
    atom_feats, atom_counts, atom_mask, token_single, pair, pair_gain, w_bias, w_atom_qkv,
    w_atom_out, w_embed, w_qkv, w_out, w_gate, w_up, w_down, cotangent,
):
    batch, atom_rows, _ = atom_feats.shape
    tok_rows = token_single.shape[0]
    shard, shards = lax.axis_index("tok"), lax.axis_size("tok")
    groups = lax.axis_size("samp")

    steps = [(i, i + 1) for i in range(shards - 1)]
    left = lax.ppermute(atom_feats[:, atom_rows - HALO :], "tok", steps)
    right = lax.ppermute(atom_feats[:, :HALO], "tok", [(j, i) for i, j in steps])

    w_bias_t = w_bias.T
    local_bias = pair_bias(pair, pair_gain, w_bias_t, groups)
    bias = lax.all_to_all(local_bias, "samp", 0, 0).reshape(-1, 2 * tok_rows)

    reach = -(-(atom_rows + 2 * HALO) // 128) * 128
    flags = jnp.pad(atom_mask.astype(f32), (HALO, reach - atom_rows - HALO))
    flags = lax.dynamic_slice(flags, (shard * atom_rows,), (reach,)).reshape(reach // 128, 128)
    flags, local_bias = lax.optimization_barrier((flags, local_bias))

    ahead = batch // 2
    tokens, gathered = [], []
    for first, size in ((0, ahead), (ahead, batch - ahead)):
        tok, normed = atom_stage(
            first, size, atom_feats, left, right, flags, atom_counts, token_single, w_atom_qkv,
            w_atom_out, w_embed,
        )
        tokens.append(tok)
        gathered.append(gather(normed, "tok"))
    att_a, probs_a, values_a = attend_stage(gathered[0], bias, w_qkv)
    resid, hidden, d_bias = token_stage(
        gathered[1], bias, *tokens, att_a, cotangent, probs_a, values_a, w_qkv, w_out, w_gate,
        w_up, w_down,
    )
    parts = lax.all_to_all(d_bias.reshape(groups, -1, 2 * tok_rows), "samp", 0, 0)
    token_out, hat, rstd = output_stage(resid, hidden, w_down, pair)
    pair_grad = pair_back(parts, hat, rstd, pair_gain, w_bias_t)
    token_out = token_out.reshape(batch, tok_rows, C_TOK)
    return (token_out, pair_grad)


def solution(mesh):
    in_specs = (
        P("samp", "tok", None),
        P("tok", None),
        P(),
        P("tok", None),
        P("tok", "samp", None),
        P(), P(), P(), P(), P(), P(), P(), P(), P(), P(),
        P("samp", "tok", None),
    )
    out_specs = (P("samp", "tok", None), P("tok", "samp", None))
    return jax.shard_map(body, mesh=mesh, in_specs=in_specs, out_specs=out_specs, check_vma=False)
```

```python
import functools

import jax
import jax.numpy as jnp
from jax import lax
from jax.experimental import pallas as pl
from jax.experimental.pallas import tpu as pltpu
from jax.sharding import PartitionSpec as P

C_ATOM = 128
ATOM_HEADS = 4
C_TOK = 768
HEADS = 16
ATOM_HD = 32
HD = 48
CZ = 128
HALO = 48
PAIRS = HEADS // 2
LOG2E = 1.4426950408889634

epsilon = 1e-05
f32 = jnp.float32
bf16 = jnp.bfloat16

WINDOWS = ((0, 128), (0, 256), (128, 384), (256, 384))


def nn(a, b):
    return lax.dot_general(a, b, (((1,), (0,)), ((), ())), preferred_element_type=f32)


def nt(a, b):
    return lax.dot_general(a, b, (((1,), (1,)), ((), ())), preferred_element_type=f32)


def tn(a, b):
    return lax.dot_general(a, b, (((0,), (0,)), ((), ())), preferred_element_type=f32)


def norm_rows(values):
    center = values - jnp.mean(values, axis=-1, keepdims=True)
    scale_inv = lax.rsqrt(jnp.mean(center * center, axis=-1, keepdims=True) + epsilon)
    return (center * scale_inv, scale_inv)


def iota(shape, dim):
    return lax.broadcasted_iota(jnp.int32, shape, dim)


def pick_heads(parity):
    row, col = iota((PAIRS, HEADS), 0), iota((PAIRS, HEADS), 1)
    return (col == 2 * row + parity).astype(f32).astype(bf16)


def split_heads(w_bias_t):
    return [nn(pick_heads(parity), w_bias_t) for parity in range(2)]


def bias_kernel(pair_ref, gain_ref, w_bias_ref, out_ref, scaled_ref, stage_ref):
    rows, keys = pair_ref.shape[0], pair_ref.shape[1]
    gain = gain_ref[...]

    def norm_step(i, carry):
        block = pair_ref[pl.ds(i * 8, 8)].astype(f32).reshape(8 * keys, CZ)
        hat, unused = norm_rows(block)
        scaled_ref[pl.ds(pl.multiple_of(i * 8 * keys, 8 * keys), 8 * keys), :] = hat * gain
        return carry

    lax.fori_loop(0, rows // 8, norm_step, 0, unroll=True)
    weights = jnp.concatenate(split_heads(w_bias_ref[...]), axis=1).astype(bf16)
    blank = jnp.zeros((rows, CZ), bf16)
    for j in range(keys):
        block = scaled_ref[pl.ds(j, rows, stride=keys), :].astype(bf16)
        both = jnp.concatenate(
            [jnp.concatenate([block, blank], axis=1), jnp.concatenate([blank, block], axis=1)],
            axis=0,
        )
        stage_ref[pl.ds(j, PAIRS, stride=keys), :] = nt(weights, both)
    for k in range(out_ref.shape[0]):
        out_ref[k] = stage_ref[...].astype(bf16)


def pair_bias(pair, pair_gain, w_bias_t, copies):
    rows, keys = pair.shape[0], pair.shape[1]
    return pl.pallas_call(
        bias_kernel,
        out_shape=jax.ShapeDtypeStruct((copies, keys * PAIRS, 2 * rows), bf16),
        scratch_shapes=[
            pltpu.VMEM((rows * keys, CZ), f32),
            pltpu.VMEM((keys * PAIRS, 2 * rows), f32),
        ],
        compiler_params=pltpu.CompilerParams(vmem_limit_bytes=60 << 20),
        cost_estimate=pl.CostEstimate(flops=10**7, bytes_accessed=10**7, transcendentals=0),
        name="pair_bias",
    )(pair, pair_gain.reshape(1, CZ), w_bias_t)


def atom_kernel(
    feats_ref, left_ref, right_ref, mask_ref, counts_ref, single_ref, w_qkv_ref, w_out_ref,
    w_embed_ref, tokens_ref, normed_ref, xn_ref, qkv_ref, scores_a, scores_b, probs_a, probs_b,
    mixed_ref, updated_ref, split_ref, keybias_ref, onehot_ref, counts_col_ref,
):
    atoms = feats_ref.shape[1]
    padded = atoms + 2 * HALO
    tok_rows = single_ref.shape[0]

    @pl.when(pl.program_id(0) == 0)
    def prepare():
        eye = iota((128, 128), 0) == iota((128, 128), 1)
        blocks = atoms // 128
        for b in range(-1, blocks + 1):
            at = lax.axis_index("tok") * blocks + b
            inside = jnp.where((at >= 0) & (at < mask_ref.shape[0]), 1, 0)
            row = mask_ref[pl.ds(jnp.clip(at, 0, mask_ref.shape[0] - 1), 1), :] * inside
            row = jnp.broadcast_to(row.astype(f32), (128, 128))
            col = jnp.sum(jnp.where(eye, row, 0.0), axis=1, keepdims=True)
            col = jnp.broadcast_to((col - 1.0) * 1e30, (128, 128))
            if b < 0:
                keybias_ref[0:HALO, :] = col[128 - HALO : 128]
            elif b < blocks:
                keybias_ref[HALO + 128 * b : HALO + 128 * b + 128, :] = col
            else:
                keybias_ref[HALO + atoms : padded, :] = col[0:HALO]
        counts = jnp.broadcast_to(counts_ref[...].astype(f32), (tok_rows, tok_rows))
        sub, lane = iota((tok_rows, tok_rows), 0), iota((tok_rows, tok_rows), 1)
        start = jnp.sum(jnp.where(lane < sub, counts, 0.0), axis=1, keepdims=True)
        own = jnp.sum(jnp.where(lane == sub, counts, 0.0), axis=1, keepdims=True)
        counts_col_ref[...] = jnp.broadcast_to(own, (tok_rows, 128))
        pos = iota((tok_rows, 256), 1).astype(f32)
        for g in range(atoms // 256):
            at = pos + float(g * 256)
            hit = jnp.where((at >= start) & (at < start + own), 1.0, 0.0).astype(bf16)
            onehot_ref[g] = jnp.concatenate([hit, hit], axis=1)

    xn_ref[0:HALO, :] = norm_rows(left_ref[0].astype(f32))[0].astype(bf16)
    xn_ref[atoms + HALO : padded, :] = norm_rows(right_ref[0].astype(f32))[0].astype(bf16)

    for i in range(atoms // 256):
        block = feats_ref[0, 256 * i : 256 * i + 256, :].astype(f32)
        xn_ref[HALO + 256 * i : HALO + 256 * i + 256, :] = norm_rows(block)[0].astype(bf16)
    chunk = padded // 4
    w_qkv = w_qkv_ref[...]
    for i in range(4):
        qkv_ref[i * chunk : (i + 1) * chunk, :] = nn(
            xn_ref[i * chunk : (i + 1) * chunk, :], w_qkv
        ).astype(bf16)

    head_of = iota((32, 128), 1) // ATOM_HD
    head_mask = [(head_of == h).astype(f32).astype(bf16) for h in range(ATOM_HEADS)]
    own_atom = (iota((32, 128), 1) % 32) == iota((32, 128), 0)
    factor = ATOM_HD ** (-0.5) * LOG2E
    groups = atoms // 128

    def score_step(group, to_ref):
        for k in range(2):
            base = pl.multiple_of(group * 128 + 64 * k, 64)
            queries = qkv_ref[pl.ds(base + HALO, 64), 0:C_ATOM]
            spread = jnp.concatenate(
                [
                    queries[32 * w : 32 * w + 32] * head_mask[h]
                    for w in range(2)
                    for h in range(ATOM_HEADS)
                ],
                axis=0,
            )
            to_ref[k] = nt(qkv_ref[pl.ds(base, 160), C_ATOM : 2 * C_ATOM], spread)

    def softmax_step(group, from_ref, to_ref):
        for k in range(2):
            base = pl.multiple_of(group * 128 + 64 * k, 64)
            for w in range(2):
                keybias = keybias_ref[pl.ds(base + 32 * w, 128), :]
                keybias = jnp.concatenate(
                    [keybias[0:48], jnp.where(own_atom, 0.0, keybias[48:80]), keybias[80:128]],
                    axis=0,
                )
                scores = from_ref[k, 32 * w : 32 * w + 128, 128 * w : 128 * w + 128] + keybias
                expo = jnp.exp2((scores - jnp.max(scores, axis=0, keepdims=True)) * factor)
                weights = expo * (1.0 / jnp.sum(expo, axis=0, keepdims=True))
                to_ref[2 * k + w] = weights.astype(bf16)

    def value_step(group, from_ref):
        for k in range(2):
            base = pl.multiple_of(group * 128 + 64 * k, 64)
            mixes = []
            for w in range(2):
                values = qkv_ref[pl.ds(base + 32 * w, 128), 2 * C_ATOM : 3 * C_ATOM]
                part = tn(from_ref[2 * k + w], values)
                mix = part[0:32]
                for h in range(1, ATOM_HEADS):
                    mix = jnp.where(head_of == h, part[32 * h : 32 * h + 32], mix)
                mixes.append(mix.astype(bf16))
            mixed_ref[pl.ds(base, 64), :] = jnp.concatenate(mixes, axis=0)

    score_step(0, scores_a)

    def window_step(i, carry):
        even, odd = 2 * i, 2 * i + 1
        score_step(odd, scores_b)
        softmax_step(even, scores_a, probs_a)
        value_step(jnp.maximum(even - 1, 0), probs_b)
        score_step(jnp.minimum(odd + 1, groups - 1), scores_a)
        softmax_step(odd, scores_b, probs_b)
        value_step(even, probs_a)
        return carry

    lax.fori_loop(0, groups // 2, window_step, 0)
    value_step(groups - 1, probs_b)

    w_out = w_out_ref[...]
    for g in range(atoms // 256):
        part = slice(256 * g, 256 * g + 256)
        feats = feats_ref[0, part, :].astype(f32)
        updated_ref[part, :] = (feats + nn(mixed_ref[part, :], w_out)).astype(bf16)
    pooled = jnp.zeros((tok_rows, C_TOK), f32)
    for g in range(atoms // 256):
        embedded = jnp.maximum(
            nn(updated_ref[256 * g : 256 * g + 256, :], w_embed_ref[...]), 0.0
        )
        high = embedded.astype(bf16)
        split_ref[g, 0:256, :] = high
        split_ref[g, 256:512, :] = (embedded - high.astype(f32)).astype(bf16)
        pooled = pooled + nn(onehot_ref[g], split_ref[g])
    tokens = pooled / counts_col_ref[:, 0:1] + single_ref[...].astype(f32)
    tokens_ref[0] = tokens
    normed_ref[0] = norm_rows(tokens)[0].astype(bf16)


def atom_stage(first, batch, feats, left, right, mask, counts, single, w_qkv, w_out, w_embed):
    atoms = feats.shape[1]
    tok_rows = single.shape[0]
    padded = atoms + 2 * HALO
    of_sample = lambda rows, cols: pl.BlockSpec((1, rows, cols), lambda s: (s + first, 0, 0))
    by_sample = lambda rows, cols: pl.BlockSpec((1, rows, cols), lambda s: (s, 0, 0))
    whole = lambda a: pl.BlockSpec(a.shape, lambda s: (0,) * a.ndim)
    return pl.pallas_call(
        atom_kernel,
        grid=(batch,),
        in_specs=[
            of_sample(atoms, C_ATOM), of_sample(HALO, C_ATOM), of_sample(HALO, C_ATOM),
            whole(mask), whole(counts), whole(single), whole(w_qkv), whole(w_out), whole(w_embed),
        ],
        out_specs=[by_sample(tok_rows, C_TOK), by_sample(tok_rows, C_TOK)],
        out_shape=[
            jax.ShapeDtypeStruct((batch, tok_rows, C_TOK), f32),
            jax.ShapeDtypeStruct((batch, tok_rows, C_TOK), bf16),
        ],
        scratch_shapes=[
            pltpu.VMEM((padded, C_ATOM), bf16),
            pltpu.VMEM((padded, 3 * C_ATOM), bf16),
            pltpu.VMEM((2, 160, 256), f32),
            pltpu.VMEM((2, 160, 256), f32),
            pltpu.VMEM((4, 128, 128), bf16),
            pltpu.VMEM((4, 128, 128), bf16),
            pltpu.VMEM((atoms, C_ATOM), bf16),
            pltpu.VMEM((atoms, C_ATOM), bf16),
            pltpu.VMEM((atoms // 256, 512, C_TOK), bf16),
            pltpu.VMEM((padded, 128), f32),
            pltpu.VMEM((atoms // 256, tok_rows, 512), bf16),
            pltpu.VMEM((tok_rows, 128), f32),
        ],
        compiler_params=pltpu.CompilerParams(vmem_limit_bytes=60 << 20),
        cost_estimate=pl.CostEstimate(
            flops=10**10, bytes_accessed=4 * 10**6, transcendentals=3 * 10**6
        ),
        name="atoms",
    )(feats, left, right, mask, counts, single, w_qkv, w_out, w_embed)


def head_masks(rows):
    masks = []
    for pair in range(4):
        low, high = WINDOWS[pair]
        lane = iota((rows, high - low), 1) + low
        first = 2 * pair * HD
        masks.append(
            [(lane >= first + HD * k) & (lane < first + HD * (k + 1)) for k in range(2)]
        )
    return masks


def two_heads(block, masks):
    blank = jnp.zeros_like(block)
    return jnp.concatenate([jnp.where(mask, block, blank) for mask in masks], axis=0)


def project(piece_refs, w_qkv_ref, copies, all_ref, queries_ref, keys_ref, values_ref):
    batch, tok_rows = piece_refs[0].shape[0], piece_refs[0].shape[1]
    here = lax.axis_index("tok")
    for k, piece in enumerate(piece_refs):
        at = pl.multiple_of((here ^ k) * tok_rows, tok_rows)
        for s in range(batch):
            all_ref[s, pl.ds(at, tok_rows), :] = piece[s]
    own = piece_refs[0][...].reshape(batch * tok_rows, C_TOK)
    copies[0].wait()
    for n in range(0, C_TOK, 256):
        queries_ref[:, n : n + 256] = nn(own, w_qkv_ref[0, :, n : n + 256]).astype(bf16)
    for which, to_ref in ((1, keys_ref), (2, values_ref)):
        copies[which].wait()
        for n in range(0, C_TOK, 256):
            for s in range(batch):
                to_ref[s, :, n : n + 256] = nn(
                    all_ref[s], w_qkv_ref[which, :, n : n + 256]
                ).astype(bf16)


def windows(pair):
    low, high = WINDOWS[pair % 4]
    return 384 * (pair // 4) + low, 384 * (pair // 4) + high


def attend(bias_ref, queries_ref, keys_ref, values_ref, probs_ref, att_ref):
    batch, keys_all = keys_ref.shape[0], keys_ref.shape[1]
    tok_rows = queries_ref.shape[0] // batch
    masks = head_masks(tok_rows)
    factor = HD ** (-0.5)

    def sample_step(s, carry):
        at = pl.multiple_of(s * tok_rows, 64)
        for pair in range(PAIRS):
            low, high = windows(pair)
            queries = two_heads(queries_ref[pl.ds(at, tok_rows), low:high], masks[pair % 4])
            probs_ref[s, pair] = nt(keys_ref[s, :, low:high], queries)
        for pair in range(PAIRS):
            scores = probs_ref[s, pair] * factor
            bias = [bias_ref[k, pair].astype(f32) for k in range(bias_ref.shape[0])]
            scores = scores + jnp.concatenate(bias, axis=0)
            expo = jnp.exp(scores - jnp.max(scores, axis=0, keepdims=True))
            probs_ref[s, pair] = expo * (1.0 / jnp.sum(expo, axis=0, keepdims=True))
        lanes = [jnp.zeros((tok_rows, 128), f32) for _ in range(C_TOK // 128)]
        for pair in range(PAIRS):
            low, high = windows(pair)
            part = tn(probs_ref[s, pair].astype(bf16), values_ref[s, :, low:high])
            first, second = masks[pair % 4]
            mix = jnp.where(first, part[0:tok_rows], 0.0)
            mix = jnp.where(second, part[tok_rows : 2 * tok_rows], mix)
            for t in range((high - low) // 128):
                lanes[low // 128 + t] = lanes[low // 128 + t] + mix[:, 128 * t : 128 * t + 128]
        for t in range(C_TOK // 128):
            att_ref[pl.ds(at, tok_rows), 128 * t : 128 * t + 128] = lanes[t].astype(bf16)
        return carry

    lax.fori_loop(0, batch, sample_step, 0)


def start_all(moves, sems):
    copies = [pltpu.make_async_copy(src, dst, sems.at[i]) for i, (src, dst) in enumerate(moves)]
    for copy in copies:
        copy.start()
    return copies


def qkv_moves(w_qkv_hbm, w_qkv_ref):
    return [
        (w_qkv_hbm.at[:, pl.ds(C_TOK * i, C_TOK)], w_qkv_ref.at[i]) for i in range(3)
    ]


def attend_kernel(*refs, count):
    piece_refs = refs[:count]
    (
        bias_ref, w_qkv_hbm, att_ref, probs_ref, values_ref, w_qkv_ref, sems, all_ref, queries_ref,
        keys_ref,
    ) = refs[count:]
    copies = start_all(qkv_moves(w_qkv_hbm, w_qkv_ref), sems)
    project(piece_refs, w_qkv_ref, copies, all_ref, queries_ref, keys_ref, values_ref)
    attend(bias_ref, queries_ref, keys_ref, values_ref, probs_ref, att_ref)


def attend_scratch(batch, tok_rows, keys_all):
    return [
        pltpu.VMEM((batch, keys_all, C_TOK), bf16),
        pltpu.VMEM((batch * tok_rows, C_TOK), bf16),
        pltpu.VMEM((batch, keys_all, C_TOK), bf16),
    ]


def attend_stage(pieces, bias, w_qkv):
    batch, tok_rows, _ = pieces[0].shape
    keys_all = tok_rows * len(pieces)
    vmem = pl.BlockSpec(memory_space=pltpu.VMEM)
    hbm = pl.BlockSpec(memory_space=pl.ANY)
    return pl.pallas_call(
        functools.partial(attend_kernel, count=len(pieces)),
        in_specs=[vmem] * (len(pieces) + 1) + [hbm],
        out_specs=[vmem] * 3,
        out_shape=[
            jax.ShapeDtypeStruct((batch * tok_rows, C_TOK), bf16),
            jax.ShapeDtypeStruct((batch, PAIRS, keys_all, 2 * tok_rows), f32),
            jax.ShapeDtypeStruct((batch, keys_all, C_TOK), bf16),
        ],
        scratch_shapes=[
            pltpu.VMEM((3, C_TOK, C_TOK), bf16),
            pltpu.SemaphoreType.DMA((3,)),
        ]
        + attend_scratch(batch, tok_rows, keys_all),
        compiler_params=pltpu.CompilerParams(vmem_limit_bytes=32 << 20),
        cost_estimate=pl.CostEstimate(
            flops=4 * 10**9, bytes_accessed=10**7, transcendentals=10**6
        ),
        name="attend",
    )(*pieces, bias, w_qkv)


def token_kernel(*refs, count):
    piece_refs = refs[:count]
    (
        bias_ref, tokens_a_ref, tokens_b_ref, att_a_ref, cot_ref, probs_a_hbm, values_a_hbm,
        w_qkv_hbm, w_out_hbm, w_gate_hbm, w_up_hbm, w_down_hbm,
        resid_ref, hidden_ref, d_bias_ref,
        w_qkv_ref, w_out_ref, w_gate_ref, w_up_ref, w_down_ref, probs_ref, values_ref, sems,
        all_ref, queries_ref, keys_ref, grads_ref, d_gate_ref, d_up_ref, hat_ref,
    ) = refs[count:]
    batch, tok_rows = cot_ref.shape[0], cot_ref.shape[1]
    keys_all = values_ref.shape[1]
    rows = batch * tok_rows
    ahead = values_a_hbm.shape[0]
    lead = ahead * tok_rows
    copies = start_all(
        qkv_moves(w_qkv_hbm, w_qkv_ref)
        + [
            (w_out_hbm, w_out_ref), (w_down_hbm, w_down_ref), (w_gate_hbm, w_gate_ref),
            (w_up_hbm, w_up_ref), (values_a_hbm, values_ref.at[pl.ds(0, ahead)]),
            (probs_a_hbm, probs_ref.at[pl.ds(0, ahead)]),
        ],
        sems,
    )
    own_values = values_ref.at[pl.ds(ahead, batch - ahead)]
    own_probs = probs_ref.at[pl.ds(ahead, batch - ahead)]
    project(piece_refs, w_qkv_ref, copies, all_ref, queries_ref, keys_ref, own_values)
    attend(bias_ref, queries_ref, keys_ref, own_values, own_probs, queries_ref)

    copies[3].wait()
    resid_ref[0:lead, :] = tokens_a_ref[...].reshape(lead, C_TOK) + nn(
        att_a_ref[...], w_out_ref[...]
    )
    resid_ref[lead:rows, :] = tokens_b_ref[...].reshape(rows - lead, C_TOK) + nn(
        queries_ref[...], w_out_ref[...]
    )
    hat, rstd = norm_rows(resid_ref[...])
    hat_ref[...] = hat
    grads_ref[...] = hat.astype(bf16)
    for copy in copies[4:7]:
        copy.wait()

    for n in range(0, w_gate_ref.shape[1], 256):
        shaped = grads_ref[...]
        gate = nn(shaped, w_gate_ref[:, n : n + 256])
        up = nn(shaped, w_up_ref[:, n : n + 256])
        d_hidden = nt(cot_ref[...].reshape(rows, C_TOK), w_down_ref[n : n + 256, :])
        sig = 1.0 / (1.0 + jnp.exp(-gate))
        act = gate * sig
        hidden_ref[:, n : n + 256] = (act * up).astype(bf16)
        d_gate_ref[:, n : n + 256] = (
            d_hidden * up * sig * (1.0 + gate * (1.0 - sig))
        ).astype(bf16)
        d_up_ref[:, n : n + 256] = (d_hidden * act).astype(bf16)

    parts = []
    for n in range(0, C_TOK, 256):
        parts.append(
            nt(d_gate_ref[...], w_gate_ref[n : n + 256, :])
            + nt(d_up_ref[...], w_up_ref[n : n + 256, :])
        )
    d_normed = jnp.concatenate(parts, axis=1)
    hat = hat_ref[...]
    first = jnp.mean(d_normed, axis=-1, keepdims=True)
    second = jnp.mean(d_normed * hat, axis=-1, keepdims=True)
    d_resid = cot_ref[...].reshape(rows, C_TOK).astype(f32) + rstd * (
        d_normed - first - hat * second
    )
    grads_ref[...] = nt(d_resid.astype(bf16), w_out_ref[...]).astype(bf16)
    for copy in copies[7:]:
        copy.wait()
    masks = head_masks(tok_rows)
    for pair in range(PAIRS):
        low, high = windows(pair)
        total = jnp.zeros((keys_all, 2 * tok_rows), f32)
        for s in range(batch):
            grads = two_heads(
                grads_ref[s * tok_rows : (s + 1) * tok_rows, low:high], masks[pair % 4]
            )
            d_probs = nt(values_ref[s, :, low:high], grads)
            probs = probs_ref[s, pair]
            delta = jnp.sum(probs * d_probs, axis=0, keepdims=True)
            total = total + probs * (d_probs - delta)
        size = d_bias_ref.shape[2]
        for k in range(d_bias_ref.shape[0]):
            d_bias_ref[k, pair] = total[size * k : size * (k + 1)].astype(bf16)


def token_stage(
    pieces, bias, tokens_a, tokens_b, att_a, cot, probs_a, values_a, w_qkv, w_out, w_gate, w_up,
    w_down,
):
    batch, tok_rows, _ = cot.shape
    keys_all = tok_rows * len(pieces)
    rows = batch * tok_rows
    hidden = w_gate.shape[1]
    vmem = pl.BlockSpec(memory_space=pltpu.VMEM)
    hbm = pl.BlockSpec(memory_space=pl.ANY)
    return pl.pallas_call(
        functools.partial(token_kernel, count=len(pieces)),
        in_specs=[vmem] * (len(pieces) + 5) + [hbm] * 7,
        out_specs=[vmem] * 3,
        out_shape=[
            jax.ShapeDtypeStruct((rows, C_TOK), f32),
            jax.ShapeDtypeStruct((rows, hidden), bf16),
            jax.ShapeDtypeStruct(bias.shape, bf16),
        ],
        scratch_shapes=[
            pltpu.VMEM((3, C_TOK, C_TOK), bf16),
            pltpu.VMEM(w_out.shape, bf16),
            pltpu.VMEM(w_gate.shape, bf16),
            pltpu.VMEM(w_up.shape, bf16),
            pltpu.VMEM(w_down.shape, bf16),
            pltpu.VMEM((batch, PAIRS, keys_all, 2 * tok_rows), f32),
            pltpu.VMEM((batch, keys_all, C_TOK), bf16),
            pltpu.SemaphoreType.DMA((9,)),
        ]
        + attend_scratch(pieces[0].shape[0], tok_rows, keys_all)
        + [
            pltpu.VMEM((rows, C_TOK), bf16),
            pltpu.VMEM((rows, hidden), bf16),
            pltpu.VMEM((rows, hidden), bf16),
            pltpu.VMEM((rows, C_TOK), f32),
        ],
        compiler_params=pltpu.CompilerParams(vmem_limit_bytes=44 << 20),
        cost_estimate=pl.CostEstimate(
            flops=10**10, bytes_accessed=2 * 10**7, transcendentals=10**6
        ),
        name="tokens",
    )(
        *pieces, bias, tokens_a, tokens_b, att_a, cot, probs_a, values_a, w_qkv, w_out, w_gate,
        w_up, w_down,
    )


def output_kernel(
    resid_ref, hidden_ref, w_down_ref, pair_ref, out_ref, hat_ref, rstd_ref, pairf_ref
):
    out_ref[...] = (resid_ref[...] + nn(hidden_ref[...], w_down_ref[...])).astype(bf16)
    rows, keys = pair_ref.shape[0], pair_ref.shape[1]
    for i in range(rows // 8):
        pairf_ref[8 * keys * i : 8 * keys * (i + 1), :] = (
            pair_ref[8 * i : 8 * i + 8].astype(f32).reshape(8 * keys, CZ)
        )

    def norm_step(j, carry):
        hat, rstd = norm_rows(pairf_ref[pl.ds(j, rows, stride=keys), :])
        at = pl.multiple_of(j * rows, rows)
        hat_ref[pl.ds(at, rows), :] = hat
        rstd_ref[pl.ds(at, rows), :] = jnp.broadcast_to(rstd, (rows, CZ))
        return carry

    lax.fori_loop(0, keys, norm_step, 0, unroll=4)


def output_stage(resid, hidden, w_down, pair):
    rows, keys = pair.shape[0], pair.shape[1]
    return pl.pallas_call(
        output_kernel,
        out_shape=[jax.ShapeDtypeStruct(resid.shape, bf16)]
        + [jax.ShapeDtypeStruct((rows * keys, CZ), f32)] * 2,
        scratch_shapes=[pltpu.VMEM((rows * keys, CZ), f32)],
        compiler_params=pltpu.CompilerParams(vmem_limit_bytes=24 << 20),
        cost_estimate=pl.CostEstimate(
            flops=10**9, bytes_accessed=8 * 10**6, transcendentals=0
        ),
        name="output",
    )(resid, hidden, w_down, pair)


def grad_kernel(parts_ref, hat_ref, rstd_ref, gain_ref, w_bias_ref, out_ref, total_ref):
    keys = parts_ref.shape[2]
    rows = hat_ref.shape[0] // keys
    for pair in range(PAIRS):
        total = parts_ref[0, pair].astype(f32)
        for k in range(1, parts_ref.shape[0]):
            total = total + parts_ref[k, pair].astype(f32)
        total_ref[pair * keys : (pair + 1) * keys, :] = total
    weights = jnp.concatenate(split_heads(w_bias_ref[...]), axis=0) * gain_ref[...]
    weights = weights - jnp.mean(weights, axis=-1, keepdims=True)
    weights = jnp.concatenate([weights[0:PAIRS], weights[PAIRS:HEADS]], axis=1)
    w_high = weights.astype(bf16).astype(f32)
    w_middle = (weights - w_high).astype(bf16).astype(f32)
    w_low = weights - w_high - w_middle
    weights = jnp.concatenate([w_high, w_middle, w_low, w_high, w_middle, w_high], axis=0)
    weights = weights.astype(bf16)
    for j in range(keys):
        total = total_ref[pl.ds(j, PAIRS, stride=keys), :]
        high = total.astype(bf16).astype(f32)
        middle = (total - high).astype(bf16).astype(f32)
        low = total - high - middle
        stack = jnp.concatenate([high, high, high, middle, middle, low], axis=0)
        both = nn(stack.T.astype(bf16), weights)
        scaled = both[0:rows, 0:CZ] + both[rows : 2 * rows, CZ : 2 * CZ]
        hat = hat_ref[rows * j : rows * (j + 1), :]
        second = jnp.mean(scaled * hat, axis=-1, keepdims=True)
        out_ref[pl.ds(j, rows, stride=keys), :] = rstd_ref[rows * j : rows * (j + 1), :] * (
            scaled - hat * second
        )


def pair_back(parts, hat, rstd, pair_gain, w_bias_t):
    keys = parts.shape[2]
    rows = hat.shape[0] // keys
    out = pl.pallas_call(
        grad_kernel,
        out_shape=jax.ShapeDtypeStruct((rows * keys, CZ), f32),
        scratch_shapes=[pltpu.VMEM((keys * PAIRS, 2 * rows), f32)],
        compiler_params=pltpu.CompilerParams(vmem_limit_bytes=16 << 20),
        cost_estimate=pl.CostEstimate(flops=10**8, bytes_accessed=4 * 10**6, transcendentals=0),
        name="pair_grad",
    )(parts, hat, rstd, pair_gain.reshape(1, CZ), w_bias_t)
    return out.reshape(rows, keys, CZ)


def swap(values, axis, k):
    return lax.ppermute(values, axis, [(i, i ^ k) for i in range(lax.axis_size(axis))])


def gather(values, axis):
    far = range(lax.axis_size(axis) - 1, 0, -1)
    return [values] + [swap(values, axis, k) for k in far][::-1]


def body(
    atom_feats, atom_counts, atom_mask, token_single, pair, pair_gain, w_bias, w_atom_qkv,
    w_atom_out, w_embed, w_qkv, w_out, w_gate, w_up, w_down, cotangent,
):
    batch, atom_rows, _ = atom_feats.shape
    tok_rows = token_single.shape[0]
    shards = lax.axis_size("tok")
    groups = lax.axis_size("samp")

    steps = [(i, i + 1) for i in range(shards - 1)]
    left = lax.ppermute(atom_feats[:, atom_rows - HALO :], "tok", steps)
    right = lax.ppermute(atom_feats[:, :HALO], "tok", [(j, i) for i, j in steps])

    w_bias_t = w_bias.T
    local_bias = pair_bias(pair, pair_gain, w_bias_t, groups)
    bias = lax.all_to_all(local_bias, "samp", 0, 0).reshape(groups, PAIRS, -1, 2 * tok_rows)

    mask = atom_mask.reshape(-1, 128)
    mask, local_bias = lax.optimization_barrier((mask, local_bias))

    ahead = batch // 2
    tokens, gathered = [], []
    for first, size in ((0, ahead), (ahead, batch - ahead)):
        tok, normed = atom_stage(
            first, size, atom_feats, left, right, mask, atom_counts, token_single, w_atom_qkv,
            w_atom_out, w_embed,
        )
        tokens.append(tok)
        gathered.append(gather(normed, "tok"))
    att_a, probs_a, values_a = attend_stage(gathered[0], bias, w_qkv)
    resid, hidden, d_bias = token_stage(
        gathered[1], bias, *tokens, att_a, cotangent, probs_a, values_a, w_qkv, w_out, w_gate,
        w_up, w_down,
    )
    parts = lax.all_to_all(d_bias, "samp", 0, 0)
    token_out, hat, rstd = output_stage(resid, hidden, w_down, pair)
    pair_grad = pair_back(parts, hat, rstd, pair_gain, w_bias_t)
    token_out = token_out.reshape(batch, tok_rows, C_TOK)
    return (token_out, pair_grad)


def solution(mesh):
    in_specs = (
        P("samp", "tok", None),
        P("tok", None),
        P(),
        P("tok", None),
        P("tok", "samp", None),
        P(), P(), P(), P(), P(), P(), P(), P(), P(), P(),
        P("samp", "tok", None),
    )
    out_specs = (P("samp", "tok", None), P("tok", "samp", None))
    return jax.shard_map(body, mesh=mesh, in_specs=in_specs, out_specs=out_specs, check_vma=False)
```

```python
import functools

import jax
import jax.numpy as jnp
from jax import lax
from jax.experimental import pallas as pl
from jax.experimental.pallas import tpu as pltpu
from jax.sharding import PartitionSpec as P

C_ATOM = 128
ATOM_HEADS = 4
C_TOK = 768
HEADS = 16
ATOM_HD = 32
HD = 48
CZ = 128
HALO = 48
PAIRS = HEADS // 2
GRANT = 64 << 20
LOG2E = 1.4426950408889634

epsilon = 1e-05
f32 = jnp.float32
bf16 = jnp.bfloat16

WINDOWS = ((0, 128), (0, 256), (128, 384), (256, 384))


def nn(a, b):
    return lax.dot_general(a, b, (((1,), (0,)), ((), ())), preferred_element_type=f32)


def nt(a, b):
    return lax.dot_general(a, b, (((1,), (1,)), ((), ())), preferred_element_type=f32)


def tn(a, b):
    return lax.dot_general(a, b, (((0,), (0,)), ((), ())), preferred_element_type=f32)


def norm_rows(values):
    center = values - jnp.mean(values, axis=-1, keepdims=True)
    scale_inv = lax.rsqrt(jnp.mean(center * center, axis=-1, keepdims=True) + epsilon)
    return (center * scale_inv, scale_inv)


def iota(shape, dim):
    return lax.broadcasted_iota(jnp.int32, shape, dim)


def pick_heads(parity):
    row, col = iota((PAIRS, HEADS), 0), iota((PAIRS, HEADS), 1)
    return (col == 2 * row + parity).astype(f32).astype(bf16)


def split_heads(w_bias_t):
    return [nn(pick_heads(parity), w_bias_t) for parity in range(2)]


def bias_kernel(pair_ref, gain_ref, w_bias_ref, out_ref, scaled_ref, stage_ref):
    rows, keys = pair_ref.shape[0], pair_ref.shape[1]
    gain = gain_ref[...]

    def norm_step(i, carry):
        block = pair_ref[pl.ds(i * 8, 8)].astype(f32).reshape(8 * keys, CZ)
        hat, unused = norm_rows(block)
        scaled_ref[pl.ds(pl.multiple_of(i * 8 * keys, 8 * keys), 8 * keys), :] = hat * gain
        return carry

    lax.fori_loop(0, rows // 8, norm_step, 0, unroll=True)
    weights = jnp.concatenate(split_heads(w_bias_ref[...]), axis=1).astype(bf16)
    blank = jnp.zeros((rows, CZ), bf16)
    for j in range(keys):
        block = scaled_ref[pl.ds(j, rows, stride=keys), :].astype(bf16)
        both = jnp.concatenate(
            [jnp.concatenate([block, blank], axis=1), jnp.concatenate([blank, block], axis=1)],
            axis=0,
        )
        stage_ref[pl.ds(j, PAIRS, stride=keys), :] = nt(weights, both)
    for k in range(out_ref.shape[0]):
        out_ref[k] = stage_ref[...].astype(bf16)


def pair_bias(pair, pair_gain, w_bias_t, copies):
    rows, keys = pair.shape[0], pair.shape[1]
    return pl.pallas_call(
        bias_kernel,
        out_shape=jax.ShapeDtypeStruct((copies, keys * PAIRS, 2 * rows), bf16),
        scratch_shapes=[
            pltpu.VMEM((rows * keys, CZ), f32),
            pltpu.VMEM((keys * PAIRS, 2 * rows), f32),
        ],
        compiler_params=pltpu.CompilerParams(vmem_limit_bytes=GRANT),
        cost_estimate=pl.CostEstimate(flops=10**7, bytes_accessed=10**7, transcendentals=0),
        name="pair_bias",
    )(pair, pair_gain.reshape(1, CZ), w_bias_t)


def atom_kernel(
    feats_ref, left_ref, right_ref, mask_ref, counts_ref, single_ref, w_qkv_ref, w_out_ref,
    w_embed_ref, tokens_ref, normed_ref, padded_ref, qkv_a, qkv_b, scores_a, scores_b, probs_a,
    probs_b, mixed_ref, split_ref, keybias_ref, onehot_ref, pooled_ref,
):
    batch, atoms = feats_ref.shape[0], feats_ref.shape[1]
    padded = atoms + 2 * HALO
    tok_rows = single_ref.shape[0]
    blocks = atoms // 128
    chunks = atoms // 256
    qkv_refs = (qkv_a, qkv_b)

    eye = iota((128, 128), 0) == iota((128, 128), 1)
    for b in range(-1, blocks + 1):
        at = lax.axis_index("tok") * blocks + b
        inside = jnp.where((at >= 0) & (at < mask_ref.shape[0]), 1, 0)
        row = mask_ref[pl.ds(jnp.clip(at, 0, mask_ref.shape[0] - 1), 1), :] * inside
        row = jnp.broadcast_to(row.astype(f32), (128, 128))
        col = jnp.sum(jnp.where(eye, row, 0.0), axis=1, keepdims=True)
        col = jnp.broadcast_to((col - 1.0) * 1e30, (128, 128))
        if b < 0:
            keybias_ref[0:HALO, :] = col[128 - HALO : 128]
        elif b < blocks:
            keybias_ref[HALO + 128 * b : HALO + 128 * b + 128, :] = col
        else:
            keybias_ref[HALO + atoms : padded, :] = col[0:HALO]
    counts = jnp.broadcast_to(counts_ref[...].astype(f32), (tok_rows, tok_rows))
    sub, lane = iota((tok_rows, tok_rows), 0), iota((tok_rows, tok_rows), 1)
    start = jnp.sum(jnp.where(lane < sub, counts, 0.0), axis=1, keepdims=True)
    own = jnp.sum(jnp.where(lane == sub, counts, 0.0), axis=1, keepdims=True)
    pos = iota((tok_rows, 256), 1).astype(f32)
    for g in range(chunks):
        at = pos + float(g * 256)
        hit = jnp.where((at >= start) & (at < start + own), 1.0, 0.0).astype(bf16)
        onehot_ref[g] = jnp.concatenate([hit, hit], axis=1)
    pooled_ref[...] = jnp.zeros_like(pooled_ref)
    for s in range(batch):
        padded_ref[s, 0:HALO, :] = left_ref[s]
        padded_ref[s, HALO : HALO + atoms, :] = feats_ref[s]
        padded_ref[s, HALO + atoms : padded, :] = right_ref[s]

    head_of = iota((32, 128), 1) // ATOM_HD
    head_mask = [(head_of == h).astype(f32).astype(bf16) for h in range(ATOM_HEADS)]
    own_atom = (iota((32, 128), 1) % 32) == iota((32, 128), 0)
    factor = ATOM_HD ** (-0.5) * LOG2E
    stride = padded // chunks // 16 * 16
    span = padded - stride * (chunks - 1)

    def qkv_step(s, i):
        at = pl.multiple_of(i * stride, 16)
        normed, unused = norm_rows(padded_ref[s, pl.ds(at, span), :].astype(f32))
        qkv_refs[s % 2][pl.ds(at, span), :] = nn(normed.astype(bf16), w_qkv_ref[...]).astype(bf16)

    def score_step(s, group, to_ref):
        qkv_ref = qkv_refs[s % 2]
        for k in range(2):
            base = pl.multiple_of(group * 128 + 64 * k, 64)
            queries = qkv_ref[pl.ds(base + HALO, 64), 0:C_ATOM]
            spread = jnp.concatenate(
                [
                    queries[32 * w : 32 * w + 32] * head_mask[h]
                    for w in range(2)
                    for h in range(ATOM_HEADS)
                ],
                axis=0,
            )
            to_ref[k] = nt(qkv_ref[pl.ds(base, 160), C_ATOM : 2 * C_ATOM], spread)

    def softmax_step(group, from_ref, to_ref):
        for k in range(2):
            base = pl.multiple_of(group * 128 + 64 * k, 64)
            for w in range(2):
                keybias = keybias_ref[pl.ds(base + 32 * w, 128), :]
                keybias = jnp.concatenate(
                    [keybias[0:48], jnp.where(own_atom, 0.0, keybias[48:80]), keybias[80:128]],
                    axis=0,
                )
                scores = from_ref[k, 32 * w : 32 * w + 128, 128 * w : 128 * w + 128] + keybias
                expo = jnp.exp2((scores - jnp.max(scores, axis=0, keepdims=True)) * factor)
                weights = expo * (1.0 / jnp.sum(expo, axis=0, keepdims=True))
                to_ref[2 * k + w] = weights.astype(bf16)

    def value_step(s, group, from_ref):
        qkv_ref = qkv_refs[s % 2]
        for k in range(2):
            base = pl.multiple_of(group * 128 + 64 * k, 64)
            mixes = []
            for w in range(2):
                values = qkv_ref[pl.ds(base + 32 * w, 128), 2 * C_ATOM : 3 * C_ATOM]
                part = tn(from_ref[2 * k + w], values)
                mix = part[0:32]
                for h in range(1, ATOM_HEADS):
                    mix = jnp.where(head_of == h, part[32 * h : 32 * h + 32], mix)
                mixes.append(mix.astype(bf16))
            mixed_ref[s, pl.ds(base, 64), :] = jnp.concatenate(mixes, axis=0)

    def embed_step(s, g):
        base = pl.multiple_of(g * 256, 256)
        feats = feats_ref[s, pl.ds(base, 256), :].astype(f32)
        updated = (feats + nn(mixed_ref[s, pl.ds(base, 256), :], w_out_ref[...])).astype(bf16)
        embedded = jnp.maximum(nn(updated, w_embed_ref[...]), 0.0)
        high = embedded.astype(bf16)
        split_ref[0:256, :] = high
        split_ref[256:512, :] = (embedded - high.astype(f32)).astype(bf16)
        pooled_ref[s] += nn(onehot_ref[g], split_ref[...])

    for i in range(chunks):
        qkv_step(0, i)
    for s in range(batch):
        score_step(s, 0, scores_a)

        def window_step(i, carry, s=s, lagging=True):
            even, odd = 2 * i, 2 * i + 1
            if lagging:
                embed_step(s, i - 2)
            if s + 1 < batch:
                qkv_step(s + 1, i)
            score_step(s, odd, scores_b)
            softmax_step(even, scores_a, probs_a)
            value_step(s, jnp.maximum(even - 1, 0), probs_b)
            score_step(s, jnp.minimum(odd + 1, 2 * chunks - 1), scores_a)
            softmax_step(odd, scores_b, probs_b)
            value_step(s, even, probs_a)
            return carry

        for i in range(2):
            if s > 0:
                embed_step(s - 1, chunks - 2 + i)
            window_step(i, 0, lagging=False)
        lax.fori_loop(2, chunks, window_step, 0)
        value_step(s, 2 * chunks - 1, probs_b)
    for i in range(2):
        embed_step(batch - 1, chunks - 2 + i)
    for s in range(batch):
        tokens = pooled_ref[s] / own + single_ref[...].astype(f32)
        tokens_ref[s] = tokens
        normed_ref[s] = norm_rows(tokens)[0].astype(bf16)


def atom_stage(part, batch, feats, left, right, mask, counts, single, w_qkv, w_out, w_embed):
    atoms = feats.shape[1]
    tok_rows = single.shape[0]
    padded = atoms + 2 * HALO
    of_part = lambda rows, cols: pl.BlockSpec((batch, rows, cols), lambda i: (part, 0, 0))
    whole = lambda a: pl.BlockSpec(a.shape, lambda i: (0,) * a.ndim)
    every = pl.BlockSpec((batch, tok_rows, C_TOK), lambda i: (0, 0, 0))
    return pl.pallas_call(
        atom_kernel,
        grid=(1,),
        in_specs=[
            of_part(atoms, C_ATOM), of_part(HALO, C_ATOM), of_part(HALO, C_ATOM),
            whole(mask), whole(counts), whole(single), whole(w_qkv), whole(w_out), whole(w_embed),
        ],
        out_specs=[every, every],
        out_shape=[
            jax.ShapeDtypeStruct((batch, tok_rows, C_TOK), f32),
            jax.ShapeDtypeStruct((batch, tok_rows, C_TOK), bf16),
        ],
        scratch_shapes=[
            pltpu.VMEM((batch, padded, C_ATOM), bf16),
            pltpu.VMEM((padded, 3 * C_ATOM), bf16),
            pltpu.VMEM((padded, 3 * C_ATOM), bf16),
            pltpu.VMEM((2, 160, 256), f32),
            pltpu.VMEM((2, 160, 256), f32),
            pltpu.VMEM((4, 128, 128), bf16),
            pltpu.VMEM((4, 128, 128), bf16),
            pltpu.VMEM((batch, atoms, C_ATOM), bf16),
            pltpu.VMEM((512, C_TOK), bf16),
            pltpu.VMEM((padded, 128), f32),
            pltpu.VMEM((atoms // 256, tok_rows, 512), bf16),
            pltpu.VMEM((batch, tok_rows, C_TOK), f32),
        ],
        compiler_params=pltpu.CompilerParams(vmem_limit_bytes=GRANT),
        cost_estimate=pl.CostEstimate(
            flops=10**10, bytes_accessed=4 * 10**6, transcendentals=3 * 10**6
        ),
        name="atoms",
    )(feats, left, right, mask, counts, single, w_qkv, w_out, w_embed)


def head_masks(rows):
    masks = []
    for pair in range(4):
        low, high = WINDOWS[pair]
        lane = iota((rows, high - low), 1) + low
        first = 2 * pair * HD
        masks.append(
            [(lane >= first + HD * k) & (lane < first + HD * (k + 1)) for k in range(2)]
        )
    return masks


def two_heads(block, masks):
    blank = jnp.zeros_like(block)
    return jnp.concatenate([jnp.where(mask, block, blank) for mask in masks], axis=0)


def project(piece_refs, w_qkv_ref, copies, all_ref, queries_ref, keys_ref, values_ref):
    batch, tok_rows = piece_refs[0].shape[0], piece_refs[0].shape[1]
    here = lax.axis_index("tok")
    for k, piece in enumerate(piece_refs):
        at = pl.multiple_of((here ^ k) * tok_rows, tok_rows)
        for s in range(batch):
            all_ref[s, pl.ds(at, tok_rows), :] = piece[s]
    own = piece_refs[0][...].reshape(batch * tok_rows, C_TOK)
    copies[0].wait()
    for n in range(0, C_TOK, 256):
        queries_ref[:, n : n + 256] = nn(own, w_qkv_ref[0, :, n : n + 256]).astype(bf16)
    for which, to_ref in ((1, keys_ref), (2, values_ref)):
        copies[which].wait()
        for n in range(0, C_TOK, 256):
            for s in range(batch):
                to_ref[s, :, n : n + 256] = nn(
                    all_ref[s], w_qkv_ref[which, :, n : n + 256]
                ).astype(bf16)


def windows(pair):
    low, high = WINDOWS[pair % 4]
    return 384 * (pair // 4) + low, 384 * (pair // 4) + high


def attend(bias_ref, queries_ref, keys_ref, values_ref, probs_ref, att_ref):
    batch, keys_all = keys_ref.shape[0], keys_ref.shape[1]
    tok_rows = queries_ref.shape[0] // batch
    masks = head_masks(tok_rows)
    factor = HD ** (-0.5)

    def sample_step(s, carry):
        at = pl.multiple_of(s * tok_rows, 64)
        for pair in range(PAIRS):
            low, high = windows(pair)
            queries = two_heads(queries_ref[pl.ds(at, tok_rows), low:high], masks[pair % 4])
            probs_ref[s, pair] = nt(keys_ref[s, :, low:high], queries)
        for pair in range(PAIRS):
            scores = probs_ref[s, pair] * factor
            bias = [bias_ref[k, pair].astype(f32) for k in range(bias_ref.shape[0])]
            scores = scores + jnp.concatenate(bias, axis=0)
            expo = jnp.exp(scores - jnp.max(scores, axis=0, keepdims=True))
            probs_ref[s, pair] = expo * (1.0 / jnp.sum(expo, axis=0, keepdims=True))
        lanes = [jnp.zeros((tok_rows, 128), f32) for _ in range(C_TOK // 128)]
        for pair in range(PAIRS):
            low, high = windows(pair)
            part = tn(probs_ref[s, pair].astype(bf16), values_ref[s, :, low:high])
            first, second = masks[pair % 4]
            mix = jnp.where(first, part[0:tok_rows], 0.0)
            mix = jnp.where(second, part[tok_rows : 2 * tok_rows], mix)
            for t in range((high - low) // 128):
                lanes[low // 128 + t] = lanes[low // 128 + t] + mix[:, 128 * t : 128 * t + 128]
        for t in range(C_TOK // 128):
            att_ref[pl.ds(at, tok_rows), 128 * t : 128 * t + 128] = lanes[t].astype(bf16)
        return carry

    lax.fori_loop(0, batch, sample_step, 0)


def start_all(moves, sems):
    copies = [pltpu.make_async_copy(src, dst, sems.at[i]) for i, (src, dst) in enumerate(moves)]
    for copy in copies:
        copy.start()
    return copies


def qkv_moves(w_qkv_hbm, w_qkv_ref):
    return [
        (w_qkv_hbm.at[:, pl.ds(C_TOK * i, C_TOK)], w_qkv_ref.at[i]) for i in range(3)
    ]


def attend_kernel(*refs, count):
    piece_refs = refs[:count]
    (
        bias_ref, w_qkv_hbm, att_ref, probs_ref, values_ref, w_qkv_ref, sems, all_ref, queries_ref,
        keys_ref,
    ) = refs[count:]
    copies = start_all(qkv_moves(w_qkv_hbm, w_qkv_ref), sems)
    project(piece_refs, w_qkv_ref, copies, all_ref, queries_ref, keys_ref, values_ref)
    attend(bias_ref, queries_ref, keys_ref, values_ref, probs_ref, att_ref)


def attend_scratch(batch, tok_rows, keys_all):
    return [
        pltpu.VMEM((batch, keys_all, C_TOK), bf16),
        pltpu.VMEM((batch * tok_rows, C_TOK), bf16),
        pltpu.VMEM((batch, keys_all, C_TOK), bf16),
    ]


def attend_stage(pieces, bias, w_qkv):
    batch, tok_rows, _ = pieces[0].shape
    keys_all = tok_rows * len(pieces)
    vmem = pl.BlockSpec(memory_space=pltpu.VMEM)
    hbm = pl.BlockSpec(memory_space=pl.ANY)
    return pl.pallas_call(
        functools.partial(attend_kernel, count=len(pieces)),
        in_specs=[vmem] * (len(pieces) + 1) + [hbm],
        out_specs=[vmem] * 3,
        out_shape=[
            jax.ShapeDtypeStruct((batch * tok_rows, C_TOK), bf16),
            jax.ShapeDtypeStruct((batch, PAIRS, keys_all, 2 * tok_rows), f32),
            jax.ShapeDtypeStruct((batch, keys_all, C_TOK), bf16),
        ],
        scratch_shapes=[
            pltpu.VMEM((3, C_TOK, C_TOK), bf16),
            pltpu.SemaphoreType.DMA((3,)),
        ]
        + attend_scratch(batch, tok_rows, keys_all),
        compiler_params=pltpu.CompilerParams(vmem_limit_bytes=GRANT),
        cost_estimate=pl.CostEstimate(
            flops=4 * 10**9, bytes_accessed=10**7, transcendentals=10**6
        ),
        name="attend",
    )(*pieces, bias, w_qkv)


def token_kernel(*refs, count):
    piece_refs = refs[:count]
    (
        bias_ref, tokens_a_ref, tokens_b_ref, att_a_ref, cot_ref, probs_a_hbm, values_a_hbm,
        w_qkv_hbm, w_out_hbm, w_gate_hbm, w_up_hbm, w_down_hbm,
        resid_ref, hidden_ref, d_bias_ref,
        w_qkv_ref, w_out_ref, w_gate_ref, w_up_ref, w_down_ref, probs_ref, values_ref, sems,
        all_ref, queries_ref, keys_ref, grads_ref, d_gate_ref, d_up_ref, hat_ref,
    ) = refs[count:]
    batch, tok_rows = cot_ref.shape[0], cot_ref.shape[1]
    keys_all = values_ref.shape[1]
    rows = batch * tok_rows
    ahead = values_a_hbm.shape[0]
    lead = ahead * tok_rows
    copies = start_all(
        qkv_moves(w_qkv_hbm, w_qkv_ref)
        + [
            (w_out_hbm, w_out_ref), (w_down_hbm, w_down_ref), (w_gate_hbm, w_gate_ref),
            (w_up_hbm, w_up_ref), (values_a_hbm, values_ref.at[pl.ds(0, ahead)]),
            (probs_a_hbm, probs_ref.at[pl.ds(0, ahead)]),
        ],
        sems,
    )
    own_values = values_ref.at[pl.ds(ahead, batch - ahead)]
    own_probs = probs_ref.at[pl.ds(ahead, batch - ahead)]
    project(piece_refs, w_qkv_ref, copies, all_ref, queries_ref, keys_ref, own_values)
    attend(bias_ref, queries_ref, keys_ref, own_values, own_probs, queries_ref)

    copies[3].wait()
    resid_ref[0:lead, :] = tokens_a_ref[...].reshape(lead, C_TOK) + nn(
        att_a_ref[...], w_out_ref[...]
    )
    resid_ref[lead:rows, :] = tokens_b_ref[...].reshape(rows - lead, C_TOK) + nn(
        queries_ref[...], w_out_ref[...]
    )
    hat, rstd = norm_rows(resid_ref[...])
    hat_ref[...] = hat
    grads_ref[...] = hat.astype(bf16)
    for copy in copies[4:7]:
        copy.wait()

    for n in range(0, w_gate_ref.shape[1], 256):
        shaped = grads_ref[...]
        gate = nn(shaped, w_gate_ref[:, n : n + 256])
        up = nn(shaped, w_up_ref[:, n : n + 256])
        d_hidden = nt(cot_ref[...].reshape(rows, C_TOK), w_down_ref[n : n + 256, :])
        sig = 1.0 / (1.0 + jnp.exp(-gate))
        act = gate * sig
        hidden_ref[:, n : n + 256] = (act * up).astype(bf16)
        d_gate_ref[:, n : n + 256] = (
            d_hidden * up * sig * (1.0 + gate * (1.0 - sig))
        ).astype(bf16)
        d_up_ref[:, n : n + 256] = (d_hidden * act).astype(bf16)

    parts = []
    for n in range(0, C_TOK, 256):
        parts.append(
            nt(d_gate_ref[...], w_gate_ref[n : n + 256, :])
            + nt(d_up_ref[...], w_up_ref[n : n + 256, :])
        )
    d_normed = jnp.concatenate(parts, axis=1)
    hat = hat_ref[...]
    first = jnp.mean(d_normed, axis=-1, keepdims=True)
    second = jnp.mean(d_normed * hat, axis=-1, keepdims=True)
    d_resid = cot_ref[...].reshape(rows, C_TOK).astype(f32) + rstd * (
        d_normed - first - hat * second
    )
    grads_ref[...] = nt(d_resid.astype(bf16), w_out_ref[...]).astype(bf16)
    for copy in copies[7:]:
        copy.wait()
    masks = head_masks(tok_rows)
    for pair in range(PAIRS):
        low, high = windows(pair)
        total = jnp.zeros((keys_all, 2 * tok_rows), f32)
        for s in range(batch):
            grads = two_heads(
                grads_ref[s * tok_rows : (s + 1) * tok_rows, low:high], masks[pair % 4]
            )
            d_probs = nt(values_ref[s, :, low:high], grads)
            probs = probs_ref[s, pair]
            delta = jnp.sum(probs * d_probs, axis=0, keepdims=True)
            total = total + probs * (d_probs - delta)
        size = d_bias_ref.shape[2]
        for k in range(d_bias_ref.shape[0]):
            d_bias_ref[k, pair] = total[size * k : size * (k + 1)].astype(bf16)


def token_stage(
    pieces, bias, tokens_a, tokens_b, att_a, cot, probs_a, values_a, w_qkv, w_out, w_gate, w_up,
    w_down,
):
    batch, tok_rows, _ = cot.shape
    keys_all = tok_rows * len(pieces)
    rows = batch * tok_rows
    hidden = w_gate.shape[1]
    vmem = pl.BlockSpec(memory_space=pltpu.VMEM)
    hbm = pl.BlockSpec(memory_space=pl.ANY)
    return pl.pallas_call(
        functools.partial(token_kernel, count=len(pieces)),
        in_specs=[vmem] * (len(pieces) + 5) + [hbm] * 7,
        out_specs=[vmem] * 3,
        out_shape=[
            jax.ShapeDtypeStruct((rows, C_TOK), f32),
            jax.ShapeDtypeStruct((rows, hidden), bf16),
            jax.ShapeDtypeStruct(bias.shape, bf16),
        ],
        scratch_shapes=[
            pltpu.VMEM((3, C_TOK, C_TOK), bf16),
            pltpu.VMEM(w_out.shape, bf16),
            pltpu.VMEM(w_gate.shape, bf16),
            pltpu.VMEM(w_up.shape, bf16),
            pltpu.VMEM(w_down.shape, bf16),
            pltpu.VMEM((batch, PAIRS, keys_all, 2 * tok_rows), f32),
            pltpu.VMEM((batch, keys_all, C_TOK), bf16),
            pltpu.SemaphoreType.DMA((9,)),
        ]
        + attend_scratch(pieces[0].shape[0], tok_rows, keys_all)
        + [
            pltpu.VMEM((rows, C_TOK), bf16),
            pltpu.VMEM((rows, hidden), bf16),
            pltpu.VMEM((rows, hidden), bf16),
            pltpu.VMEM((rows, C_TOK), f32),
        ],
        compiler_params=pltpu.CompilerParams(vmem_limit_bytes=GRANT),
        cost_estimate=pl.CostEstimate(
            flops=10**10, bytes_accessed=2 * 10**7, transcendentals=10**6
        ),
        name="tokens",
    )(
        *pieces, bias, tokens_a, tokens_b, att_a, cot, probs_a, values_a, w_qkv, w_out, w_gate,
        w_up, w_down,
    )


def output_kernel(
    resid_ref, hidden_ref, w_down_ref, pair_ref, out_ref, hat_ref, rstd_ref, pairf_ref
):
    out_ref[...] = (resid_ref[...] + nn(hidden_ref[...], w_down_ref[...])).astype(bf16)
    rows, keys = pair_ref.shape[0], pair_ref.shape[1]
    for i in range(rows // 8):
        pairf_ref[8 * keys * i : 8 * keys * (i + 1), :] = (
            pair_ref[8 * i : 8 * i + 8].astype(f32).reshape(8 * keys, CZ)
        )

    def norm_step(j, carry):
        hat, rstd = norm_rows(pairf_ref[pl.ds(j, rows, stride=keys), :])
        at = pl.multiple_of(j * rows, rows)
        hat_ref[pl.ds(at, rows), :] = hat
        rstd_ref[pl.ds(at, rows), :] = jnp.broadcast_to(rstd, (rows, CZ))
        return carry

    lax.fori_loop(0, keys, norm_step, 0, unroll=4)


def output_stage(resid, hidden, w_down, pair):
    rows, keys = pair.shape[0], pair.shape[1]
    return pl.pallas_call(
        output_kernel,
        out_shape=[jax.ShapeDtypeStruct(resid.shape, bf16)]
        + [jax.ShapeDtypeStruct((rows * keys, CZ), f32)] * 2,
        scratch_shapes=[pltpu.VMEM((rows * keys, CZ), f32)],
        compiler_params=pltpu.CompilerParams(vmem_limit_bytes=GRANT),
        cost_estimate=pl.CostEstimate(
            flops=10**9, bytes_accessed=8 * 10**6, transcendentals=0
        ),
        name="output",
    )(resid, hidden, w_down, pair)


def grad_kernel(parts_ref, hat_ref, rstd_ref, gain_ref, w_bias_ref, out_ref, total_ref):
    keys = parts_ref.shape[2]
    rows = hat_ref.shape[0] // keys
    for pair in range(PAIRS):
        total = parts_ref[0, pair].astype(f32)
        for k in range(1, parts_ref.shape[0]):
            total = total + parts_ref[k, pair].astype(f32)
        total_ref[pair * keys : (pair + 1) * keys, :] = total
    weights = jnp.concatenate(split_heads(w_bias_ref[...]), axis=0) * gain_ref[...]
    weights = weights - jnp.mean(weights, axis=-1, keepdims=True)
    weights = jnp.concatenate([weights[0:PAIRS], weights[PAIRS:HEADS]], axis=1)
    w_high = weights.astype(bf16).astype(f32)
    w_middle = (weights - w_high).astype(bf16).astype(f32)
    w_low = weights - w_high - w_middle
    weights = jnp.concatenate([w_high, w_middle, w_low, w_high, w_middle, w_high], axis=0)
    weights = weights.astype(bf16)
    for j in range(keys):
        total = total_ref[pl.ds(j, PAIRS, stride=keys), :]
        high = total.astype(bf16).astype(f32)
        middle = (total - high).astype(bf16).astype(f32)
        low = total - high - middle
        stack = jnp.concatenate([high, high, high, middle, middle, low], axis=0)
        both = nn(stack.T.astype(bf16), weights)
        scaled = both[0:rows, 0:CZ] + both[rows : 2 * rows, CZ : 2 * CZ]
        hat = hat_ref[rows * j : rows * (j + 1), :]
        second = jnp.mean(scaled * hat, axis=-1, keepdims=True)
        out_ref[pl.ds(j, rows, stride=keys), :] = rstd_ref[rows * j : rows * (j + 1), :] * (
            scaled - hat * second
        )


def pair_back(parts, hat, rstd, pair_gain, w_bias_t):
    keys = parts.shape[2]
    rows = hat.shape[0] // keys
    out = pl.pallas_call(
        grad_kernel,
        out_shape=jax.ShapeDtypeStruct((rows * keys, CZ), f32),
        scratch_shapes=[pltpu.VMEM((keys * PAIRS, 2 * rows), f32)],
        compiler_params=pltpu.CompilerParams(vmem_limit_bytes=GRANT),
        cost_estimate=pl.CostEstimate(flops=10**8, bytes_accessed=4 * 10**6, transcendentals=0),
        name="pair_grad",
    )(parts, hat, rstd, pair_gain.reshape(1, CZ), w_bias_t)
    return out.reshape(rows, keys, CZ)


def swap(values, axis, k):
    return lax.ppermute(values, axis, [(i, i ^ k) for i in range(lax.axis_size(axis))])


def gather(values, axis):
    far = range(lax.axis_size(axis) - 1, 0, -1)
    return [values] + [swap(values, axis, k) for k in far][::-1]


def body(
    atom_feats, atom_counts, atom_mask, token_single, pair, pair_gain, w_bias, w_atom_qkv,
    w_atom_out, w_embed, w_qkv, w_out, w_gate, w_up, w_down, cotangent,
):
    batch, atom_rows, _ = atom_feats.shape
    tok_rows = token_single.shape[0]
    shards = lax.axis_size("tok")
    groups = lax.axis_size("samp")

    steps = [(i, i + 1) for i in range(shards - 1)]
    left = lax.ppermute(atom_feats[:, atom_rows - HALO :], "tok", steps)
    right = lax.ppermute(atom_feats[:, :HALO], "tok", [(j, i) for i, j in steps])

    w_bias_t = w_bias.T
    local_bias = pair_bias(pair, pair_gain, w_bias_t, groups)
    bias = lax.all_to_all(local_bias, "samp", 0, 0).reshape(groups, PAIRS, -1, 2 * tok_rows)

    mask = atom_mask.reshape(-1, 128)
    mask, local_bias = lax.optimization_barrier((mask, local_bias))

    each = batch // 2
    tokens, gathered = [], []
    for part in range(2):
        tok, normed = atom_stage(
            part, each, atom_feats, left, right, mask, atom_counts, token_single, w_atom_qkv,
            w_atom_out, w_embed,
        )
        tokens.append(tok)
        gathered.append(gather(normed, "tok"))
    att_a, probs_a, values_a = attend_stage(gathered[0], bias, w_qkv)
    resid, hidden, d_bias = token_stage(
        gathered[1], bias, *tokens, att_a, cotangent, probs_a, values_a, w_qkv, w_out, w_gate,
        w_up, w_down,
    )
    parts = lax.all_to_all(d_bias, "samp", 0, 0)
    token_out, hat, rstd = output_stage(resid, hidden, w_down, pair)
    pair_grad = pair_back(parts, hat, rstd, pair_gain, w_bias_t)
    token_out = token_out.reshape(batch, tok_rows, C_TOK)
    return (token_out, pair_grad)


def solution(mesh):
    in_specs = (
        P("samp", "tok", None),
        P("tok", None),
        P(),
        P("tok", None),
        P("tok", "samp", None),
        P(), P(), P(), P(), P(), P(), P(), P(), P(), P(),
        P("samp", "tok", None),
    )
    out_specs = (P("samp", "tok", None), P("tok", "samp", None))
    return jax.shard_map(body, mesh=mesh, in_specs=in_specs, out_specs=out_specs, check_vma=False)
```

```python
import functools

import jax
import jax.numpy as jnp
from jax import lax
from jax.experimental import pallas as pl
from jax.experimental.pallas import tpu as pltpu
from jax.sharding import PartitionSpec as P

C_ATOM = 128
ATOM_HEADS = 4
C_TOK = 768
HEADS = 16
ATOM_HD = 32
HD = 48
CZ = 128
HALO = 48
PAIRS = HEADS // 2
GRANT = 64 << 20
LOG2E = 1.4426950408889634

epsilon = 1e-05
f32 = jnp.float32
bf16 = jnp.bfloat16

WINDOWS = ((0, 128), (0, 256), (128, 384), (256, 384))


def nn(a, b):
    return lax.dot_general(a, b, (((1,), (0,)), ((), ())), preferred_element_type=f32)


def nt(a, b):
    return lax.dot_general(a, b, (((1,), (1,)), ((), ())), preferred_element_type=f32)


def tn(a, b):
    return lax.dot_general(a, b, (((0,), (0,)), ((), ())), preferred_element_type=f32)


def start_all(moves, sems):
    copies = [pltpu.make_async_copy(src, dst, sems.at[i]) for i, (src, dst) in enumerate(moves)]
    for copy in copies:
        copy.start()
    return copies


def norm_rows(values):
    center = values - jnp.mean(values, axis=-1, keepdims=True)
    scale_inv = lax.rsqrt(jnp.mean(center * center, axis=-1, keepdims=True) + epsilon)
    return (center * scale_inv, scale_inv)


def iota(shape, dim):
    return lax.broadcasted_iota(jnp.int32, shape, dim)


def pick_heads(parity):
    row, col = iota((PAIRS, HEADS), 0), iota((PAIRS, HEADS), 1)
    return (col == 2 * row + parity).astype(f32).astype(bf16)


def split_heads(w_bias_t):
    return [nn(pick_heads(parity), w_bias_t) for parity in range(2)]


def bias_kernel(pair_ref, gain_ref, w_bias_ref, out_ref, scaled_ref, stage_ref):
    rows, keys = pair_ref.shape[0], pair_ref.shape[1]
    gain = gain_ref[...]

    def norm_step(i, carry):
        block = pair_ref[pl.ds(i * 8, 8)].astype(f32).reshape(8 * keys, CZ)
        hat, unused = norm_rows(block)
        scaled_ref[pl.ds(pl.multiple_of(i * 8 * keys, 8 * keys), 8 * keys), :] = hat * gain
        return carry

    lax.fori_loop(0, rows // 8, norm_step, 0, unroll=True)
    weights = jnp.concatenate(split_heads(w_bias_ref[...]), axis=1).astype(bf16)
    blank = jnp.zeros((rows, CZ), bf16)
    for j in range(keys):
        block = scaled_ref[pl.ds(j, rows, stride=keys), :].astype(bf16)
        both = jnp.concatenate(
            [jnp.concatenate([block, blank], axis=1), jnp.concatenate([blank, block], axis=1)],
            axis=0,
        )
        stage_ref[pl.ds(j, PAIRS, stride=keys), :] = nt(weights, both)
    for k in range(out_ref.shape[0]):
        out_ref[k] = stage_ref[...].astype(bf16)


def pair_bias(pair, pair_gain, w_bias_t, copies):
    rows, keys = pair.shape[0], pair.shape[1]
    return pl.pallas_call(
        bias_kernel,
        out_shape=jax.ShapeDtypeStruct((copies, keys * PAIRS, 2 * rows), bf16),
        scratch_shapes=[
            pltpu.VMEM((rows * keys, CZ), f32),
            pltpu.VMEM((keys * PAIRS, 2 * rows), f32),
        ],
        compiler_params=pltpu.CompilerParams(vmem_limit_bytes=GRANT),
        cost_estimate=pl.CostEstimate(flops=10**7, bytes_accessed=10**7, transcendentals=0),
        name="pair_bias",
    )(pair, pair_gain.reshape(1, CZ), w_bias_t)


def atom_kernel(
    feats_hbm, left_hbm, right_hbm, mask_hbm, counts_hbm, single_hbm, w_qkv_hbm, w_out_hbm,
    w_embed_hbm, tokens_ref, normed_ref, mask_ref, counts_ref, single_ref, w_qkv_ref, w_out_ref,
    w_embed_ref, sems, padded_ref, qkv_a, qkv_b, scores_a, scores_b, probs_a, probs_b, mixed_ref,
    split_ref, keybias_ref, onehot_ref, pooled_ref, *, first,
):
    batch, atoms = tokens_ref.shape[0], feats_hbm.shape[1]
    padded = atoms + 2 * HALO
    moves = [(counts_hbm, counts_ref), (mask_hbm, mask_ref), (w_qkv_hbm, w_qkv_ref)]
    for s in range(batch):
        moves.append((left_hbm.at[first + s], padded_ref.at[s, pl.ds(0, HALO)]))
        moves.append((feats_hbm.at[first + s], padded_ref.at[s, pl.ds(HALO, atoms)]))
        moves.append((right_hbm.at[first + s], padded_ref.at[s, pl.ds(HALO + atoms, HALO)]))
    moves += [(w_out_hbm, w_out_ref), (w_embed_hbm, w_embed_ref), (single_hbm, single_ref)]
    copies = start_all(moves, sems)
    for copy in copies[0:2]:
        copy.wait()
    tok_rows = single_ref.shape[0]
    blocks = atoms // 128
    chunks = atoms // 256
    qkv_refs = (qkv_a, qkv_b)

    eye = iota((128, 128), 0) == iota((128, 128), 1)
    for b in range(-1, blocks + 1):
        at = lax.axis_index("tok") * blocks + b
        inside = jnp.where((at >= 0) & (at < mask_ref.shape[0]), 1, 0)
        row = mask_ref[pl.ds(jnp.clip(at, 0, mask_ref.shape[0] - 1), 1), :] * inside
        row = jnp.broadcast_to(row.astype(f32), (128, 128))
        col = jnp.sum(jnp.where(eye, row, 0.0), axis=1, keepdims=True)
        col = jnp.broadcast_to((col - 1.0) * 1e30, (128, 128))
        if b < 0:
            keybias_ref[0:HALO, :] = col[128 - HALO : 128]
        elif b < blocks:
            keybias_ref[HALO + 128 * b : HALO + 128 * b + 128, :] = col
        else:
            keybias_ref[HALO + atoms : padded, :] = col[0:HALO]
    counts = jnp.broadcast_to(counts_ref[...].astype(f32), (tok_rows, tok_rows))
    sub, lane = iota((tok_rows, tok_rows), 0), iota((tok_rows, tok_rows), 1)
    start = jnp.sum(jnp.where(lane < sub, counts, 0.0), axis=1, keepdims=True)
    own = jnp.sum(jnp.where(lane == sub, counts, 0.0), axis=1, keepdims=True)
    pos = iota((tok_rows, 256), 1).astype(f32)
    for g in range(chunks):
        at = pos + float(g * 256)
        hit = jnp.where((at >= start) & (at < start + own), 1.0, 0.0).astype(bf16)
        onehot_ref[g] = jnp.concatenate([hit, hit], axis=1)
    pooled_ref[...] = jnp.zeros_like(pooled_ref)
    head_of = iota((32, 128), 1) // ATOM_HD
    head_mask = [(head_of == h).astype(f32).astype(bf16) for h in range(ATOM_HEADS)]
    own_atom = (iota((32, 128), 1) % 32) == iota((32, 128), 0)
    factor = ATOM_HD ** (-0.5) * LOG2E
    stride = padded // chunks // 16 * 16
    span = padded - stride * (chunks - 1)

    def qkv_step(s, i):
        at = pl.multiple_of(i * stride, 16)
        normed, unused = norm_rows(padded_ref[s, pl.ds(at, span), :].astype(f32))
        qkv_refs[s % 2][pl.ds(at, span), :] = nn(normed.astype(bf16), w_qkv_ref[...]).astype(bf16)

    def score_step(s, group, to_ref):
        qkv_ref = qkv_refs[s % 2]
        for k in range(2):
            base = pl.multiple_of(group * 128 + 64 * k, 64)
            queries = qkv_ref[pl.ds(base + HALO, 64), 0:C_ATOM]
            spread = jnp.concatenate(
                [
                    queries[32 * w : 32 * w + 32] * head_mask[h]
                    for w in range(2)
                    for h in range(ATOM_HEADS)
                ],
                axis=0,
            )
            to_ref[k] = nt(qkv_ref[pl.ds(base, 160), C_ATOM : 2 * C_ATOM], spread)

    def softmax_step(group, from_ref, to_ref):
        for k in range(2):
            base = pl.multiple_of(group * 128 + 64 * k, 64)
            for w in range(2):
                keybias = keybias_ref[pl.ds(base + 32 * w, 128), :]
                keybias = jnp.concatenate(
                    [keybias[0:48], jnp.where(own_atom, 0.0, keybias[48:80]), keybias[80:128]],
                    axis=0,
                )
                scores = from_ref[k, 32 * w : 32 * w + 128, 128 * w : 128 * w + 128] + keybias
                expo = jnp.exp2((scores - jnp.max(scores, axis=0, keepdims=True)) * factor)
                weights = expo * (1.0 / jnp.sum(expo, axis=0, keepdims=True))
                to_ref[2 * k + w] = weights.astype(bf16)

    def value_step(s, group, from_ref):
        qkv_ref = qkv_refs[s % 2]
        for k in range(2):
            base = pl.multiple_of(group * 128 + 64 * k, 64)
            mixes = []
            for w in range(2):
                values = qkv_ref[pl.ds(base + 32 * w, 128), 2 * C_ATOM : 3 * C_ATOM]
                part = tn(from_ref[2 * k + w], values)
                mix = part[0:32]
                for h in range(1, ATOM_HEADS):
                    mix = jnp.where(head_of == h, part[32 * h : 32 * h + 32], mix)
                mixes.append(mix.astype(bf16))
            mixed_ref[s, pl.ds(base, 64), :] = jnp.concatenate(mixes, axis=0)

    def embed_step(s, g):
        base = pl.multiple_of(g * 256, 256)
        feats = padded_ref[s, pl.ds(base + HALO, 256), :].astype(f32)
        updated = (feats + nn(mixed_ref[s, pl.ds(base, 256), :], w_out_ref[...])).astype(bf16)
        embedded = jnp.maximum(nn(updated, w_embed_ref[...]), 0.0)
        high = embedded.astype(bf16)
        split_ref[0:256, :] = high
        split_ref[256:512, :] = (embedded - high.astype(f32)).astype(bf16)
        pooled_ref[s] += nn(onehot_ref[g], split_ref[...])

    for copy in copies[2:6]:
        copy.wait()
    for i in range(chunks):
        qkv_step(0, i)
    for copy in copies[6:]:
        copy.wait()
    for s in range(batch):
        score_step(s, 0, scores_a)

        def window_step(i, carry, s=s, lagging=True):
            even, odd = 2 * i, 2 * i + 1
            if lagging:
                embed_step(s, i - 2)
            if s + 1 < batch:
                qkv_step(s + 1, i)
            score_step(s, odd, scores_b)
            softmax_step(even, scores_a, probs_a)
            value_step(s, jnp.maximum(even - 1, 0), probs_b)
            score_step(s, jnp.minimum(odd + 1, 2 * chunks - 1), scores_a)
            softmax_step(odd, scores_b, probs_b)
            value_step(s, even, probs_a)
            return carry

        for i in range(2):
            if s > 0:
                embed_step(s - 1, chunks - 2 + i)
            window_step(i, 0, lagging=False)
        lax.fori_loop(2, chunks, window_step, 0)
        value_step(s, 2 * chunks - 1, probs_b)
    for i in range(2):
        embed_step(batch - 1, chunks - 2 + i)
    for s in range(batch):
        tokens = pooled_ref[s] / own + single_ref[...].astype(f32)
        tokens_ref[s] = tokens
        normed_ref[s] = norm_rows(tokens)[0].astype(bf16)


def atom_stage(part, batch, feats, left, right, mask, counts, single, w_qkv, w_out, w_embed):
    atoms = feats.shape[1]
    tok_rows = single.shape[0]
    padded = atoms + 2 * HALO
    return pl.pallas_call(
        functools.partial(atom_kernel, first=part * batch),
        in_specs=[pl.BlockSpec(memory_space=pl.ANY)] * 9,
        out_specs=[pl.BlockSpec(memory_space=pltpu.VMEM)] * 2,
        out_shape=[
            jax.ShapeDtypeStruct((batch, tok_rows, C_TOK), f32),
            jax.ShapeDtypeStruct((batch, tok_rows, C_TOK), bf16),
        ],
        scratch_shapes=[
            pltpu.VMEM(mask.shape, jnp.int32),
            pltpu.VMEM(counts.shape, jnp.int32),
            pltpu.VMEM(single.shape, bf16),
            pltpu.VMEM(w_qkv.shape, bf16),
            pltpu.VMEM(w_out.shape, bf16),
            pltpu.VMEM(w_embed.shape, bf16),
            pltpu.SemaphoreType.DMA((6 + 3 * batch,)),
            pltpu.VMEM((batch, padded, C_ATOM), bf16),
            pltpu.VMEM((padded, 3 * C_ATOM), bf16),
            pltpu.VMEM((padded, 3 * C_ATOM), bf16),
            pltpu.VMEM((2, 160, 256), f32),
            pltpu.VMEM((2, 160, 256), f32),
            pltpu.VMEM((4, 128, 128), bf16),
            pltpu.VMEM((4, 128, 128), bf16),
            pltpu.VMEM((batch, atoms, C_ATOM), bf16),
            pltpu.VMEM((512, C_TOK), bf16),
            pltpu.VMEM((padded, 128), f32),
            pltpu.VMEM((atoms // 256, tok_rows, 512), bf16),
            pltpu.VMEM((batch, tok_rows, C_TOK), f32),
        ],
        compiler_params=pltpu.CompilerParams(vmem_limit_bytes=GRANT),
        cost_estimate=pl.CostEstimate(
            flops=10**10, bytes_accessed=4 * 10**6, transcendentals=3 * 10**6
        ),
        name="atoms",
    )(feats, left, right, mask, counts, single, w_qkv, w_out, w_embed)


def head_masks(rows):
    masks = []
    for pair in range(4):
        low, high = WINDOWS[pair]
        lane = iota((rows, high - low), 1) + low
        first = 2 * pair * HD
        masks.append(
            [(lane >= first + HD * k) & (lane < first + HD * (k + 1)) for k in range(2)]
        )
    return masks


def two_heads(block, masks):
    blank = jnp.zeros_like(block)
    return jnp.concatenate([jnp.where(mask, block, blank) for mask in masks], axis=0)


def project_moves(piece_hbms, w_qkv_hbm, w_qkv_ref, all_ref):
    tok_rows = piece_hbms[0].shape[1]
    weights = [
        (w_qkv_hbm.at[:, pl.ds(C_TOK * i, C_TOK)], w_qkv_ref.at[i]) for i in range(3)
    ]
    here = lax.axis_index("tok")
    pieces = []
    for k, piece in enumerate(piece_hbms):
        at = pl.multiple_of((here ^ k) * tok_rows, tok_rows)
        pieces.append((piece, all_ref.at[:, pl.ds(at, tok_rows), :]))
    return [pieces[0], weights[0]] + pieces[1:] + weights[1:]


def project(copies, w_qkv_ref, all_ref, queries_ref, keys_ref, values_ref):
    batch = all_ref.shape[0]
    tok_rows = queries_ref.shape[0] // batch
    at = pl.multiple_of(lax.axis_index("tok") * tok_rows, tok_rows)
    for copy in copies[0:2]:
        copy.wait()
    own = jnp.concatenate([all_ref[s, pl.ds(at, tok_rows), :] for s in range(batch)], axis=0)
    for n in range(0, C_TOK, 256):
        queries_ref[:, n : n + 256] = nn(own, w_qkv_ref[0, :, n : n + 256]).astype(bf16)
    for copy in copies[2:-1]:
        copy.wait()
    for which, to_ref in ((1, keys_ref), (2, values_ref)):
        if which == 2:
            copies[-1].wait()
        for n in range(0, C_TOK, 256):
            for s in range(batch):
                to_ref[s, :, n : n + 256] = nn(
                    all_ref[s], w_qkv_ref[which, :, n : n + 256]
                ).astype(bf16)


def windows(pair):
    low, high = WINDOWS[pair % 4]
    return 384 * (pair // 4) + low, 384 * (pair // 4) + high


def attend(bias_ref, queries_ref, keys_ref, values_ref, probs_ref, att_ref, done=None):
    batch, keys_all = keys_ref.shape[0], keys_ref.shape[1]
    tok_rows = queries_ref.shape[0] // batch
    masks = head_masks(tok_rows)
    factor = HD ** (-0.5)

    for s in range(batch):
        at = s * tok_rows
        for pair in range(PAIRS):
            low, high = windows(pair)
            queries = two_heads(queries_ref[pl.ds(at, tok_rows), low:high], masks[pair % 4])
            probs_ref[s, pair] = nt(keys_ref[s, :, low:high], queries)
        for pair in range(PAIRS):
            scores = probs_ref[s, pair] * factor
            bias = [bias_ref[k, pair].astype(f32) for k in range(bias_ref.shape[0])]
            scores = scores + jnp.concatenate(bias, axis=0)
            expo = jnp.exp(scores - jnp.max(scores, axis=0, keepdims=True))
            probs_ref[s, pair] = expo * (1.0 / jnp.sum(expo, axis=0, keepdims=True))
        lanes = [jnp.zeros((tok_rows, 128), f32) for _ in range(C_TOK // 128)]
        for pair in range(PAIRS):
            low, high = windows(pair)
            part = tn(probs_ref[s, pair].astype(bf16), values_ref[s, :, low:high])
            first, second = masks[pair % 4]
            mix = jnp.where(first, part[0:tok_rows], 0.0)
            mix = jnp.where(second, part[tok_rows : 2 * tok_rows], mix)
            for t in range((high - low) // 128):
                lanes[low // 128 + t] = lanes[low // 128 + t] + mix[:, 128 * t : 128 * t + 128]
        for t in range(C_TOK // 128):
            att_ref[pl.ds(at, tok_rows), 128 * t : 128 * t + 128] = lanes[t].astype(bf16)
        if done is not None:
            done(s)


def attend_kernel(*refs, count):
    (
        bias_hbm, w_qkv_hbm, att_ref, probs_hbm, values_hbm, w_qkv_ref, bias_ref, probs_ref,
        values_ref, sems, all_ref, queries_ref, keys_ref,
    ) = refs[count:]
    batch = all_ref.shape[0]
    moves = project_moves(refs[:count], w_qkv_hbm, w_qkv_ref, all_ref)
    copies = start_all(moves + [(bias_hbm, bias_ref)], sems)
    project(copies[:-1], w_qkv_ref, all_ref, queries_ref, keys_ref, values_ref)
    copies[-1].wait()
    back = [
        pltpu.make_async_copy(probs_ref.at[s], probs_hbm.at[s], sems.at[s]) for s in range(batch)
    ] + [pltpu.make_async_copy(values_ref, values_hbm, sems.at[batch])]
    back[batch].start()
    attend(
        bias_ref, queries_ref, keys_ref, values_ref, probs_ref, att_ref, lambda s: back[s].start()
    )
    for copy in back:
        copy.wait()


def attend_scratch(batch, tok_rows, keys_all):
    return [
        pltpu.VMEM((batch, keys_all, C_TOK), bf16),
        pltpu.VMEM((batch * tok_rows, C_TOK), bf16),
        pltpu.VMEM((batch, keys_all, C_TOK), bf16),
    ]


def attend_stage(pieces, bias, w_qkv):
    batch, tok_rows, _ = pieces[0].shape
    keys_all = tok_rows * len(pieces)
    vmem = pl.BlockSpec(memory_space=pltpu.VMEM)
    hbm = pl.BlockSpec(memory_space=pl.ANY)
    return pl.pallas_call(
        functools.partial(attend_kernel, count=len(pieces)),
        in_specs=[hbm] * (len(pieces) + 2),
        out_specs=[vmem, hbm, hbm],
        out_shape=[
            jax.ShapeDtypeStruct((batch * tok_rows, C_TOK), bf16),
            jax.ShapeDtypeStruct((batch, PAIRS, keys_all, 2 * tok_rows), f32),
            jax.ShapeDtypeStruct((batch, keys_all, C_TOK), bf16),
        ],
        scratch_shapes=[
            pltpu.VMEM((3, C_TOK, C_TOK), bf16),
            pltpu.VMEM(bias.shape, bf16),
            pltpu.VMEM((batch, PAIRS, keys_all, 2 * tok_rows), f32),
            pltpu.VMEM((batch, keys_all, C_TOK), bf16),
            pltpu.SemaphoreType.DMA((4 + len(pieces),)),
        ]
        + attend_scratch(batch, tok_rows, keys_all),
        compiler_params=pltpu.CompilerParams(vmem_limit_bytes=GRANT),
        cost_estimate=pl.CostEstimate(
            flops=4 * 10**9, bytes_accessed=10**7, transcendentals=10**6
        ),
        name="attend",
    )(*pieces, bias, w_qkv)


def token_kernel(*refs, count):
    (
        bias_hbm, tokens_a_hbm, tokens_b_hbm, att_a_hbm, cot_hbm, probs_a_hbm, values_a_hbm,
        w_qkv_hbm, w_out_hbm, w_gate_hbm, w_up_hbm, w_down_hbm,
        resid_hbm, hidden_hbm, d_bias_ref,
        bias_ref, tokens_ref, att_a_ref, cot_ref, resid_ref, hidden_ref,
        w_qkv_ref, w_out_ref, w_gate_ref, w_up_ref, w_down_ref, probs_ref, values_ref, sems,
        all_ref, queries_ref, keys_ref, grads_ref, d_gate_ref, d_up_ref, hat_ref,
    ) = refs[count:]
    batch, tok_rows = cot_ref.shape[0], cot_ref.shape[1]
    keys_all = values_ref.shape[1]
    rows = batch * tok_rows
    ahead = values_a_hbm.shape[0]
    lead = ahead * tok_rows
    moves = project_moves(refs[:count], w_qkv_hbm, w_qkv_ref, all_ref)
    projecting = len(moves)
    moves += [
        (bias_hbm, bias_ref), (w_out_hbm, w_out_ref), (att_a_hbm, att_a_ref),
        (tokens_a_hbm, tokens_ref.at[pl.ds(0, ahead)]),
        (tokens_b_hbm, tokens_ref.at[pl.ds(ahead, batch - ahead)]), (cot_hbm, cot_ref),
        (w_down_hbm, w_down_ref), (w_gate_hbm, w_gate_ref), (w_up_hbm, w_up_ref),
        (values_a_hbm, values_ref.at[pl.ds(0, ahead)]), (probs_a_hbm, probs_ref.at[pl.ds(0, ahead)]),
    ]
    copies = start_all(moves, sems)
    own_values = values_ref.at[pl.ds(ahead, batch - ahead)]
    own_probs = probs_ref.at[pl.ds(ahead, batch - ahead)]
    project(copies[:projecting], w_qkv_ref, all_ref, queries_ref, keys_ref, own_values)
    copies = copies[projecting:]
    copies[0].wait()
    attend(bias_ref, queries_ref, keys_ref, own_values, own_probs, queries_ref)

    for copy in copies[1:5]:
        copy.wait()
    tokens = tokens_ref[...].reshape(rows, C_TOK)
    resid_ref[0:lead, :] = tokens[0:lead] + nn(att_a_ref[...], w_out_ref[...])
    resid_ref[lead:rows, :] = tokens[lead:rows] + nn(queries_ref[...], w_out_ref[...])
    back = [
        pltpu.make_async_copy(resid_ref, resid_hbm, sems.at[0]),
        pltpu.make_async_copy(hidden_ref, hidden_hbm, sems.at[1]),
    ]
    back[0].start()
    hat, rstd = norm_rows(resid_ref[...])
    hat_ref[...] = hat
    grads_ref[...] = hat.astype(bf16)
    for copy in copies[5:9]:
        copy.wait()

    for n in range(0, w_gate_ref.shape[1], 256):
        shaped = grads_ref[...]
        gate = nn(shaped, w_gate_ref[:, n : n + 256])
        up = nn(shaped, w_up_ref[:, n : n + 256])
        d_hidden = nt(cot_ref[...].reshape(rows, C_TOK), w_down_ref[n : n + 256, :])
        sig = 1.0 / (1.0 + jnp.exp(-gate))
        act = gate * sig
        hidden_ref[:, n : n + 256] = (act * up).astype(bf16)
        d_gate_ref[:, n : n + 256] = (
            d_hidden * up * sig * (1.0 + gate * (1.0 - sig))
        ).astype(bf16)
        d_up_ref[:, n : n + 256] = (d_hidden * act).astype(bf16)

    back[1].start()
    parts = []
    for n in range(0, C_TOK, 256):
        parts.append(
            nt(d_gate_ref[...], w_gate_ref[n : n + 256, :])
            + nt(d_up_ref[...], w_up_ref[n : n + 256, :])
        )
    d_normed = jnp.concatenate(parts, axis=1)
    hat = hat_ref[...]
    first = jnp.mean(d_normed, axis=-1, keepdims=True)
    second = jnp.mean(d_normed * hat, axis=-1, keepdims=True)
    d_resid = cot_ref[...].reshape(rows, C_TOK).astype(f32) + rstd * (
        d_normed - first - hat * second
    )
    grads_ref[...] = nt(d_resid.astype(bf16), w_out_ref[...]).astype(bf16)
    for copy in copies[9:]:
        copy.wait()
    masks = head_masks(tok_rows)
    for pair in range(PAIRS):
        low, high = windows(pair)
        total = jnp.zeros((keys_all, 2 * tok_rows), f32)
        for s in range(batch):
            grads = two_heads(
                grads_ref[s * tok_rows : (s + 1) * tok_rows, low:high], masks[pair % 4]
            )
            d_probs = nt(values_ref[s, :, low:high], grads)
            probs = probs_ref[s, pair]
            delta = jnp.sum(probs * d_probs, axis=0, keepdims=True)
            total = total + probs * (d_probs - delta)
        size = d_bias_ref.shape[2]
        for k in range(d_bias_ref.shape[0]):
            d_bias_ref[k, pair] = total[size * k : size * (k + 1)].astype(bf16)
    for copy in back:
        copy.wait()


def token_stage(
    pieces, bias, tokens_a, tokens_b, att_a, cot, probs_a, values_a, w_qkv, w_out, w_gate, w_up,
    w_down,
):
    batch, tok_rows, _ = cot.shape
    keys_all = tok_rows * len(pieces)
    rows = batch * tok_rows
    hidden = w_gate.shape[1]
    vmem = pl.BlockSpec(memory_space=pltpu.VMEM)
    hbm = pl.BlockSpec(memory_space=pl.ANY)
    return pl.pallas_call(
        functools.partial(token_kernel, count=len(pieces)),
        in_specs=[hbm] * (len(pieces) + 12),
        out_specs=[hbm, hbm, vmem],
        out_shape=[
            jax.ShapeDtypeStruct((rows, C_TOK), f32),
            jax.ShapeDtypeStruct((rows, hidden), bf16),
            jax.ShapeDtypeStruct(bias.shape, bf16),
        ],
        scratch_shapes=[
            pltpu.VMEM(bias.shape, bf16),
            pltpu.VMEM(cot.shape, f32),
            pltpu.VMEM(att_a.shape, bf16),
            pltpu.VMEM(cot.shape, bf16),
            pltpu.VMEM((rows, C_TOK), f32),
            pltpu.VMEM((rows, hidden), bf16),
            pltpu.VMEM((3, C_TOK, C_TOK), bf16),
            pltpu.VMEM(w_out.shape, bf16),
            pltpu.VMEM(w_gate.shape, bf16),
            pltpu.VMEM(w_up.shape, bf16),
            pltpu.VMEM(w_down.shape, bf16),
            pltpu.VMEM((batch, PAIRS, keys_all, 2 * tok_rows), f32),
            pltpu.VMEM((batch, keys_all, C_TOK), bf16),
            pltpu.SemaphoreType.DMA((14 + len(pieces),)),
        ]
        + attend_scratch(pieces[0].shape[0], tok_rows, keys_all)
        + [
            pltpu.VMEM((rows, C_TOK), bf16),
            pltpu.VMEM((rows, hidden), bf16),
            pltpu.VMEM((rows, hidden), bf16),
            pltpu.VMEM((rows, C_TOK), f32),
        ],
        compiler_params=pltpu.CompilerParams(vmem_limit_bytes=GRANT),
        cost_estimate=pl.CostEstimate(
            flops=10**10, bytes_accessed=2 * 10**7, transcendentals=10**6
        ),
        name="tokens",
    )(
        *pieces, bias, tokens_a, tokens_b, att_a, cot, probs_a, values_a, w_qkv, w_out, w_gate,
        w_up, w_down,
    )


def output_kernel(
    resid_ref, hidden_ref, w_down_ref, pair_ref, out_ref, hat_ref, rstd_ref, pairf_ref
):
    out_ref[...] = (resid_ref[...] + nn(hidden_ref[...], w_down_ref[...])).astype(bf16)
    rows, keys = pair_ref.shape[0], pair_ref.shape[1]
    for i in range(rows // 8):
        pairf_ref[8 * keys * i : 8 * keys * (i + 1), :] = (
            pair_ref[8 * i : 8 * i + 8].astype(f32).reshape(8 * keys, CZ)
        )

    def norm_step(j, carry):
        hat, rstd = norm_rows(pairf_ref[pl.ds(j, rows, stride=keys), :])
        at = pl.multiple_of(j * rows, rows)
        hat_ref[pl.ds(at, rows), :] = hat
        rstd_ref[pl.ds(at, rows), :] = jnp.broadcast_to(rstd, (rows, CZ))
        return carry

    lax.fori_loop(0, keys, norm_step, 0, unroll=4)


def output_stage(resid, hidden, w_down, pair):
    rows, keys = pair.shape[0], pair.shape[1]
    return pl.pallas_call(
        output_kernel,
        out_shape=[jax.ShapeDtypeStruct(resid.shape, bf16)]
        + [jax.ShapeDtypeStruct((rows * keys, CZ), f32)] * 2,
        scratch_shapes=[pltpu.VMEM((rows * keys, CZ), f32)],
        compiler_params=pltpu.CompilerParams(vmem_limit_bytes=GRANT),
        cost_estimate=pl.CostEstimate(
            flops=10**9, bytes_accessed=8 * 10**6, transcendentals=0
        ),
        name="output",
    )(resid, hidden, w_down, pair)


def grad_kernel(parts_ref, hat_ref, rstd_ref, gain_ref, w_bias_ref, out_ref, total_ref):
    keys = parts_ref.shape[2]
    rows = hat_ref.shape[0] // keys
    for pair in range(PAIRS):
        total = parts_ref[0, pair].astype(f32)
        for k in range(1, parts_ref.shape[0]):
            total = total + parts_ref[k, pair].astype(f32)
        total_ref[pair * keys : (pair + 1) * keys, :] = total
    weights = jnp.concatenate(split_heads(w_bias_ref[...]), axis=0) * gain_ref[...]
    weights = weights - jnp.mean(weights, axis=-1, keepdims=True)
    weights = jnp.concatenate([weights[0:PAIRS], weights[PAIRS:HEADS]], axis=1)
    w_high = weights.astype(bf16).astype(f32)
    w_middle = (weights - w_high).astype(bf16).astype(f32)
    w_low = weights - w_high - w_middle
    weights = jnp.concatenate([w_high, w_middle, w_low, w_high, w_middle, w_high], axis=0)
    weights = weights.astype(bf16)
    for j in range(keys):
        total = total_ref[pl.ds(j, PAIRS, stride=keys), :]
        high = total.astype(bf16).astype(f32)
        middle = (total - high).astype(bf16).astype(f32)
        low = total - high - middle
        stack = jnp.concatenate([high, high, high, middle, middle, low], axis=0)
        both = nn(stack.T.astype(bf16), weights)
        scaled = both[0:rows, 0:CZ] + both[rows : 2 * rows, CZ : 2 * CZ]
        hat = hat_ref[rows * j : rows * (j + 1), :]
        second = jnp.mean(scaled * hat, axis=-1, keepdims=True)
        out_ref[pl.ds(j, rows, stride=keys), :] = rstd_ref[rows * j : rows * (j + 1), :] * (
            scaled - hat * second
        )


def pair_back(parts, hat, rstd, pair_gain, w_bias_t):
    keys = parts.shape[2]
    rows = hat.shape[0] // keys
    out = pl.pallas_call(
        grad_kernel,
        out_shape=jax.ShapeDtypeStruct((rows * keys, CZ), f32),
        scratch_shapes=[pltpu.VMEM((keys * PAIRS, 2 * rows), f32)],
        compiler_params=pltpu.CompilerParams(vmem_limit_bytes=GRANT),
        cost_estimate=pl.CostEstimate(flops=10**8, bytes_accessed=4 * 10**6, transcendentals=0),
        name="pair_grad",
    )(parts, hat, rstd, pair_gain.reshape(1, CZ), w_bias_t)
    return out.reshape(rows, keys, CZ)


def swap(values, axis, k):
    return lax.ppermute(values, axis, [(i, i ^ k) for i in range(lax.axis_size(axis))])


def gather(values, axis):
    far = range(lax.axis_size(axis) - 1, 0, -1)
    return [values] + [swap(values, axis, k) for k in far][::-1]


def body(
    atom_feats, atom_counts, atom_mask, token_single, pair, pair_gain, w_bias, w_atom_qkv,
    w_atom_out, w_embed, w_qkv, w_out, w_gate, w_up, w_down, cotangent,
):
    batch, atom_rows, _ = atom_feats.shape
    tok_rows = token_single.shape[0]
    shards = lax.axis_size("tok")
    groups = lax.axis_size("samp")

    steps = [(i, i + 1) for i in range(shards - 1)]
    left = lax.ppermute(atom_feats[:, atom_rows - HALO :], "tok", steps)
    right = lax.ppermute(atom_feats[:, :HALO], "tok", [(j, i) for i, j in steps])

    w_bias_t = w_bias.T
    local_bias = pair_bias(pair, pair_gain, w_bias_t, groups)
    bias = lax.all_to_all(local_bias, "samp", 0, 0).reshape(groups, PAIRS, -1, 2 * tok_rows)

    mask = atom_mask.reshape(-1, 128)
    mask, local_bias = lax.optimization_barrier((mask, local_bias))

    each = batch // 2
    tokens, gathered = [], []
    for part in range(2):
        tok, normed = atom_stage(
            part, each, atom_feats, left, right, mask, atom_counts, token_single, w_atom_qkv,
            w_atom_out, w_embed,
        )
        tokens.append(tok)
        gathered.append(gather(normed, "tok"))
    att_a, probs_a, values_a = attend_stage(gathered[0], bias, w_qkv)
    resid, hidden, d_bias = token_stage(
        gathered[1], bias, *tokens, att_a, cotangent, probs_a, values_a, w_qkv, w_out, w_gate,
        w_up, w_down,
    )
    parts = lax.all_to_all(d_bias, "samp", 0, 0)
    token_out, hat, rstd = output_stage(resid, hidden, w_down, pair)
    pair_grad = pair_back(parts, hat, rstd, pair_gain, w_bias_t)
    token_out = token_out.reshape(batch, tok_rows, C_TOK)
    return (token_out, pair_grad)


def solution(mesh):
    in_specs = (
        P("samp", "tok", None),
        P("tok", None),
        P(),
        P("tok", None),
        P("tok", "samp", None),
        P(), P(), P(), P(), P(), P(), P(), P(), P(), P(),
        P("samp", "tok", None),
    )
    out_specs = (P("samp", "tok", None), P("tok", "samp", None))
    return jax.shard_map(body, mesh=mesh, in_specs=in_specs, out_specs=out_specs, check_vma=False)
```

```python
import functools

import jax
import jax.numpy as jnp
from jax import lax
from jax.experimental import pallas as pl
from jax.experimental.pallas import tpu as pltpu
from jax.sharding import PartitionSpec as P

C_ATOM = 128
ATOM_HEADS = 4
C_TOK = 768
HEADS = 16
ATOM_HD = 32
HD = 48
CZ = 128
HALO = 48
PAIRS = HEADS // 2
GRANT = 64 << 20
LOG2E = 1.4426950408889634

epsilon = 1e-05
f32 = jnp.float32
bf16 = jnp.bfloat16

WINDOWS = ((0, 128), (0, 256), (128, 384), (256, 384))


def nn(a, b):
    return lax.dot_general(a, b, (((1,), (0,)), ((), ())), preferred_element_type=f32)


def nt(a, b):
    return lax.dot_general(a, b, (((1,), (1,)), ((), ())), preferred_element_type=f32)


def tn(a, b):
    return lax.dot_general(a, b, (((0,), (0,)), ((), ())), preferred_element_type=f32)


def start_all(moves, sems):
    copies = [pltpu.make_async_copy(src, dst, sems.at[i]) for i, (src, dst) in enumerate(moves)]
    for copy in copies:
        copy.start()
    return copies


def norm_rows(values):
    center = values - jnp.mean(values, axis=-1, keepdims=True)
    scale_inv = lax.rsqrt(jnp.mean(center * center, axis=-1, keepdims=True) + epsilon)
    return (center * scale_inv, scale_inv)


def iota(shape, dim):
    return lax.broadcasted_iota(jnp.int32, shape, dim)


def pick_heads(parity):
    row, col = iota((PAIRS, HEADS), 0), iota((PAIRS, HEADS), 1)
    return (col == 2 * row + parity).astype(f32).astype(bf16)


def split_heads(w_bias_t):
    return [nn(pick_heads(parity), w_bias_t) for parity in range(2)]


def bias_kernel(
    pair_hbm, gain_hbm, w_bias_hbm, feats_hbm, out_hbm, head_hbm, tail_hbm, pair_ref, gain_ref,
    w_bias_ref, scaled_ref, stage_ref, local_ref, sems,
):
    rows, keys = pair_ref.shape[0], pair_ref.shape[1]
    atoms = feats_hbm.shape[1]
    part = rows // 4
    moves = [(gain_hbm, gain_ref), (w_bias_hbm, w_bias_ref)]
    for i in range(4):
        moves.append((pair_hbm.at[pl.ds(part * i, part)], pair_ref.at[pl.ds(part * i, part)]))
    moves.append((feats_hbm.at[:, pl.ds(0, HALO), :], head_hbm))
    moves.append((feats_hbm.at[:, pl.ds(atoms - HALO, HALO), :], tail_hbm))
    copies = start_all(moves, sems)
    for copy in copies[0:2]:
        copy.wait()
    gain = gain_ref[...]
    weights = jnp.concatenate(split_heads(w_bias_ref[...]), axis=1).astype(bf16)
    for i in range(rows // 8):
        if 8 * i % part == 0:
            copies[2 + 8 * i // part].wait()
        block = pair_ref[8 * i : 8 * i + 8].astype(f32).reshape(8 * keys, CZ)
        scaled_ref[8 * keys * i : 8 * keys * (i + 1), :] = norm_rows(block)[0] * gain
    blank = jnp.zeros((rows, CZ), bf16)
    for j in range(keys):
        block = scaled_ref[pl.ds(j, rows, stride=keys), :].astype(bf16)
        both = jnp.concatenate(
            [jnp.concatenate([block, blank], axis=1), jnp.concatenate([blank, block], axis=1)],
            axis=0,
        )
        stage_ref[pl.ds(j, PAIRS, stride=keys), :] = nt(weights, both)
    local_ref[...] = stage_ref[...].astype(bf16)
    for copy in copies[6:]:
        copy.wait()
    back = start_all([(local_ref, out_hbm.at[k]) for k in range(out_hbm.shape[0])], sems)
    for copy in back:
        copy.wait()


def pair_bias(pair, pair_gain, w_bias_t, feats, copies):
    rows, keys = pair.shape[0], pair.shape[1]
    edge = jax.ShapeDtypeStruct((feats.shape[0], HALO, C_ATOM), bf16)
    hbm = pl.BlockSpec(memory_space=pl.ANY)
    return pl.pallas_call(
        bias_kernel,
        in_specs=[hbm] * 4,
        out_specs=[hbm] * 3,
        out_shape=[
            jax.ShapeDtypeStruct((copies, keys * PAIRS, 2 * rows), bf16), edge, edge,
        ],
        scratch_shapes=[
            pltpu.VMEM(pair.shape, bf16),
            pltpu.VMEM((1, CZ), f32),
            pltpu.VMEM(w_bias_t.shape, bf16),
            pltpu.VMEM((rows * keys, CZ), f32),
            pltpu.VMEM((keys * PAIRS, 2 * rows), f32),
            pltpu.VMEM((keys * PAIRS, 2 * rows), bf16),
            pltpu.SemaphoreType.DMA((max(8, copies),)),
        ],
        compiler_params=pltpu.CompilerParams(vmem_limit_bytes=GRANT),
        cost_estimate=pl.CostEstimate(flops=10**7, bytes_accessed=10**7, transcendentals=0),
        name="pair_bias",
    )(pair, pair_gain.reshape(1, CZ), w_bias_t, feats)


def atom_kernel(
    feats_hbm, left_hbm, right_hbm, mask_hbm, counts_hbm, single_hbm, w_qkv_hbm, w_out_hbm,
    w_embed_hbm, tokens_ref, normed_ref, mask_ref, counts_ref, single_ref, w_qkv_ref, w_out_ref,
    w_embed_ref, sems, padded_ref, normed_atoms_ref, qkv_a, qkv_b, scores_a, scores_b, probs_a, probs_b, mixed_ref,
    updated_ref, split_ref, keybias_ref, onehot_ref, *, first,
):
    batch, atoms = tokens_ref.shape[0], feats_hbm.shape[1]
    padded = atoms + 2 * HALO
    moves = [(counts_hbm, counts_ref), (mask_hbm, mask_ref), (w_qkv_hbm, w_qkv_ref)]
    for s in range(batch):
        moves.append((left_hbm.at[first + s], padded_ref.at[s, pl.ds(0, HALO)]))
        moves.append((feats_hbm.at[first + s], padded_ref.at[s, pl.ds(HALO, atoms)]))
        moves.append((right_hbm.at[first + s], padded_ref.at[s, pl.ds(HALO + atoms, HALO)]))
    moves += [(w_out_hbm, w_out_ref), (w_embed_hbm, w_embed_ref), (single_hbm, single_ref)]
    copies = start_all(moves, sems)
    for copy in copies[0:2]:
        copy.wait()
    tok_rows = single_ref.shape[0]
    blocks = atoms // 128
    chunks = atoms // 256
    qkv_refs = (qkv_a, qkv_b)

    eye = iota((128, 128), 0) == iota((128, 128), 1)
    for b in range(-1, blocks + 1):
        at = lax.axis_index("tok") * blocks + b
        inside = jnp.where((at >= 0) & (at < mask_ref.shape[0]), 1, 0)
        row = mask_ref[pl.ds(jnp.clip(at, 0, mask_ref.shape[0] - 1), 1), :] * inside
        row = jnp.broadcast_to(row.astype(f32), (128, 128))
        col = jnp.sum(jnp.where(eye, row, 0.0), axis=1, keepdims=True)
        col = jnp.broadcast_to((col - 1.0) * 1e30, (128, 128))
        if b < 0:
            keybias_ref[0:HALO, :] = col[128 - HALO : 128]
        elif b < blocks:
            keybias_ref[HALO + 128 * b : HALO + 128 * b + 128, :] = col
        else:
            keybias_ref[HALO + atoms : padded, :] = col[0:HALO]
    counts = jnp.broadcast_to(counts_ref[...].astype(f32), (tok_rows, tok_rows))
    sub, lane = iota((tok_rows, tok_rows), 0), iota((tok_rows, tok_rows), 1)
    start = jnp.sum(jnp.where(lane < sub, counts, 0.0), axis=1, keepdims=True)
    own = jnp.sum(jnp.where(lane == sub, counts, 0.0), axis=1, keepdims=True)
    pos = iota((tok_rows, 256), 1).astype(f32)
    for g in range(chunks):
        at = pos + float(g * 256)
        hit = jnp.where((at >= start) & (at < start + own), 1.0, 0.0).astype(bf16)
        onehot_ref[:, 256 * g : 256 * g + 256] = hit
        onehot_ref[:, atoms + 256 * g : atoms + 256 * g + 256] = hit
    probs_a[...] = jnp.zeros_like(probs_a)
    probs_b[...] = jnp.zeros_like(probs_b)
    head_of = iota((32, 128), 1) // ATOM_HD
    head_mask = [(head_of == h).astype(f32).astype(bf16) for h in range(ATOM_HEADS)]
    own_atom = (iota((32, 128), 1) % 32) == iota((32, 128), 0)
    factor = ATOM_HD ** (-0.5) * LOG2E
    def qkv_step(s):
        for low in range(0, padded, padded // 4):
            part = slice(low, low + padded // 4)
            normed, unused = norm_rows(padded_ref[s, part, :].astype(f32))
            normed_atoms_ref[part, :] = normed.astype(bf16)
        qkv_refs[s % 2][...] = nn(normed_atoms_ref[...], w_qkv_ref[...]).astype(bf16)

    def score_step(s, group, to_ref):
        qkv_ref = qkv_refs[s % 2]
        for k in range(2):
            base = pl.multiple_of(group * 128 + 64 * k, 64)
            queries = qkv_ref[pl.ds(base + HALO, 64), 0:C_ATOM]
            spread = jnp.concatenate(
                [
                    queries[32 * w : 32 * w + 32] * head_mask[h]
                    for w in range(2)
                    for h in range(ATOM_HEADS)
                ],
                axis=0,
            )
            to_ref[k] = nt(qkv_ref[pl.ds(base, 160), C_ATOM : 2 * C_ATOM], spread)

    def softmax_step(group, from_ref, to_ref):
        for k in range(2):
            base = pl.multiple_of(group * 128 + 64 * k, 64)
            for w in range(2):
                keybias = keybias_ref[pl.ds(base + 32 * w, 128), :]
                keybias = jnp.concatenate(
                    [keybias[0:48], jnp.where(own_atom, 0.0, keybias[48:80]), keybias[80:128]],
                    axis=0,
                )
                scores = from_ref[k, 32 * w : 32 * w + 128, 128 * w : 128 * w + 128] + keybias
                expo = jnp.exp2((scores - jnp.max(scores, axis=0, keepdims=True)) * factor)
                weights = expo * (1.0 / jnp.sum(expo, axis=0, keepdims=True))
                to_ref[k, 32 * w : 32 * w + 128, 128 * w : 128 * w + 128] = weights.astype(bf16)

    def value_step(s, group, from_ref):
        qkv_ref = qkv_refs[s % 2]
        for k in range(2):
            base = pl.multiple_of(group * 128 + 64 * k, 64)
            part = tn(from_ref[k], qkv_ref[pl.ds(base, 160), 2 * C_ATOM : 3 * C_ATOM])
            mixes = []
            for w in range(2):
                mix = part[128 * w : 128 * w + 32]
                for h in range(1, ATOM_HEADS):
                    low = 128 * w + 32 * h
                    mix = jnp.where(head_of == h, part[low : low + 32], mix)
                mixes.append(mix.astype(bf16))
            mixed_ref[pl.ds(base, 64), :] = jnp.concatenate(mixes, axis=0)

    def embed_step(s):
        feats = padded_ref[s, HALO : HALO + atoms, :].astype(f32)
        updated_ref[...] = (feats + nn(mixed_ref[...], w_out_ref[...])).astype(bf16)
        for n in range(0, C_TOK, 256):
            embedded = jnp.maximum(nn(updated_ref[...], w_embed_ref[:, n : n + 256]), 0.0)
            high = embedded.astype(bf16)
            split_ref[0:atoms, n : n + 256] = high
            split_ref[atoms : 2 * atoms, n : n + 256] = (embedded - high.astype(f32)).astype(bf16)
        pooled = nn(onehot_ref[...], split_ref[...])
        tokens = pooled / own + single_ref[...].astype(f32)
        tokens_ref[s] = tokens
        normed_ref[s] = norm_rows(tokens)[0].astype(bf16)

    for copy in copies[2:6]:
        copy.wait()
    qkv_step(0)
    for copy in copies[6:]:
        copy.wait()
    for s in range(batch):
        score_step(s, 0, scores_a)

        def window_step(i, carry, s=s):
            even, odd = 2 * i, 2 * i + 1
            score_step(s, odd, scores_b)
            softmax_step(even, scores_a, probs_a)
            value_step(s, jnp.maximum(even - 1, 0), probs_b)
            score_step(s, jnp.minimum(odd + 1, 2 * chunks - 1), scores_a)
            softmax_step(odd, scores_b, probs_b)
            value_step(s, even, probs_a)
            return carry

        lax.fori_loop(0, chunks, window_step, 0)
        value_step(s, 2 * chunks - 1, probs_b)
        embed_step(s)
        if s + 1 < batch:
            qkv_step(s + 1)


def atom_stage(part, batch, feats, left, right, mask, counts, single, w_qkv, w_out, w_embed):
    atoms = feats.shape[1]
    tok_rows = single.shape[0]
    padded = atoms + 2 * HALO
    return pl.pallas_call(
        functools.partial(atom_kernel, first=part * batch),
        in_specs=[pl.BlockSpec(memory_space=pl.ANY)] * 9,
        out_specs=[pl.BlockSpec(memory_space=pltpu.VMEM)] * 2,
        out_shape=[
            jax.ShapeDtypeStruct((batch, tok_rows, C_TOK), f32),
            jax.ShapeDtypeStruct((batch, tok_rows, C_TOK), bf16),
        ],
        scratch_shapes=[
            pltpu.VMEM(mask.shape, jnp.int32),
            pltpu.VMEM(counts.shape, jnp.int32),
            pltpu.VMEM(single.shape, bf16),
            pltpu.VMEM(w_qkv.shape, bf16),
            pltpu.VMEM(w_out.shape, bf16),
            pltpu.VMEM(w_embed.shape, bf16),
            pltpu.SemaphoreType.DMA((6 + 3 * batch,)),
            pltpu.VMEM((batch, padded, C_ATOM), bf16),
            pltpu.VMEM((padded, C_ATOM), bf16),
            pltpu.VMEM((padded, 3 * C_ATOM), bf16),
            pltpu.VMEM((padded, 3 * C_ATOM), bf16),
            pltpu.VMEM((2, 160, 256), f32),
            pltpu.VMEM((2, 160, 256), f32),
            pltpu.VMEM((2, 160, 256), bf16),
            pltpu.VMEM((2, 160, 256), bf16),
            pltpu.VMEM((atoms, C_ATOM), bf16),
            pltpu.VMEM((atoms, C_ATOM), bf16),
            pltpu.VMEM((2 * atoms, C_TOK), bf16),
            pltpu.VMEM((padded, 128), f32),
            pltpu.VMEM((tok_rows, 2 * atoms), bf16),
        ],
        compiler_params=pltpu.CompilerParams(vmem_limit_bytes=GRANT),
        cost_estimate=pl.CostEstimate(
            flops=10**10, bytes_accessed=4 * 10**6, transcendentals=3 * 10**6
        ),
        name="atoms",
    )(feats, left, right, mask, counts, single, w_qkv, w_out, w_embed)


def head_masks(rows):
    masks = []
    for pair in range(4):
        low, high = WINDOWS[pair]
        lane = iota((rows, high - low), 1) + low
        first = 2 * pair * HD
        masks.append(
            [(lane >= first + HD * k) & (lane < first + HD * (k + 1)) for k in range(2)]
        )
    return masks


def two_heads(block, masks):
    blank = jnp.zeros_like(block)
    return jnp.concatenate([jnp.where(mask, block, blank) for mask in masks], axis=0)


def project_moves(piece_hbms, w_qkv_hbm, w_qkv_ref, all_ref):
    tok_rows = piece_hbms[0].shape[1]
    weights = [
        (w_qkv_hbm.at[:, pl.ds(C_TOK * i, C_TOK)], w_qkv_ref.at[i]) for i in range(3)
    ]
    here = lax.axis_index("tok")
    pieces = []
    for k, piece in enumerate(piece_hbms):
        at = pl.multiple_of((here ^ k) * tok_rows, tok_rows)
        pieces.append((piece, all_ref.at[:, pl.ds(at, tok_rows), :]))
    return [pieces[0], weights[0]] + pieces[1:] + weights[1:]


def project(copies, w_qkv_ref, all_ref, queries_ref, keys_ref, values_ref):
    batch = all_ref.shape[0]
    tok_rows = queries_ref.shape[0] // batch
    at = pl.multiple_of(lax.axis_index("tok") * tok_rows, tok_rows)
    for copy in copies[0:2]:
        copy.wait()
    own = jnp.concatenate([all_ref[s, pl.ds(at, tok_rows), :] for s in range(batch)], axis=0)
    for n in range(0, C_TOK, 256):
        queries_ref[:, n : n + 256] = nn(own, w_qkv_ref[0, :, n : n + 256]).astype(bf16)
    for copy in copies[2:-1]:
        copy.wait()
    for which, to_ref in ((1, keys_ref), (2, values_ref)):
        if which == 2:
            copies[-1].wait()
        for n in range(0, C_TOK, 256):
            for s in range(batch):
                to_ref[s, :, n : n + 256] = nn(
                    all_ref[s], w_qkv_ref[which, :, n : n + 256]
                ).astype(bf16)


def windows(pair):
    low, high = WINDOWS[pair % 4]
    return 384 * (pair // 4) + low, 384 * (pair // 4) + high


def attend(bias_ref, queries_ref, keys_ref, values_ref, probs_ref, att_ref, done=None):
    batch, keys_all = keys_ref.shape[0], keys_ref.shape[1]
    tok_rows = queries_ref.shape[0] // batch
    masks = head_masks(tok_rows)
    factor = HD ** (-0.5)

    for s in range(batch):
        at = s * tok_rows
        for pair in range(PAIRS):
            low, high = windows(pair)
            queries = two_heads(queries_ref[pl.ds(at, tok_rows), low:high], masks[pair % 4])
            probs_ref[s, pair] = nt(keys_ref[s, :, low:high], queries)
        for pair in range(PAIRS):
            scores = probs_ref[s, pair] * factor
            bias = [bias_ref[k, pair].astype(f32) for k in range(bias_ref.shape[0])]
            scores = scores + jnp.concatenate(bias, axis=0)
            expo = jnp.exp(scores - jnp.max(scores, axis=0, keepdims=True))
            probs_ref[s, pair] = expo * (1.0 / jnp.sum(expo, axis=0, keepdims=True))
        lanes = [jnp.zeros((tok_rows, 128), f32) for _ in range(C_TOK // 128)]
        for pair in range(PAIRS):
            low, high = windows(pair)
            part = tn(probs_ref[s, pair].astype(bf16), values_ref[s, :, low:high])
            first, second = masks[pair % 4]
            mix = jnp.where(first, part[0:tok_rows], 0.0)
            mix = jnp.where(second, part[tok_rows : 2 * tok_rows], mix)
            for t in range((high - low) // 128):
                lanes[low // 128 + t] = lanes[low // 128 + t] + mix[:, 128 * t : 128 * t + 128]
        for t in range(C_TOK // 128):
            att_ref[pl.ds(at, tok_rows), 128 * t : 128 * t + 128] = lanes[t].astype(bf16)
        if done is not None:
            done(s)


def attend_kernel(*refs, count):
    (
        bias_hbm, w_qkv_hbm, cot_hbm, w_down_hbm, att_ref, probs_hbm, values_hbm, d_hidden_hbm,
        w_qkv_ref, bias_ref, cot_ref, w_down_ref, probs_ref, values_ref, d_hidden_ref, sems,
        all_ref, queries_ref, keys_ref,
    ) = refs[count:]
    batch = all_ref.shape[0]
    moves = project_moves(refs[:count], w_qkv_hbm, w_qkv_ref, all_ref)
    moves += [(bias_hbm, bias_ref), (cot_hbm, cot_ref), (w_down_hbm, w_down_ref)]
    copies = start_all(moves, sems)
    project(copies[:-3], w_qkv_ref, all_ref, queries_ref, keys_ref, values_ref)
    for copy in copies[-3:]:
        copy.wait()
    back = [
        pltpu.make_async_copy(probs_ref.at[s], probs_hbm.at[s], sems.at[s]) for s in range(batch)
    ] + [
        pltpu.make_async_copy(values_ref, values_hbm, sems.at[batch]),
        pltpu.make_async_copy(d_hidden_ref, d_hidden_hbm, sems.at[batch + 1]),
    ]
    back[batch].start()
    cot = cot_ref[...].reshape(-1, C_TOK)
    for n in range(0, w_down_ref.shape[0], 256):
        d_hidden_ref[:, n : n + 256] = nt(cot, w_down_ref[n : n + 256, :])
    back[batch + 1].start()
    attend(
        bias_ref, queries_ref, keys_ref, values_ref, probs_ref, att_ref, lambda s: back[s].start()
    )
    for copy in back:
        copy.wait()


def attend_scratch(batch, tok_rows, keys_all):
    return [
        pltpu.VMEM((batch, keys_all, C_TOK), bf16),
        pltpu.VMEM((batch * tok_rows, C_TOK), bf16),
        pltpu.VMEM((batch, keys_all, C_TOK), bf16),
    ]


def attend_stage(pieces, bias, w_qkv, cot, w_down):
    batch, tok_rows, _ = pieces[0].shape
    keys_all = tok_rows * len(pieces)
    vmem = pl.BlockSpec(memory_space=pltpu.VMEM)
    hbm = pl.BlockSpec(memory_space=pl.ANY)
    d_hidden = jax.ShapeDtypeStruct((cot.shape[0] * tok_rows, w_down.shape[0]), f32)
    return pl.pallas_call(
        functools.partial(attend_kernel, count=len(pieces)),
        in_specs=[hbm] * (len(pieces) + 4),
        out_specs=[vmem, hbm, hbm, hbm],
        out_shape=[
            jax.ShapeDtypeStruct((batch * tok_rows, C_TOK), bf16),
            jax.ShapeDtypeStruct((batch, PAIRS, keys_all, 2 * tok_rows), f32),
            jax.ShapeDtypeStruct((batch, keys_all, C_TOK), bf16),
            d_hidden,
        ],
        scratch_shapes=[
            pltpu.VMEM((3, C_TOK, C_TOK), bf16),
            pltpu.VMEM(bias.shape, bf16),
            pltpu.VMEM(cot.shape, bf16),
            pltpu.VMEM(w_down.shape, bf16),
            pltpu.VMEM((batch, PAIRS, keys_all, 2 * tok_rows), f32),
            pltpu.VMEM((batch, keys_all, C_TOK), bf16),
            pltpu.VMEM(d_hidden.shape, f32),
            pltpu.SemaphoreType.DMA((6 + len(pieces),)),
        ]
        + attend_scratch(batch, tok_rows, keys_all),
        compiler_params=pltpu.CompilerParams(vmem_limit_bytes=GRANT),
        cost_estimate=pl.CostEstimate(
            flops=4 * 10**9, bytes_accessed=10**7, transcendentals=10**6
        ),
        name="attend",
    )(*pieces, bias, w_qkv, cot, w_down)


def token_kernel(*refs, count):
    (
        bias_hbm, tokens_a_hbm, tokens_b_hbm, att_a_hbm, cot_hbm, probs_a_hbm, values_a_hbm,
        w_qkv_hbm, w_out_hbm, w_gate_hbm, w_up_hbm, d_hidden_hbm,
        resid_hbm, hidden_hbm, d_bias_ref,
        bias_ref, tokens_ref, att_a_ref, cot_ref, resid_ref, hidden_ref,
        w_qkv_ref, w_out_ref, w_gate_ref, w_up_ref, d_hidden_ref, probs_ref, values_ref, sems,
        all_ref, queries_ref, keys_ref, grads_ref, d_gate_ref, d_up_ref, hat_ref,
    ) = refs[count:]
    batch, tok_rows = cot_ref.shape[0], cot_ref.shape[1]
    keys_all = values_ref.shape[1]
    rows = batch * tok_rows
    ahead = values_a_hbm.shape[0]
    lead = ahead * tok_rows
    moves = project_moves(refs[:count], w_qkv_hbm, w_qkv_ref, all_ref)
    projecting = len(moves)
    moves += [
        (bias_hbm, bias_ref), (w_out_hbm, w_out_ref), (att_a_hbm, att_a_ref),
        (tokens_a_hbm, tokens_ref.at[pl.ds(0, ahead)]),
        (tokens_b_hbm, tokens_ref.at[pl.ds(ahead, batch - ahead)]), (cot_hbm, cot_ref),
        (d_hidden_hbm, d_hidden_ref), (w_gate_hbm, w_gate_ref), (w_up_hbm, w_up_ref),
        (values_a_hbm, values_ref.at[pl.ds(0, ahead)]), (probs_a_hbm, probs_ref.at[pl.ds(0, ahead)]),
    ]
    copies = start_all(moves, sems)
    own_values = values_ref.at[pl.ds(ahead, batch - ahead)]
    own_probs = probs_ref.at[pl.ds(ahead, batch - ahead)]
    project(copies[:projecting], w_qkv_ref, all_ref, queries_ref, keys_ref, own_values)
    copies = copies[projecting:]
    copies[0].wait()
    attend(bias_ref, queries_ref, keys_ref, own_values, own_probs, queries_ref)

    for copy in copies[1:5]:
        copy.wait()
    tokens = tokens_ref[...].reshape(rows, C_TOK)
    resid_ref[0:lead, :] = tokens[0:lead] + nn(att_a_ref[...], w_out_ref[...])
    resid_ref[lead:rows, :] = tokens[lead:rows] + nn(queries_ref[...], w_out_ref[...])
    back = [
        pltpu.make_async_copy(resid_ref, resid_hbm, sems.at[0]),
        pltpu.make_async_copy(hidden_ref, hidden_hbm, sems.at[1]),
    ]
    back[0].start()
    hat, rstd = norm_rows(resid_ref[...])
    hat_ref[...] = hat
    grads_ref[...] = hat.astype(bf16)
    for copy in copies[5:9]:
        copy.wait()

    for n in range(0, w_gate_ref.shape[1], 256):
        shaped = grads_ref[...]
        gate = nn(shaped, w_gate_ref[:, n : n + 256])
        up = nn(shaped, w_up_ref[:, n : n + 256])
        d_hidden = d_hidden_ref[:, n : n + 256]
        sig = 1.0 / (1.0 + jnp.exp(-gate))
        act = gate * sig
        hidden_ref[:, n : n + 256] = (act * up).astype(bf16)
        d_gate_ref[:, n : n + 256] = (
            d_hidden * up * sig * (1.0 + gate * (1.0 - sig))
        ).astype(bf16)
        d_up_ref[:, n : n + 256] = (d_hidden * act).astype(bf16)

    back[1].start()
    parts = []
    for n in range(0, C_TOK, 256):
        parts.append(
            nt(d_gate_ref[...], w_gate_ref[n : n + 256, :])
            + nt(d_up_ref[...], w_up_ref[n : n + 256, :])
        )
    d_normed = jnp.concatenate(parts, axis=1)
    hat = hat_ref[...]
    first = jnp.mean(d_normed, axis=-1, keepdims=True)
    second = jnp.mean(d_normed * hat, axis=-1, keepdims=True)
    d_resid = cot_ref[...].reshape(rows, C_TOK).astype(f32) + rstd * (
        d_normed - first - hat * second
    )
    grads_ref[...] = nt(d_resid.astype(bf16), w_out_ref[...]).astype(bf16)
    for copy in copies[9:]:
        copy.wait()
    masks = head_masks(tok_rows)
    for pair in range(PAIRS):
        low, high = windows(pair)
        total = jnp.zeros((keys_all, 2 * tok_rows), f32)
        for s in range(batch):
            grads = two_heads(
                grads_ref[s * tok_rows : (s + 1) * tok_rows, low:high], masks[pair % 4]
            )
            d_probs = nt(values_ref[s, :, low:high], grads)
            probs = probs_ref[s, pair]
            delta = jnp.sum(probs * d_probs, axis=0, keepdims=True)
            total = total + probs * (d_probs - delta)
        size = d_bias_ref.shape[2]
        for k in range(d_bias_ref.shape[0]):
            d_bias_ref[k, pair] = total[size * k : size * (k + 1)].astype(bf16)
    for copy in back:
        copy.wait()


def token_stage(
    pieces, bias, tokens_a, tokens_b, att_a, cot, probs_a, values_a, w_qkv, w_out, w_gate, w_up,
    d_hidden,
):
    batch, tok_rows, _ = cot.shape
    keys_all = tok_rows * len(pieces)
    rows = batch * tok_rows
    hidden = w_gate.shape[1]
    vmem = pl.BlockSpec(memory_space=pltpu.VMEM)
    hbm = pl.BlockSpec(memory_space=pl.ANY)
    return pl.pallas_call(
        functools.partial(token_kernel, count=len(pieces)),
        in_specs=[hbm] * (len(pieces) + 12),
        out_specs=[hbm, hbm, vmem],
        out_shape=[
            jax.ShapeDtypeStruct((rows, C_TOK), f32),
            jax.ShapeDtypeStruct((rows, hidden), bf16),
            jax.ShapeDtypeStruct(bias.shape, bf16),
        ],
        scratch_shapes=[
            pltpu.VMEM(bias.shape, bf16),
            pltpu.VMEM(cot.shape, f32),
            pltpu.VMEM(att_a.shape, bf16),
            pltpu.VMEM(cot.shape, bf16),
            pltpu.VMEM((rows, C_TOK), f32),
            pltpu.VMEM((rows, hidden), bf16),
            pltpu.VMEM((3, C_TOK, C_TOK), bf16),
            pltpu.VMEM(w_out.shape, bf16),
            pltpu.VMEM(w_gate.shape, bf16),
            pltpu.VMEM(w_up.shape, bf16),
            pltpu.VMEM(d_hidden.shape, f32),
            pltpu.VMEM((batch, PAIRS, keys_all, 2 * tok_rows), f32),
            pltpu.VMEM((batch, keys_all, C_TOK), bf16),
            pltpu.SemaphoreType.DMA((14 + len(pieces),)),
        ]
        + attend_scratch(pieces[0].shape[0], tok_rows, keys_all)
        + [
            pltpu.VMEM((rows, C_TOK), bf16),
            pltpu.VMEM((rows, hidden), bf16),
            pltpu.VMEM((rows, hidden), bf16),
            pltpu.VMEM((rows, C_TOK), f32),
        ],
        compiler_params=pltpu.CompilerParams(vmem_limit_bytes=GRANT),
        cost_estimate=pl.CostEstimate(
            flops=10**10, bytes_accessed=2 * 10**7, transcendentals=10**6
        ),
        name="tokens",
    )(
        *pieces, bias, tokens_a, tokens_b, att_a, cot, probs_a, values_a, w_qkv, w_out, w_gate,
        w_up, d_hidden,
    )


def output_kernel(
    resid_ref, hidden_ref, w_down_ref, pair_ref, out_ref, hat_ref, rstd_ref, pairf_ref
):
    out_ref[...] = (resid_ref[...] + nn(hidden_ref[...], w_down_ref[...])).astype(bf16)
    rows, keys = pair_ref.shape[0], pair_ref.shape[1]
    for i in range(rows // 8):
        pairf_ref[8 * keys * i : 8 * keys * (i + 1), :] = (
            pair_ref[8 * i : 8 * i + 8].astype(f32).reshape(8 * keys, CZ)
        )

    def norm_step(j, carry):
        hat, rstd = norm_rows(pairf_ref[pl.ds(j, rows, stride=keys), :])
        at = pl.multiple_of(j * rows, rows)
        hat_ref[pl.ds(at, rows), :] = hat
        rstd = jnp.broadcast_to(rstd, (rows, CZ)).T[0:1]
        rstd_ref[pl.ds(j, 1), :] = jnp.concatenate([rstd, rstd], axis=1)
        return carry

    lax.fori_loop(0, keys, norm_step, 0, unroll=4)


def output_stage(resid, hidden, w_down, pair):
    rows, keys = pair.shape[0], pair.shape[1]
    return pl.pallas_call(
        output_kernel,
        out_shape=[jax.ShapeDtypeStruct(resid.shape, bf16)]
        + [
            jax.ShapeDtypeStruct((rows * keys, CZ), f32),
            jax.ShapeDtypeStruct((keys, 2 * rows), f32),
        ],
        scratch_shapes=[pltpu.VMEM((rows * keys, CZ), f32)],
        compiler_params=pltpu.CompilerParams(vmem_limit_bytes=GRANT),
        cost_estimate=pl.CostEstimate(
            flops=10**9, bytes_accessed=8 * 10**6, transcendentals=0
        ),
        name="output",
    )(resid, hidden, w_down, pair)


def grad_kernel(
    parts_hbm, hat_hbm, rstd_hbm, gain_hbm, w_bias_hbm, out_hbm, parts_ref, hat_ref, rstd_ref,
    gain_ref, w_bias_ref, total_ref, out_ref, sems,
):
    keys = parts_ref.shape[2]
    rows = hat_ref.shape[0] // keys
    size = 8 * rows
    moves = [
        (gain_hbm, gain_ref), (w_bias_hbm, w_bias_ref), (parts_hbm, parts_ref),
        (rstd_hbm, rstd_ref),
    ]
    for c in range(keys // 8):
        moves.append((hat_hbm.at[pl.ds(size * c, size)], hat_ref.at[pl.ds(size * c, size)]))
    copies = start_all(moves, sems)
    for copy in copies[0:2]:
        copy.wait()
    weights = jnp.concatenate(split_heads(w_bias_ref[...]), axis=0) * gain_ref[...]
    weights = weights - jnp.mean(weights, axis=-1, keepdims=True)
    weights = jnp.concatenate([weights[0:PAIRS], weights[PAIRS:HEADS]], axis=1)
    w_high = weights.astype(bf16).astype(f32)
    w_middle = (weights - w_high).astype(bf16).astype(f32)
    w_low = weights - w_high - w_middle
    weights = jnp.concatenate([w_high, w_middle, w_low, w_high, w_middle, w_high], axis=0)
    weights = weights.astype(bf16)
    for copy in copies[2:4]:
        copy.wait()
    for pair in range(PAIRS):
        total = parts_ref[0, pair].astype(f32)
        for k in range(1, parts_ref.shape[0]):
            total = total + parts_ref[k, pair].astype(f32)
        total_ref[pair * keys : (pair + 1) * keys, :] = total * rstd_ref[...]
    back = []
    for c in range(keys // 8):
        copies[4 + c].wait()
        for j in range(8 * c, 8 * c + 8):
            total = total_ref[pl.ds(j, PAIRS, stride=keys), :]
            high = total.astype(bf16).astype(f32)
            middle = (total - high).astype(bf16).astype(f32)
            low = total - high - middle
            stack = jnp.concatenate([high, high, high, middle, middle, low], axis=0)
            both = nn(stack.T.astype(bf16), weights)
            scaled = both[0:rows, 0:CZ] + both[rows : 2 * rows, CZ : 2 * CZ]
            hat = hat_ref[rows * j : rows * (j + 1), :]
            second = jnp.mean(scaled * hat, axis=-1, keepdims=True)
            out_ref[pl.ds(size * c + j % 8, rows, stride=8), :] = scaled - hat * second
        back.append(
            pltpu.make_async_copy(
                out_ref.at[pl.ds(size * c, size)].reshape(rows, 8, CZ),
                out_hbm.at[:, pl.ds(8 * c, 8), :],
                sems.at[c],
            )
        )
        back[c].start()
    for copy in back:
        copy.wait()


def pair_back(parts, hat, rstd, pair_gain, w_bias_t):
    keys = parts.shape[2]
    rows = hat.shape[0] // keys
    hbm = pl.BlockSpec(memory_space=pl.ANY)
    return pl.pallas_call(
        grad_kernel,
        in_specs=[hbm] * 5,
        out_specs=hbm,
        out_shape=jax.ShapeDtypeStruct((rows, keys, CZ), f32),
        scratch_shapes=[
            pltpu.VMEM(parts.shape, bf16),
            pltpu.VMEM(hat.shape, f32),
            pltpu.VMEM(rstd.shape, f32),
            pltpu.VMEM((1, CZ), f32),
            pltpu.VMEM(w_bias_t.shape, bf16),
            pltpu.VMEM((keys * PAIRS, 2 * rows), f32),
            pltpu.VMEM((rows * keys, CZ), f32),
            pltpu.SemaphoreType.DMA((4 + keys // 8,)),
        ],
        compiler_params=pltpu.CompilerParams(vmem_limit_bytes=GRANT),
        cost_estimate=pl.CostEstimate(flops=10**8, bytes_accessed=4 * 10**6, transcendentals=0),
        name="pair_grad",
    )(parts, hat, rstd, pair_gain.reshape(1, CZ), w_bias_t)


def swap(values, axis, k):
    return lax.ppermute(values, axis, [(i, i ^ k) for i in range(lax.axis_size(axis))])


def gather(values, axis):
    far = range(lax.axis_size(axis) - 1, 0, -1)
    return [values] + [swap(values, axis, k) for k in far][::-1]


def body(
    atom_feats, atom_counts, atom_mask, token_single, pair, pair_gain, w_bias, w_atom_qkv,
    w_atom_out, w_embed, w_qkv, w_out, w_gate, w_up, w_down, cotangent,
):
    batch, atom_rows, _ = atom_feats.shape
    tok_rows = token_single.shape[0]
    shards = lax.axis_size("tok")
    groups = lax.axis_size("samp")

    w_bias_t = w_bias.T
    local_bias, head, tail = pair_bias(pair, pair_gain, w_bias_t, atom_feats, groups)
    steps = [(i, i + 1) for i in range(shards - 1)]
    left = lax.ppermute(tail, "tok", steps)
    right = lax.ppermute(head, "tok", [(j, i) for i, j in steps])

    bias = lax.all_to_all(local_bias, "samp", 0, 0).reshape(groups, PAIRS, -1, 2 * tok_rows)

    mask = atom_mask.reshape(-1, 128)
    mask, local_bias = lax.optimization_barrier((mask, local_bias))

    each = batch // 2
    tokens, gathered = [], []
    for part in range(2):
        tok, normed = atom_stage(
            part, each, atom_feats, left, right, mask, atom_counts, token_single, w_atom_qkv,
            w_atom_out, w_embed,
        )
        tokens.append(tok)
        gathered.append(gather(normed, "tok"))
    att_a, probs_a, values_a, d_hidden = attend_stage(
        gathered[0], bias, w_qkv, cotangent, w_down
    )
    resid, hidden, d_bias = token_stage(
        gathered[1], bias, *tokens, att_a, cotangent, probs_a, values_a, w_qkv, w_out, w_gate,
        w_up, d_hidden,
    )
    parts = lax.all_to_all(d_bias, "samp", 0, 0)
    token_out, hat, rstd = output_stage(resid, hidden, w_down, pair)
    pair_grad = pair_back(parts, hat, rstd, pair_gain, w_bias_t)
    token_out = token_out.reshape(batch, tok_rows, C_TOK)
    return (token_out, pair_grad)


def solution(mesh):
    in_specs = (
        P("samp", "tok", None),
        P("tok", None),
        P(),
        P("tok", None),
        P("tok", "samp", None),
        P(), P(), P(), P(), P(), P(), P(), P(), P(), P(),
        P("samp", "tok", None),
    )
    out_specs = (P("samp", "tok", None), P("tok", "samp", None))
    return jax.shard_map(body, mesh=mesh, in_specs=in_specs, out_specs=out_specs, check_vma=False)
```

```python
import functools

import jax
import jax.numpy as jnp
from jax import lax
from jax.experimental import pallas as pl
from jax.experimental.pallas import tpu as pltpu
from jax.sharding import PartitionSpec as P

C_ATOM = 128
ATOM_HEADS = 4
C_TOK = 768
HEADS = 16
ATOM_HD = 32
HD = 48
CZ = 128
HALO = 48
PAIRS = HEADS // 2
GRANT = 64 << 20
LOG2E = 1.4426950408889634

epsilon = 1e-05
f32 = jnp.float32
bf16 = jnp.bfloat16

QUADS = HEADS // 4
QUAD_WINDOWS = tuple((384 * (q // 2) + 128 * (q % 2), 384 * (q // 2) + 128 * (q % 2) + 256) for q in range(QUADS))


def nn(a, b):
    return lax.dot_general(a, b, (((1,), (0,)), ((), ())), preferred_element_type=f32)


def nt(a, b):
    return lax.dot_general(a, b, (((1,), (1,)), ((), ())), preferred_element_type=f32)


def tn(a, b):
    return lax.dot_general(a, b, (((0,), (0,)), ((), ())), preferred_element_type=f32)


def start_all(moves, sems):
    copies = [pltpu.make_async_copy(src, dst, sems.at[i]) for i, (src, dst) in enumerate(moves)]
    for copy in copies:
        copy.start()
    return copies


def norm_rows(values):
    center = values - jnp.mean(values, axis=-1, keepdims=True)
    scale_inv = lax.rsqrt(jnp.mean(center * center, axis=-1, keepdims=True) + epsilon)
    return (center * scale_inv, scale_inv)


def iota(shape, dim):
    return lax.broadcasted_iota(jnp.int32, shape, dim)


def pick_heads(parity):
    row, col = iota((PAIRS, HEADS), 0), iota((PAIRS, HEADS), 1)
    return (col == 2 * row + parity).astype(f32).astype(bf16)


def split_heads(w_bias_t):
    return [nn(pick_heads(parity), w_bias_t) for parity in range(2)]


def bias_kernel(
    pair_hbm, gain_hbm, w_bias_hbm, feats_hbm, out_hbm, head_hbm, tail_hbm, pair_ref, gain_ref,
    w_bias_ref, scaled_ref, stage_ref, local_ref, head_ref, tail_ref, sems,
):
    rows, keys = pair_ref.shape[0], pair_ref.shape[1]
    atoms = feats_hbm.shape[1]
    part = rows // 4
    moves = [
        (gain_hbm, gain_ref), (w_bias_hbm, w_bias_ref),
        (feats_hbm.at[:, pl.ds(0, HALO), :], head_ref),
        (feats_hbm.at[:, pl.ds(atoms - HALO, HALO), :], tail_ref),
    ]
    for i in range(4):
        moves.append((pair_hbm.at[pl.ds(part * i, part)], pair_ref.at[pl.ds(part * i, part)]))
    copies = start_all(moves, sems)
    for copy in copies[0:2]:
        copy.wait()
    gain = gain_ref[...]
    weights = jnp.concatenate(split_heads(w_bias_ref[...]), axis=1).astype(bf16)
    for i in range(rows // 8):
        if 8 * i % part == 0:
            copies[4 + 8 * i // part].wait()
        block = pair_ref[8 * i : 8 * i + 8].astype(f32).reshape(8 * keys, CZ)
        scaled_ref[8 * keys * i : 8 * keys * (i + 1), :] = norm_rows(block)[0] * gain
    for copy in copies[2:4]:
        copy.wait()
    edges = start_all([(head_ref, head_hbm), (tail_ref, tail_hbm)], sems)
    blank = jnp.zeros((rows, CZ), bf16)
    for j in range(keys):
        block = scaled_ref[pl.ds(j, rows, stride=keys), :].astype(bf16)
        both = jnp.concatenate(
            [jnp.concatenate([block, blank], axis=1), jnp.concatenate([blank, block], axis=1)],
            axis=0,
        )
        stage_ref[pl.ds(j, PAIRS, stride=keys), :] = nt(weights, both)
    local_ref[...] = stage_ref[...].astype(bf16)
    back = [
        pltpu.make_async_copy(local_ref, out_hbm.at[k], sems.at[2 + k])
        for k in range(out_hbm.shape[0])
    ]
    for copy in back:
        copy.start()
    for copy in edges + back:
        copy.wait()


def pair_bias(pair, pair_gain, w_bias_t, feats, copies):
    rows, keys = pair.shape[0], pair.shape[1]
    edge = jax.ShapeDtypeStruct((feats.shape[0], HALO, C_ATOM), bf16)
    hbm = pl.BlockSpec(memory_space=pl.ANY)
    return pl.pallas_call(
        bias_kernel,
        in_specs=[hbm] * 4,
        out_specs=[hbm] * 3,
        out_shape=[
            jax.ShapeDtypeStruct((copies, keys * PAIRS, 2 * rows), bf16), edge, edge,
        ],
        scratch_shapes=[
            pltpu.VMEM(pair.shape, bf16),
            pltpu.VMEM((1, CZ), f32),
            pltpu.VMEM(w_bias_t.shape, bf16),
            pltpu.VMEM((rows * keys, CZ), f32),
            pltpu.VMEM((keys * PAIRS, 2 * rows), f32),
            pltpu.VMEM((keys * PAIRS, 2 * rows), bf16),
            pltpu.VMEM(edge.shape, bf16),
            pltpu.VMEM(edge.shape, bf16),
            pltpu.SemaphoreType.DMA((8 + copies,)),
        ],
        compiler_params=pltpu.CompilerParams(vmem_limit_bytes=GRANT),
        cost_estimate=pl.CostEstimate(flops=10**7, bytes_accessed=10**7, transcendentals=0),
        name="pair_bias",
    )(pair, pair_gain.reshape(1, CZ), w_bias_t, feats)


def atom_kernel(
    feats_hbm, left_hbm, right_hbm, mask_hbm, counts_hbm, single_hbm, w_qkv_hbm, w_out_hbm,
    w_embed_hbm, tokens_ref, normed_ref, mask_ref, counts_ref, single_ref, w_qkv_ref, w_out_ref,
    w_embed_ref, sems, padded_ref, normed_atoms_ref, qkv_a, qkv_b, scores_a, scores_b, probs_a, probs_b, mixed_ref,
    updated_ref, split_ref, keybias_ref, onehot_ref, *, first,
):
    batch, atoms = tokens_ref.shape[0], feats_hbm.shape[1]
    padded = atoms + 2 * HALO
    moves = [(counts_hbm, counts_ref), (mask_hbm, mask_ref), (w_qkv_hbm, w_qkv_ref)]
    for s in range(batch):
        moves.append((left_hbm.at[first + s], padded_ref.at[s, pl.ds(0, HALO)]))
        moves.append((feats_hbm.at[first + s], padded_ref.at[s, pl.ds(HALO, atoms)]))
        moves.append((right_hbm.at[first + s], padded_ref.at[s, pl.ds(HALO + atoms, HALO)]))
    moves += [(w_out_hbm, w_out_ref), (w_embed_hbm, w_embed_ref), (single_hbm, single_ref)]
    copies = start_all(moves, sems)
    for copy in copies[0:2]:
        copy.wait()
    tok_rows = single_ref.shape[0]
    blocks = atoms // 128
    chunks = atoms // 256
    qkv_refs = (qkv_a, qkv_b)

    eye = iota((128, 128), 0) == iota((128, 128), 1)
    for b in range(-1, blocks + 1):
        at = lax.axis_index("tok") * blocks + b
        inside = jnp.where((at >= 0) & (at < mask_ref.shape[0]), 1, 0)
        row = mask_ref[pl.ds(jnp.clip(at, 0, mask_ref.shape[0] - 1), 1), :] * inside
        row = jnp.broadcast_to(row.astype(f32), (128, 128))
        col = jnp.sum(jnp.where(eye, row, 0.0), axis=1, keepdims=True)
        col = jnp.broadcast_to((col - 1.0) * 1e30, (128, 128))
        if b < 0:
            keybias_ref[0:HALO, :] = col[128 - HALO : 128]
        elif b < blocks:
            keybias_ref[HALO + 128 * b : HALO + 128 * b + 128, :] = col
        else:
            keybias_ref[HALO + atoms : padded, :] = col[0:HALO]
    counts = jnp.broadcast_to(counts_ref[...].astype(f32), (tok_rows, tok_rows))
    sub, lane = iota((tok_rows, tok_rows), 0), iota((tok_rows, tok_rows), 1)
    start = jnp.sum(jnp.where(lane < sub, counts, 0.0), axis=1, keepdims=True)
    own = jnp.sum(jnp.where(lane == sub, counts, 0.0), axis=1, keepdims=True)
    pos = iota((tok_rows, 256), 1).astype(f32)
    for g in range(chunks):
        at = pos + float(g * 256)
        hit = jnp.where((at >= start) & (at < start + own), 1.0, 0.0).astype(bf16)
        onehot_ref[:, 256 * g : 256 * g + 256] = hit
        onehot_ref[:, atoms + 256 * g : atoms + 256 * g + 256] = hit
    probs_a[...] = jnp.zeros_like(probs_a)
    probs_b[...] = jnp.zeros_like(probs_b)
    head_of = iota((32, 128), 1) // ATOM_HD
    head_mask = [(head_of == h).astype(f32).astype(bf16) for h in range(ATOM_HEADS)]
    own_atom = (iota((32, 128), 1) % 32) == iota((32, 128), 0)
    factor = ATOM_HD ** (-0.5) * LOG2E
    def qkv_step(s):
        for low in range(0, padded, padded // 4):
            part = slice(low, low + padded // 4)
            normed, unused = norm_rows(padded_ref[s, part, :].astype(f32))
            normed_atoms_ref[part, :] = normed.astype(bf16)
        qkv_refs[s % 2][...] = nn(normed_atoms_ref[...], w_qkv_ref[...]).astype(bf16)

    def score_step(s, group, to_ref):
        qkv_ref = qkv_refs[s % 2]
        for k in range(2):
            base = pl.multiple_of(group * 128 + 64 * k, 64)
            queries = qkv_ref[pl.ds(base + HALO, 64), 0:C_ATOM]
            spread = jnp.concatenate(
                [
                    queries[32 * w : 32 * w + 32] * head_mask[h]
                    for w in range(2)
                    for h in range(ATOM_HEADS)
                ],
                axis=0,
            )
            to_ref[k] = nt(qkv_ref[pl.ds(base, 160), C_ATOM : 2 * C_ATOM], spread)

    def softmax_step(group, from_ref, to_ref):
        for k in range(2):
            base = pl.multiple_of(group * 128 + 64 * k, 64)
            for w in range(2):
                keybias = keybias_ref[pl.ds(base + 32 * w, 128), :]
                keybias = jnp.concatenate(
                    [keybias[0:48], jnp.where(own_atom, 0.0, keybias[48:80]), keybias[80:128]],
                    axis=0,
                )
                scores = from_ref[k, 32 * w : 32 * w + 128, 128 * w : 128 * w + 128] + keybias
                expo = jnp.exp2((scores - jnp.max(scores, axis=0, keepdims=True)) * factor)
                weights = expo * (1.0 / jnp.sum(expo, axis=0, keepdims=True))
                to_ref[k, 32 * w : 32 * w + 128, 128 * w : 128 * w + 128] = weights.astype(bf16)

    def value_step(s, group, from_ref):
        qkv_ref = qkv_refs[s % 2]
        for k in range(2):
            base = pl.multiple_of(group * 128 + 64 * k, 64)
            part = tn(from_ref[k], qkv_ref[pl.ds(base, 160), 2 * C_ATOM : 3 * C_ATOM])
            mixes = []
            for w in range(2):
                mix = part[128 * w : 128 * w + 32]
                for h in range(1, ATOM_HEADS):
                    low = 128 * w + 32 * h
                    mix = jnp.where(head_of == h, part[low : low + 32], mix)
                mixes.append(mix.astype(bf16))
            mixed_ref[pl.ds(base, 64), :] = jnp.concatenate(mixes, axis=0)

    def embed_step(s):
        feats = padded_ref[s, HALO : HALO + atoms, :].astype(f32)
        updated_ref[...] = (feats + nn(mixed_ref[...], w_out_ref[...])).astype(bf16)
        for n in range(0, C_TOK, 256):
            embedded = jnp.maximum(nn(updated_ref[...], w_embed_ref[:, n : n + 256]), 0.0)
            high = embedded.astype(bf16)
            split_ref[0:atoms, n : n + 256] = high
            split_ref[atoms : 2 * atoms, n : n + 256] = (embedded - high.astype(f32)).astype(bf16)
        pooled = nn(onehot_ref[...], split_ref[...])
        tokens = pooled / own + single_ref[...].astype(f32)
        tokens_ref[s] = tokens
        normed_ref[s] = norm_rows(tokens)[0].astype(bf16)

    for copy in copies[2:6]:
        copy.wait()
    qkv_step(0)
    for copy in copies[6:]:
        copy.wait()
    for s in range(batch):
        score_step(s, 0, scores_a)

        def window_step(i, carry, s=s):
            even, odd = 2 * i, 2 * i + 1
            score_step(s, odd, scores_b)
            softmax_step(even, scores_a, probs_a)
            value_step(s, jnp.maximum(even - 1, 0), probs_b)
            score_step(s, jnp.minimum(odd + 1, 2 * chunks - 1), scores_a)
            softmax_step(odd, scores_b, probs_b)
            value_step(s, even, probs_a)
            return carry

        lax.fori_loop(0, chunks, window_step, 0)
        value_step(s, 2 * chunks - 1, probs_b)
        embed_step(s)
        if s + 1 < batch:
            qkv_step(s + 1)


def atom_stage(part, batch, feats, left, right, mask, counts, single, w_qkv, w_out, w_embed):
    atoms = feats.shape[1]
    tok_rows = single.shape[0]
    padded = atoms + 2 * HALO
    return pl.pallas_call(
        functools.partial(atom_kernel, first=part * batch),
        in_specs=[pl.BlockSpec(memory_space=pl.ANY)] * 9,
        out_specs=[pl.BlockSpec(memory_space=pltpu.VMEM)] * 2,
        out_shape=[
            jax.ShapeDtypeStruct((batch, tok_rows, C_TOK), f32),
            jax.ShapeDtypeStruct((batch, tok_rows, C_TOK), bf16),
        ],
        scratch_shapes=[
            pltpu.VMEM(mask.shape, jnp.int32),
            pltpu.VMEM(counts.shape, jnp.int32),
            pltpu.VMEM(single.shape, bf16),
            pltpu.VMEM(w_qkv.shape, bf16),
            pltpu.VMEM(w_out.shape, bf16),
            pltpu.VMEM(w_embed.shape, bf16),
            pltpu.SemaphoreType.DMA((6 + 3 * batch,)),
            pltpu.VMEM((batch, padded, C_ATOM), bf16),
            pltpu.VMEM((padded, C_ATOM), bf16),
            pltpu.VMEM((padded, 3 * C_ATOM), bf16),
            pltpu.VMEM((padded, 3 * C_ATOM), bf16),
            pltpu.VMEM((2, 160, 256), f32),
            pltpu.VMEM((2, 160, 256), f32),
            pltpu.VMEM((2, 160, 256), bf16),
            pltpu.VMEM((2, 160, 256), bf16),
            pltpu.VMEM((atoms, C_ATOM), bf16),
            pltpu.VMEM((atoms, C_ATOM), bf16),
            pltpu.VMEM((2 * atoms, C_TOK), bf16),
            pltpu.VMEM((padded, 128), f32),
            pltpu.VMEM((tok_rows, 2 * atoms), bf16),
        ],
        compiler_params=pltpu.CompilerParams(vmem_limit_bytes=GRANT),
        cost_estimate=pl.CostEstimate(
            flops=10**10, bytes_accessed=4 * 10**6, transcendentals=3 * 10**6
        ),
        name="atoms",
    )(feats, left, right, mask, counts, single, w_qkv, w_out, w_embed)


def head_masks(rows):
    masks = []
    for quad, (low, high) in enumerate(QUAD_WINDOWS):
        lane = iota((rows, high - low), 1) + low
        first = 4 * quad * HD
        masks.append(
            [(lane >= first + HD * k) & (lane < first + HD * (k + 1)) for k in range(4)]
        )
    return masks


def spread_heads(block, masks):
    blank = jnp.zeros_like(block)
    return jnp.concatenate([jnp.where(mask, block, blank) for mask in masks], axis=0)


def project_moves(piece_hbms, w_qkv_hbm, w_qkv_ref, all_ref):
    tok_rows = piece_hbms[0].shape[1]
    weights = [
        (w_qkv_hbm.at[:, pl.ds(C_TOK * i, C_TOK)], w_qkv_ref.at[i]) for i in range(3)
    ]
    here = lax.axis_index("tok")
    pieces = []
    for k, piece in enumerate(piece_hbms):
        at = pl.multiple_of((here ^ k) * tok_rows, tok_rows)
        pieces.append((piece, all_ref.at[:, pl.ds(at, tok_rows), :]))
    return [pieces[0], weights[0]] + pieces[1:] + weights[1:]


def project(copies, w_qkv_ref, all_ref, queries_ref, keys_ref, values_ref, loaded):
    batch = all_ref.shape[0]
    tok_rows = queries_ref.shape[0] // batch
    at = pl.multiple_of(lax.axis_index("tok") * tok_rows, tok_rows)
    for copy in copies[0:2]:
        copy.wait()
    own = jnp.concatenate([all_ref[s, pl.ds(at, tok_rows), :] for s in range(batch)], axis=0)
    for n in range(0, C_TOK, 256):
        queries_ref[:, n : n + 256] = nn(own, w_qkv_ref[0, :, n : n + 256]).astype(bf16)
    for copy in copies[2:-1]:
        copy.wait()
    for which, to_ref in ((1, keys_ref), (2, values_ref)):
        if which == 2:
            copies[-1].wait()
            loaded()
        for n in range(0, C_TOK, 256):
            for s in range(batch):
                to_ref[s, :, n : n + 256] = nn(
                    all_ref[s], w_qkv_ref[which, :, n : n + 256]
                ).astype(bf16)


def attend(bias_ref, queries_ref, keys_ref, values_ref, probs_ref, att_ref, done=None):
    batch, keys_all = keys_ref.shape[0], keys_ref.shape[1]
    tok_rows = queries_ref.shape[0] // batch
    masks = head_masks(tok_rows)
    factor = HD ** (-0.5)

    for s in range(batch):
        at = s * tok_rows
        for quad, (low, high) in enumerate(QUAD_WINDOWS):
            queries = spread_heads(queries_ref[at : at + tok_rows, low:high], masks[quad])
            scores = nt(keys_ref[s, :, low:high], queries)
            for half in range(2):
                probs_ref[s, 2 * quad + half] = scores[
                    :, 2 * tok_rows * half : 2 * tok_rows * (half + 1)
                ]
        for pair in range(PAIRS):
            scores = probs_ref[s, pair] * factor
            bias = [bias_ref[k, pair].astype(f32) for k in range(bias_ref.shape[0])]
            scores = scores + jnp.concatenate(bias, axis=0)
            expo = jnp.exp(scores - jnp.max(scores, axis=0, keepdims=True))
            probs_ref[s, pair] = expo * (1.0 / jnp.sum(expo, axis=0, keepdims=True))
        lanes = [jnp.zeros((tok_rows, 128), f32) for _ in range(C_TOK // 128)]
        for quad, (low, high) in enumerate(QUAD_WINDOWS):
            probs = jnp.concatenate(
                [probs_ref[s, 2 * quad + half].astype(bf16) for half in range(2)], axis=1
            )
            part = tn(probs, values_ref[s, :, low:high])
            mix = jnp.where(masks[quad][0], part[0:tok_rows], 0.0)
            for k in range(1, 4):
                mix = jnp.where(masks[quad][k], part[tok_rows * k : tok_rows * (k + 1)], mix)
            for t in range((high - low) // 128):
                lanes[low // 128 + t] = lanes[low // 128 + t] + mix[:, 128 * t : 128 * t + 128]
        for t in range(C_TOK // 128):
            att_ref[at : at + tok_rows, 128 * t : 128 * t + 128] = lanes[t].astype(bf16)
        if done is not None:
            done(s)


def attend_kernel(*refs, count):
    (
        bias_hbm, w_qkv_hbm, cot_hbm, w_down_hbm, att_ref, probs_hbm, values_hbm, d_hidden_hbm,
        w_qkv_ref, bias_ref, cot_ref, w_down_ref, probs_ref, values_ref, d_hidden_ref, sems,
        all_ref, queries_ref, keys_ref,
    ) = refs[count:]
    batch = all_ref.shape[0]
    moves = project_moves(refs[:count], w_qkv_hbm, w_qkv_ref, all_ref)
    moves += [(bias_hbm, bias_ref), (cot_hbm, cot_ref), (w_down_hbm, w_down_ref)]
    copies = [pltpu.make_async_copy(src, dst, sems.at[i]) for i, (src, dst) in enumerate(moves)]
    for copy in copies[:-2]:
        copy.start()

    def start_rest():
        for copy in copies[-2:]:
            copy.start()

    project(copies[:-3], w_qkv_ref, all_ref, queries_ref, keys_ref, values_ref, start_rest)
    copies[-3].wait()
    back = [
        pltpu.make_async_copy(probs_ref.at[s], probs_hbm.at[s], sems.at[s]) for s in range(batch)
    ] + [
        pltpu.make_async_copy(values_ref, values_hbm, sems.at[batch]),
        pltpu.make_async_copy(d_hidden_ref, d_hidden_hbm, sems.at[batch + 1]),
    ]
    back[batch].start()

    def done(s):
        back[s].start()
        if s == 0:
            for copy in copies[-2:]:
                copy.wait()
            cot = cot_ref[...].reshape(-1, C_TOK)
            for n in range(0, w_down_ref.shape[0], 256):
                d_hidden_ref[:, n : n + 256] = nt(cot, w_down_ref[n : n + 256, :])
            back[batch + 1].start()

    attend(bias_ref, queries_ref, keys_ref, values_ref, probs_ref, att_ref, done)
    for copy in back:
        copy.wait()


def attend_scratch(batch, tok_rows, keys_all):
    return [
        pltpu.VMEM((batch, keys_all, C_TOK), bf16),
        pltpu.VMEM((batch * tok_rows, C_TOK), bf16),
        pltpu.VMEM((batch, keys_all, C_TOK), bf16),
    ]


def attend_stage(pieces, bias, w_qkv, cot, w_down):
    batch, tok_rows, _ = pieces[0].shape
    keys_all = tok_rows * len(pieces)
    vmem = pl.BlockSpec(memory_space=pltpu.VMEM)
    hbm = pl.BlockSpec(memory_space=pl.ANY)
    d_hidden = jax.ShapeDtypeStruct((cot.shape[0] * tok_rows, w_down.shape[0]), f32)
    return pl.pallas_call(
        functools.partial(attend_kernel, count=len(pieces)),
        in_specs=[hbm] * (len(pieces) + 4),
        out_specs=[vmem, hbm, hbm, hbm],
        out_shape=[
            jax.ShapeDtypeStruct((batch * tok_rows, C_TOK), bf16),
            jax.ShapeDtypeStruct((batch, PAIRS, keys_all, 2 * tok_rows), f32),
            jax.ShapeDtypeStruct((batch, keys_all, C_TOK), bf16),
            d_hidden,
        ],
        scratch_shapes=[
            pltpu.VMEM((3, C_TOK, C_TOK), bf16),
            pltpu.VMEM(bias.shape, bf16),
            pltpu.VMEM(cot.shape, bf16),
            pltpu.VMEM(w_down.shape, bf16),
            pltpu.VMEM((batch, PAIRS, keys_all, 2 * tok_rows), f32),
            pltpu.VMEM((batch, keys_all, C_TOK), bf16),
            pltpu.VMEM(d_hidden.shape, f32),
            pltpu.SemaphoreType.DMA((6 + len(pieces),)),
        ]
        + attend_scratch(batch, tok_rows, keys_all),
        compiler_params=pltpu.CompilerParams(vmem_limit_bytes=GRANT),
        cost_estimate=pl.CostEstimate(
            flops=4 * 10**9, bytes_accessed=10**7, transcendentals=10**6
        ),
        name="attend",
    )(*pieces, bias, w_qkv, cot, w_down)


def token_kernel(*refs, count):
    (
        bias_hbm, tokens_a_hbm, tokens_b_hbm, att_a_hbm, cot_hbm, probs_a_hbm, values_a_hbm,
        w_qkv_hbm, w_out_hbm, w_gate_hbm, w_up_hbm, d_hidden_hbm,
        resid_hbm, hidden_hbm, d_bias_ref,
        bias_ref, tokens_ref, att_a_ref, cot_ref, resid_ref, hidden_ref,
        w_qkv_ref, w_out_ref, w_gate_ref, w_up_ref, d_hidden_ref, probs_ref, values_ref, sems,
        all_ref, queries_ref, keys_ref, grads_ref, d_gate_ref, d_up_ref, hat_ref,
    ) = refs[count:]
    batch, tok_rows = cot_ref.shape[0], cot_ref.shape[1]
    keys_all = values_ref.shape[1]
    rows = batch * tok_rows
    ahead = values_a_hbm.shape[0]
    lead = ahead * tok_rows
    moves = project_moves(refs[:count], w_qkv_hbm, w_qkv_ref, all_ref)
    projecting = len(moves)
    moves += [
        (bias_hbm, bias_ref), (w_out_hbm, w_out_ref), (att_a_hbm, att_a_ref),
        (tokens_a_hbm, tokens_ref.at[pl.ds(0, ahead)]),
        (tokens_b_hbm, tokens_ref.at[pl.ds(ahead, batch - ahead)]), (cot_hbm, cot_ref),
        (d_hidden_hbm, d_hidden_ref), (w_gate_hbm, w_gate_ref), (w_up_hbm, w_up_ref),
        (values_a_hbm, values_ref.at[pl.ds(0, ahead)]), (probs_a_hbm, probs_ref.at[pl.ds(0, ahead)]),
    ]
    copies = [pltpu.make_async_copy(src, dst, sems.at[i]) for i, (src, dst) in enumerate(moves)]
    for copy in copies[: projecting + 1]:
        copy.start()

    def start_rest():
        for copy in copies[projecting + 1 :]:
            copy.start()

    own_values = values_ref.at[pl.ds(ahead, batch - ahead)]
    own_probs = probs_ref.at[pl.ds(ahead, batch - ahead)]
    project(
        copies[:projecting], w_qkv_ref, all_ref, queries_ref, keys_ref, own_values, start_rest
    )
    copies = copies[projecting:]
    copies[0].wait()
    attend(bias_ref, queries_ref, keys_ref, own_values, own_probs, queries_ref)

    for copy in copies[1:5]:
        copy.wait()
    tokens = tokens_ref[...].reshape(rows, C_TOK)
    resid_ref[0:lead, :] = tokens[0:lead] + nn(att_a_ref[...], w_out_ref[...])
    resid_ref[lead:rows, :] = tokens[lead:rows] + nn(queries_ref[...], w_out_ref[...])
    back = [
        pltpu.make_async_copy(resid_ref, resid_hbm, sems.at[0]),
        pltpu.make_async_copy(hidden_ref, hidden_hbm, sems.at[1]),
    ]
    back[0].start()
    hat, rstd = norm_rows(resid_ref[...])
    hat_ref[...] = hat
    grads_ref[...] = hat.astype(bf16)
    for copy in copies[5:9]:
        copy.wait()

    for n in range(0, w_gate_ref.shape[1], 256):
        shaped = grads_ref[...]
        gate = nn(shaped, w_gate_ref[:, n : n + 256])
        up = nn(shaped, w_up_ref[:, n : n + 256])
        d_hidden = d_hidden_ref[:, n : n + 256]
        sig = 1.0 / (1.0 + jnp.exp(-gate))
        act = gate * sig
        hidden_ref[:, n : n + 256] = (act * up).astype(bf16)
        d_gate_ref[:, n : n + 256] = (
            d_hidden * up * sig * (1.0 + gate * (1.0 - sig))
        ).astype(bf16)
        d_up_ref[:, n : n + 256] = (d_hidden * act).astype(bf16)

    back[1].start()
    d_normed = (
        nt(w_gate_ref[...], d_gate_ref[...]) + nt(w_up_ref[...], d_up_ref[...])
    ).T
    hat = hat_ref[...]
    first = jnp.mean(d_normed, axis=-1, keepdims=True)
    second = jnp.mean(d_normed * hat, axis=-1, keepdims=True)
    d_resid = cot_ref[...].reshape(rows, C_TOK).astype(f32) + rstd * (
        d_normed - first - hat * second
    )
    grads_ref[...] = nt(d_resid.astype(bf16), w_out_ref[...]).astype(bf16)
    for copy in copies[9:]:
        copy.wait()
    masks = head_masks(tok_rows)
    size = d_bias_ref.shape[2]
    for quad, (low, high) in enumerate(QUAD_WINDOWS):
        totals = [jnp.zeros((keys_all, 2 * tok_rows), f32) for _ in range(2)]
        for s in range(batch):
            grads = spread_heads(
                grads_ref[s * tok_rows : (s + 1) * tok_rows, low:high], masks[quad]
            )
            d_both = nt(values_ref[s, :, low:high], grads)
            for half in range(2):
                d_probs = d_both[:, 2 * tok_rows * half : 2 * tok_rows * (half + 1)]
                probs = probs_ref[s, 2 * quad + half]
                delta = jnp.sum(probs * d_probs, axis=0, keepdims=True)
                totals[half] = totals[half] + probs * (d_probs - delta)
        for half in range(2):
            for k in range(d_bias_ref.shape[0]):
                d_bias_ref[k, 2 * quad + half] = totals[half][size * k : size * (k + 1)].astype(
                    bf16
                )
    for copy in back:
        copy.wait()


def token_stage(
    pieces, bias, tokens_a, tokens_b, att_a, cot, probs_a, values_a, w_qkv, w_out, w_gate, w_up,
    d_hidden,
):
    batch, tok_rows, _ = cot.shape
    keys_all = tok_rows * len(pieces)
    rows = batch * tok_rows
    hidden = w_gate.shape[1]
    vmem = pl.BlockSpec(memory_space=pltpu.VMEM)
    hbm = pl.BlockSpec(memory_space=pl.ANY)
    return pl.pallas_call(
        functools.partial(token_kernel, count=len(pieces)),
        in_specs=[hbm] * (len(pieces) + 12),
        out_specs=[hbm, hbm, vmem],
        out_shape=[
            jax.ShapeDtypeStruct((rows, C_TOK), f32),
            jax.ShapeDtypeStruct((rows, hidden), bf16),
            jax.ShapeDtypeStruct(bias.shape, bf16),
        ],
        scratch_shapes=[
            pltpu.VMEM(bias.shape, bf16),
            pltpu.VMEM(cot.shape, f32),
            pltpu.VMEM(att_a.shape, bf16),
            pltpu.VMEM(cot.shape, bf16),
            pltpu.VMEM((rows, C_TOK), f32),
            pltpu.VMEM((rows, hidden), bf16),
            pltpu.VMEM((3, C_TOK, C_TOK), bf16),
            pltpu.VMEM(w_out.shape, bf16),
            pltpu.VMEM(w_gate.shape, bf16),
            pltpu.VMEM(w_up.shape, bf16),
            pltpu.VMEM(d_hidden.shape, f32),
            pltpu.VMEM((batch, PAIRS, keys_all, 2 * tok_rows), f32),
            pltpu.VMEM((batch, keys_all, C_TOK), bf16),
            pltpu.SemaphoreType.DMA((14 + len(pieces),)),
        ]
        + attend_scratch(pieces[0].shape[0], tok_rows, keys_all)
        + [
            pltpu.VMEM((rows, C_TOK), bf16),
            pltpu.VMEM((rows, hidden), bf16),
            pltpu.VMEM((rows, hidden), bf16),
            pltpu.VMEM((rows, C_TOK), f32),
        ],
        compiler_params=pltpu.CompilerParams(vmem_limit_bytes=GRANT),
        cost_estimate=pl.CostEstimate(
            flops=10**10, bytes_accessed=2 * 10**7, transcendentals=10**6
        ),
        name="tokens",
    )(
        *pieces, bias, tokens_a, tokens_b, att_a, cot, probs_a, values_a, w_qkv, w_out, w_gate,
        w_up, d_hidden,
    )


def output_kernel(
    resid_ref, hidden_ref, w_down_ref, pair_ref, out_ref, hat_ref, rstd_ref, pairf_ref
):
    out_ref[...] = (resid_ref[...] + nn(hidden_ref[...], w_down_ref[...])).astype(bf16)
    rows, keys = pair_ref.shape[0], pair_ref.shape[1]
    for i in range(rows // 8):
        pairf_ref[8 * keys * i : 8 * keys * (i + 1), :] = (
            pair_ref[8 * i : 8 * i + 8].astype(f32).reshape(8 * keys, CZ)
        )

    def norm_step(j, carry):
        hat, rstd = norm_rows(pairf_ref[pl.ds(j, rows, stride=keys), :])
        at = pl.multiple_of(j * rows, rows)
        hat_ref[pl.ds(at, rows), :] = hat
        rstd = jnp.broadcast_to(rstd, (rows, CZ)).T[0:1]
        rstd_ref[pl.ds(j, 1), :] = jnp.concatenate([rstd, rstd], axis=1)
        return carry

    lax.fori_loop(0, keys, norm_step, 0, unroll=4)


def output_stage(resid, hidden, w_down, pair):
    rows, keys = pair.shape[0], pair.shape[1]
    return pl.pallas_call(
        output_kernel,
        out_shape=[jax.ShapeDtypeStruct(resid.shape, bf16)]
        + [
            jax.ShapeDtypeStruct((rows * keys, CZ), f32),
            jax.ShapeDtypeStruct((keys, 2 * rows), f32),
        ],
        scratch_shapes=[pltpu.VMEM((rows * keys, CZ), f32)],
        compiler_params=pltpu.CompilerParams(vmem_limit_bytes=GRANT),
        cost_estimate=pl.CostEstimate(
            flops=10**9, bytes_accessed=8 * 10**6, transcendentals=0
        ),
        name="output",
    )(resid, hidden, w_down, pair)


def grad_kernel(
    parts_hbm, hat_hbm, rstd_hbm, gain_hbm, w_bias_hbm, out_hbm, parts_ref, hat_ref, rstd_ref,
    gain_ref, w_bias_ref, total_ref, out_ref, sems,
):
    keys = parts_ref.shape[2]
    rows = hat_ref.shape[0] // keys
    size = 8 * rows
    moves = [
        (gain_hbm, gain_ref), (w_bias_hbm, w_bias_ref), (parts_hbm, parts_ref),
        (rstd_hbm, rstd_ref),
    ]
    for c in range(keys // 8):
        moves.append((hat_hbm.at[pl.ds(size * c, size)], hat_ref.at[pl.ds(size * c, size)]))
    copies = start_all(moves, sems)
    for copy in copies[0:2]:
        copy.wait()
    weights = jnp.concatenate(split_heads(w_bias_ref[...]), axis=0) * gain_ref[...]
    weights = weights - jnp.mean(weights, axis=-1, keepdims=True)
    weights = jnp.concatenate([weights[0:PAIRS], weights[PAIRS:HEADS]], axis=1)
    w_high = weights.astype(bf16).astype(f32)
    w_middle = (weights - w_high).astype(bf16).astype(f32)
    w_low = weights - w_high - w_middle
    weights = jnp.concatenate([w_high, w_middle, w_low, w_high, w_middle, w_high], axis=0)
    weights = weights.astype(bf16)
    for copy in copies[2:4]:
        copy.wait()
    for pair in range(PAIRS):
        total = parts_ref[0, pair].astype(f32)
        for k in range(1, parts_ref.shape[0]):
            total = total + parts_ref[k, pair].astype(f32)
        total_ref[pair * keys : (pair + 1) * keys, :] = total * rstd_ref[...]
    back = []
    for c in range(keys // 8):
        copies[4 + c].wait()
        for j in range(8 * c, 8 * c + 8):
            total = total_ref[pl.ds(j, PAIRS, stride=keys), :]
            high = total.astype(bf16).astype(f32)
            middle = (total - high).astype(bf16).astype(f32)
            low = total - high - middle
            stack = jnp.concatenate([high, high, high, middle, middle, low], axis=0)
            both = nn(stack.T.astype(bf16), weights)
            scaled = both[0:rows, 0:CZ] + both[rows : 2 * rows, CZ : 2 * CZ]
            hat = hat_ref[rows * j : rows * (j + 1), :]
            second = jnp.mean(scaled * hat, axis=-1, keepdims=True)
            out_ref[pl.ds(size * c + j % 8, rows, stride=8), :] = scaled - hat * second
        back.append(
            pltpu.make_async_copy(
                out_ref.at[pl.ds(size * c, size)].reshape(rows, 8, CZ),
                out_hbm.at[:, pl.ds(8 * c, 8), :],
                sems.at[c],
            )
        )
        back[c].start()
    for copy in back:
        copy.wait()


def pair_back(parts, hat, rstd, pair_gain, w_bias_t):
    keys = parts.shape[2]
    rows = hat.shape[0] // keys
    hbm = pl.BlockSpec(memory_space=pl.ANY)
    return pl.pallas_call(
        grad_kernel,
        in_specs=[hbm] * 5,
        out_specs=hbm,
        out_shape=jax.ShapeDtypeStruct((rows, keys, CZ), f32),
        scratch_shapes=[
            pltpu.VMEM(parts.shape, bf16),
            pltpu.VMEM(hat.shape, f32),
            pltpu.VMEM(rstd.shape, f32),
            pltpu.VMEM((1, CZ), f32),
            pltpu.VMEM(w_bias_t.shape, bf16),
            pltpu.VMEM((keys * PAIRS, 2 * rows), f32),
            pltpu.VMEM((rows * keys, CZ), f32),
            pltpu.SemaphoreType.DMA((4 + keys // 8,)),
        ],
        compiler_params=pltpu.CompilerParams(vmem_limit_bytes=GRANT),
        cost_estimate=pl.CostEstimate(flops=10**8, bytes_accessed=4 * 10**6, transcendentals=0),
        name="pair_grad",
    )(parts, hat, rstd, pair_gain.reshape(1, CZ), w_bias_t)


def swap(values, axis, k):
    return lax.ppermute(values, axis, [(i, i ^ k) for i in range(lax.axis_size(axis))])


def gather(values, axis):
    far = range(lax.axis_size(axis) - 1, 0, -1)
    return [values] + [swap(values, axis, k) for k in far][::-1]


def body(
    atom_feats, atom_counts, atom_mask, token_single, pair, pair_gain, w_bias, w_atom_qkv,
    w_atom_out, w_embed, w_qkv, w_out, w_gate, w_up, w_down, cotangent,
):
    batch, atom_rows, _ = atom_feats.shape
    tok_rows = token_single.shape[0]
    shards = lax.axis_size("tok")
    groups = lax.axis_size("samp")

    w_bias_t = w_bias.T
    local_bias, head, tail = pair_bias(pair, pair_gain, w_bias_t, atom_feats, groups)
    steps = [(i, i + 1) for i in range(shards - 1)]
    left = lax.ppermute(tail, "tok", steps)
    right = lax.ppermute(head, "tok", [(j, i) for i, j in steps])

    bias = lax.all_to_all(local_bias, "samp", 0, 0).reshape(groups, PAIRS, -1, 2 * tok_rows)

    mask = atom_mask.reshape(-1, 128)
    mask, local_bias = lax.optimization_barrier((mask, local_bias))

    each = batch // 2
    tokens, gathered = [], []
    for part in range(2):
        tok, normed = atom_stage(
            part, each, atom_feats, left, right, mask, atom_counts, token_single, w_atom_qkv,
            w_atom_out, w_embed,
        )
        tokens.append(tok)
        gathered.append(gather(normed, "tok"))
    att_a, probs_a, values_a, d_hidden = attend_stage(
        gathered[0], bias, w_qkv, cotangent, w_down
    )
    resid, hidden, d_bias = token_stage(
        gathered[1], bias, *tokens, att_a, cotangent, probs_a, values_a, w_qkv, w_out, w_gate,
        w_up, d_hidden,
    )
    parts = lax.all_to_all(d_bias, "samp", 0, 0)
    token_out, hat, rstd = output_stage(resid, hidden, w_down, pair)
    pair_grad = pair_back(parts, hat, rstd, pair_gain, w_bias_t)
    token_out = token_out.reshape(batch, tok_rows, C_TOK)
    return (token_out, pair_grad)


def solution(mesh):
    in_specs = (
        P("samp", "tok", None),
        P("tok", None),
        P(),
        P("tok", None),
        P("tok", "samp", None),
        P(), P(), P(), P(), P(), P(), P(), P(), P(), P(),
        P("samp", "tok", None),
    )
    out_specs = (P("samp", "tok", None), P("tok", "samp", None))
    return jax.shard_map(body, mesh=mesh, in_specs=in_specs, out_specs=out_specs, check_vma=False)
```

```python
import functools

import jax
import jax.numpy as jnp
from jax import lax
from jax.experimental import pallas as pl
from jax.experimental.pallas import tpu as pltpu
from jax.sharding import PartitionSpec as P

C_ATOM = 128
ATOM_HEADS = 4
C_TOK = 768
HEADS = 16
ATOM_HD = 32
HD = 48
CZ = 128
HALO = 48
PAIRS = HEADS // 2
GRANT = 64 << 20
LOG2E = 1.4426950408889634

epsilon = 1e-05
f32 = jnp.float32
bf16 = jnp.bfloat16

WINDOWS = ((0, 128), (0, 256), (128, 384), (256, 384))


def nn(a, b):
    return lax.dot_general(a, b, (((1,), (0,)), ((), ())), preferred_element_type=f32)


def nt(a, b):
    return lax.dot_general(a, b, (((1,), (1,)), ((), ())), preferred_element_type=f32)


def tn(a, b):
    return lax.dot_general(a, b, (((0,), (0,)), ((), ())), preferred_element_type=f32)


def start_all(moves, sems):
    copies = [pltpu.make_async_copy(src, dst, sems.at[i]) for i, (src, dst) in enumerate(moves)]
    for copy in copies:
        copy.start()
    return copies


def norm_rows(values):
    center = values - jnp.mean(values, axis=-1, keepdims=True)
    scale_inv = lax.rsqrt(jnp.mean(center * center, axis=-1, keepdims=True) + epsilon)
    return (center * scale_inv, scale_inv)


def iota(shape, dim):
    return lax.broadcasted_iota(jnp.int32, shape, dim)


def pick_heads(parity):
    row, col = iota((PAIRS, HEADS), 0), iota((PAIRS, HEADS), 1)
    return (col == 2 * row + parity).astype(f32).astype(bf16)


def split_heads(w_bias_t):
    return [nn(pick_heads(parity), w_bias_t) for parity in range(2)]


def bias_kernel(
    pair_hbm, gain_hbm, w_bias_hbm, feats_hbm, out_hbm, edges_hbm, pair_ref, gain_ref, w_bias_ref,
    scaled_ref, stage_ref, local_ref, head_ref, tail_ref, edges_ref, sems,
):
    rows, keys = pair_ref.shape[0], pair_ref.shape[1]
    atoms = feats_hbm.shape[1]
    part = rows // 4
    moves = [
        (gain_hbm, gain_ref), (w_bias_hbm, w_bias_ref),
        (feats_hbm.at[:, pl.ds(0, HALO), :], head_ref),
        (feats_hbm.at[:, pl.ds(atoms - HALO, HALO), :], tail_ref),
    ]
    for i in range(4):
        moves.append((pair_hbm.at[pl.ds(part * i, part)], pair_ref.at[pl.ds(part * i, part)]))
    copies = start_all(moves, sems)
    for copy in copies[0:2]:
        copy.wait()
    gain = gain_ref[...]
    weights = jnp.concatenate(split_heads(w_bias_ref[...]), axis=1).astype(bf16)
    for i in range(rows // 8):
        if 8 * i % part == 0:
            copies[4 + 8 * i // part].wait()
        block = pair_ref[8 * i : 8 * i + 8].astype(f32).reshape(8 * keys, CZ)
        scaled_ref[8 * keys * i : 8 * keys * (i + 1), :] = norm_rows(block)[0] * gain
    for copy in copies[2:4]:
        copy.wait()
    here = lax.axis_index("tok")
    head, tail = head_ref[...].astype(f32), tail_ref[...].astype(f32)
    for k in range(edges_ref.shape[0]):
        before = jnp.where(here == k + 1, 1.0, 0.0)
        after = jnp.where(here == k - 1, 1.0, 0.0)
        edges_ref[k] = (head * before + tail * after).astype(bf16)
    edges = start_all([(edges_ref, edges_hbm)], sems)
    blank = jnp.zeros((rows, CZ), bf16)
    for j in range(keys):
        block = scaled_ref[pl.ds(j, rows, stride=keys), :].astype(bf16)
        both = jnp.concatenate(
            [jnp.concatenate([block, blank], axis=1), jnp.concatenate([blank, block], axis=1)],
            axis=0,
        )
        stage_ref[pl.ds(j, PAIRS, stride=keys), :] = nt(weights, both)
    local_ref[...] = stage_ref[...].astype(bf16)
    back = [
        pltpu.make_async_copy(local_ref, out_hbm.at[k], sems.at[2 + k])
        for k in range(out_hbm.shape[0])
    ]
    for copy in back:
        copy.start()
    for copy in edges + back:
        copy.wait()


def pair_bias(pair, pair_gain, w_bias_t, feats, copies, shards):
    rows, keys = pair.shape[0], pair.shape[1]
    edge = (feats.shape[0], HALO, C_ATOM)
    hbm = pl.BlockSpec(memory_space=pl.ANY)
    return pl.pallas_call(
        bias_kernel,
        in_specs=[hbm] * 4,
        out_specs=[hbm] * 2,
        out_shape=[
            jax.ShapeDtypeStruct((copies, keys * PAIRS, 2 * rows), bf16),
            jax.ShapeDtypeStruct((shards,) + edge, bf16),
        ],
        scratch_shapes=[
            pltpu.VMEM(pair.shape, bf16),
            pltpu.VMEM((1, CZ), f32),
            pltpu.VMEM(w_bias_t.shape, bf16),
            pltpu.VMEM((rows * keys, CZ), f32),
            pltpu.VMEM((keys * PAIRS, 2 * rows), f32),
            pltpu.VMEM((keys * PAIRS, 2 * rows), bf16),
            pltpu.VMEM(edge, bf16),
            pltpu.VMEM(edge, bf16),
            pltpu.VMEM((shards,) + edge, bf16),
            pltpu.SemaphoreType.DMA((8 + copies,)),
        ],
        compiler_params=pltpu.CompilerParams(vmem_limit_bytes=GRANT),
        cost_estimate=pl.CostEstimate(flops=10**7, bytes_accessed=10**7, transcendentals=0),
        name="pair_bias",
    )(pair, pair_gain.reshape(1, CZ), w_bias_t, feats)


def atom_kernel(
    feats_hbm, halos_hbm, mask_hbm, counts_hbm, single_hbm, w_qkv_hbm, w_out_hbm,
    w_embed_hbm, tokens_ref, normed_ref, mask_ref, counts_ref, single_ref, w_qkv_ref, w_out_ref,
    w_embed_ref, sems, padded_ref, normed_atoms_ref, qkv_a, qkv_b, scores_a, scores_b, probs_a, probs_b, mixed_ref,
    updated_ref, split_ref, keybias_ref, onehot_ref, *, first,
):
    batch, atoms = tokens_ref.shape[0], feats_hbm.shape[1]
    padded = atoms + 2 * HALO
    moves = [(counts_hbm, counts_ref), (mask_hbm, mask_ref), (w_qkv_hbm, w_qkv_ref)]
    here = lax.axis_index("tok")
    left = halos_hbm.at[jnp.maximum(here - 1, 0)]
    right = halos_hbm.at[jnp.minimum(here + 1, halos_hbm.shape[0] - 1)]
    for s in range(batch):
        moves.append((left.at[first + s], padded_ref.at[s, pl.ds(0, HALO)]))
        moves.append((feats_hbm.at[first + s], padded_ref.at[s, pl.ds(HALO, atoms)]))
        moves.append((right.at[first + s], padded_ref.at[s, pl.ds(HALO + atoms, HALO)]))
    moves += [(w_out_hbm, w_out_ref), (w_embed_hbm, w_embed_ref), (single_hbm, single_ref)]
    copies = start_all(moves, sems)
    for copy in copies:
        copy.wait()
    tok_rows = single_ref.shape[0]
    blocks = atoms // 128
    chunks = atoms // 256
    qkv_refs = (qkv_a, qkv_b)

    eye = iota((128, 128), 0) == iota((128, 128), 1)
    for b in range(-1, blocks + 1):
        at = lax.axis_index("tok") * blocks + b
        inside = jnp.where((at >= 0) & (at < mask_ref.shape[0]), 1, 0)
        row = mask_ref[pl.ds(jnp.clip(at, 0, mask_ref.shape[0] - 1), 1), :] * inside
        row = jnp.broadcast_to(row.astype(f32), (128, 128))
        col = jnp.sum(jnp.where(eye, row, 0.0), axis=1, keepdims=True)
        col = jnp.broadcast_to((col - 1.0) * 1e30, (128, 128))
        if b < 0:
            keybias_ref[0:HALO, :] = col[128 - HALO : 128]
        elif b < blocks:
            keybias_ref[HALO + 128 * b : HALO + 128 * b + 128, :] = col
        else:
            keybias_ref[HALO + atoms : padded, :] = col[0:HALO]
    counts = jnp.broadcast_to(counts_ref[...].astype(f32), (tok_rows, tok_rows))
    sub, lane = iota((tok_rows, tok_rows), 0), iota((tok_rows, tok_rows), 1)
    start = jnp.sum(jnp.where(lane < sub, counts, 0.0), axis=1, keepdims=True)
    own = jnp.sum(jnp.where(lane == sub, counts, 0.0), axis=1, keepdims=True)
    pos = iota((tok_rows, 256), 1).astype(f32)
    for g in range(chunks):
        at = pos + float(g * 256)
        hit = jnp.where((at >= start) & (at < start + own), 1.0, 0.0).astype(bf16)
        onehot_ref[:, 256 * g : 256 * g + 256] = hit
        onehot_ref[:, atoms + 256 * g : atoms + 256 * g + 256] = hit
    probs_a[...] = jnp.zeros_like(probs_a)
    probs_b[...] = jnp.zeros_like(probs_b)
    head_of = iota((32, 128), 1) // ATOM_HD
    head_mask = [(head_of == h).astype(f32).astype(bf16) for h in range(ATOM_HEADS)]
    own_atom = (iota((32, 128), 1) % 32) == iota((32, 128), 0)
    factor = ATOM_HD ** (-0.5) * LOG2E
    def qkv_step(s):
        for low in range(0, padded, padded // 4):
            part = slice(low, low + padded // 4)
            normed, unused = norm_rows(padded_ref[s, part, :].astype(f32))
            normed_atoms_ref[part, :] = normed.astype(bf16)
        qkv_refs[s % 2][...] = nn(normed_atoms_ref[...], w_qkv_ref[...]).astype(bf16)

    def score_step(s, group, to_ref):
        qkv_ref = qkv_refs[s % 2]
        for k in range(2):
            base = pl.multiple_of(group * 128 + 64 * k, 64)
            queries = qkv_ref[pl.ds(base + HALO, 64), 0:C_ATOM]
            spread = jnp.concatenate(
                [
                    queries[32 * w : 32 * w + 32] * head_mask[h]
                    for w in range(2)
                    for h in range(ATOM_HEADS)
                ],
                axis=0,
            )
            to_ref[k] = nt(qkv_ref[pl.ds(base, 160), C_ATOM : 2 * C_ATOM], spread)

    def softmax_step(group, from_ref, to_ref):
        for k in range(2):
            base = pl.multiple_of(group * 128 + 64 * k, 64)
            for w in range(2):
                keybias = keybias_ref[pl.ds(base + 32 * w, 128), :]
                keybias = jnp.concatenate(
                    [keybias[0:48], jnp.where(own_atom, 0.0, keybias[48:80]), keybias[80:128]],
                    axis=0,
                )
                scores = from_ref[k, 32 * w : 32 * w + 128, 128 * w : 128 * w + 128] + keybias
                expo = jnp.exp2((scores - jnp.max(scores, axis=0, keepdims=True)) * factor)
                weights = expo * (1.0 / jnp.sum(expo, axis=0, keepdims=True))
                to_ref[k, 32 * w : 32 * w + 128, 128 * w : 128 * w + 128] = weights.astype(bf16)

    def value_step(s, group, from_ref):
        qkv_ref = qkv_refs[s % 2]
        for k in range(2):
            base = pl.multiple_of(group * 128 + 64 * k, 64)
            part = tn(from_ref[k], qkv_ref[pl.ds(base, 160), 2 * C_ATOM : 3 * C_ATOM])
            mixes = []
            for w in range(2):
                mix = part[128 * w : 128 * w + 32]
                for h in range(1, ATOM_HEADS):
                    low = 128 * w + 32 * h
                    mix = jnp.where(head_of == h, part[low : low + 32], mix)
                mixes.append(mix.astype(bf16))
            mixed_ref[pl.ds(base, 64), :] = jnp.concatenate(mixes, axis=0)

    def embed_step(s):
        feats = padded_ref[s, HALO : HALO + atoms, :].astype(f32)
        updated_ref[...] = (feats + nn(mixed_ref[...], w_out_ref[...])).astype(bf16)
        for n in range(0, C_TOK, 256):
            embedded = jnp.maximum(nn(updated_ref[...], w_embed_ref[:, n : n + 256]), 0.0)
            high = embedded.astype(bf16)
            split_ref[0:atoms, n : n + 256] = high
            split_ref[atoms : 2 * atoms, n : n + 256] = (embedded - high.astype(f32)).astype(bf16)
        pooled = nn(onehot_ref[...], split_ref[...])
        tokens = pooled / own + single_ref[...].astype(f32)
        tokens_ref[s] = tokens
        normed_ref[s] = norm_rows(tokens)[0].astype(bf16)

    qkv_step(0)
    for s in range(batch):
        score_step(s, 0, scores_a)

        def window_step(i, carry, s=s):
            even, odd = 2 * i, 2 * i + 1
            score_step(s, odd, scores_b)
            softmax_step(even, scores_a, probs_a)
            value_step(s, jnp.maximum(even - 1, 0), probs_b)
            score_step(s, jnp.minimum(odd + 1, 2 * chunks - 1), scores_a)
            softmax_step(odd, scores_b, probs_b)
            value_step(s, even, probs_a)
            return carry

        lax.fori_loop(0, chunks, window_step, 0)
        value_step(s, 2 * chunks - 1, probs_b)
        embed_step(s)
        if s + 1 < batch:
            qkv_step(s + 1)


def atom_stage(part, batch, feats, halos, mask, counts, single, w_qkv, w_out, w_embed):
    atoms = feats.shape[1]
    tok_rows = single.shape[0]
    padded = atoms + 2 * HALO
    return pl.pallas_call(
        functools.partial(atom_kernel, first=part * batch),
        in_specs=[pl.BlockSpec(memory_space=pl.ANY)] * 8,
        out_specs=[pl.BlockSpec(memory_space=pltpu.VMEM)] * 2,
        out_shape=[
            jax.ShapeDtypeStruct((batch, tok_rows, C_TOK), f32),
            jax.ShapeDtypeStruct((batch, tok_rows, C_TOK), bf16),
        ],
        scratch_shapes=[
            pltpu.VMEM(mask.shape, jnp.int32),
            pltpu.VMEM(counts.shape, jnp.int32),
            pltpu.VMEM(single.shape, bf16),
            pltpu.VMEM(w_qkv.shape, bf16),
            pltpu.VMEM(w_out.shape, bf16),
            pltpu.VMEM(w_embed.shape, bf16),
            pltpu.SemaphoreType.DMA((6 + 3 * batch,)),
            pltpu.VMEM((batch, padded, C_ATOM), bf16),
            pltpu.VMEM((padded, C_ATOM), bf16),
            pltpu.VMEM((padded, 3 * C_ATOM), bf16),
            pltpu.VMEM((padded, 3 * C_ATOM), bf16),
            pltpu.VMEM((2, 160, 256), f32),
            pltpu.VMEM((2, 160, 256), f32),
            pltpu.VMEM((2, 160, 256), bf16),
            pltpu.VMEM((2, 160, 256), bf16),
            pltpu.VMEM((atoms, C_ATOM), bf16),
            pltpu.VMEM((atoms, C_ATOM), bf16),
            pltpu.VMEM((2 * atoms, C_TOK), bf16),
            pltpu.VMEM((padded, 128), f32),
            pltpu.VMEM((tok_rows, 2 * atoms), bf16),
        ],
        compiler_params=pltpu.CompilerParams(vmem_limit_bytes=GRANT),
        cost_estimate=pl.CostEstimate(
            flops=10**10, bytes_accessed=4 * 10**6, transcendentals=3 * 10**6
        ),
        name="atoms",
    )(feats, halos, mask, counts, single, w_qkv, w_out, w_embed)


def head_masks(rows):
    masks = []
    for pair in range(4):
        low, high = WINDOWS[pair]
        lane = iota((rows, high - low), 1) + low
        first = 2 * pair * HD
        masks.append(
            [(lane >= first + HD * k) & (lane < first + HD * (k + 1)) for k in range(2)]
        )
    return masks


def two_heads(block, masks):
    blank = jnp.zeros_like(block)
    return jnp.concatenate([jnp.where(mask, block, blank) for mask in masks], axis=0)


def project_moves(piece_hbms, w_qkv_hbm, w_qkv_ref, all_ref):
    tok_rows = piece_hbms[0].shape[1]
    weights = [
        (w_qkv_hbm.at[:, pl.ds(C_TOK * i, C_TOK)], w_qkv_ref.at[i]) for i in range(3)
    ]
    here = lax.axis_index("tok")
    pieces = []
    for k, piece in enumerate(piece_hbms):
        at = pl.multiple_of((here ^ k) * tok_rows, tok_rows)
        pieces.append((piece, all_ref.at[:, pl.ds(at, tok_rows), :]))
    return [pieces[0], weights[0]] + pieces[1:] + weights[1:]


def project(copies, w_qkv_ref, all_ref, queries_ref, keys_ref, values_ref, loaded):
    batch = all_ref.shape[0]
    tok_rows = queries_ref.shape[0] // batch
    at = pl.multiple_of(lax.axis_index("tok") * tok_rows, tok_rows)
    for copy in copies[0:2]:
        copy.wait()
    own = jnp.concatenate([all_ref[s, pl.ds(at, tok_rows), :] for s in range(batch)], axis=0)
    for n in range(0, C_TOK, 256):
        queries_ref[:, n : n + 256] = nn(own, w_qkv_ref[0, :, n : n + 256]).astype(bf16)
    for copy in copies[2:-1]:
        copy.wait()
    for which, to_ref in ((1, keys_ref), (2, values_ref)):
        if which == 2:
            copies[-1].wait()
            loaded()
        for n in range(0, C_TOK, 256):
            for s in range(batch):
                to_ref[s, :, n : n + 256] = nn(
                    all_ref[s], w_qkv_ref[which, :, n : n + 256]
                ).astype(bf16)


def windows(pair):
    low, high = WINDOWS[pair % 4]
    return 384 * (pair // 4) + low, 384 * (pair // 4) + high


def attend(bias_ref, queries_ref, keys_ref, values_ref, probs_ref, att_ref, done=None):
    batch, keys_all = keys_ref.shape[0], keys_ref.shape[1]
    tok_rows = queries_ref.shape[0] // batch
    masks = head_masks(tok_rows)
    factor = HD ** (-0.5)

    for s in range(batch):
        at = s * tok_rows
        for pair in range(PAIRS):
            low, high = windows(pair)
            queries = two_heads(queries_ref[pl.ds(at, tok_rows), low:high], masks[pair % 4])
            probs_ref[s, pair] = nt(keys_ref[s, :, low:high], queries)
        for pair in range(PAIRS):
            scores = probs_ref[s, pair] * factor
            bias = [bias_ref[k, pair].astype(f32) for k in range(bias_ref.shape[0])]
            scores = scores + jnp.concatenate(bias, axis=0)
            expo = jnp.exp(scores - jnp.max(scores, axis=0, keepdims=True))
            probs_ref[s, pair] = expo * (1.0 / jnp.sum(expo, axis=0, keepdims=True))
        lanes = [jnp.zeros((tok_rows, 128), f32) for _ in range(C_TOK // 128)]
        for pair in range(PAIRS):
            low, high = windows(pair)
            part = tn(probs_ref[s, pair].astype(bf16), values_ref[s, :, low:high])
            first, second = masks[pair % 4]
            mix = jnp.where(first, part[0:tok_rows], 0.0)
            mix = jnp.where(second, part[tok_rows : 2 * tok_rows], mix)
            for t in range((high - low) // 128):
                lanes[low // 128 + t] = lanes[low // 128 + t] + mix[:, 128 * t : 128 * t + 128]
        for t in range(C_TOK // 128):
            att_ref[pl.ds(at, tok_rows), 128 * t : 128 * t + 128] = lanes[t].astype(bf16)
        if done is not None:
            done(s)


def attend_kernel(*refs, count):
    (
        bias_hbm, w_qkv_hbm, cot_hbm, w_down_hbm, att_ref, probs_hbm, values_hbm, d_hidden_hbm,
        w_qkv_ref, bias_ref, cot_ref, w_down_ref, probs_ref, values_ref, d_hidden_ref, sems,
        all_ref, queries_ref, keys_ref,
    ) = refs[count:]
    batch = all_ref.shape[0]
    moves = project_moves(refs[:count], w_qkv_hbm, w_qkv_ref, all_ref)
    moves += [(bias_hbm, bias_ref), (cot_hbm, cot_ref), (w_down_hbm, w_down_ref)]
    copies = start_all(moves, sems)
    project(copies[:-3], w_qkv_ref, all_ref, queries_ref, keys_ref, values_ref, lambda: None)
    for copy in copies[-3:]:
        copy.wait()
    back = [
        pltpu.make_async_copy(probs_ref.at[s], probs_hbm.at[s], sems.at[s]) for s in range(batch)
    ] + [
        pltpu.make_async_copy(values_ref, values_hbm, sems.at[batch]),
        pltpu.make_async_copy(d_hidden_ref, d_hidden_hbm, sems.at[batch + 1]),
    ]
    back[batch].start()
    cot = cot_ref[...].reshape(-1, C_TOK)
    for n in range(0, w_down_ref.shape[0], 256):
        d_hidden_ref[:, n : n + 256] = nt(cot, w_down_ref[n : n + 256, :])
    back[batch + 1].start()
    attend(
        bias_ref, queries_ref, keys_ref, values_ref, probs_ref, att_ref, lambda s: back[s].start()
    )
    for copy in back:
        copy.wait()


def attend_scratch(batch, tok_rows, keys_all):
    return [
        pltpu.VMEM((batch, keys_all, C_TOK), bf16),
        pltpu.VMEM((batch * tok_rows, C_TOK), bf16),
        pltpu.VMEM((batch, keys_all, C_TOK), bf16),
    ]


def attend_stage(pieces, bias, w_qkv, cot, w_down):
    batch, tok_rows, _ = pieces[0].shape
    keys_all = tok_rows * len(pieces)
    vmem = pl.BlockSpec(memory_space=pltpu.VMEM)
    hbm = pl.BlockSpec(memory_space=pl.ANY)
    d_hidden = jax.ShapeDtypeStruct((cot.shape[0] * tok_rows, w_down.shape[0]), f32)
    return pl.pallas_call(
        functools.partial(attend_kernel, count=len(pieces)),
        in_specs=[hbm] * (len(pieces) + 4),
        out_specs=[vmem, hbm, hbm, hbm],
        out_shape=[
            jax.ShapeDtypeStruct((batch * tok_rows, C_TOK), bf16),
            jax.ShapeDtypeStruct((batch, PAIRS, keys_all, 2 * tok_rows), f32),
            jax.ShapeDtypeStruct((batch, keys_all, C_TOK), bf16),
            d_hidden,
        ],
        scratch_shapes=[
            pltpu.VMEM((3, C_TOK, C_TOK), bf16),
            pltpu.VMEM(bias.shape, bf16),
            pltpu.VMEM(cot.shape, bf16),
            pltpu.VMEM(w_down.shape, bf16),
            pltpu.VMEM((batch, PAIRS, keys_all, 2 * tok_rows), f32),
            pltpu.VMEM((batch, keys_all, C_TOK), bf16),
            pltpu.VMEM(d_hidden.shape, f32),
            pltpu.SemaphoreType.DMA((6 + len(pieces),)),
        ]
        + attend_scratch(batch, tok_rows, keys_all),
        compiler_params=pltpu.CompilerParams(vmem_limit_bytes=GRANT),
        cost_estimate=pl.CostEstimate(
            flops=4 * 10**9, bytes_accessed=10**7, transcendentals=10**6
        ),
        name="attend",
    )(*pieces, bias, w_qkv, cot, w_down)


def token_kernel(*refs, count):
    (
        bias_hbm, tokens_a_hbm, tokens_b_hbm, att_a_hbm, cot_hbm, probs_a_hbm, values_a_hbm,
        w_qkv_hbm, w_out_hbm, w_gate_hbm, w_up_hbm, d_hidden_hbm,
        resid_hbm, hidden_hbm, d_bias_ref,
        bias_ref, tokens_ref, att_a_ref, cot_ref, resid_ref, hidden_ref,
        w_qkv_ref, w_out_ref, w_gate_ref, w_up_ref, d_hidden_ref, probs_ref, values_ref, sems,
        all_ref, queries_ref, keys_ref, grads_ref, d_gate_ref, d_up_ref, hat_ref,
    ) = refs[count:]
    batch, tok_rows = cot_ref.shape[0], cot_ref.shape[1]
    keys_all = values_ref.shape[1]
    rows = batch * tok_rows
    ahead = values_a_hbm.shape[0]
    lead = ahead * tok_rows
    moves = project_moves(refs[:count], w_qkv_hbm, w_qkv_ref, all_ref)
    projecting = len(moves)
    moves += [
        (bias_hbm, bias_ref), (w_out_hbm, w_out_ref), (att_a_hbm, att_a_ref),
        (tokens_a_hbm, tokens_ref.at[pl.ds(0, ahead)]),
        (tokens_b_hbm, tokens_ref.at[pl.ds(ahead, batch - ahead)]), (cot_hbm, cot_ref),
        (d_hidden_hbm, d_hidden_ref), (w_gate_hbm, w_gate_ref), (w_up_hbm, w_up_ref),
        (values_a_hbm, values_ref.at[pl.ds(0, ahead)]), (probs_a_hbm, probs_ref.at[pl.ds(0, ahead)]),
    ]
    copies = [pltpu.make_async_copy(src, dst, sems.at[i]) for i, (src, dst) in enumerate(moves)]
    for copy in copies[: projecting + 1]:
        copy.start()

    def start_rest():
        for copy in copies[projecting + 1 :]:
            copy.start()

    own_values = values_ref.at[pl.ds(ahead, batch - ahead)]
    own_probs = probs_ref.at[pl.ds(ahead, batch - ahead)]
    project(
        copies[:projecting], w_qkv_ref, all_ref, queries_ref, keys_ref, own_values, start_rest
    )
    copies = copies[projecting:]
    copies[0].wait()
    attend(bias_ref, queries_ref, keys_ref, own_values, own_probs, queries_ref)

    for copy in copies[1:5]:
        copy.wait()
    tokens = tokens_ref[...].reshape(rows, C_TOK)
    resid_ref[0:lead, :] = tokens[0:lead] + nn(att_a_ref[...], w_out_ref[...])
    resid_ref[lead:rows, :] = tokens[lead:rows] + nn(queries_ref[...], w_out_ref[...])
    back = [
        pltpu.make_async_copy(resid_ref, resid_hbm, sems.at[0]),
        pltpu.make_async_copy(hidden_ref, hidden_hbm, sems.at[1]),
    ]
    back[0].start()
    hat, rstd = norm_rows(resid_ref[...])
    hat_ref[...] = hat
    grads_ref[...] = hat.astype(bf16)
    for copy in copies[5:9]:
        copy.wait()

    for n in range(0, w_gate_ref.shape[1], 256):
        shaped = grads_ref[...]
        gate = nn(shaped, w_gate_ref[:, n : n + 256])
        up = nn(shaped, w_up_ref[:, n : n + 256])
        d_hidden = d_hidden_ref[:, n : n + 256]
        sig = 1.0 / (1.0 + jnp.exp(-gate))
        act = gate * sig
        hidden_ref[:, n : n + 256] = (act * up).astype(bf16)
        d_gate_ref[:, n : n + 256] = (
            d_hidden * up * sig * (1.0 + gate * (1.0 - sig))
        ).astype(bf16)
        d_up_ref[:, n : n + 256] = (d_hidden * act).astype(bf16)

    back[1].start()
    parts = []
    for n in range(0, C_TOK, 256):
        parts.append(
            nt(d_gate_ref[...], w_gate_ref[n : n + 256, :])
            + nt(d_up_ref[...], w_up_ref[n : n + 256, :])
        )
    d_normed = jnp.concatenate(parts, axis=1)
    hat = hat_ref[...]
    first = jnp.mean(d_normed, axis=-1, keepdims=True)
    second = jnp.mean(d_normed * hat, axis=-1, keepdims=True)
    d_resid = cot_ref[...].reshape(rows, C_TOK).astype(f32) + rstd * (
        d_normed - first - hat * second
    )
    grads_ref[...] = nt(d_resid.astype(bf16), w_out_ref[...]).astype(bf16)
    for copy in copies[9:]:
        copy.wait()
    masks = head_masks(tok_rows)
    for pair in range(PAIRS):
        low, high = windows(pair)
        total = jnp.zeros((keys_all, 2 * tok_rows), f32)
        for s in range(batch):
            grads = two_heads(
                grads_ref[s * tok_rows : (s + 1) * tok_rows, low:high], masks[pair % 4]
            )
            d_probs = nt(values_ref[s, :, low:high], grads)
            probs = probs_ref[s, pair]
            delta = jnp.sum(probs * d_probs, axis=0, keepdims=True)
            total = total + probs * (d_probs - delta)
        size = d_bias_ref.shape[2]
        for k in range(d_bias_ref.shape[0]):
            d_bias_ref[k, pair] = total[size * k : size * (k + 1)].astype(bf16)
    for copy in back:
        copy.wait()


def token_stage(
    pieces, bias, tokens_a, tokens_b, att_a, cot, probs_a, values_a, w_qkv, w_out, w_gate, w_up,
    d_hidden,
):
    batch, tok_rows, _ = cot.shape
    keys_all = tok_rows * len(pieces)
    rows = batch * tok_rows
    hidden = w_gate.shape[1]
    vmem = pl.BlockSpec(memory_space=pltpu.VMEM)
    hbm = pl.BlockSpec(memory_space=pl.ANY)
    return pl.pallas_call(
        functools.partial(token_kernel, count=len(pieces)),
        in_specs=[hbm] * (len(pieces) + 12),
        out_specs=[hbm, hbm, vmem],
        out_shape=[
            jax.ShapeDtypeStruct((rows, C_TOK), f32),
            jax.ShapeDtypeStruct((rows, hidden), bf16),
            jax.ShapeDtypeStruct(bias.shape, bf16),
        ],
        scratch_shapes=[
            pltpu.VMEM(bias.shape, bf16),
            pltpu.VMEM(cot.shape, f32),
            pltpu.VMEM(att_a.shape, bf16),
            pltpu.VMEM(cot.shape, bf16),
            pltpu.VMEM((rows, C_TOK), f32),
            pltpu.VMEM((rows, hidden), bf16),
            pltpu.VMEM((3, C_TOK, C_TOK), bf16),
            pltpu.VMEM(w_out.shape, bf16),
            pltpu.VMEM(w_gate.shape, bf16),
            pltpu.VMEM(w_up.shape, bf16),
            pltpu.VMEM(d_hidden.shape, f32),
            pltpu.VMEM((batch, PAIRS, keys_all, 2 * tok_rows), f32),
            pltpu.VMEM((batch, keys_all, C_TOK), bf16),
            pltpu.SemaphoreType.DMA((14 + len(pieces),)),
        ]
        + attend_scratch(pieces[0].shape[0], tok_rows, keys_all)
        + [
            pltpu.VMEM((rows, C_TOK), bf16),
            pltpu.VMEM((rows, hidden), bf16),
            pltpu.VMEM((rows, hidden), bf16),
            pltpu.VMEM((rows, C_TOK), f32),
        ],
        compiler_params=pltpu.CompilerParams(vmem_limit_bytes=GRANT),
        cost_estimate=pl.CostEstimate(
            flops=10**10, bytes_accessed=2 * 10**7, transcendentals=10**6
        ),
        name="tokens",
    )(
        *pieces, bias, tokens_a, tokens_b, att_a, cot, probs_a, values_a, w_qkv, w_out, w_gate,
        w_up, d_hidden,
    )


def output_kernel(
    resid_ref, hidden_ref, w_down_ref, pair_ref, out_ref, hat_ref, rstd_ref, pairf_ref
):
    out_ref[...] = (resid_ref[...] + nn(hidden_ref[...], w_down_ref[...])).astype(bf16)
    rows, keys = pair_ref.shape[0], pair_ref.shape[1]
    for i in range(rows // 8):
        pairf_ref[8 * keys * i : 8 * keys * (i + 1), :] = (
            pair_ref[8 * i : 8 * i + 8].astype(f32).reshape(8 * keys, CZ)
        )

    def norm_step(j, carry):
        hat, rstd = norm_rows(pairf_ref[pl.ds(j, rows, stride=keys), :])
        at = pl.multiple_of(j * rows, rows)
        hat_ref[pl.ds(at, rows), :] = hat
        rstd = jnp.broadcast_to(rstd, (rows, CZ)).T[0:1]
        rstd_ref[pl.ds(j, 1), :] = jnp.concatenate([rstd, rstd], axis=1)
        return carry

    lax.fori_loop(0, keys, norm_step, 0, unroll=4)


def output_stage(resid, hidden, w_down, pair):
    rows, keys = pair.shape[0], pair.shape[1]
    return pl.pallas_call(
        output_kernel,
        out_shape=[jax.ShapeDtypeStruct(resid.shape, bf16)]
        + [
            jax.ShapeDtypeStruct((rows * keys, CZ), f32),
            jax.ShapeDtypeStruct((keys, 2 * rows), f32),
        ],
        scratch_shapes=[pltpu.VMEM((rows * keys, CZ), f32)],
        compiler_params=pltpu.CompilerParams(vmem_limit_bytes=GRANT),
        cost_estimate=pl.CostEstimate(
            flops=10**9, bytes_accessed=8 * 10**6, transcendentals=0
        ),
        name="output",
    )(resid, hidden, w_down, pair)


def grad_kernel(
    parts_hbm, hat_hbm, rstd_hbm, gain_hbm, w_bias_hbm, out_hbm, parts_ref, hat_ref, rstd_ref,
    gain_ref, w_bias_ref, total_ref, out_ref, sems,
):
    keys = parts_ref.shape[2]
    rows = hat_ref.shape[0] // keys
    size = 8 * rows
    moves = [
        (gain_hbm, gain_ref), (w_bias_hbm, w_bias_ref), (parts_hbm, parts_ref),
        (rstd_hbm, rstd_ref),
    ]
    for c in range(keys // 8):
        moves.append((hat_hbm.at[pl.ds(size * c, size)], hat_ref.at[pl.ds(size * c, size)]))
    copies = start_all(moves, sems)
    for copy in copies[0:2]:
        copy.wait()
    weights = jnp.concatenate(split_heads(w_bias_ref[...]), axis=0) * gain_ref[...]
    weights = weights - jnp.mean(weights, axis=-1, keepdims=True)
    weights = jnp.concatenate([weights[0:PAIRS], weights[PAIRS:HEADS]], axis=1)
    w_high = weights.astype(bf16).astype(f32)
    w_middle = (weights - w_high).astype(bf16).astype(f32)
    w_low = weights - w_high - w_middle
    weights = jnp.concatenate([w_high, w_middle, w_low, w_high, w_middle, w_high], axis=0)
    weights = weights.astype(bf16)
    for copy in copies[2:4]:
        copy.wait()
    for pair in range(PAIRS):
        total = parts_ref[0, pair].astype(f32)
        for k in range(1, parts_ref.shape[0]):
            total = total + parts_ref[k, pair].astype(f32)
        total_ref[pair * keys : (pair + 1) * keys, :] = total * rstd_ref[...]
    back = []
    for c in range(keys // 8):
        copies[4 + c].wait()
        for j in range(8 * c, 8 * c + 8):
            total = total_ref[pl.ds(j, PAIRS, stride=keys), :]
            high = total.astype(bf16).astype(f32)
            middle = (total - high).astype(bf16).astype(f32)
            low = total - high - middle
            stack = jnp.concatenate([high, high, high, middle, middle, low], axis=0)
            both = nn(stack.T.astype(bf16), weights)
            scaled = both[0:rows, 0:CZ] + both[rows : 2 * rows, CZ : 2 * CZ]
            hat = hat_ref[rows * j : rows * (j + 1), :]
            second = jnp.mean(scaled * hat, axis=-1, keepdims=True)
            out_ref[pl.ds(size * c + j % 8, rows, stride=8), :] = scaled - hat * second
        back.append(
            pltpu.make_async_copy(
                out_ref.at[pl.ds(size * c, size)].reshape(rows, 8, CZ),
                out_hbm.at[:, pl.ds(8 * c, 8), :],
                sems.at[c],
            )
        )
        back[c].start()
    for copy in back:
        copy.wait()


def pair_back(parts, hat, rstd, pair_gain, w_bias_t):
    keys = parts.shape[2]
    rows = hat.shape[0] // keys
    hbm = pl.BlockSpec(memory_space=pl.ANY)
    return pl.pallas_call(
        grad_kernel,
        in_specs=[hbm] * 5,
        out_specs=hbm,
        out_shape=jax.ShapeDtypeStruct((rows, keys, CZ), f32),
        scratch_shapes=[
            pltpu.VMEM(parts.shape, bf16),
            pltpu.VMEM(hat.shape, f32),
            pltpu.VMEM(rstd.shape, f32),
            pltpu.VMEM((1, CZ), f32),
            pltpu.VMEM(w_bias_t.shape, bf16),
            pltpu.VMEM((keys * PAIRS, 2 * rows), f32),
            pltpu.VMEM((rows * keys, CZ), f32),
            pltpu.SemaphoreType.DMA((4 + keys // 8,)),
        ],
        compiler_params=pltpu.CompilerParams(vmem_limit_bytes=GRANT),
        cost_estimate=pl.CostEstimate(flops=10**8, bytes_accessed=4 * 10**6, transcendentals=0),
        name="pair_grad",
    )(parts, hat, rstd, pair_gain.reshape(1, CZ), w_bias_t)


def swap(values, axis, k):
    return lax.ppermute(values, axis, [(i, i ^ k) for i in range(lax.axis_size(axis))])


def gather(values, axis):
    far = range(lax.axis_size(axis) - 1, 0, -1)
    return [values] + [swap(values, axis, k) for k in far][::-1]


def body(
    atom_feats, atom_counts, atom_mask, token_single, pair, pair_gain, w_bias, w_atom_qkv,
    w_atom_out, w_embed, w_qkv, w_out, w_gate, w_up, w_down, cotangent,
):
    batch, atom_rows, _ = atom_feats.shape
    tok_rows = token_single.shape[0]
    shards = lax.axis_size("tok")
    groups = lax.axis_size("samp")

    w_bias_t = w_bias.T
    local_bias, edges = pair_bias(pair, pair_gain, w_bias_t, atom_feats, groups, shards)
    halos = lax.all_to_all(edges, "tok", 0, 0)
    bias = lax.all_to_all(local_bias, "samp", 0, 0).reshape(groups, PAIRS, -1, 2 * tok_rows)

    mask = atom_mask.reshape(-1, 128)
    mask, local_bias = lax.optimization_barrier((mask, local_bias))

    each = batch // 2
    tokens, gathered = [], []
    for part in range(2):
        tok, normed = atom_stage(
            part, each, atom_feats, halos, mask, atom_counts, token_single, w_atom_qkv,
            w_atom_out, w_embed,
        )
        tokens.append(tok)
        gathered.append(gather(normed, "tok"))
    att_a, probs_a, values_a, d_hidden = attend_stage(
        gathered[0], bias, w_qkv, cotangent, w_down
    )
    resid, hidden, d_bias = token_stage(
        gathered[1], bias, *tokens, att_a, cotangent, probs_a, values_a, w_qkv, w_out, w_gate,
        w_up, d_hidden,
    )
    parts = lax.all_to_all(d_bias, "samp", 0, 0)
    token_out, hat, rstd = output_stage(resid, hidden, w_down, pair)
    pair_grad = pair_back(parts, hat, rstd, pair_gain, w_bias_t)
    token_out = token_out.reshape(batch, tok_rows, C_TOK)
    return (token_out, pair_grad)


def solution(mesh):
    in_specs = (
        P("samp", "tok", None),
        P("tok", None),
        P(),
        P("tok", None),
        P("tok", "samp", None),
        P(), P(), P(), P(), P(), P(), P(), P(), P(), P(),
        P("samp", "tok", None),
    )
    out_specs = (P("samp", "tok", None), P("tok", "samp", None))
    return jax.shard_map(body, mesh=mesh, in_specs=in_specs, out_specs=out_specs, check_vma=False)
```

```python
import functools

import jax
import jax.numpy as jnp
from jax import lax
from jax.experimental import pallas as pl
from jax.experimental.pallas import tpu as pltpu
from jax.sharding import PartitionSpec as P

C_ATOM = 128
ATOM_HEADS = 4
C_TOK = 768
HEADS = 16
ATOM_HD = 32
HD = 48
CZ = 128
HALO = 48
PAIRS = HEADS // 2
GRANT = 64 << 20
LOG2E = 1.4426950408889634

epsilon = 1e-05
f32 = jnp.float32
bf16 = jnp.bfloat16

WINDOWS = ((0, 128), (0, 256), (128, 384), (256, 384))


def nn(a, b):
    return lax.dot_general(a, b, (((1,), (0,)), ((), ())), preferred_element_type=f32)


def nt(a, b):
    return lax.dot_general(a, b, (((1,), (1,)), ((), ())), preferred_element_type=f32)


def tn(a, b):
    return lax.dot_general(a, b, (((0,), (0,)), ((), ())), preferred_element_type=f32)


def start_all(moves, sems):
    copies = [pltpu.make_async_copy(src, dst, sems.at[i]) for i, (src, dst) in enumerate(moves)]
    for copy in copies:
        copy.start()
    return copies


def norm_rows(values):
    center = values - jnp.mean(values, axis=-1, keepdims=True)
    scale_inv = lax.rsqrt(jnp.mean(center * center, axis=-1, keepdims=True) + epsilon)
    return (center * scale_inv, scale_inv)


def iota(shape, dim):
    return lax.broadcasted_iota(jnp.int32, shape, dim)


def pick_heads(parity):
    row, col = iota((PAIRS, HEADS), 0), iota((PAIRS, HEADS), 1)
    return (col == 2 * row + parity).astype(f32).astype(bf16)


def split_heads(w_bias_t):
    return [nn(pick_heads(parity), w_bias_t) for parity in range(2)]


def bias_kernel(
    pair_hbm, gain_hbm, w_bias_hbm, feats_hbm, out_hbm, head_hbm, tail_hbm, pair_ref, gain_ref,
    w_bias_ref, scaled_ref, stage_ref, local_ref, head_ref, tail_ref, sems,
):
    rows, keys = pair_ref.shape[0], pair_ref.shape[1]
    atoms = feats_hbm.shape[1]
    part = rows // 4
    moves = [
        (gain_hbm, gain_ref), (w_bias_hbm, w_bias_ref),
        (feats_hbm.at[:, pl.ds(0, HALO), :], head_ref),
        (feats_hbm.at[:, pl.ds(atoms - HALO, HALO), :], tail_ref),
    ]
    for i in range(4):
        moves.append((pair_hbm.at[pl.ds(part * i, part)], pair_ref.at[pl.ds(part * i, part)]))
    copies = start_all(moves, sems)
    for copy in copies[0:2]:
        copy.wait()
    gain = gain_ref[...]
    weights = jnp.concatenate(split_heads(w_bias_ref[...]), axis=1).astype(bf16)
    for i in range(rows // 8):
        if 8 * i % part == 0:
            copies[4 + 8 * i // part].wait()
        block = pair_ref[8 * i : 8 * i + 8].astype(f32).reshape(8 * keys, CZ)
        scaled_ref[8 * keys * i : 8 * keys * (i + 1), :] = norm_rows(block)[0] * gain
    for copy in copies[2:4]:
        copy.wait()
    edges = start_all([(head_ref, head_hbm), (tail_ref, tail_hbm)], sems)
    blank = jnp.zeros((rows, CZ), bf16)
    for j in range(keys):
        block = scaled_ref[pl.ds(j, rows, stride=keys), :].astype(bf16)
        both = jnp.concatenate(
            [jnp.concatenate([block, blank], axis=1), jnp.concatenate([blank, block], axis=1)],
            axis=0,
        )
        stage_ref[pl.ds(j, PAIRS, stride=keys), :] = nt(weights, both)
    local_ref[...] = stage_ref[...].astype(bf16)
    back = [
        pltpu.make_async_copy(local_ref, out_hbm.at[k], sems.at[2 + k])
        for k in range(out_hbm.shape[0])
    ]
    for copy in back:
        copy.start()
    for copy in edges + back:
        copy.wait()


def pair_bias(pair, pair_gain, w_bias_t, feats, copies):
    rows, keys = pair.shape[0], pair.shape[1]
    edge = jax.ShapeDtypeStruct((feats.shape[0], HALO, C_ATOM), bf16)
    hbm = pl.BlockSpec(memory_space=pl.ANY)
    return pl.pallas_call(
        bias_kernel,
        in_specs=[hbm] * 4,
        out_specs=[hbm] * 3,
        out_shape=[
            jax.ShapeDtypeStruct((copies, keys * PAIRS, 2 * rows), bf16), edge, edge,
        ],
        scratch_shapes=[
            pltpu.VMEM(pair.shape, bf16),
            pltpu.VMEM((1, CZ), f32),
            pltpu.VMEM(w_bias_t.shape, bf16),
            pltpu.VMEM((rows * keys, CZ), f32),
            pltpu.VMEM((keys * PAIRS, 2 * rows), f32),
            pltpu.VMEM((keys * PAIRS, 2 * rows), bf16),
            pltpu.VMEM(edge.shape, bf16),
            pltpu.VMEM(edge.shape, bf16),
            pltpu.SemaphoreType.DMA((8 + copies,)),
        ],
        compiler_params=pltpu.CompilerParams(vmem_limit_bytes=GRANT),
        cost_estimate=pl.CostEstimate(flops=10**7, bytes_accessed=10**7, transcendentals=0),
        name="pair_bias",
    )(pair, pair_gain.reshape(1, CZ), w_bias_t, feats)


def atom_kernel(
    feats_hbm, left_hbm, right_hbm, mask_hbm, counts_hbm, single_hbm, w_qkv_hbm, w_out_hbm,
    w_embed_hbm, tokens_ref, normed_ref, mask_ref, counts_ref, single_ref, w_qkv_ref, w_out_ref,
    w_embed_ref, sems, padded_ref, normed_atoms_ref, qkv_a, qkv_b, scores_a, scores_b, probs_a, probs_b, mixed_ref,
    updated_ref, split_ref, keybias_ref, onehot_ref, *, first,
):
    batch, atoms = tokens_ref.shape[0], feats_hbm.shape[1]
    padded = atoms + 2 * HALO
    moves = [(counts_hbm, counts_ref), (mask_hbm, mask_ref), (w_qkv_hbm, w_qkv_ref)]
    for s in range(batch):
        moves.append((left_hbm.at[first + s], padded_ref.at[s, pl.ds(0, HALO)]))
        moves.append((feats_hbm.at[first + s], padded_ref.at[s, pl.ds(HALO, atoms)]))
        moves.append((right_hbm.at[first + s], padded_ref.at[s, pl.ds(HALO + atoms, HALO)]))
    moves += [(w_out_hbm, w_out_ref), (w_embed_hbm, w_embed_ref), (single_hbm, single_ref)]
    copies = start_all(moves, sems)
    for copy in copies[0:2]:
        copy.wait()
    tok_rows = single_ref.shape[0]
    blocks = atoms // 128
    chunks = atoms // 256
    qkv_refs = (qkv_a, qkv_b)

    eye = iota((128, 128), 0) == iota((128, 128), 1)
    for b in range(-1, blocks + 1):
        at = lax.axis_index("tok") * blocks + b
        inside = jnp.where((at >= 0) & (at < mask_ref.shape[0]), 1, 0)
        row = mask_ref[pl.ds(jnp.clip(at, 0, mask_ref.shape[0] - 1), 1), :] * inside
        row = jnp.broadcast_to(row.astype(f32), (128, 128))
        col = jnp.sum(jnp.where(eye, row, 0.0), axis=1, keepdims=True)
        col = jnp.broadcast_to((col - 1.0) * 1e30, (128, 128))
        if b < 0:
            keybias_ref[0:HALO, :] = col[128 - HALO : 128]
        elif b < blocks:
            keybias_ref[HALO + 128 * b : HALO + 128 * b + 128, :] = col
        else:
            keybias_ref[HALO + atoms : padded, :] = col[0:HALO]
    counts = jnp.broadcast_to(counts_ref[...].astype(f32), (tok_rows, tok_rows))
    sub, lane = iota((tok_rows, tok_rows), 0), iota((tok_rows, tok_rows), 1)
    start = jnp.sum(jnp.where(lane < sub, counts, 0.0), axis=1, keepdims=True)
    own = jnp.sum(jnp.where(lane == sub, counts, 0.0), axis=1, keepdims=True)
    pos = iota((tok_rows, 256), 1).astype(f32)
    for g in range(chunks):
        at = pos + float(g * 256)
        hit = jnp.where((at >= start) & (at < start + own), 1.0, 0.0).astype(bf16)
        onehot_ref[:, 256 * g : 256 * g + 256] = hit
        onehot_ref[:, atoms + 256 * g : atoms + 256 * g + 256] = hit
    probs_a[...] = jnp.zeros_like(probs_a)
    probs_b[...] = jnp.zeros_like(probs_b)
    head_of = iota((32, 128), 1) // ATOM_HD
    head_mask = [(head_of == h).astype(f32).astype(bf16) for h in range(ATOM_HEADS)]
    own_atom = (iota((32, 128), 1) % 32) == iota((32, 128), 0)
    factor = ATOM_HD ** (-0.5) * LOG2E
    def qkv_step(s):
        for low in range(0, padded, padded // 4):
            part = slice(low, low + padded // 4)
            normed, unused = norm_rows(padded_ref[s, part, :].astype(f32))
            normed_atoms_ref[part, :] = normed.astype(bf16)
        qkv_refs[s % 2][...] = nn(normed_atoms_ref[...], w_qkv_ref[...]).astype(bf16)

    def score_step(s, group, to_ref):
        qkv_ref = qkv_refs[s % 2]
        for k in range(2):
            base = pl.multiple_of(group * 128 + 64 * k, 64)
            queries = qkv_ref[pl.ds(base + HALO, 64), 0:C_ATOM]
            spread = jnp.concatenate(
                [
                    queries[32 * w : 32 * w + 32] * head_mask[h]
                    for w in range(2)
                    for h in range(ATOM_HEADS)
                ],
                axis=0,
            )
            to_ref[k] = nt(qkv_ref[pl.ds(base, 160), C_ATOM : 2 * C_ATOM], spread)

    def softmax_step(group, from_ref, to_ref):
        for k in range(2):
            base = pl.multiple_of(group * 128 + 64 * k, 64)
            for w in range(2):
                keybias = keybias_ref[pl.ds(base + 32 * w, 128), :]
                keybias = jnp.concatenate(
                    [keybias[0:48], jnp.where(own_atom, 0.0, keybias[48:80]), keybias[80:128]],
                    axis=0,
                )
                scores = from_ref[k, 32 * w : 32 * w + 128, 128 * w : 128 * w + 128] + keybias
                expo = jnp.exp2((scores - jnp.max(scores, axis=0, keepdims=True)) * factor)
                weights = expo * (1.0 / jnp.sum(expo, axis=0, keepdims=True))
                to_ref[k, 32 * w : 32 * w + 128, 128 * w : 128 * w + 128] = weights.astype(bf16)

    def value_step(s, group, from_ref):
        qkv_ref = qkv_refs[s % 2]
        for k in range(2):
            base = pl.multiple_of(group * 128 + 64 * k, 64)
            part = tn(from_ref[k], qkv_ref[pl.ds(base, 160), 2 * C_ATOM : 3 * C_ATOM])
            mixes = []
            for w in range(2):
                mix = part[128 * w : 128 * w + 32]
                for h in range(1, ATOM_HEADS):
                    low = 128 * w + 32 * h
                    mix = jnp.where(head_of == h, part[low : low + 32], mix)
                mixes.append(mix.astype(bf16))
            mixed_ref[pl.ds(base, 64), :] = jnp.concatenate(mixes, axis=0)

    def embed_step(s):
        feats = padded_ref[s, HALO : HALO + atoms, :].astype(f32)
        updated_ref[...] = (feats + nn(mixed_ref[...], w_out_ref[...])).astype(bf16)
        for n in range(0, C_TOK, 256):
            embedded = jnp.maximum(nn(updated_ref[...], w_embed_ref[:, n : n + 256]), 0.0)
            high = embedded.astype(bf16)
            split_ref[0:atoms, n : n + 256] = high
            split_ref[atoms : 2 * atoms, n : n + 256] = (embedded - high.astype(f32)).astype(bf16)
        pooled = nn(onehot_ref[...], split_ref[...])
        tokens = pooled / own + single_ref[...].astype(f32)
        tokens_ref[s] = tokens
        normed_ref[s] = norm_rows(tokens)[0].astype(bf16)

    for copy in copies[2:6]:
        copy.wait()
    qkv_step(0)
    for copy in copies[6:]:
        copy.wait()
    for s in range(batch):
        score_step(s, 0, scores_a)

        def window_step(i, carry, s=s):
            even, odd = 2 * i, 2 * i + 1
            score_step(s, odd, scores_b)
            softmax_step(even, scores_a, probs_a)
            value_step(s, jnp.maximum(even - 1, 0), probs_b)
            score_step(s, jnp.minimum(odd + 1, 2 * chunks - 1), scores_a)
            softmax_step(odd, scores_b, probs_b)
            value_step(s, even, probs_a)
            return carry

        lax.fori_loop(0, chunks, window_step, 0)
        value_step(s, 2 * chunks - 1, probs_b)
        embed_step(s)
        if s + 1 < batch:
            qkv_step(s + 1)


def atom_stage(part, batch, feats, left, right, mask, counts, single, w_qkv, w_out, w_embed):
    atoms = feats.shape[1]
    tok_rows = single.shape[0]
    padded = atoms + 2 * HALO
    return pl.pallas_call(
        functools.partial(atom_kernel, first=part * batch),
        in_specs=[pl.BlockSpec(memory_space=pl.ANY)] * 9,
        out_specs=[pl.BlockSpec(memory_space=pltpu.VMEM)] * 2,
        out_shape=[
            jax.ShapeDtypeStruct((batch, tok_rows, C_TOK), f32),
            jax.ShapeDtypeStruct((batch, tok_rows, C_TOK), bf16),
        ],
        scratch_shapes=[
            pltpu.VMEM(mask.shape, jnp.int32),
            pltpu.VMEM(counts.shape, jnp.int32),
            pltpu.VMEM(single.shape, bf16),
            pltpu.VMEM(w_qkv.shape, bf16),
            pltpu.VMEM(w_out.shape, bf16),
            pltpu.VMEM(w_embed.shape, bf16),
            pltpu.SemaphoreType.DMA((6 + 3 * batch,)),
            pltpu.VMEM((batch, padded, C_ATOM), bf16),
            pltpu.VMEM((padded, C_ATOM), bf16),
            pltpu.VMEM((padded, 3 * C_ATOM), bf16),
            pltpu.VMEM((padded, 3 * C_ATOM), bf16),
            pltpu.VMEM((2, 160, 256), f32),
            pltpu.VMEM((2, 160, 256), f32),
            pltpu.VMEM((2, 160, 256), bf16),
            pltpu.VMEM((2, 160, 256), bf16),
            pltpu.VMEM((atoms, C_ATOM), bf16),
            pltpu.VMEM((atoms, C_ATOM), bf16),
            pltpu.VMEM((2 * atoms, C_TOK), bf16),
            pltpu.VMEM((padded, 128), f32),
            pltpu.VMEM((tok_rows, 2 * atoms), bf16),
        ],
        compiler_params=pltpu.CompilerParams(vmem_limit_bytes=GRANT),
        cost_estimate=pl.CostEstimate(
            flops=10**10, bytes_accessed=4 * 10**6, transcendentals=3 * 10**6
        ),
        name="atoms",
    )(feats, left, right, mask, counts, single, w_qkv, w_out, w_embed)


def head_masks(rows):
    masks = []
    for pair in range(4):
        low, high = WINDOWS[pair]
        lane = iota((rows, high - low), 1) + low
        first = 2 * pair * HD
        masks.append(
            [(lane >= first + HD * k) & (lane < first + HD * (k + 1)) for k in range(2)]
        )
    return masks


def two_heads(block, masks):
    blank = jnp.zeros_like(block)
    return jnp.concatenate([jnp.where(mask, block, blank) for mask in masks], axis=0)


def project_moves(piece_hbms, w_qkv_hbm, w_kv_ref, all_ref):
    tok_rows = piece_hbms[0].shape[1]
    here = lax.axis_index("tok")
    moves = []
    for k, piece in enumerate(piece_hbms):
        at = pl.multiple_of((here ^ k) * tok_rows, tok_rows)
        moves.append((piece, all_ref.at[:, pl.ds(at, tok_rows), :]))
    for i in range(2):
        moves.append((w_qkv_hbm.at[:, pl.ds(C_TOK * (i + 1), C_TOK)], w_kv_ref.at[i]))
    return moves


def project(copies, w_kv_ref, all_ref, keys_ref, values_ref):
    batch = all_ref.shape[0]
    for copy in copies[:-1]:
        copy.wait()
    for which, to_ref in enumerate((keys_ref, values_ref)):
        if which == 1:
            copies[-1].wait()
        for n in range(0, C_TOK, 256):
            for s in range(batch):
                to_ref[s, :, n : n + 256] = nn(
                    all_ref[s], w_kv_ref[which, :, n : n + 256]
                ).astype(bf16)


def windows(pair):
    low, high = WINDOWS[pair % 4]
    return 384 * (pair // 4) + low, 384 * (pair // 4) + high


def attend(bias_ref, queries_ref, keys_ref, values_ref, probs_ref, att_ref, done=None):
    batch, keys_all = keys_ref.shape[0], keys_ref.shape[1]
    tok_rows = queries_ref.shape[0] // batch
    masks = head_masks(tok_rows)
    factor = HD ** (-0.5)

    for s in range(batch):
        at = s * tok_rows
        for pair in range(PAIRS):
            low, high = windows(pair)
            queries = two_heads(queries_ref[pl.ds(at, tok_rows), low:high], masks[pair % 4])
            probs_ref[s, pair] = nt(keys_ref[s, :, low:high], queries)
        for pair in range(PAIRS):
            scores = probs_ref[s, pair] * factor
            bias = [bias_ref[k, pair].astype(f32) for k in range(bias_ref.shape[0])]
            scores = scores + jnp.concatenate(bias, axis=0)
            expo = jnp.exp(scores - jnp.max(scores, axis=0, keepdims=True))
            probs_ref[s, pair] = expo * (1.0 / jnp.sum(expo, axis=0, keepdims=True))
        lanes = [jnp.zeros((tok_rows, 128), f32) for _ in range(C_TOK // 128)]
        for pair in range(PAIRS):
            low, high = windows(pair)
            part = tn(probs_ref[s, pair].astype(bf16), values_ref[s, :, low:high])
            first, second = masks[pair % 4]
            mix = jnp.where(first, part[0:tok_rows], 0.0)
            mix = jnp.where(second, part[tok_rows : 2 * tok_rows], mix)
            for t in range((high - low) // 128):
                lanes[low // 128 + t] = lanes[low // 128 + t] + mix[:, 128 * t : 128 * t + 128]
        for t in range(C_TOK // 128):
            att_ref[pl.ds(at, tok_rows), 128 * t : 128 * t + 128] = lanes[t].astype(bf16)
        if done is not None:
            done(s)


def attend_kernel(*refs, count):
    (
        later_hbm, bias_hbm, w_qkv_hbm, cot_hbm, w_down_hbm, att_ref, probs_hbm, values_hbm,
        d_hidden_hbm, later_queries_ref, w_q_ref, w_kv_ref, own_ref, bias_ref, cot_ref, w_down_ref,
        probs_ref, values_ref, d_hidden_ref, sems, all_ref, queries_ref, keys_ref,
    ) = refs[count:]
    batch, tok_rows = all_ref.shape[0], refs[0].shape[1]
    moves = [
        (refs[0], own_ref.at[pl.ds(0, batch)]),
        (later_hbm, own_ref.at[pl.ds(batch, own_ref.shape[0] - batch)]),
        (w_qkv_hbm.at[:, pl.ds(0, C_TOK)], w_q_ref),
    ]
    moves += project_moves(refs[:count], w_qkv_hbm, w_kv_ref, all_ref)
    moves += [(bias_hbm, bias_ref), (cot_hbm, cot_ref), (w_down_hbm, w_down_ref)]
    copies = start_all(moves, sems)
    for copy in copies[0:3]:
        copy.wait()
    own = own_ref[...].reshape(-1, C_TOK)
    split = batch * tok_rows
    for n in range(0, C_TOK, 256):
        queries = nn(own, w_q_ref[:, n : n + 256]).astype(bf16)
        queries_ref[:, n : n + 256] = queries[0:split]
        later_queries_ref[:, n : n + 256] = queries[split:]
    project(copies[3:-3], w_kv_ref, all_ref, keys_ref, values_ref)
    for copy in copies[-3:]:
        copy.wait()
    back = [
        pltpu.make_async_copy(probs_ref.at[s], probs_hbm.at[s], sems.at[s]) for s in range(batch)
    ] + [
        pltpu.make_async_copy(values_ref, values_hbm, sems.at[batch]),
        pltpu.make_async_copy(d_hidden_ref, d_hidden_hbm, sems.at[batch + 1]),
    ]
    back[batch].start()
    cot = cot_ref[...].reshape(-1, C_TOK)
    for n in range(0, w_down_ref.shape[0], 256):
        d_hidden_ref[:, n : n + 256] = nt(cot, w_down_ref[n : n + 256, :])
    back[batch + 1].start()
    attend(
        bias_ref, queries_ref, keys_ref, values_ref, probs_ref, att_ref, lambda s: back[s].start()
    )
    for copy in back:
        copy.wait()


def attend_scratch(batch, tok_rows, keys_all):
    return [
        pltpu.VMEM((batch, keys_all, C_TOK), bf16),
        pltpu.VMEM((batch * tok_rows, C_TOK), bf16),
        pltpu.VMEM((batch, keys_all, C_TOK), bf16),
    ]


def attend_stage(pieces, later, bias, w_qkv, cot, w_down):
    batch, tok_rows, _ = pieces[0].shape
    keys_all = tok_rows * len(pieces)
    vmem = pl.BlockSpec(memory_space=pltpu.VMEM)
    hbm = pl.BlockSpec(memory_space=pl.ANY)
    d_hidden = jax.ShapeDtypeStruct((cot.shape[0] * tok_rows, w_down.shape[0]), f32)
    return pl.pallas_call(
        functools.partial(attend_kernel, count=len(pieces)),
        in_specs=[hbm] * (len(pieces) + 5),
        out_specs=[vmem, hbm, hbm, hbm, vmem],
        out_shape=[
            jax.ShapeDtypeStruct((batch * tok_rows, C_TOK), bf16),
            jax.ShapeDtypeStruct((batch, PAIRS, keys_all, 2 * tok_rows), f32),
            jax.ShapeDtypeStruct((batch, keys_all, C_TOK), bf16),
            d_hidden,
            jax.ShapeDtypeStruct((later.shape[0] * tok_rows, C_TOK), bf16),
        ],
        scratch_shapes=[
            pltpu.VMEM((C_TOK, C_TOK), bf16),
            pltpu.VMEM((2, C_TOK, C_TOK), bf16),
            pltpu.VMEM(cot.shape, bf16),
            pltpu.VMEM(bias.shape, bf16),
            pltpu.VMEM(cot.shape, bf16),
            pltpu.VMEM(w_down.shape, bf16),
            pltpu.VMEM((batch, PAIRS, keys_all, 2 * tok_rows), f32),
            pltpu.VMEM((batch, keys_all, C_TOK), bf16),
            pltpu.VMEM(d_hidden.shape, f32),
            pltpu.SemaphoreType.DMA((8 + len(pieces),)),
        ]
        + attend_scratch(batch, tok_rows, keys_all),
        compiler_params=pltpu.CompilerParams(vmem_limit_bytes=GRANT),
        cost_estimate=pl.CostEstimate(
            flops=4 * 10**9, bytes_accessed=10**7, transcendentals=10**6
        ),
        name="attend",
    )(*pieces, later, bias, w_qkv, cot, w_down)


def token_kernel(*refs, count):
    (
        queries_hbm, bias_hbm, tokens_a_hbm, tokens_b_hbm, att_a_hbm, cot_hbm, probs_a_hbm, values_a_hbm,
        w_qkv_hbm, w_out_hbm, w_gate_hbm, w_up_hbm, d_hidden_hbm,
        resid_hbm, hidden_hbm, d_bias_ref,
        bias_ref, tokens_ref, att_a_ref, cot_ref, resid_ref, hidden_ref,
        w_kv_ref, w_out_ref, w_gate_ref, w_up_ref, d_hidden_ref, probs_ref, values_ref, sems,
        all_ref, queries_ref, keys_ref, grads_ref, d_gate_ref, d_up_ref, hat_ref,
    ) = refs[count:]
    batch, tok_rows = cot_ref.shape[0], cot_ref.shape[1]
    keys_all = values_ref.shape[1]
    rows = batch * tok_rows
    ahead = values_a_hbm.shape[0]
    lead = ahead * tok_rows
    moves = project_moves(refs[:count], w_qkv_hbm, w_kv_ref, all_ref)
    projecting = len(moves)
    moves += [
        (queries_hbm, queries_ref), (bias_hbm, bias_ref), (w_out_hbm, w_out_ref), (att_a_hbm, att_a_ref),
        (tokens_a_hbm, tokens_ref.at[pl.ds(0, ahead)]),
        (tokens_b_hbm, tokens_ref.at[pl.ds(ahead, batch - ahead)]), (cot_hbm, cot_ref),
        (d_hidden_hbm, d_hidden_ref), (w_gate_hbm, w_gate_ref), (w_up_hbm, w_up_ref),
        (values_a_hbm, values_ref.at[pl.ds(0, ahead)]), (probs_a_hbm, probs_ref.at[pl.ds(0, ahead)]),
    ]
    copies = start_all(moves, sems)
    own_values = values_ref.at[pl.ds(ahead, batch - ahead)]
    own_probs = probs_ref.at[pl.ds(ahead, batch - ahead)]
    project(copies[:projecting], w_kv_ref, all_ref, keys_ref, own_values)
    copies[projecting].wait()
    copies = copies[projecting + 1 :]
    copies[0].wait()
    attend(bias_ref, queries_ref, keys_ref, own_values, own_probs, queries_ref)

    for copy in copies[1:5]:
        copy.wait()
    tokens = tokens_ref[...].reshape(rows, C_TOK)
    resid_ref[0:lead, :] = tokens[0:lead] + nn(att_a_ref[...], w_out_ref[...])
    resid_ref[lead:rows, :] = tokens[lead:rows] + nn(queries_ref[...], w_out_ref[...])
    back = [
        pltpu.make_async_copy(resid_ref, resid_hbm, sems.at[0]),
        pltpu.make_async_copy(hidden_ref, hidden_hbm, sems.at[1]),
    ]
    back[0].start()
    hat, rstd = norm_rows(resid_ref[...])
    hat_ref[...] = hat
    grads_ref[...] = hat.astype(bf16)
    for copy in copies[5:9]:
        copy.wait()

    for n in range(0, w_gate_ref.shape[1], 256):
        shaped = grads_ref[...]
        gate = nn(shaped, w_gate_ref[:, n : n + 256])
        up = nn(shaped, w_up_ref[:, n : n + 256])
        d_hidden = d_hidden_ref[:, n : n + 256]
        sig = 1.0 / (1.0 + jnp.exp(-gate))
        act = gate * sig
        hidden_ref[:, n : n + 256] = (act * up).astype(bf16)
        d_gate_ref[:, n : n + 256] = (
            d_hidden * up * sig * (1.0 + gate * (1.0 - sig))
        ).astype(bf16)
        d_up_ref[:, n : n + 256] = (d_hidden * act).astype(bf16)

    back[1].start()
    parts = []
    for n in range(0, C_TOK, 256):
        parts.append(
            nt(d_gate_ref[...], w_gate_ref[n : n + 256, :])
            + nt(d_up_ref[...], w_up_ref[n : n + 256, :])
        )
    d_normed = jnp.concatenate(parts, axis=1)
    hat = hat_ref[...]
    first = jnp.mean(d_normed, axis=-1, keepdims=True)
    second = jnp.mean(d_normed * hat, axis=-1, keepdims=True)
    d_resid = cot_ref[...].reshape(rows, C_TOK).astype(f32) + rstd * (
        d_normed - first - hat * second
    )
    grads_ref[...] = nt(d_resid.astype(bf16), w_out_ref[...]).astype(bf16)
    for copy in copies[9:]:
        copy.wait()
    masks = head_masks(tok_rows)
    for pair in range(PAIRS):
        low, high = windows(pair)
        total = jnp.zeros((keys_all, 2 * tok_rows), f32)
        for s in range(batch):
            grads = two_heads(
                grads_ref[s * tok_rows : (s + 1) * tok_rows, low:high], masks[pair % 4]
            )
            d_probs = nt(values_ref[s, :, low:high], grads)
            probs = probs_ref[s, pair]
            delta = jnp.sum(probs * d_probs, axis=0, keepdims=True)
            total = total + probs * (d_probs - delta)
        size = d_bias_ref.shape[2]
        for k in range(d_bias_ref.shape[0]):
            d_bias_ref[k, pair] = total[size * k : size * (k + 1)].astype(bf16)
    for copy in back:
        copy.wait()


def token_stage(
    pieces, queries, bias, tokens_a, tokens_b, att_a, cot, probs_a, values_a, w_qkv, w_out, w_gate, w_up,
    d_hidden,
):
    batch, tok_rows, _ = cot.shape
    keys_all = tok_rows * len(pieces)
    rows = batch * tok_rows
    hidden = w_gate.shape[1]
    vmem = pl.BlockSpec(memory_space=pltpu.VMEM)
    hbm = pl.BlockSpec(memory_space=pl.ANY)
    return pl.pallas_call(
        functools.partial(token_kernel, count=len(pieces)),
        in_specs=[hbm] * (len(pieces) + 13),
        out_specs=[hbm, hbm, vmem],
        out_shape=[
            jax.ShapeDtypeStruct((rows, C_TOK), f32),
            jax.ShapeDtypeStruct((rows, hidden), bf16),
            jax.ShapeDtypeStruct(bias.shape, bf16),
        ],
        scratch_shapes=[
            pltpu.VMEM(bias.shape, bf16),
            pltpu.VMEM(cot.shape, f32),
            pltpu.VMEM(att_a.shape, bf16),
            pltpu.VMEM(cot.shape, bf16),
            pltpu.VMEM((rows, C_TOK), f32),
            pltpu.VMEM((rows, hidden), bf16),
            pltpu.VMEM((2, C_TOK, C_TOK), bf16),
            pltpu.VMEM(w_out.shape, bf16),
            pltpu.VMEM(w_gate.shape, bf16),
            pltpu.VMEM(w_up.shape, bf16),
            pltpu.VMEM(d_hidden.shape, f32),
            pltpu.VMEM((batch, PAIRS, keys_all, 2 * tok_rows), f32),
            pltpu.VMEM((batch, keys_all, C_TOK), bf16),
            pltpu.SemaphoreType.DMA((16 + len(pieces),)),
        ]
        + attend_scratch(pieces[0].shape[0], tok_rows, keys_all)
        + [
            pltpu.VMEM((rows, C_TOK), bf16),
            pltpu.VMEM((rows, hidden), bf16),
            pltpu.VMEM((rows, hidden), bf16),
            pltpu.VMEM((rows, C_TOK), f32),
        ],
        compiler_params=pltpu.CompilerParams(vmem_limit_bytes=GRANT),
        cost_estimate=pl.CostEstimate(
            flops=10**10, bytes_accessed=2 * 10**7, transcendentals=10**6
        ),
        name="tokens",
    )(
        *pieces, queries, bias, tokens_a, tokens_b, att_a, cot, probs_a, values_a, w_qkv, w_out, w_gate,
        w_up, d_hidden,
    )


def output_kernel(
    resid_ref, hidden_ref, w_down_ref, pair_ref, out_ref, hat_ref, rstd_ref, pairf_ref
):
    out_ref[...] = (resid_ref[...] + nn(hidden_ref[...], w_down_ref[...])).astype(bf16)
    rows, keys = pair_ref.shape[0], pair_ref.shape[1]
    for i in range(rows // 8):
        pairf_ref[8 * keys * i : 8 * keys * (i + 1), :] = (
            pair_ref[8 * i : 8 * i + 8].astype(f32).reshape(8 * keys, CZ)
        )

    def norm_step(j, carry):
        hat, rstd = norm_rows(pairf_ref[pl.ds(j, rows, stride=keys), :])
        at = pl.multiple_of(j * rows, rows)
        hat_ref[pl.ds(at, rows), :] = hat
        rstd = jnp.broadcast_to(rstd, (rows, CZ)).T[0:1]
        rstd_ref[pl.ds(j, 1), :] = jnp.concatenate([rstd, rstd], axis=1)
        return carry

    lax.fori_loop(0, keys, norm_step, 0, unroll=4)


def output_stage(resid, hidden, w_down, pair):
    rows, keys = pair.shape[0], pair.shape[1]
    return pl.pallas_call(
        output_kernel,
        out_shape=[jax.ShapeDtypeStruct(resid.shape, bf16)]
        + [
            jax.ShapeDtypeStruct((rows * keys, CZ), f32),
            jax.ShapeDtypeStruct((keys, 2 * rows), f32),
        ],
        scratch_shapes=[pltpu.VMEM((rows * keys, CZ), f32)],
        compiler_params=pltpu.CompilerParams(vmem_limit_bytes=GRANT),
        cost_estimate=pl.CostEstimate(
            flops=10**9, bytes_accessed=8 * 10**6, transcendentals=0
        ),
        name="output",
    )(resid, hidden, w_down, pair)


def grad_kernel(
    parts_hbm, hat_hbm, rstd_hbm, gain_hbm, w_bias_hbm, out_hbm, parts_ref, hat_ref, rstd_ref,
    gain_ref, w_bias_ref, total_ref, out_ref, sems,
):
    keys = parts_ref.shape[2]
    rows = hat_ref.shape[0] // keys
    size = 8 * rows
    moves = [
        (gain_hbm, gain_ref), (w_bias_hbm, w_bias_ref), (parts_hbm, parts_ref),
        (rstd_hbm, rstd_ref),
    ]
    for c in range(keys // 8):
        moves.append((hat_hbm.at[pl.ds(size * c, size)], hat_ref.at[pl.ds(size * c, size)]))
    copies = start_all(moves, sems)
    for copy in copies[0:2]:
        copy.wait()
    weights = jnp.concatenate(split_heads(w_bias_ref[...]), axis=0) * gain_ref[...]
    weights = weights - jnp.mean(weights, axis=-1, keepdims=True)
    weights = jnp.concatenate([weights[0:PAIRS], weights[PAIRS:HEADS]], axis=1)
    w_high = weights.astype(bf16).astype(f32)
    w_middle = (weights - w_high).astype(bf16).astype(f32)
    w_low = weights - w_high - w_middle
    weights = jnp.concatenate([w_high, w_middle, w_low, w_high, w_middle, w_high], axis=0)
    weights = weights.astype(bf16)
    for copy in copies[2:4]:
        copy.wait()
    for pair in range(PAIRS):
        total = parts_ref[0, pair].astype(f32)
        for k in range(1, parts_ref.shape[0]):
            total = total + parts_ref[k, pair].astype(f32)
        total_ref[pair * keys : (pair + 1) * keys, :] = total * rstd_ref[...]
    back = []
    for c in range(keys // 8):
        copies[4 + c].wait()
        for j in range(8 * c, 8 * c + 8):
            total = total_ref[pl.ds(j, PAIRS, stride=keys), :]
            high = total.astype(bf16).astype(f32)
            middle = (total - high).astype(bf16).astype(f32)
            low = total - high - middle
            stack = jnp.concatenate([high, high, high, middle, middle, low], axis=0)
            both = nn(stack.T.astype(bf16), weights)
            scaled = both[0:rows, 0:CZ] + both[rows : 2 * rows, CZ : 2 * CZ]
            hat = hat_ref[rows * j : rows * (j + 1), :]
            second = jnp.mean(scaled * hat, axis=-1, keepdims=True)
            out_ref[pl.ds(size * c + j % 8, rows, stride=8), :] = scaled - hat * second
        back.append(
            pltpu.make_async_copy(
                out_ref.at[pl.ds(size * c, size)].reshape(rows, 8, CZ),
                out_hbm.at[:, pl.ds(8 * c, 8), :],
                sems.at[c],
            )
        )
        back[c].start()
    for copy in back:
        copy.wait()


def pair_back(parts, hat, rstd, pair_gain, w_bias_t):
    keys = parts.shape[2]
    rows = hat.shape[0] // keys
    hbm = pl.BlockSpec(memory_space=pl.ANY)
    return pl.pallas_call(
        grad_kernel,
        in_specs=[hbm] * 5,
        out_specs=hbm,
        out_shape=jax.ShapeDtypeStruct((rows, keys, CZ), f32),
        scratch_shapes=[
            pltpu.VMEM(parts.shape, bf16),
            pltpu.VMEM(hat.shape, f32),
            pltpu.VMEM(rstd.shape, f32),
            pltpu.VMEM((1, CZ), f32),
            pltpu.VMEM(w_bias_t.shape, bf16),
            pltpu.VMEM((keys * PAIRS, 2 * rows), f32),
            pltpu.VMEM((rows * keys, CZ), f32),
            pltpu.SemaphoreType.DMA((4 + keys // 8,)),
        ],
        compiler_params=pltpu.CompilerParams(vmem_limit_bytes=GRANT),
        cost_estimate=pl.CostEstimate(flops=10**8, bytes_accessed=4 * 10**6, transcendentals=0),
        name="pair_grad",
    )(parts, hat, rstd, pair_gain.reshape(1, CZ), w_bias_t)


def swap(values, axis, k):
    return lax.ppermute(values, axis, [(i, i ^ k) for i in range(lax.axis_size(axis))])


def gather(values, axis):
    far = range(lax.axis_size(axis) - 1, 0, -1)
    return [values] + [swap(values, axis, k) for k in far][::-1]


def body(
    atom_feats, atom_counts, atom_mask, token_single, pair, pair_gain, w_bias, w_atom_qkv,
    w_atom_out, w_embed, w_qkv, w_out, w_gate, w_up, w_down, cotangent,
):
    batch, atom_rows, _ = atom_feats.shape
    tok_rows = token_single.shape[0]
    shards = lax.axis_size("tok")
    groups = lax.axis_size("samp")

    w_bias_t = w_bias.T
    local_bias, head, tail = pair_bias(pair, pair_gain, w_bias_t, atom_feats, groups)
    steps = [(i, i + 1) for i in range(shards - 1)]
    left = lax.ppermute(tail, "tok", steps)
    right = lax.ppermute(head, "tok", [(j, i) for i, j in steps])

    bias = lax.all_to_all(local_bias, "samp", 0, 0).reshape(groups, PAIRS, -1, 2 * tok_rows)

    mask = atom_mask.reshape(-1, 128)
    mask, local_bias = lax.optimization_barrier((mask, local_bias))

    each = batch // 2
    tokens, gathered = [], []
    for part in range(2):
        tok, normed = atom_stage(
            part, each, atom_feats, left, right, mask, atom_counts, token_single, w_atom_qkv,
            w_atom_out, w_embed,
        )
        tokens.append(tok)
        gathered.append(gather(normed, "tok"))
    att_a, probs_a, values_a, d_hidden, queries_b = attend_stage(
        gathered[0], gathered[1][0], bias, w_qkv, cotangent, w_down
    )
    resid, hidden, d_bias = token_stage(
        gathered[1], queries_b, bias, *tokens, att_a, cotangent, probs_a, values_a, w_qkv, w_out, w_gate,
        w_up, d_hidden,
    )
    parts = lax.all_to_all(d_bias, "samp", 0, 0)
    token_out, hat, rstd = output_stage(resid, hidden, w_down, pair)
    pair_grad = pair_back(parts, hat, rstd, pair_gain, w_bias_t)
    token_out = token_out.reshape(batch, tok_rows, C_TOK)
    return (token_out, pair_grad)


def solution(mesh):
    in_specs = (
        P("samp", "tok", None),
        P("tok", None),
        P(),
        P("tok", None),
        P("tok", "samp", None),
        P(), P(), P(), P(), P(), P(), P(), P(), P(), P(),
        P("samp", "tok", None),
    )
    out_specs = (P("samp", "tok", None), P("tok", "samp", None))
    return jax.shard_map(body, mesh=mesh, in_specs=in_specs, out_specs=out_specs, check_vma=False)
```

```python
import functools

import jax
import jax.numpy as jnp
from jax import lax
from jax.experimental import pallas as pl
from jax.experimental.pallas import tpu as pltpu
from jax.sharding import PartitionSpec as P

C_ATOM = 128
ATOM_HEADS = 4
C_TOK = 768
HEADS = 16
ATOM_HD = 32
HD = 48
CZ = 128
HALO = 48
PAIRS = HEADS // 2
GRANT = 64 << 20
LOG2E = 1.4426950408889634

epsilon = 1e-05
f32 = jnp.float32
bf16 = jnp.bfloat16

WINDOWS = ((0, 128), (0, 256), (128, 384), (256, 384))


def nn(a, b):
    return lax.dot_general(a, b, (((1,), (0,)), ((), ())), preferred_element_type=f32)


def nt(a, b):
    return lax.dot_general(a, b, (((1,), (1,)), ((), ())), preferred_element_type=f32)


def tn(a, b):
    return lax.dot_general(a, b, (((0,), (0,)), ((), ())), preferred_element_type=f32)


def start_all(moves, sems):
    copies = [pltpu.make_async_copy(src, dst, sems.at[i]) for i, (src, dst) in enumerate(moves)]
    for copy in copies:
        copy.start()
    return copies


def norm_rows(values):
    center = values - jnp.mean(values, axis=-1, keepdims=True)
    scale_inv = lax.rsqrt(jnp.mean(center * center, axis=-1, keepdims=True) + epsilon)
    return (center * scale_inv, scale_inv)


def iota(shape, dim):
    return lax.broadcasted_iota(jnp.int32, shape, dim)


def pick_heads(parity):
    row, col = iota((PAIRS, HEADS), 0), iota((PAIRS, HEADS), 1)
    return (col == 2 * row + parity).astype(f32).astype(bf16)


def split_heads(w_bias_t):
    return [nn(pick_heads(parity), w_bias_t) for parity in range(2)]


def bias_kernel(
    pair_hbm, gain_hbm, w_bias_hbm, feats_hbm, out_hbm, near_hbm, next_hbm, pair_ref, gain_ref,
    w_bias_ref, scaled_ref, stage_ref, local_ref, head_ref, tail_ref, sems,
):
    rows, keys = pair_ref.shape[0], pair_ref.shape[1]
    atoms = feats_hbm.shape[1]
    part = rows // 4
    stride = scaled_ref.shape[0] // rows
    moves = [
        (gain_hbm, gain_ref), (w_bias_hbm, w_bias_ref),
        (feats_hbm.at[:, pl.ds(0, HALO), :], head_ref),
        (feats_hbm.at[:, pl.ds(atoms - HALO, HALO), :], tail_ref),
    ]
    for i in range(4):
        moves.append((pair_hbm.at[pl.ds(part * i, part)], pair_ref.at[pl.ds(part * i, part)]))
    copies = start_all(moves, sems)
    for copy in copies[0:2]:
        copy.wait()
    gain = gain_ref[...]
    weights = jnp.concatenate(split_heads(w_bias_ref[...]), axis=1).astype(bf16)
    for i in range(rows // 8):
        if 8 * i % part == 0:
            copies[4 + 8 * i // part].wait()
        block = pair_ref[8 * i : 8 * i + 8].astype(f32).reshape(8 * keys, CZ)
        scaled = norm_rows(block)[0] * gain
        for k in range(8):
            at = (8 * i + k) * stride
            scaled_ref[at : at + keys, :] = scaled[keys * k : keys * (k + 1)]
    for copy in copies[2:4]:
        copy.wait()
    even = jnp.where(lax.axis_index("tok") % 2 == 0, 1.0, 0.0)
    head, tail = head_ref[...].astype(f32), tail_ref[...].astype(f32)
    head_ref[...] = (tail * even + head * (1.0 - even)).astype(bf16)
    tail_ref[...] = (head * even + tail * (1.0 - even)).astype(bf16)
    edges = start_all([(head_ref, near_hbm), (tail_ref, next_hbm)], sems)
    blank = jnp.zeros((rows, CZ), bf16)
    for j in range(keys):
        block = scaled_ref[pl.ds(j, rows, stride=stride), :].astype(bf16)
        both = jnp.concatenate(
            [jnp.concatenate([block, blank], axis=1), jnp.concatenate([blank, block], axis=1)],
            axis=0,
        )
        stage_ref[pl.ds(j, PAIRS, stride=keys), :] = nt(weights, both)
    local_ref[...] = stage_ref[...].astype(bf16)
    back = [
        pltpu.make_async_copy(local_ref, out_hbm.at[k], sems.at[2 + k])
        for k in range(out_hbm.shape[0])
    ]
    for copy in back:
        copy.start()
    for copy in edges + back:
        copy.wait()


def pair_bias(pair, pair_gain, w_bias_t, feats, copies):
    rows, keys = pair.shape[0], pair.shape[1]
    edge = jax.ShapeDtypeStruct((feats.shape[0], HALO, C_ATOM), bf16)
    hbm = pl.BlockSpec(memory_space=pl.ANY)
    return pl.pallas_call(
        bias_kernel,
        in_specs=[hbm] * 4,
        out_specs=[hbm] * 3,
        out_shape=[
            jax.ShapeDtypeStruct((copies, keys * PAIRS, 2 * rows), bf16), edge, edge,
        ],
        scratch_shapes=[
            pltpu.VMEM(pair.shape, bf16),
            pltpu.VMEM((1, CZ), f32),
            pltpu.VMEM(w_bias_t.shape, bf16),
            pltpu.VMEM((rows * (keys + 8), CZ), f32),
            pltpu.VMEM((keys * PAIRS, 2 * rows), f32),
            pltpu.VMEM((keys * PAIRS, 2 * rows), bf16),
            pltpu.VMEM(edge.shape, bf16),
            pltpu.VMEM(edge.shape, bf16),
            pltpu.SemaphoreType.DMA((8 + copies,)),
        ],
        compiler_params=pltpu.CompilerParams(vmem_limit_bytes=GRANT),
        cost_estimate=pl.CostEstimate(flops=10**7, bytes_accessed=10**7, transcendentals=0),
        name="pair_bias",
    )(pair, pair_gain.reshape(1, CZ), w_bias_t, feats)


def atom_kernel(
    feats_hbm, near_hbm, next_hbm, mask_hbm, counts_hbm, single_hbm, w_qkv_hbm, w_out_hbm,
    w_embed_hbm, tokens_ref, normed_ref, mask_ref, counts_ref, single_ref, w_qkv_ref, w_out_ref,
    w_embed_ref, sems, halos_ref, padded_ref, normed_atoms_ref, qkv_a, qkv_b, scores_a, scores_b,
    probs_a, probs_b, mixed_ref,
    updated_ref, split_ref, keybias_ref, onehot_ref, *, first,
):
    batch, atoms = tokens_ref.shape[0], feats_hbm.shape[1]
    padded = atoms + 2 * HALO
    moves = [(counts_hbm, counts_ref), (mask_hbm, mask_ref), (w_qkv_hbm, w_qkv_ref)]
    for s in range(batch):
        moves.append((near_hbm.at[first + s], halos_ref.at[0, s]))
        moves.append((feats_hbm.at[first + s], padded_ref.at[s, pl.ds(HALO, atoms)]))
        moves.append((next_hbm.at[first + s], halos_ref.at[1, s]))
    moves += [(w_out_hbm, w_out_ref), (w_embed_hbm, w_embed_ref), (single_hbm, single_ref)]
    copies = start_all(moves, sems)
    for copy in copies[0:2]:
        copy.wait()
    tok_rows = single_ref.shape[0]
    blocks = atoms // 128
    chunks = atoms // 256
    qkv_refs = (qkv_a, qkv_b)

    eye = iota((128, 128), 0) == iota((128, 128), 1)
    for b in range(-1, blocks + 1):
        at = lax.axis_index("tok") * blocks + b
        inside = jnp.where((at >= 0) & (at < mask_ref.shape[0]), 1, 0)
        row = mask_ref[pl.ds(jnp.clip(at, 0, mask_ref.shape[0] - 1), 1), :] * inside
        row = jnp.broadcast_to(row.astype(f32), (128, 128))
        col = jnp.sum(jnp.where(eye, row, 0.0), axis=1, keepdims=True)
        col = jnp.broadcast_to((col - 1.0) * 1e30, (128, 128))
        if b < 0:
            keybias_ref[0:HALO, :] = col[128 - HALO : 128]
        elif b < blocks:
            keybias_ref[HALO + 128 * b : HALO + 128 * b + 128, :] = col
        else:
            keybias_ref[HALO + atoms : padded, :] = col[0:HALO]
    counts = jnp.broadcast_to(counts_ref[...].astype(f32), (tok_rows, tok_rows))
    sub, lane = iota((tok_rows, tok_rows), 0), iota((tok_rows, tok_rows), 1)
    start = jnp.sum(jnp.where(lane < sub, counts, 0.0), axis=1, keepdims=True)
    own = jnp.sum(jnp.where(lane == sub, counts, 0.0), axis=1, keepdims=True)
    pos = iota((tok_rows, 256), 1).astype(f32)
    for g in range(chunks):
        at = pos + float(g * 256)
        hit = jnp.where((at >= start) & (at < start + own), 1.0, 0.0).astype(bf16)
        onehot_ref[:, 256 * g : 256 * g + 256] = hit
        onehot_ref[:, atoms + 256 * g : atoms + 256 * g + 256] = hit
    head_of = iota((32, 128), 1) // ATOM_HD
    head_mask = [(head_of == h).astype(f32).astype(bf16) for h in range(ATOM_HEADS)]
    own_atom = (iota((32, 128), 1) % 32) == iota((32, 128), 0)
    factor = ATOM_HD ** (-0.5) * LOG2E
    def qkv_step(s):
        for low in range(0, padded, padded // 4):
            part = slice(low, low + padded // 4)
            normed, unused = norm_rows(padded_ref[s, part, :].astype(f32))
            normed_atoms_ref[part, :] = normed.astype(bf16)
        qkv_refs[s % 2][...] = nn(normed_atoms_ref[...], w_qkv_ref[...]).astype(bf16)

    def score_step(s, group, to_ref):
        qkv_ref = qkv_refs[s % 2]
        for k in range(2):
            base = pl.multiple_of(group * 128 + 64 * k, 64)
            queries = qkv_ref[pl.ds(base + HALO, 64), 0:C_ATOM]
            spread = jnp.concatenate(
                [
                    queries[32 * w : 32 * w + 32] * head_mask[h]
                    for w in range(2)
                    for h in range(ATOM_HEADS)
                ],
                axis=0,
            )
            to_ref[k] = nt(qkv_ref[pl.ds(base, 160), C_ATOM : 2 * C_ATOM], spread)

    def softmax_step(group, from_ref, to_ref):
        for k in range(2):
            base = pl.multiple_of(group * 128 + 64 * k, 64)
            for w in range(2):
                keybias = keybias_ref[pl.ds(base + 32 * w, 128), :]
                keybias = jnp.concatenate(
                    [keybias[0:48], jnp.where(own_atom, 0.0, keybias[48:80]), keybias[80:128]],
                    axis=0,
                )
                scores = from_ref[k, 32 * w : 32 * w + 128, 128 * w : 128 * w + 128] + keybias
                expo = jnp.exp2((scores - jnp.max(scores, axis=0, keepdims=True)) * factor)
                weights = expo * (1.0 / jnp.sum(expo, axis=0, keepdims=True))
                to_ref[2 * k + w] = weights.astype(bf16)

    def value_step(s, group, from_ref):
        qkv_ref = qkv_refs[s % 2]
        for k in range(2):
            base = pl.multiple_of(group * 128 + 64 * k, 64)
            mixes = []
            for w in range(2):
                values = qkv_ref[pl.ds(base + 32 * w, 128), 2 * C_ATOM : 3 * C_ATOM]
                part = tn(from_ref[2 * k + w], values)
                mix = part[0:32]
                for h in range(1, ATOM_HEADS):
                    mix = jnp.where(head_of == h, part[32 * h : 32 * h + 32], mix)
                mixes.append(mix.astype(bf16))
            mixed_ref[pl.ds(base, 64), :] = jnp.concatenate(mixes, axis=0)

    def embed_step(s):
        feats = padded_ref[s, HALO : HALO + atoms, :].astype(f32)
        updated_ref[...] = (feats + nn(mixed_ref[...], w_out_ref[...])).astype(bf16)
        for n in range(0, C_TOK, 256):
            embedded = jnp.maximum(nn(updated_ref[...], w_embed_ref[:, n : n + 256]), 0.0)
            high = embedded.astype(bf16)
            split_ref[0:atoms, n : n + 256] = high
            split_ref[atoms : 2 * atoms, n : n + 256] = (embedded - high.astype(f32)).astype(bf16)
        pooled = nn(onehot_ref[...], split_ref[...])
        tokens = pooled / own + single_ref[...].astype(f32)
        tokens_ref[s] = tokens
        normed_ref[s] = norm_rows(tokens)[0].astype(bf16)

    for copy in copies[2:]:
        copy.wait()
    even = jnp.where(lax.axis_index("tok") % 2 == 0, 1.0, 0.0)
    near, after = halos_ref[0].astype(f32), halos_ref[1].astype(f32)
    padded_ref[:, 0:HALO, :] = (after * even + near * (1.0 - even)).astype(bf16)
    padded_ref[:, HALO + atoms : padded, :] = (near * even + after * (1.0 - even)).astype(bf16)
    qkv_step(0)
    for s in range(batch):
        score_step(s, 0, scores_a)

        def window_step(i, carry, s=s):
            even, odd = 2 * i, 2 * i + 1
            score_step(s, odd, scores_b)
            softmax_step(even, scores_a, probs_a)
            value_step(s, jnp.maximum(even - 1, 0), probs_b)
            score_step(s, jnp.minimum(odd + 1, 2 * chunks - 1), scores_a)
            softmax_step(odd, scores_b, probs_b)
            value_step(s, even, probs_a)
            return carry

        lax.fori_loop(0, chunks, window_step, 0)
        value_step(s, 2 * chunks - 1, probs_b)
        embed_step(s)
        if s + 1 < batch:
            qkv_step(s + 1)


def atom_stage(part, batch, feats, near, next_, mask, counts, single, w_qkv, w_out, w_embed):
    atoms = feats.shape[1]
    tok_rows = single.shape[0]
    padded = atoms + 2 * HALO
    return pl.pallas_call(
        functools.partial(atom_kernel, first=part * batch),
        in_specs=[pl.BlockSpec(memory_space=pl.ANY)] * 9,
        out_specs=[pl.BlockSpec(memory_space=pltpu.VMEM)] * 2,
        out_shape=[
            jax.ShapeDtypeStruct((batch, tok_rows, C_TOK), f32),
            jax.ShapeDtypeStruct((batch, tok_rows, C_TOK), bf16),
        ],
        scratch_shapes=[
            pltpu.VMEM(mask.shape, jnp.int32),
            pltpu.VMEM(counts.shape, jnp.int32),
            pltpu.VMEM(single.shape, bf16),
            pltpu.VMEM(w_qkv.shape, bf16),
            pltpu.VMEM(w_out.shape, bf16),
            pltpu.VMEM(w_embed.shape, bf16),
            pltpu.SemaphoreType.DMA((6 + 3 * batch,)),
            pltpu.VMEM((2, batch, HALO, C_ATOM), bf16),
            pltpu.VMEM((batch, padded, C_ATOM), bf16),
            pltpu.VMEM((padded, C_ATOM), bf16),
            pltpu.VMEM((padded, 3 * C_ATOM), bf16),
            pltpu.VMEM((padded, 3 * C_ATOM), bf16),
            pltpu.VMEM((2, 160, 256), f32),
            pltpu.VMEM((2, 160, 256), f32),
            pltpu.VMEM((4, 128, 128), bf16),
            pltpu.VMEM((4, 128, 128), bf16),
            pltpu.VMEM((atoms, C_ATOM), bf16),
            pltpu.VMEM((atoms, C_ATOM), bf16),
            pltpu.VMEM((2 * atoms, C_TOK), bf16),
            pltpu.VMEM((padded, 128), f32),
            pltpu.VMEM((tok_rows, 2 * atoms), bf16),
        ],
        compiler_params=pltpu.CompilerParams(vmem_limit_bytes=GRANT),
        cost_estimate=pl.CostEstimate(
            flops=10**10, bytes_accessed=4 * 10**6, transcendentals=3 * 10**6
        ),
        name="atoms",
    )(feats, near, next_, mask, counts, single, w_qkv, w_out, w_embed)


def head_masks(rows):
    masks = []
    for pair in range(4):
        low, high = WINDOWS[pair]
        lane = iota((rows, high - low), 1) + low
        first = 2 * pair * HD
        masks.append(
            [(lane >= first + HD * k) & (lane < first + HD * (k + 1)) for k in range(2)]
        )
    return masks


def two_heads(block, masks):
    blank = jnp.zeros_like(block)
    return jnp.concatenate([jnp.where(mask, block, blank) for mask in masks], axis=0)


def project_moves(piece_hbms, w_qkv_hbm, w_kv_ref, all_ref):
    tok_rows = piece_hbms[0].shape[1]
    here = lax.axis_index("tok")
    moves = []
    for k, piece in enumerate(piece_hbms):
        at = pl.multiple_of((here ^ k) * tok_rows, tok_rows)
        moves.append((piece, all_ref.at[:, pl.ds(at, tok_rows), :]))
    for i in range(2):
        moves.append((w_qkv_hbm.at[:, pl.ds(C_TOK * (i + 1), C_TOK)], w_kv_ref.at[i]))
    return moves


def project(copies, w_kv_ref, all_ref, keys_ref, values_ref):
    batch = all_ref.shape[0]
    for copy in copies[:-1]:
        copy.wait()
    for which, to_ref in enumerate((keys_ref, values_ref)):
        if which == 1:
            copies[-1].wait()
        for n in range(0, C_TOK, 256):
            for s in range(batch):
                to_ref[s, :, n : n + 256] = nn(
                    all_ref[s], w_kv_ref[which, :, n : n + 256]
                ).astype(bf16)


def windows(pair):
    low, high = WINDOWS[pair % 4]
    return 384 * (pair // 4) + low, 384 * (pair // 4) + high


def attend(bias_ref, queries_ref, keys_ref, values_ref, probs_ref, att_ref, done=None):
    batch, keys_all = keys_ref.shape[0], keys_ref.shape[1]
    tok_rows = queries_ref.shape[0] // batch
    masks = head_masks(tok_rows)
    factor = HD ** (-0.5)

    for s in range(batch):
        at = s * tok_rows
        for pair in range(PAIRS):
            low, high = windows(pair)
            queries = two_heads(queries_ref[pl.ds(at, tok_rows), low:high], masks[pair % 4])
            probs_ref[s, pair] = nt(keys_ref[s, :, low:high], queries)
        for pair in range(PAIRS):
            scores = probs_ref[s, pair] * factor
            bias = [bias_ref[k, pair].astype(f32) for k in range(bias_ref.shape[0])]
            scores = scores + jnp.concatenate(bias, axis=0)
            expo = jnp.exp(scores - jnp.max(scores, axis=0, keepdims=True))
            probs_ref[s, pair] = expo * (1.0 / jnp.sum(expo, axis=0, keepdims=True))
        lanes = [jnp.zeros((tok_rows, 128), f32) for _ in range(C_TOK // 128)]
        for pair in range(PAIRS):
            low, high = windows(pair)
            part = tn(probs_ref[s, pair].astype(bf16), values_ref[s, :, low:high])
            first, second = masks[pair % 4]
            mix = jnp.where(first, part[0:tok_rows], 0.0)
            mix = jnp.where(second, part[tok_rows : 2 * tok_rows], mix)
            for t in range((high - low) // 128):
                lanes[low // 128 + t] = lanes[low // 128 + t] + mix[:, 128 * t : 128 * t + 128]
        for t in range(C_TOK // 128):
            att_ref[pl.ds(at, tok_rows), 128 * t : 128 * t + 128] = lanes[t].astype(bf16)
        if done is not None:
            done(s)


def attend_kernel(*refs, count):
    (
        later_hbm, bias_hbm, w_qkv_hbm, cot_hbm, w_down_hbm, att_ref, probs_hbm, values_hbm,
        d_hidden_hbm, later_queries_ref, w_q_ref, w_kv_ref, own_ref, bias_ref, cot_ref, w_down_ref,
        probs_ref, values_ref, d_hidden_ref, sems, all_ref, queries_ref, keys_ref,
    ) = refs[count:]
    batch, tok_rows = all_ref.shape[0], refs[0].shape[1]
    moves = [
        (refs[0], own_ref.at[pl.ds(0, batch)]),
        (later_hbm, own_ref.at[pl.ds(batch, own_ref.shape[0] - batch)]),
        (w_qkv_hbm.at[:, pl.ds(0, C_TOK)], w_q_ref),
    ]
    moves += project_moves(refs[:count], w_qkv_hbm, w_kv_ref, all_ref)
    moves += [(bias_hbm, bias_ref), (cot_hbm, cot_ref), (w_down_hbm, w_down_ref)]
    copies = start_all(moves, sems)
    for copy in copies[0:3]:
        copy.wait()
    own = own_ref[...].reshape(-1, C_TOK)
    split = batch * tok_rows
    for n in range(0, C_TOK, 256):
        queries = nn(own, w_q_ref[:, n : n + 256]).astype(bf16)
        queries_ref[:, n : n + 256] = queries[0:split]
        later_queries_ref[:, n : n + 256] = queries[split:]
    project(copies[3:-3], w_kv_ref, all_ref, keys_ref, values_ref)
    for copy in copies[-3:]:
        copy.wait()
    back = [
        pltpu.make_async_copy(probs_ref.at[s], probs_hbm.at[s], sems.at[s]) for s in range(batch)
    ] + [
        pltpu.make_async_copy(values_ref, values_hbm, sems.at[batch]),
        pltpu.make_async_copy(d_hidden_ref, d_hidden_hbm, sems.at[batch + 1]),
    ]
    back[batch].start()
    cot = cot_ref[...].reshape(-1, C_TOK)
    for n in range(0, w_down_ref.shape[0], 256):
        d_hidden_ref[:, n : n + 256] = nt(cot, w_down_ref[n : n + 256, :])
    back[batch + 1].start()
    attend(
        bias_ref, queries_ref, keys_ref, values_ref, probs_ref, att_ref, lambda s: back[s].start()
    )
    for copy in back:
        copy.wait()


def attend_scratch(batch, tok_rows, keys_all):
    return [
        pltpu.VMEM((batch, keys_all, C_TOK), bf16),
        pltpu.VMEM((batch * tok_rows, C_TOK), bf16),
        pltpu.VMEM((batch, keys_all, C_TOK), bf16),
    ]


def attend_stage(pieces, later, bias, w_qkv, cot, w_down):
    batch, tok_rows, _ = pieces[0].shape
    keys_all = tok_rows * len(pieces)
    vmem = pl.BlockSpec(memory_space=pltpu.VMEM)
    hbm = pl.BlockSpec(memory_space=pl.ANY)
    d_hidden = jax.ShapeDtypeStruct((cot.shape[0] * tok_rows, w_down.shape[0]), f32)
    return pl.pallas_call(
        functools.partial(attend_kernel, count=len(pieces)),
        in_specs=[hbm] * (len(pieces) + 5),
        out_specs=[vmem, hbm, hbm, hbm, vmem],
        out_shape=[
            jax.ShapeDtypeStruct((batch * tok_rows, C_TOK), bf16),
            jax.ShapeDtypeStruct((batch, PAIRS, keys_all, 2 * tok_rows), f32),
            jax.ShapeDtypeStruct((batch, keys_all, C_TOK), bf16),
            d_hidden,
            jax.ShapeDtypeStruct((later.shape[0] * tok_rows, C_TOK), bf16),
        ],
        scratch_shapes=[
            pltpu.VMEM((C_TOK, C_TOK), bf16),
            pltpu.VMEM((2, C_TOK, C_TOK), bf16),
            pltpu.VMEM(cot.shape, bf16),
            pltpu.VMEM(bias.shape, bf16),
            pltpu.VMEM(cot.shape, bf16),
            pltpu.VMEM(w_down.shape, bf16),
            pltpu.VMEM((batch, PAIRS, keys_all, 2 * tok_rows), f32),
            pltpu.VMEM((batch, keys_all, C_TOK), bf16),
            pltpu.VMEM(d_hidden.shape, f32),
            pltpu.SemaphoreType.DMA((8 + len(pieces),)),
        ]
        + attend_scratch(batch, tok_rows, keys_all),
        compiler_params=pltpu.CompilerParams(vmem_limit_bytes=GRANT),
        cost_estimate=pl.CostEstimate(
            flops=4 * 10**9, bytes_accessed=10**7, transcendentals=10**6
        ),
        name="attend",
    )(*pieces, later, bias, w_qkv, cot, w_down)


def token_kernel(*refs, count):
    (
        queries_hbm, bias_hbm, tokens_a_hbm, tokens_b_hbm, att_a_hbm, cot_hbm, probs_a_hbm, values_a_hbm,
        w_qkv_hbm, w_out_hbm, w_gate_hbm, w_up_hbm, d_hidden_hbm,
        resid_hbm, hidden_hbm, d_bias_ref,
        bias_ref, tokens_ref, att_a_ref, cot_ref, resid_ref, hidden_ref,
        w_kv_ref, w_out_ref, w_gate_ref, w_up_ref, d_hidden_ref, probs_ref, values_ref, sems,
        all_ref, queries_ref, keys_ref, grads_ref, d_gate_ref, d_up_ref, hat_ref,
    ) = refs[count:]
    batch, tok_rows = cot_ref.shape[0], cot_ref.shape[1]
    keys_all = values_ref.shape[1]
    rows = batch * tok_rows
    ahead = values_a_hbm.shape[0]
    lead = ahead * tok_rows
    moves = project_moves(refs[:count], w_qkv_hbm, w_kv_ref, all_ref)
    projecting = len(moves)
    moves += [
        (queries_hbm, queries_ref), (bias_hbm, bias_ref), (w_out_hbm, w_out_ref), (att_a_hbm, att_a_ref),
        (tokens_a_hbm, tokens_ref.at[pl.ds(0, ahead)]),
        (tokens_b_hbm, tokens_ref.at[pl.ds(ahead, batch - ahead)]), (cot_hbm, cot_ref),
        (d_hidden_hbm, d_hidden_ref), (w_gate_hbm, w_gate_ref), (w_up_hbm, w_up_ref),
        (values_a_hbm, values_ref.at[pl.ds(0, ahead)]), (probs_a_hbm, probs_ref.at[pl.ds(0, ahead)]),
    ]
    copies = start_all(moves, sems)
    own_values = values_ref.at[pl.ds(ahead, batch - ahead)]
    own_probs = probs_ref.at[pl.ds(ahead, batch - ahead)]
    project(copies[:projecting], w_kv_ref, all_ref, keys_ref, own_values)
    copies[projecting].wait()
    copies = copies[projecting + 1 :]
    copies[0].wait()
    attend(bias_ref, queries_ref, keys_ref, own_values, own_probs, queries_ref)

    for copy in copies[1:5]:
        copy.wait()
    tokens = tokens_ref[...].reshape(rows, C_TOK)
    resid_ref[0:lead, :] = tokens[0:lead] + nn(att_a_ref[...], w_out_ref[...])
    resid_ref[lead:rows, :] = tokens[lead:rows] + nn(queries_ref[...], w_out_ref[...])
    back = [
        pltpu.make_async_copy(resid_ref, resid_hbm, sems.at[0]),
        pltpu.make_async_copy(hidden_ref, hidden_hbm, sems.at[1]),
    ]
    back[0].start()
    hat, rstd = norm_rows(resid_ref[...])
    hat_ref[...] = hat
    grads_ref[...] = hat.astype(bf16)
    for copy in copies[5:9]:
        copy.wait()

    for n in range(0, w_gate_ref.shape[1], 256):
        shaped = grads_ref[...]
        gate = nn(shaped, w_gate_ref[:, n : n + 256])
        up = nn(shaped, w_up_ref[:, n : n + 256])
        d_hidden = d_hidden_ref[:, n : n + 256]
        sig = 1.0 / (1.0 + jnp.exp(-gate))
        act = gate * sig
        hidden_ref[:, n : n + 256] = (act * up).astype(bf16)
        d_gate_ref[:, n : n + 256] = (
            d_hidden * up * sig * (1.0 + gate * (1.0 - sig))
        ).astype(bf16)
        d_up_ref[:, n : n + 256] = (d_hidden * act).astype(bf16)

    back[1].start()
    parts = []
    for n in range(0, C_TOK, 256):
        parts.append(
            nt(d_gate_ref[...], w_gate_ref[n : n + 256, :])
            + nt(d_up_ref[...], w_up_ref[n : n + 256, :])
        )
    d_normed = jnp.concatenate(parts, axis=1)
    hat = hat_ref[...]
    first = jnp.mean(d_normed, axis=-1, keepdims=True)
    second = jnp.mean(d_normed * hat, axis=-1, keepdims=True)
    d_resid = cot_ref[...].reshape(rows, C_TOK).astype(f32) + rstd * (
        d_normed - first - hat * second
    )
    grads_ref[...] = nt(d_resid.astype(bf16), w_out_ref[...]).astype(bf16)
    for copy in copies[9:]:
        copy.wait()
    masks = head_masks(tok_rows)
    for pair in range(PAIRS):
        low, high = windows(pair)
        total = jnp.zeros((keys_all, 2 * tok_rows), f32)
        for s in range(batch):
            grads = two_heads(
                grads_ref[s * tok_rows : (s + 1) * tok_rows, low:high], masks[pair % 4]
            )
            d_probs = nt(values_ref[s, :, low:high], grads)
            probs = probs_ref[s, pair]
            delta = jnp.sum(probs * d_probs, axis=0, keepdims=True)
            total = total + probs * (d_probs - delta)
        size = d_bias_ref.shape[2]
        for k in range(d_bias_ref.shape[0]):
            d_bias_ref[k, pair] = total[size * k : size * (k + 1)].astype(bf16)
    for copy in back:
        copy.wait()


def token_stage(
    pieces, queries, bias, tokens_a, tokens_b, att_a, cot, probs_a, values_a, w_qkv, w_out, w_gate, w_up,
    d_hidden,
):
    batch, tok_rows, _ = cot.shape
    keys_all = tok_rows * len(pieces)
    rows = batch * tok_rows
    hidden = w_gate.shape[1]
    vmem = pl.BlockSpec(memory_space=pltpu.VMEM)
    hbm = pl.BlockSpec(memory_space=pl.ANY)
    return pl.pallas_call(
        functools.partial(token_kernel, count=len(pieces)),
        in_specs=[hbm] * (len(pieces) + 13),
        out_specs=[hbm, hbm, vmem],
        out_shape=[
            jax.ShapeDtypeStruct((rows, C_TOK), f32),
            jax.ShapeDtypeStruct((rows, hidden), bf16),
            jax.ShapeDtypeStruct(bias.shape, bf16),
        ],
        scratch_shapes=[
            pltpu.VMEM(bias.shape, bf16),
            pltpu.VMEM(cot.shape, f32),
            pltpu.VMEM(att_a.shape, bf16),
            pltpu.VMEM(cot.shape, bf16),
            pltpu.VMEM((rows, C_TOK), f32),
            pltpu.VMEM((rows, hidden), bf16),
            pltpu.VMEM((2, C_TOK, C_TOK), bf16),
            pltpu.VMEM(w_out.shape, bf16),
            pltpu.VMEM(w_gate.shape, bf16),
            pltpu.VMEM(w_up.shape, bf16),
            pltpu.VMEM(d_hidden.shape, f32),
            pltpu.VMEM((batch, PAIRS, keys_all, 2 * tok_rows), f32),
            pltpu.VMEM((batch, keys_all, C_TOK), bf16),
            pltpu.SemaphoreType.DMA((16 + len(pieces),)),
        ]
        + attend_scratch(pieces[0].shape[0], tok_rows, keys_all)
        + [
            pltpu.VMEM((rows, C_TOK), bf16),
            pltpu.VMEM((rows, hidden), bf16),
            pltpu.VMEM((rows, hidden), bf16),
            pltpu.VMEM((rows, C_TOK), f32),
        ],
        compiler_params=pltpu.CompilerParams(vmem_limit_bytes=GRANT),
        cost_estimate=pl.CostEstimate(
            flops=10**10, bytes_accessed=2 * 10**7, transcendentals=10**6
        ),
        name="tokens",
    )(
        *pieces, queries, bias, tokens_a, tokens_b, att_a, cot, probs_a, values_a, w_qkv, w_out, w_gate,
        w_up, d_hidden,
    )


def output_kernel(
    resid_ref, hidden_ref, w_down_ref, pair_ref, out_ref, hat_ref, rstd_ref, pairf_ref
):
    out_ref[...] = (resid_ref[...] + nn(hidden_ref[...], w_down_ref[...])).astype(bf16)
    rows, keys = pair_ref.shape[0], pair_ref.shape[1]
    for i in range(rows // 8):
        pairf_ref[8 * keys * i : 8 * keys * (i + 1), :] = (
            pair_ref[8 * i : 8 * i + 8].astype(f32).reshape(8 * keys, CZ)
        )

    def norm_step(j, carry):
        hat, rstd = norm_rows(pairf_ref[pl.ds(j, rows, stride=keys), :])
        at = pl.multiple_of(j * rows, rows)
        hat_ref[pl.ds(at, rows), :] = hat
        rstd = jnp.broadcast_to(rstd, (rows, CZ)).T[0:1]
        rstd_ref[pl.ds(j, 1), :] = jnp.concatenate([rstd, rstd], axis=1)
        return carry

    lax.fori_loop(0, keys, norm_step, 0, unroll=4)


def output_stage(resid, hidden, w_down, pair):
    rows, keys = pair.shape[0], pair.shape[1]
    return pl.pallas_call(
        output_kernel,
        out_shape=[jax.ShapeDtypeStruct(resid.shape, bf16)]
        + [
            jax.ShapeDtypeStruct((rows * keys, CZ), f32),
            jax.ShapeDtypeStruct((keys, 2 * rows), f32),
        ],
        scratch_shapes=[pltpu.VMEM((rows * keys, CZ), f32)],
        compiler_params=pltpu.CompilerParams(vmem_limit_bytes=GRANT),
        cost_estimate=pl.CostEstimate(
            flops=10**9, bytes_accessed=8 * 10**6, transcendentals=0
        ),
        name="output",
    )(resid, hidden, w_down, pair)


def grad_kernel(
    parts_hbm, hat_hbm, rstd_hbm, gain_hbm, w_bias_hbm, out_hbm, parts_ref, hat_ref, rstd_ref,
    gain_ref, w_bias_ref, total_ref, out_ref, sems,
):
    keys = parts_ref.shape[2]
    rows = hat_ref.shape[0] // keys
    size = 8 * rows
    moves = [
        (gain_hbm, gain_ref), (w_bias_hbm, w_bias_ref), (parts_hbm, parts_ref),
        (rstd_hbm, rstd_ref),
    ]
    for c in range(keys // 8):
        moves.append((hat_hbm.at[pl.ds(size * c, size)], hat_ref.at[pl.ds(size * c, size)]))
    copies = start_all(moves, sems)
    for copy in copies[0:2]:
        copy.wait()
    weights = jnp.concatenate(split_heads(w_bias_ref[...]), axis=0) * gain_ref[...]
    weights = weights - jnp.mean(weights, axis=-1, keepdims=True)
    weights = jnp.concatenate([weights[0:PAIRS], weights[PAIRS:HEADS]], axis=1)
    w_high = weights.astype(bf16).astype(f32)
    w_middle = (weights - w_high).astype(bf16).astype(f32)
    w_low = weights - w_high - w_middle
    weights = jnp.concatenate([w_high, w_middle, w_low, w_high, w_middle, w_high], axis=0)
    weights = weights.astype(bf16)
    for copy in copies[2:4]:
        copy.wait()
    for pair in range(PAIRS):
        total = parts_ref[0, pair].astype(f32)
        for k in range(1, parts_ref.shape[0]):
            total = total + parts_ref[k, pair].astype(f32)
        total_ref[pair * keys : (pair + 1) * keys, :] = total * rstd_ref[...]
    back = []
    for c in range(keys // 8):
        copies[4 + c].wait()
        for j in range(8 * c, 8 * c + 8):
            total = total_ref[pl.ds(j, PAIRS, stride=keys), :]
            high = total.astype(bf16).astype(f32)
            middle = (total - high).astype(bf16).astype(f32)
            low = total - high - middle
            stack = jnp.concatenate([high, high, high, middle, middle, low], axis=0)
            both = nn(stack.T.astype(bf16), weights)
            scaled = both[0:rows, 0:CZ] + both[rows : 2 * rows, CZ : 2 * CZ]
            hat = hat_ref[rows * j : rows * (j + 1), :]
            second = jnp.mean(scaled * hat, axis=-1, keepdims=True)
            out_ref[pl.ds(size * c + j % 8, rows, stride=8), :] = scaled - hat * second
        back.append(
            pltpu.make_async_copy(
                out_ref.at[pl.ds(size * c, size)].reshape(rows, 8, CZ),
                out_hbm.at[:, pl.ds(8 * c, 8), :],
                sems.at[c],
            )
        )
        back[c].start()
    for copy in back:
        copy.wait()


def pair_back(parts, hat, rstd, pair_gain, w_bias_t):
    keys = parts.shape[2]
    rows = hat.shape[0] // keys
    hbm = pl.BlockSpec(memory_space=pl.ANY)
    return pl.pallas_call(
        grad_kernel,
        in_specs=[hbm] * 5,
        out_specs=hbm,
        out_shape=jax.ShapeDtypeStruct((rows, keys, CZ), f32),
        scratch_shapes=[
            pltpu.VMEM(parts.shape, bf16),
            pltpu.VMEM(hat.shape, f32),
            pltpu.VMEM(rstd.shape, f32),
            pltpu.VMEM((1, CZ), f32),
            pltpu.VMEM(w_bias_t.shape, bf16),
            pltpu.VMEM((keys * PAIRS, 2 * rows), f32),
            pltpu.VMEM((rows * keys, CZ), f32),
            pltpu.SemaphoreType.DMA((4 + keys // 8,)),
        ],
        compiler_params=pltpu.CompilerParams(vmem_limit_bytes=GRANT),
        cost_estimate=pl.CostEstimate(flops=10**8, bytes_accessed=4 * 10**6, transcendentals=0),
        name="pair_grad",
    )(parts, hat, rstd, pair_gain.reshape(1, CZ), w_bias_t)


def swap(values, axis, k):
    return lax.ppermute(values, axis, [(i, i ^ k) for i in range(lax.axis_size(axis))])


def gather(values, axis):
    far = range(lax.axis_size(axis) - 1, 0, -1)
    return [values] + [swap(values, axis, k) for k in far][::-1]


def body(
    atom_feats, atom_counts, atom_mask, token_single, pair, pair_gain, w_bias, w_atom_qkv,
    w_atom_out, w_embed, w_qkv, w_out, w_gate, w_up, w_down, cotangent,
):
    batch, atom_rows, _ = atom_feats.shape
    tok_rows = token_single.shape[0]
    shards = lax.axis_size("tok")
    groups = lax.axis_size("samp")

    w_bias_t = w_bias.T
    local_bias, near, next_ = pair_bias(pair, pair_gain, w_bias_t, atom_feats, groups)
    near = swap(near, "tok", 1)
    steps = [(i, i + 1) for i in range(1, shards - 1, 2)]
    next_ = lax.ppermute(next_, "tok", steps + [(j, i) for i, j in steps])

    bias = lax.all_to_all(local_bias, "samp", 0, 0).reshape(groups, PAIRS, -1, 2 * tok_rows)

    mask = atom_mask.reshape(-1, 128)
    mask, local_bias = lax.optimization_barrier((mask, local_bias))

    each = batch // 2
    tokens, gathered = [], []
    for part in range(2):
        tok, normed = atom_stage(
            part, each, atom_feats, near, next_, mask, atom_counts, token_single, w_atom_qkv,
            w_atom_out, w_embed,
        )
        tokens.append(tok)
        gathered.append(gather(normed, "tok"))
    att_a, probs_a, values_a, d_hidden, queries_b = attend_stage(
        gathered[0], gathered[1][0], bias, w_qkv, cotangent, w_down
    )
    resid, hidden, d_bias = token_stage(
        gathered[1], queries_b, bias, *tokens, att_a, cotangent, probs_a, values_a, w_qkv, w_out, w_gate,
        w_up, d_hidden,
    )
    parts = lax.all_to_all(d_bias, "samp", 0, 0)
    token_out, hat, rstd = output_stage(resid, hidden, w_down, pair)
    pair_grad = pair_back(parts, hat, rstd, pair_gain, w_bias_t)
    token_out = token_out.reshape(batch, tok_rows, C_TOK)
    return (token_out, pair_grad)


def solution(mesh):
    in_specs = (
        P("samp", "tok", None),
        P("tok", None),
        P(),
        P("tok", None),
        P("tok", "samp", None),
        P(), P(), P(), P(), P(), P(), P(), P(), P(), P(),
        P("samp", "tok", None),
    )
    out_specs = (P("samp", "tok", None), P("tok", "samp", None))
    return jax.shard_map(body, mesh=mesh, in_specs=in_specs, out_specs=out_specs, check_vma=False)
```

```python
import functools

import jax
import jax.numpy as jnp
from jax import lax
from jax.experimental import pallas as pl
from jax.experimental.pallas import tpu as pltpu
from jax.sharding import PartitionSpec as P

C_ATOM = 128
ATOM_HEADS = 4
C_TOK = 768
HEADS = 16
ATOM_HD = 32
HD = 48
CZ = 128
HALO = 48
PAIRS = HEADS // 2
GRANT = 64 << 20
LOG2E = 1.4426950408889634

epsilon = 1e-05
f32 = jnp.float32
bf16 = jnp.bfloat16

WINDOWS = ((0, 128), (0, 256), (128, 384), (256, 384))


def nn(a, b):
    return lax.dot_general(a, b, (((1,), (0,)), ((), ())), preferred_element_type=f32)


def nt(a, b):
    return lax.dot_general(a, b, (((1,), (1,)), ((), ())), preferred_element_type=f32)


def tn(a, b):
    return lax.dot_general(a, b, (((0,), (0,)), ((), ())), preferred_element_type=f32)


def start_all(moves, sems):
    copies = [pltpu.make_async_copy(src, dst, sems.at[i]) for i, (src, dst) in enumerate(moves)]
    for copy in copies:
        copy.start()
    return copies


def norm_rows(values):
    center = values - jnp.mean(values, axis=-1, keepdims=True)
    scale_inv = lax.rsqrt(jnp.mean(center * center, axis=-1, keepdims=True) + epsilon)
    return (center * scale_inv, scale_inv)


def iota(shape, dim):
    return lax.broadcasted_iota(jnp.int32, shape, dim)


def pick_heads(parity):
    row, col = iota((PAIRS, HEADS), 0), iota((PAIRS, HEADS), 1)
    return (col == 2 * row + parity).astype(f32).astype(bf16)


def split_heads(w_bias_t):
    return [nn(pick_heads(parity), w_bias_t) for parity in range(2)]


def bias_kernel(
    pair_hbm, gain_hbm, w_bias_hbm, feats_hbm, out_hbm, near_hbm, next_hbm, pair_ref, gain_ref,
    w_bias_ref, scaled_ref, stage_ref, local_ref, head_ref, tail_ref, sems,
):
    rows, keys = pair_ref.shape[0], pair_ref.shape[1]
    atoms = feats_hbm.shape[1]
    part = rows // 4
    stride = scaled_ref.shape[0] // rows
    moves = [
        (gain_hbm, gain_ref), (w_bias_hbm, w_bias_ref),
        (feats_hbm.at[:, pl.ds(0, HALO), :], head_ref),
        (feats_hbm.at[:, pl.ds(atoms - HALO, HALO), :], tail_ref),
    ]
    for i in range(4):
        moves.append((pair_hbm.at[pl.ds(part * i, part)], pair_ref.at[pl.ds(part * i, part)]))
    copies = start_all(moves, sems)
    for copy in copies[0:2]:
        copy.wait()
    gain = gain_ref[...]
    weights = jnp.concatenate(split_heads(w_bias_ref[...]), axis=1).astype(bf16)
    for i in range(rows // 8):
        if 8 * i % part == 0:
            copies[4 + 8 * i // part].wait()
        block = pair_ref[8 * i : 8 * i + 8].astype(f32).reshape(8 * keys, CZ)
        scaled = norm_rows(block)[0] * gain
        for k in range(8):
            at = (8 * i + k) * stride
            scaled_ref[at : at + keys, :] = scaled[keys * k : keys * (k + 1)]
    for copy in copies[2:4]:
        copy.wait()
    even = jnp.where(lax.axis_index("tok") % 2 == 0, 1.0, 0.0)
    head, tail = head_ref[...].astype(f32), tail_ref[...].astype(f32)
    head_ref[...] = (tail * even + head * (1.0 - even)).astype(bf16)
    tail_ref[...] = (head * even + tail * (1.0 - even)).astype(bf16)
    edges = start_all([(head_ref, near_hbm), (tail_ref, next_hbm)], sems)
    blank = jnp.zeros((rows, CZ), bf16)
    for j in range(keys):
        block = scaled_ref[pl.ds(j, rows, stride=stride), :].astype(bf16)
        both = jnp.concatenate(
            [jnp.concatenate([block, blank], axis=1), jnp.concatenate([blank, block], axis=1)],
            axis=0,
        )
        stage_ref[pl.ds(j, PAIRS, stride=keys), :] = nt(weights, both)
    local_ref[...] = stage_ref[...].astype(bf16)
    back = [
        pltpu.make_async_copy(local_ref, out_hbm.at[k], sems.at[2 + k])
        for k in range(out_hbm.shape[0])
    ]
    for copy in back:
        copy.start()
    for copy in edges + back:
        copy.wait()


def pair_bias(pair, pair_gain, w_bias_t, feats, copies):
    rows, keys = pair.shape[0], pair.shape[1]
    edge = jax.ShapeDtypeStruct((feats.shape[0], HALO, C_ATOM), bf16)
    hbm = pl.BlockSpec(memory_space=pl.ANY)
    return pl.pallas_call(
        bias_kernel,
        in_specs=[hbm] * 4,
        out_specs=[hbm] * 3,
        out_shape=[
            jax.ShapeDtypeStruct((copies, keys * PAIRS, 2 * rows), bf16), edge, edge,
        ],
        scratch_shapes=[
            pltpu.VMEM(pair.shape, bf16),
            pltpu.VMEM((1, CZ), f32),
            pltpu.VMEM(w_bias_t.shape, bf16),
            pltpu.VMEM((rows * (keys + 8), CZ), f32),
            pltpu.VMEM((keys * PAIRS, 2 * rows), f32),
            pltpu.VMEM((keys * PAIRS, 2 * rows), bf16),
            pltpu.VMEM(edge.shape, bf16),
            pltpu.VMEM(edge.shape, bf16),
            pltpu.SemaphoreType.DMA((8 + copies,)),
        ],
        compiler_params=pltpu.CompilerParams(vmem_limit_bytes=GRANT),
        cost_estimate=pl.CostEstimate(flops=10**7, bytes_accessed=10**7, transcendentals=0),
        name="pair_bias",
    )(pair, pair_gain.reshape(1, CZ), w_bias_t, feats)


def atom_kernel(
    feats_hbm, near_hbm, next_hbm, mask_hbm, counts_hbm, single_hbm, w_qkv_hbm, w_out_hbm,
    w_embed_hbm, tokens_ref, normed_ref, mask_ref, counts_ref, single_ref, w_qkv_ref, w_out_ref,
    w_embed_ref, sems, halos_ref, padded_ref, normed_atoms_ref, qkv_a, qkv_b, scores_a, scores_b,
    probs_a, probs_b, mixed_ref,
    updated_ref, split_ref, keybias_ref, onehot_ref, *, first,
):
    batch, atoms = tokens_ref.shape[0], feats_hbm.shape[1]
    padded = atoms + 2 * HALO
    moves = [(counts_hbm, counts_ref), (mask_hbm, mask_ref), (w_qkv_hbm, w_qkv_ref)]
    for s in range(batch):
        moves.append((near_hbm.at[first + s], halos_ref.at[0, s]))
        moves.append((feats_hbm.at[first + s], padded_ref.at[s, pl.ds(HALO, atoms)]))
        moves.append((next_hbm.at[first + s], halos_ref.at[1, s]))
    moves += [(w_out_hbm, w_out_ref), (w_embed_hbm, w_embed_ref), (single_hbm, single_ref)]
    copies = start_all(moves, sems)
    for copy in copies[0:2]:
        copy.wait()
    tok_rows = single_ref.shape[0]
    blocks = atoms // 128
    chunks = atoms // 256
    qkv_refs = (qkv_a, qkv_b)

    eye = iota((128, 128), 0) == iota((128, 128), 1)
    for b in range(-1, blocks + 1):
        at = lax.axis_index("tok") * blocks + b
        inside = jnp.where((at >= 0) & (at < mask_ref.shape[0]), 1, 0)
        row = mask_ref[pl.ds(jnp.clip(at, 0, mask_ref.shape[0] - 1), 1), :] * inside
        row = jnp.broadcast_to(row.astype(f32), (128, 128))
        col = jnp.sum(jnp.where(eye, row, 0.0), axis=1, keepdims=True)
        col = jnp.broadcast_to((col - 1.0) * 1e30, (128, 128))
        if b < 0:
            keybias_ref[0:HALO, :] = col[128 - HALO : 128]
        elif b < blocks:
            keybias_ref[HALO + 128 * b : HALO + 128 * b + 128, :] = col
        else:
            keybias_ref[HALO + atoms : padded, :] = col[0:HALO]
    counts = jnp.broadcast_to(counts_ref[...].astype(f32), (tok_rows, tok_rows))
    sub, lane = iota((tok_rows, tok_rows), 0), iota((tok_rows, tok_rows), 1)
    start = jnp.sum(jnp.where(lane < sub, counts, 0.0), axis=1, keepdims=True)
    own = jnp.sum(jnp.where(lane == sub, counts, 0.0), axis=1, keepdims=True)
    pos = iota((tok_rows, 256), 1).astype(f32)
    for g in range(chunks):
        at = pos + float(g * 256)
        hit = jnp.where((at >= start) & (at < start + own), 1.0, 0.0).astype(bf16)
        onehot_ref[:, 256 * g : 256 * g + 256] = hit
        onehot_ref[:, atoms + 256 * g : atoms + 256 * g + 256] = hit
    head_of = iota((32, 128), 1) // ATOM_HD
    head_mask = [(head_of == h).astype(f32).astype(bf16) for h in range(ATOM_HEADS)]
    own_atom = (iota((32, 128), 1) % 32) == iota((32, 128), 0)
    factor = ATOM_HD ** (-0.5) * LOG2E
    def qkv_step(s):
        for low in range(0, padded, padded // 4):
            part = slice(low, low + padded // 4)
            normed, unused = norm_rows(padded_ref[s, part, :].astype(f32))
            normed_atoms_ref[part, :] = normed.astype(bf16)
        qkv_refs[s % 2][...] = nn(normed_atoms_ref[...], w_qkv_ref[...]).astype(bf16)

    def score_step(s, group, to_ref):
        qkv_ref = qkv_refs[s % 2]
        for k in range(2):
            base = group * 128 + 64 * k
            queries = qkv_ref[pl.ds(base + HALO, 64), 0:C_ATOM]
            spread = jnp.concatenate(
                [
                    queries[32 * w : 32 * w + 32] * head_mask[h]
                    for w in range(2)
                    for h in range(ATOM_HEADS)
                ],
                axis=0,
            )
            to_ref[k] = nt(qkv_ref[pl.ds(base, 160), C_ATOM : 2 * C_ATOM], spread)

    def softmax_step(group, from_ref, to_ref):
        for k in range(2):
            base = group * 128 + 64 * k
            for w in range(2):
                keybias = keybias_ref[pl.ds(base + 32 * w, 128), :]
                keybias = jnp.concatenate(
                    [keybias[0:48], jnp.where(own_atom, 0.0, keybias[48:80]), keybias[80:128]],
                    axis=0,
                )
                scores = from_ref[k, 32 * w : 32 * w + 128, 128 * w : 128 * w + 128] + keybias
                expo = jnp.exp2((scores - jnp.max(scores, axis=0, keepdims=True)) * factor)
                weights = expo * (1.0 / jnp.sum(expo, axis=0, keepdims=True))
                to_ref[2 * k + w] = weights.astype(bf16)

    def value_step(s, group, from_ref):
        qkv_ref = qkv_refs[s % 2]
        for k in range(2):
            base = group * 128 + 64 * k
            mixes = []
            for w in range(2):
                values = qkv_ref[pl.ds(base + 32 * w, 128), 2 * C_ATOM : 3 * C_ATOM]
                part = tn(from_ref[2 * k + w], values)
                mix = part[0:32]
                for h in range(1, ATOM_HEADS):
                    mix = jnp.where(head_of == h, part[32 * h : 32 * h + 32], mix)
                mixes.append(mix.astype(bf16))
            mixed_ref[pl.ds(base, 64), :] = jnp.concatenate(mixes, axis=0)

    def embed_step(s):
        feats = padded_ref[s, HALO : HALO + atoms, :].astype(f32)
        updated_ref[...] = (feats + nn(mixed_ref[...], w_out_ref[...])).astype(bf16)
        for n in range(0, C_TOK, 256):
            embedded = jnp.maximum(nn(updated_ref[...], w_embed_ref[:, n : n + 256]), 0.0)
            high = embedded.astype(bf16)
            split_ref[0:atoms, n : n + 256] = high
            split_ref[atoms : 2 * atoms, n : n + 256] = (embedded - high.astype(f32)).astype(bf16)
        pooled = nn(onehot_ref[...], split_ref[...])
        tokens = pooled / own + single_ref[...].astype(f32)
        tokens_ref[s] = tokens
        normed_ref[s] = norm_rows(tokens)[0].astype(bf16)

    for copy in copies[2:]:
        copy.wait()
    even = jnp.where(lax.axis_index("tok") % 2 == 0, 1.0, 0.0)
    near, after = halos_ref[0].astype(f32), halos_ref[1].astype(f32)
    padded_ref[:, 0:HALO, :] = (after * even + near * (1.0 - even)).astype(bf16)
    padded_ref[:, HALO + atoms : padded, :] = (near * even + after * (1.0 - even)).astype(bf16)
    qkv_step(0)
    for s in range(batch):
        score_step(s, 0, scores_a)

        for i in range(chunks):
            even, odd = 2 * i, 2 * i + 1
            score_step(s, odd, scores_b)
            softmax_step(even, scores_a, probs_a)
            if even > 0:
                value_step(s, even - 1, probs_b)
            if odd + 1 < 2 * chunks:
                score_step(s, odd + 1, scores_a)
            softmax_step(odd, scores_b, probs_b)
            value_step(s, even, probs_a)
        value_step(s, 2 * chunks - 1, probs_b)
        embed_step(s)
        if s + 1 < batch:
            qkv_step(s + 1)


def atom_stage(part, batch, feats, near, next_, mask, counts, single, w_qkv, w_out, w_embed):
    atoms = feats.shape[1]
    tok_rows = single.shape[0]
    padded = atoms + 2 * HALO
    return pl.pallas_call(
        functools.partial(atom_kernel, first=part * batch),
        in_specs=[pl.BlockSpec(memory_space=pl.ANY)] * 9,
        out_specs=[pl.BlockSpec(memory_space=pltpu.VMEM)] * 2,
        out_shape=[
            jax.ShapeDtypeStruct((batch, tok_rows, C_TOK), f32),
            jax.ShapeDtypeStruct((batch, tok_rows, C_TOK), bf16),
        ],
        scratch_shapes=[
            pltpu.VMEM(mask.shape, jnp.int32),
            pltpu.VMEM(counts.shape, jnp.int32),
            pltpu.VMEM(single.shape, bf16),
            pltpu.VMEM(w_qkv.shape, bf16),
            pltpu.VMEM(w_out.shape, bf16),
            pltpu.VMEM(w_embed.shape, bf16),
            pltpu.SemaphoreType.DMA((6 + 3 * batch,)),
            pltpu.VMEM((2, batch, HALO, C_ATOM), bf16),
            pltpu.VMEM((batch, padded, C_ATOM), bf16),
            pltpu.VMEM((padded, C_ATOM), bf16),
            pltpu.VMEM((padded, 3 * C_ATOM), bf16),
            pltpu.VMEM((padded, 3 * C_ATOM), bf16),
            pltpu.VMEM((2, 160, 256), f32),
            pltpu.VMEM((2, 160, 256), f32),
            pltpu.VMEM((4, 128, 128), bf16),
            pltpu.VMEM((4, 128, 128), bf16),
            pltpu.VMEM((atoms, C_ATOM), bf16),
            pltpu.VMEM((atoms, C_ATOM), bf16),
            pltpu.VMEM((2 * atoms, C_TOK), bf16),
            pltpu.VMEM((padded, 128), f32),
            pltpu.VMEM((tok_rows, 2 * atoms), bf16),
        ],
        compiler_params=pltpu.CompilerParams(vmem_limit_bytes=GRANT),
        cost_estimate=pl.CostEstimate(
            flops=10**10, bytes_accessed=4 * 10**6, transcendentals=3 * 10**6
        ),
        name="atoms",
    )(feats, near, next_, mask, counts, single, w_qkv, w_out, w_embed)


def head_masks(rows):
    masks = []
    for pair in range(4):
        low, high = WINDOWS[pair]
        lane = iota((rows, high - low), 1) + low
        first = 2 * pair * HD
        masks.append(
            [(lane >= first + HD * k) & (lane < first + HD * (k + 1)) for k in range(2)]
        )
    return masks


def two_heads(block, masks):
    blank = jnp.zeros_like(block)
    return jnp.concatenate([jnp.where(mask, block, blank) for mask in masks], axis=0)


def project_moves(piece_hbms, w_qkv_hbm, w_kv_ref, all_ref):
    tok_rows = piece_hbms[0].shape[1]
    here = lax.axis_index("tok")
    moves = []
    for k, piece in enumerate(piece_hbms):
        at = pl.multiple_of((here ^ k) * tok_rows, tok_rows)
        moves.append((piece, all_ref.at[:, pl.ds(at, tok_rows), :]))
    for i in range(2):
        moves.append((w_qkv_hbm.at[:, pl.ds(C_TOK * (i + 1), C_TOK)], w_kv_ref.at[i]))
    return moves


def project(copies, w_kv_ref, all_ref, keys_ref, values_ref):
    batch = all_ref.shape[0]
    for copy in copies[:-1]:
        copy.wait()
    for which, to_ref in enumerate((keys_ref, values_ref)):
        if which == 1:
            copies[-1].wait()
        for n in range(0, C_TOK, 256):
            for s in range(batch):
                to_ref[s, :, n : n + 256] = nn(
                    all_ref[s], w_kv_ref[which, :, n : n + 256]
                ).astype(bf16)


def windows(pair):
    low, high = WINDOWS[pair % 4]
    return 384 * (pair // 4) + low, 384 * (pair // 4) + high


def attend(bias_ref, queries_ref, keys_ref, values_ref, probs_ref, att_ref, done=None):
    batch, keys_all = keys_ref.shape[0], keys_ref.shape[1]
    tok_rows = queries_ref.shape[0] // batch
    masks = head_masks(tok_rows)
    factor = HD ** (-0.5)

    for s in range(batch):
        at = s * tok_rows
        for pair in range(PAIRS):
            low, high = windows(pair)
            queries = two_heads(queries_ref[pl.ds(at, tok_rows), low:high], masks[pair % 4])
            probs_ref[s, pair] = nt(keys_ref[s, :, low:high], queries)
        for pair in range(PAIRS):
            scores = probs_ref[s, pair] * factor
            bias = [bias_ref[k, pair].astype(f32) for k in range(bias_ref.shape[0])]
            scores = scores + jnp.concatenate(bias, axis=0)
            expo = jnp.exp(scores - jnp.max(scores, axis=0, keepdims=True))
            probs_ref[s, pair] = expo * (1.0 / jnp.sum(expo, axis=0, keepdims=True))
        lanes = [jnp.zeros((tok_rows, 128), f32) for _ in range(C_TOK // 128)]
        for pair in range(PAIRS):
            low, high = windows(pair)
            part = tn(probs_ref[s, pair].astype(bf16), values_ref[s, :, low:high])
            first, second = masks[pair % 4]
            mix = jnp.where(first, part[0:tok_rows], 0.0)
            mix = jnp.where(second, part[tok_rows : 2 * tok_rows], mix)
            for t in range((high - low) // 128):
                lanes[low // 128 + t] = lanes[low // 128 + t] + mix[:, 128 * t : 128 * t + 128]
        for t in range(C_TOK // 128):
            att_ref[pl.ds(at, tok_rows), 128 * t : 128 * t + 128] = lanes[t].astype(bf16)
        if done is not None:
            done(s)


def attend_kernel(*refs, count):
    (
        later_hbm, bias_hbm, w_qkv_hbm, cot_hbm, w_down_hbm, att_ref, probs_hbm, values_hbm,
        d_hidden_hbm, later_queries_ref, w_q_ref, w_kv_ref, own_ref, bias_ref, cot_ref, w_down_ref,
        probs_ref, values_ref, d_hidden_ref, sems, all_ref, queries_ref, keys_ref,
    ) = refs[count:]
    batch, tok_rows = all_ref.shape[0], refs[0].shape[1]
    moves = [
        (refs[0], own_ref.at[pl.ds(0, batch)]),
        (later_hbm, own_ref.at[pl.ds(batch, own_ref.shape[0] - batch)]),
        (w_qkv_hbm.at[:, pl.ds(0, C_TOK)], w_q_ref),
    ]
    moves += project_moves(refs[:count], w_qkv_hbm, w_kv_ref, all_ref)
    moves += [(bias_hbm, bias_ref), (cot_hbm, cot_ref), (w_down_hbm, w_down_ref)]
    copies = start_all(moves, sems)
    for copy in copies[0:3]:
        copy.wait()
    own = own_ref[...].reshape(-1, C_TOK)
    split = batch * tok_rows
    for n in range(0, C_TOK, 256):
        queries = nn(own, w_q_ref[:, n : n + 256]).astype(bf16)
        queries_ref[:, n : n + 256] = queries[0:split]
        later_queries_ref[:, n : n + 256] = queries[split:]
    project(copies[3:-3], w_kv_ref, all_ref, keys_ref, values_ref)
    for copy in copies[-3:]:
        copy.wait()
    back = [
        pltpu.make_async_copy(probs_ref.at[s], probs_hbm.at[s], sems.at[s]) for s in range(batch)
    ] + [
        pltpu.make_async_copy(values_ref, values_hbm, sems.at[batch]),
        pltpu.make_async_copy(d_hidden_ref, d_hidden_hbm, sems.at[batch + 1]),
    ]
    back[batch].start()
    cot = cot_ref[...].reshape(-1, C_TOK)
    for n in range(0, w_down_ref.shape[0], 256):
        d_hidden_ref[:, n : n + 256] = nt(cot, w_down_ref[n : n + 256, :])
    back[batch + 1].start()
    attend(
        bias_ref, queries_ref, keys_ref, values_ref, probs_ref, att_ref, lambda s: back[s].start()
    )
    for copy in back:
        copy.wait()


def attend_scratch(batch, tok_rows, keys_all):
    return [
        pltpu.VMEM((batch, keys_all, C_TOK), bf16),
        pltpu.VMEM((batch * tok_rows, C_TOK), bf16),
        pltpu.VMEM((batch, keys_all, C_TOK), bf16),
    ]


def attend_stage(pieces, later, bias, w_qkv, cot, w_down):
    batch, tok_rows, _ = pieces[0].shape
    keys_all = tok_rows * len(pieces)
    vmem = pl.BlockSpec(memory_space=pltpu.VMEM)
    hbm = pl.BlockSpec(memory_space=pl.ANY)
    d_hidden = jax.ShapeDtypeStruct((cot.shape[0] * tok_rows, w_down.shape[0]), f32)
    return pl.pallas_call(
        functools.partial(attend_kernel, count=len(pieces)),
        in_specs=[hbm] * (len(pieces) + 5),
        out_specs=[vmem, hbm, hbm, hbm, vmem],
        out_shape=[
            jax.ShapeDtypeStruct((batch * tok_rows, C_TOK), bf16),
            jax.ShapeDtypeStruct((batch, PAIRS, keys_all, 2 * tok_rows), f32),
            jax.ShapeDtypeStruct((batch, keys_all, C_TOK), bf16),
            d_hidden,
            jax.ShapeDtypeStruct((later.shape[0] * tok_rows, C_TOK), bf16),
        ],
        scratch_shapes=[
            pltpu.VMEM((C_TOK, C_TOK), bf16),
            pltpu.VMEM((2, C_TOK, C_TOK), bf16),
            pltpu.VMEM(cot.shape, bf16),
            pltpu.VMEM(bias.shape, bf16),
            pltpu.VMEM(cot.shape, bf16),
            pltpu.VMEM(w_down.shape, bf16),
            pltpu.VMEM((batch, PAIRS, keys_all, 2 * tok_rows), f32),
            pltpu.VMEM((batch, keys_all, C_TOK), bf16),
            pltpu.VMEM(d_hidden.shape, f32),
            pltpu.SemaphoreType.DMA((8 + len(pieces),)),
        ]
        + attend_scratch(batch, tok_rows, keys_all),
        compiler_params=pltpu.CompilerParams(vmem_limit_bytes=GRANT),
        cost_estimate=pl.CostEstimate(
            flops=4 * 10**9, bytes_accessed=10**7, transcendentals=10**6
        ),
        name="attend",
    )(*pieces, later, bias, w_qkv, cot, w_down)


def token_kernel(*refs, count):
    (
        queries_hbm, bias_hbm, tokens_a_hbm, tokens_b_hbm, att_a_hbm, cot_hbm, probs_a_hbm, values_a_hbm,
        w_qkv_hbm, w_out_hbm, w_gate_hbm, w_up_hbm, d_hidden_hbm,
        resid_hbm, hidden_hbm, d_bias_hbm,
        d_bias_ref, bias_ref, tokens_ref, att_a_ref, cot_ref, resid_ref, hidden_ref,
        w_kv_ref, w_out_ref, w_gate_ref, w_up_ref, d_hidden_ref, probs_ref, values_ref, sems,
        all_ref, queries_ref, keys_ref, grads_ref, d_gate_ref, d_up_ref, hat_ref,
    ) = refs[count:]
    batch, tok_rows = cot_ref.shape[0], cot_ref.shape[1]
    keys_all = values_ref.shape[1]
    rows = batch * tok_rows
    ahead = values_a_hbm.shape[0]
    lead = ahead * tok_rows
    moves = project_moves(refs[:count], w_qkv_hbm, w_kv_ref, all_ref)
    projecting = len(moves)
    moves += [
        (queries_hbm, queries_ref), (bias_hbm, bias_ref), (w_out_hbm, w_out_ref), (att_a_hbm, att_a_ref),
        (tokens_a_hbm, tokens_ref.at[pl.ds(0, ahead)]),
        (tokens_b_hbm, tokens_ref.at[pl.ds(ahead, batch - ahead)]), (cot_hbm, cot_ref),
        (d_hidden_hbm, d_hidden_ref), (w_gate_hbm, w_gate_ref), (w_up_hbm, w_up_ref),
        (values_a_hbm, values_ref.at[pl.ds(0, ahead)]), (probs_a_hbm, probs_ref.at[pl.ds(0, ahead)]),
    ]
    copies = start_all(moves, sems)
    own_values = values_ref.at[pl.ds(ahead, batch - ahead)]
    own_probs = probs_ref.at[pl.ds(ahead, batch - ahead)]
    project(copies[:projecting], w_kv_ref, all_ref, keys_ref, own_values)
    copies[projecting].wait()
    copies = copies[projecting + 1 :]
    copies[0].wait()
    attend(bias_ref, queries_ref, keys_ref, own_values, own_probs, queries_ref)

    for copy in copies[1:5]:
        copy.wait()
    tokens = tokens_ref[...].reshape(rows, C_TOK)
    resid_ref[0:lead, :] = tokens[0:lead] + nn(att_a_ref[...], w_out_ref[...])
    resid_ref[lead:rows, :] = tokens[lead:rows] + nn(queries_ref[...], w_out_ref[...])
    back = [
        pltpu.make_async_copy(resid_ref, resid_hbm, sems.at[0]),
        pltpu.make_async_copy(hidden_ref, hidden_hbm, sems.at[1]),
    ]
    back[0].start()
    hat, rstd = norm_rows(resid_ref[...])
    hat_ref[...] = hat
    grads_ref[...] = hat.astype(bf16)
    for copy in copies[5:9]:
        copy.wait()

    for n in range(0, w_gate_ref.shape[1], 256):
        shaped = grads_ref[...]
        gate = nn(shaped, w_gate_ref[:, n : n + 256])
        up = nn(shaped, w_up_ref[:, n : n + 256])
        d_hidden = d_hidden_ref[:, n : n + 256]
        sig = 1.0 / (1.0 + jnp.exp(-gate))
        act = gate * sig
        hidden_ref[:, n : n + 256] = (act * up).astype(bf16)
        d_gate_ref[:, n : n + 256] = (
            d_hidden * up * sig * (1.0 + gate * (1.0 - sig))
        ).astype(bf16)
        d_up_ref[:, n : n + 256] = (d_hidden * act).astype(bf16)

    back[1].start()
    parts = []
    for n in range(0, C_TOK, 256):
        parts.append(
            nt(d_gate_ref[...], w_gate_ref[n : n + 256, :])
            + nt(d_up_ref[...], w_up_ref[n : n + 256, :])
        )
    d_normed = jnp.concatenate(parts, axis=1)
    hat = hat_ref[...]
    first = jnp.mean(d_normed, axis=-1, keepdims=True)
    second = jnp.mean(d_normed * hat, axis=-1, keepdims=True)
    d_resid = cot_ref[...].reshape(rows, C_TOK).astype(f32) + rstd * (
        d_normed - first - hat * second
    )
    grads_ref[...] = nt(d_resid.astype(bf16), w_out_ref[...]).astype(bf16)
    for copy in copies[9:]:
        copy.wait()
    masks = head_masks(tok_rows)
    for pair in range(PAIRS):
        low, high = windows(pair)
        total = jnp.zeros((keys_all, 2 * tok_rows), f32)
        for s in range(batch):
            grads = two_heads(
                grads_ref[s * tok_rows : (s + 1) * tok_rows, low:high], masks[pair % 4]
            )
            d_probs = nt(values_ref[s, :, low:high], grads)
            probs = probs_ref[s, pair]
            delta = jnp.sum(probs * d_probs, axis=0, keepdims=True)
            total = total + probs * (d_probs - delta)
        size = d_bias_ref.shape[2]
        for k in range(d_bias_ref.shape[0]):
            d_bias_ref[k, pair] = total[size * k : size * (k + 1)].astype(bf16)
        back.append(
            pltpu.make_async_copy(
                d_bias_ref.at[:, pair], d_bias_hbm.at[:, pair], sems.at[2 + pair]
            )
        )
        back[-1].start()
    for copy in back:
        copy.wait()


def token_stage(
    pieces, queries, bias, tokens_a, tokens_b, att_a, cot, probs_a, values_a, w_qkv, w_out, w_gate, w_up,
    d_hidden,
):
    batch, tok_rows, _ = cot.shape
    keys_all = tok_rows * len(pieces)
    rows = batch * tok_rows
    hidden = w_gate.shape[1]
    vmem = pl.BlockSpec(memory_space=pltpu.VMEM)
    hbm = pl.BlockSpec(memory_space=pl.ANY)
    return pl.pallas_call(
        functools.partial(token_kernel, count=len(pieces)),
        in_specs=[hbm] * (len(pieces) + 13),
        out_specs=[hbm, hbm, hbm],
        out_shape=[
            jax.ShapeDtypeStruct((rows, C_TOK), f32),
            jax.ShapeDtypeStruct((rows, hidden), bf16),
            jax.ShapeDtypeStruct(bias.shape, bf16),
        ],
        scratch_shapes=[
            pltpu.VMEM(bias.shape, bf16),
            pltpu.VMEM(bias.shape, bf16),
            pltpu.VMEM(cot.shape, f32),
            pltpu.VMEM(att_a.shape, bf16),
            pltpu.VMEM(cot.shape, bf16),
            pltpu.VMEM((rows, C_TOK), f32),
            pltpu.VMEM((rows, hidden), bf16),
            pltpu.VMEM((2, C_TOK, C_TOK), bf16),
            pltpu.VMEM(w_out.shape, bf16),
            pltpu.VMEM(w_gate.shape, bf16),
            pltpu.VMEM(w_up.shape, bf16),
            pltpu.VMEM(d_hidden.shape, f32),
            pltpu.VMEM((batch, PAIRS, keys_all, 2 * tok_rows), f32),
            pltpu.VMEM((batch, keys_all, C_TOK), bf16),
            pltpu.SemaphoreType.DMA((16 + len(pieces),)),
        ]
        + attend_scratch(pieces[0].shape[0], tok_rows, keys_all)
        + [
            pltpu.VMEM((rows, C_TOK), bf16),
            pltpu.VMEM((rows, hidden), bf16),
            pltpu.VMEM((rows, hidden), bf16),
            pltpu.VMEM((rows, C_TOK), f32),
        ],
        compiler_params=pltpu.CompilerParams(vmem_limit_bytes=GRANT),
        cost_estimate=pl.CostEstimate(
            flops=10**10, bytes_accessed=2 * 10**7, transcendentals=10**6
        ),
        name="tokens",
    )(
        *pieces, queries, bias, tokens_a, tokens_b, att_a, cot, probs_a, values_a, w_qkv, w_out, w_gate,
        w_up, d_hidden,
    )


def output_kernel(
    resid_ref, hidden_ref, w_down_ref, pair_ref, out_ref, hat_ref, rstd_ref, pairf_ref
):
    out_ref[...] = (resid_ref[...] + nn(hidden_ref[...], w_down_ref[...])).astype(bf16)
    rows, keys = pair_ref.shape[0], pair_ref.shape[1]
    for i in range(rows // 8):
        pairf_ref[8 * keys * i : 8 * keys * (i + 1), :] = (
            pair_ref[8 * i : 8 * i + 8].astype(f32).reshape(8 * keys, CZ)
        )

    def norm_step(j, carry):
        hat, rstd = norm_rows(pairf_ref[pl.ds(j, rows, stride=keys), :])
        at = pl.multiple_of(j * rows, rows)
        hat_ref[pl.ds(at, rows), :] = hat
        rstd = jnp.broadcast_to(rstd, (rows, CZ)).T[0:1]
        rstd_ref[pl.ds(j, 1), :] = jnp.concatenate([rstd, rstd], axis=1)
        return carry

    lax.fori_loop(0, keys, norm_step, 0, unroll=4)


def output_stage(resid, hidden, w_down, pair):
    rows, keys = pair.shape[0], pair.shape[1]
    return pl.pallas_call(
        output_kernel,
        out_shape=[jax.ShapeDtypeStruct(resid.shape, bf16)]
        + [
            jax.ShapeDtypeStruct((rows * keys, CZ), f32),
            jax.ShapeDtypeStruct((keys, 2 * rows), f32),
        ],
        scratch_shapes=[pltpu.VMEM((rows * keys, CZ), f32)],
        compiler_params=pltpu.CompilerParams(vmem_limit_bytes=GRANT),
        cost_estimate=pl.CostEstimate(
            flops=10**9, bytes_accessed=8 * 10**6, transcendentals=0
        ),
        name="output",
    )(resid, hidden, w_down, pair)


def grad_kernel(
    parts_hbm, hat_hbm, rstd_hbm, gain_hbm, w_bias_hbm, out_hbm, parts_ref, hat_ref, rstd_ref,
    gain_ref, w_bias_ref, total_ref, out_ref, sems,
):
    keys = parts_ref.shape[2]
    rows = hat_ref.shape[0] // keys
    size = 8 * rows
    moves = [
        (gain_hbm, gain_ref), (w_bias_hbm, w_bias_ref), (parts_hbm, parts_ref),
        (rstd_hbm, rstd_ref),
    ]
    for c in range(keys // 8):
        moves.append((hat_hbm.at[pl.ds(size * c, size)], hat_ref.at[pl.ds(size * c, size)]))
    copies = start_all(moves, sems)
    for copy in copies[0:2]:
        copy.wait()
    weights = jnp.concatenate(split_heads(w_bias_ref[...]), axis=0) * gain_ref[...]
    weights = weights - jnp.mean(weights, axis=-1, keepdims=True)
    weights = jnp.concatenate([weights[0:PAIRS], weights[PAIRS:HEADS]], axis=1)
    w_high = weights.astype(bf16).astype(f32)
    w_middle = (weights - w_high).astype(bf16).astype(f32)
    w_low = weights - w_high - w_middle
    weights = jnp.concatenate([w_high, w_middle, w_low, w_high, w_middle, w_high], axis=0)
    weights = weights.astype(bf16)
    for copy in copies[2:4]:
        copy.wait()
    for pair in range(PAIRS):
        total = parts_ref[0, pair].astype(f32)
        for k in range(1, parts_ref.shape[0]):
            total = total + parts_ref[k, pair].astype(f32)
        total_ref[pair * keys : (pair + 1) * keys, :] = total * rstd_ref[...]
    back = []
    for c in range(keys // 8):
        copies[4 + c].wait()
        for j in range(8 * c, 8 * c + 8):
            total = total_ref[pl.ds(j, PAIRS, stride=keys), :]
            high = total.astype(bf16).astype(f32)
            middle = (total - high).astype(bf16).astype(f32)
            low = total - high - middle
            stack = jnp.concatenate([high, high, high, middle, middle, low], axis=0)
            both = nn(stack.T.astype(bf16), weights)
            scaled = both[0:rows, 0:CZ] + both[rows : 2 * rows, CZ : 2 * CZ]
            hat = hat_ref[rows * j : rows * (j + 1), :]
            second = jnp.mean(scaled * hat, axis=-1, keepdims=True)
            out_ref[pl.ds(size * c + j % 8, rows, stride=8), :] = scaled - hat * second
        back.append(
            pltpu.make_async_copy(
                out_ref.at[pl.ds(size * c, size)].reshape(rows, 8, CZ),
                out_hbm.at[:, pl.ds(8 * c, 8), :],
                sems.at[c],
            )
        )
        back[c].start()
    for copy in back:
        copy.wait()


def pair_back(parts, hat, rstd, pair_gain, w_bias_t):
    keys = parts.shape[2]
    rows = hat.shape[0] // keys
    hbm = pl.BlockSpec(memory_space=pl.ANY)
    return pl.pallas_call(
        grad_kernel,
        in_specs=[hbm] * 5,
        out_specs=hbm,
        out_shape=jax.ShapeDtypeStruct((rows, keys, CZ), f32),
        scratch_shapes=[
            pltpu.VMEM(parts.shape, bf16),
            pltpu.VMEM(hat.shape, f32),
            pltpu.VMEM(rstd.shape, f32),
            pltpu.VMEM((1, CZ), f32),
            pltpu.VMEM(w_bias_t.shape, bf16),
            pltpu.VMEM((keys * PAIRS, 2 * rows), f32),
            pltpu.VMEM((rows * keys, CZ), f32),
            pltpu.SemaphoreType.DMA((4 + keys // 8,)),
        ],
        compiler_params=pltpu.CompilerParams(vmem_limit_bytes=GRANT),
        cost_estimate=pl.CostEstimate(flops=10**8, bytes_accessed=4 * 10**6, transcendentals=0),
        name="pair_grad",
    )(parts, hat, rstd, pair_gain.reshape(1, CZ), w_bias_t)


def swap(values, axis, k):
    return lax.ppermute(values, axis, [(i, i ^ k) for i in range(lax.axis_size(axis))])


def gather(values, axis):
    far = range(lax.axis_size(axis) - 1, 0, -1)
    return [values] + [swap(values, axis, k) for k in far][::-1]


def body(
    atom_feats, atom_counts, atom_mask, token_single, pair, pair_gain, w_bias, w_atom_qkv,
    w_atom_out, w_embed, w_qkv, w_out, w_gate, w_up, w_down, cotangent,
):
    batch, atom_rows, _ = atom_feats.shape
    tok_rows = token_single.shape[0]
    shards = lax.axis_size("tok")
    groups = lax.axis_size("samp")

    w_bias_t = w_bias.T
    local_bias, near, next_ = pair_bias(pair, pair_gain, w_bias_t, atom_feats, groups)
    near = swap(near, "tok", 1)
    steps = [(i, i + 1) for i in range(1, shards - 1, 2)]
    next_ = lax.ppermute(next_, "tok", steps + [(j, i) for i, j in steps])

    bias = lax.all_to_all(local_bias, "samp", 0, 0).reshape(groups, PAIRS, -1, 2 * tok_rows)

    mask = atom_mask.reshape(-1, 128)
    mask, local_bias = lax.optimization_barrier((mask, local_bias))

    each = batch // 2
    tokens, gathered = [], []
    for part in range(2):
        tok, normed = atom_stage(
            part, each, atom_feats, near, next_, mask, atom_counts, token_single, w_atom_qkv,
            w_atom_out, w_embed,
        )
        tokens.append(tok)
        gathered.append(gather(normed, "tok"))
    att_a, probs_a, values_a, d_hidden, queries_b = attend_stage(
        gathered[0], gathered[1][0], bias, w_qkv, cotangent, w_down
    )
    resid, hidden, d_bias = token_stage(
        gathered[1], queries_b, bias, *tokens, att_a, cotangent, probs_a, values_a, w_qkv, w_out, w_gate,
        w_up, d_hidden,
    )
    parts = lax.all_to_all(d_bias, "samp", 0, 0)
    token_out, hat, rstd = output_stage(resid, hidden, w_down, pair)
    pair_grad = pair_back(parts, hat, rstd, pair_gain, w_bias_t)
    token_out = token_out.reshape(batch, tok_rows, C_TOK)
    return (token_out, pair_grad)


def solution(mesh):
    in_specs = (
        P("samp", "tok", None),
        P("tok", None),
        P(),
        P("tok", None),
        P("tok", "samp", None),
        P(), P(), P(), P(), P(), P(), P(), P(), P(), P(),
        P("samp", "tok", None),
    )
    out_specs = (P("samp", "tok", None), P("tok", "samp", None))
    return jax.shard_map(body, mesh=mesh, in_specs=in_specs, out_specs=out_specs, check_vma=False)
```

```python
import functools

import jax
import jax.numpy as jnp
from jax import lax
from jax.experimental import pallas as pl
from jax.experimental.pallas import tpu as pltpu
from jax.sharding import PartitionSpec as P

C_ATOM = 128
ATOM_HEADS = 4
C_TOK = 768
HEADS = 16
ATOM_HD = 32
HD = 48
CZ = 128
HALO = 48
PAIRS = HEADS // 2
GRANT = 64 << 20
LOG2E = 1.4426950408889634

epsilon = 1e-05
f32 = jnp.float32
bf16 = jnp.bfloat16

WINDOWS = ((0, 128), (0, 256), (128, 384), (256, 384))


def nn(a, b):
    return lax.dot_general(a, b, (((1,), (0,)), ((), ())), preferred_element_type=f32)


def nt(a, b):
    return lax.dot_general(a, b, (((1,), (1,)), ((), ())), preferred_element_type=f32)


def tn(a, b):
    return lax.dot_general(a, b, (((0,), (0,)), ((), ())), preferred_element_type=f32)


def start_all(moves, sems):
    copies = [pltpu.make_async_copy(src, dst, sems.at[i]) for i, (src, dst) in enumerate(moves)]
    for copy in copies:
        copy.start()
    return copies


def norm_rows(values):
    center = values - jnp.mean(values, axis=-1, keepdims=True)
    scale_inv = lax.rsqrt(jnp.mean(center * center, axis=-1, keepdims=True) + epsilon)
    return (center * scale_inv, scale_inv)


def iota(shape, dim):
    return lax.broadcasted_iota(jnp.int32, shape, dim)


def pick_heads(parity):
    row, col = iota((PAIRS, HEADS), 0), iota((PAIRS, HEADS), 1)
    return (col == 2 * row + parity).astype(f32).astype(bf16)


def split_heads(w_bias_t):
    return [nn(pick_heads(parity), w_bias_t) for parity in range(2)]


def bias_kernel(
    pair_hbm, gain_hbm, w_bias_hbm, feats_hbm, out_hbm, near_hbm, next_hbm, pair_ref, gain_ref,
    w_bias_ref, scaled_ref, stage_ref, local_ref, head_ref, tail_ref, sems,
):
    rows, keys = pair_ref.shape[0], pair_ref.shape[1]
    atoms = feats_hbm.shape[1]
    part = rows // 4
    stride = scaled_ref.shape[0] // rows
    moves = [
        (gain_hbm, gain_ref), (w_bias_hbm, w_bias_ref),
        (feats_hbm.at[:, pl.ds(0, HALO), :], head_ref),
        (feats_hbm.at[:, pl.ds(atoms - HALO, HALO), :], tail_ref),
    ]
    for i in range(4):
        moves.append((pair_hbm.at[pl.ds(part * i, part)], pair_ref.at[pl.ds(part * i, part)]))
    copies = start_all(moves, sems)
    for copy in copies[0:2]:
        copy.wait()
    gain = gain_ref[...]
    weights = jnp.concatenate(split_heads(w_bias_ref[...]), axis=1).astype(bf16)
    for i in range(rows // 8):
        if 8 * i % part == 0:
            copies[4 + 8 * i // part].wait()
        block = pair_ref[8 * i : 8 * i + 8].astype(f32).reshape(8 * keys, CZ)
        scaled = norm_rows(block)[0] * gain
        for k in range(8):
            at = (8 * i + k) * stride
            scaled_ref[at : at + keys, :] = scaled[keys * k : keys * (k + 1)]
    for copy in copies[2:4]:
        copy.wait()
    even = jnp.where(lax.axis_index("tok") % 2 == 0, 1.0, 0.0)
    head, tail = head_ref[...].astype(f32), tail_ref[...].astype(f32)
    head_ref[...] = (tail * even + head * (1.0 - even)).astype(bf16)
    tail_ref[...] = (head * even + tail * (1.0 - even)).astype(bf16)
    edges = start_all([(head_ref, near_hbm), (tail_ref, next_hbm)], sems)
    blank = jnp.zeros((rows, CZ), bf16)
    for j in range(keys):
        block = scaled_ref[pl.ds(j, rows, stride=stride), :].astype(bf16)
        both = jnp.concatenate(
            [jnp.concatenate([block, blank], axis=1), jnp.concatenate([blank, block], axis=1)],
            axis=0,
        )
        stage_ref[pl.ds(j, PAIRS, stride=keys), :] = nt(weights, both)
    local_ref[...] = stage_ref[...].astype(bf16)
    back = [
        pltpu.make_async_copy(local_ref, out_hbm.at[k], sems.at[2 + k])
        for k in range(out_hbm.shape[0])
    ]
    for copy in back:
        copy.start()
    for copy in edges + back:
        copy.wait()


def pair_bias(pair, pair_gain, w_bias_t, feats, copies):
    rows, keys = pair.shape[0], pair.shape[1]
    edge = jax.ShapeDtypeStruct((feats.shape[0], HALO, C_ATOM), bf16)
    hbm = pl.BlockSpec(memory_space=pl.ANY)
    return pl.pallas_call(
        bias_kernel,
        in_specs=[hbm] * 4,
        out_specs=[hbm] * 3,
        out_shape=[
            jax.ShapeDtypeStruct((copies, keys * PAIRS, 2 * rows), bf16), edge, edge,
        ],
        scratch_shapes=[
            pltpu.VMEM(pair.shape, bf16),
            pltpu.VMEM((1, CZ), f32),
            pltpu.VMEM(w_bias_t.shape, bf16),
            pltpu.VMEM((rows * (keys + 8), CZ), f32),
            pltpu.VMEM((keys * PAIRS, 2 * rows), f32),
            pltpu.VMEM((keys * PAIRS, 2 * rows), bf16),
            pltpu.VMEM(edge.shape, bf16),
            pltpu.VMEM(edge.shape, bf16),
            pltpu.SemaphoreType.DMA((8 + copies,)),
        ],
        compiler_params=pltpu.CompilerParams(vmem_limit_bytes=GRANT),
        cost_estimate=pl.CostEstimate(flops=10**7, bytes_accessed=10**7, transcendentals=0),
        name="pair_bias",
    )(pair, pair_gain.reshape(1, CZ), w_bias_t, feats)


def atom_kernel(
    feats_hbm, near_hbm, next_hbm, mask_hbm, counts_hbm, single_hbm, w_qkv_hbm, w_out_hbm,
    w_embed_hbm, tokens_ref, normed_ref, mask_ref, counts_ref, single_ref, w_qkv_ref, w_out_ref,
    w_embed_ref, sems, halos_ref, padded_ref, normed_atoms_ref, qkv_a, qkv_b, scores_a, scores_b,
    probs_a, probs_b, mixed_a, mixed_b,
    updated_ref, split_ref, keybias_ref, onehot_ref, *, first,
):
    batch, atoms = tokens_ref.shape[0], feats_hbm.shape[1]
    padded = atoms + 2 * HALO
    moves = [(counts_hbm, counts_ref), (mask_hbm, mask_ref), (w_qkv_hbm, w_qkv_ref)]
    for s in range(batch):
        moves.append((near_hbm.at[first + s], halos_ref.at[0, s]))
        moves.append((feats_hbm.at[first + s], padded_ref.at[s, pl.ds(HALO, atoms)]))
        moves.append((next_hbm.at[first + s], halos_ref.at[1, s]))
    moves += [(w_out_hbm, w_out_ref), (w_embed_hbm, w_embed_ref), (single_hbm, single_ref)]
    copies = start_all(moves, sems)
    for copy in copies[0:2]:
        copy.wait()
    tok_rows = single_ref.shape[0]
    blocks = atoms // 128
    chunks = atoms // 256
    qkv_refs, mixed_refs = (qkv_a, qkv_b), (mixed_a, mixed_b)

    eye = iota((128, 128), 0) == iota((128, 128), 1)
    for b in range(-1, blocks + 1):
        at = lax.axis_index("tok") * blocks + b
        inside = jnp.where((at >= 0) & (at < mask_ref.shape[0]), 1, 0)
        row = mask_ref[pl.ds(jnp.clip(at, 0, mask_ref.shape[0] - 1), 1), :] * inside
        row = jnp.broadcast_to(row.astype(f32), (128, 128))
        col = jnp.sum(jnp.where(eye, row, 0.0), axis=1, keepdims=True)
        col = jnp.broadcast_to((col - 1.0) * 1e30, (128, 128))
        if b < 0:
            keybias_ref[0:HALO, :] = col[128 - HALO : 128]
        elif b < blocks:
            keybias_ref[HALO + 128 * b : HALO + 128 * b + 128, :] = col
        else:
            keybias_ref[HALO + atoms : padded, :] = col[0:HALO]
    counts = jnp.broadcast_to(counts_ref[...].astype(f32), (tok_rows, tok_rows))
    sub, lane = iota((tok_rows, tok_rows), 0), iota((tok_rows, tok_rows), 1)
    start = jnp.sum(jnp.where(lane < sub, counts, 0.0), axis=1, keepdims=True)
    own = jnp.sum(jnp.where(lane == sub, counts, 0.0), axis=1, keepdims=True)
    pos = iota((tok_rows, 256), 1).astype(f32)
    for g in range(chunks):
        at = pos + float(g * 256)
        hit = jnp.where((at >= start) & (at < start + own), 1.0, 0.0).astype(bf16)
        onehot_ref[:, 256 * g : 256 * g + 256] = hit
        onehot_ref[:, atoms + 256 * g : atoms + 256 * g + 256] = hit
    head_of = iota((32, 128), 1) // ATOM_HD
    head_mask = [(head_of == h).astype(f32).astype(bf16) for h in range(ATOM_HEADS)]
    own_atom = (iota((32, 128), 1) % 32) == iota((32, 128), 0)
    factor = ATOM_HD ** (-0.5) * LOG2E
    def qkv_step(s):
        for low in range(0, padded, padded // 4):
            part = slice(low, low + padded // 4)
            normed, unused = norm_rows(padded_ref[s, part, :].astype(f32))
            normed_atoms_ref[part, :] = normed.astype(bf16)
        qkv_refs[s % 2][...] = nn(normed_atoms_ref[...], w_qkv_ref[...]).astype(bf16)

    def score_step(s, group, to_ref):
        qkv_ref = qkv_refs[s % 2]
        for k in range(2):
            base = group * 128 + 64 * k
            queries = qkv_ref[pl.ds(base + HALO, 64), 0:C_ATOM]
            spread = jnp.concatenate(
                [
                    queries[32 * w : 32 * w + 32] * head_mask[h]
                    for w in range(2)
                    for h in range(ATOM_HEADS)
                ],
                axis=0,
            )
            to_ref[k] = nt(qkv_ref[pl.ds(base, 160), C_ATOM : 2 * C_ATOM], spread)

    def softmax_step(group, from_ref, to_ref):
        for k in range(2):
            base = group * 128 + 64 * k
            for w in range(2):
                keybias = keybias_ref[pl.ds(base + 32 * w, 128), :]
                keybias = jnp.concatenate(
                    [keybias[0:48], jnp.where(own_atom, 0.0, keybias[48:80]), keybias[80:128]],
                    axis=0,
                )
                scores = from_ref[k, 32 * w : 32 * w + 128, 128 * w : 128 * w + 128] + keybias
                expo = jnp.exp2((scores - jnp.max(scores, axis=0, keepdims=True)) * factor)
                weights = expo * (1.0 / jnp.sum(expo, axis=0, keepdims=True))
                to_ref[2 * k + w] = weights.astype(bf16)

    def value_step(s, group, from_ref):
        qkv_ref = qkv_refs[s % 2]
        for k in range(2):
            base = group * 128 + 64 * k
            mixes = []
            for w in range(2):
                values = qkv_ref[pl.ds(base + 32 * w, 128), 2 * C_ATOM : 3 * C_ATOM]
                part = tn(from_ref[2 * k + w], values)
                mix = part[0:32]
                for h in range(1, ATOM_HEADS):
                    mix = jnp.where(head_of == h, part[32 * h : 32 * h + 32], mix)
                mixes.append(mix.astype(bf16))
            mixed_refs[s % 2][pl.ds(base, 64), :] = jnp.concatenate(mixes, axis=0)

    def embed_step(s, part):
        if part == 0:
            feats = padded_ref[s, HALO : HALO + atoms, :].astype(f32)
            mixed = mixed_refs[s % 2][...]
            updated_ref[...] = (feats + nn(mixed, w_out_ref[...])).astype(bf16)
        elif part < 4:
            cols = slice(256 * (part - 1), 256 * part)
            embedded = jnp.maximum(nn(updated_ref[...], w_embed_ref[:, cols]), 0.0)
            high = embedded.astype(bf16)
            split_ref[0:atoms, cols] = high
            split_ref[atoms : 2 * atoms, cols] = (embedded - high.astype(f32)).astype(bf16)
        else:
            pooled = nn(onehot_ref[...], split_ref[...])
            tokens = pooled / own + single_ref[...].astype(f32)
            tokens_ref[s] = tokens
            normed_ref[s] = norm_rows(tokens)[0].astype(bf16)

    for copy in copies[2:]:
        copy.wait()
    even = jnp.where(lax.axis_index("tok") % 2 == 0, 1.0, 0.0)
    near, after = halos_ref[0].astype(f32), halos_ref[1].astype(f32)
    padded_ref[:, 0:HALO, :] = (after * even + near * (1.0 - even)).astype(bf16)
    padded_ref[:, HALO + atoms : padded, :] = (near * even + after * (1.0 - even)).astype(bf16)
    qkv_step(0)
    for s in range(batch):
        score_step(s, 0, scores_a)

        for i in range(chunks):
            even, odd = 2 * i, 2 * i + 1
            score_step(s, odd, scores_b)
            softmax_step(even, scores_a, probs_a)
            if even > 0:
                value_step(s, even - 1, probs_b)
            if odd + 1 < 2 * chunks:
                score_step(s, odd + 1, scores_a)
            softmax_step(odd, scores_b, probs_b)
            value_step(s, even, probs_a)
            if s > 0:
                embed_step(s - 1, i)
            if s + 1 < batch and i == chunks // 2:
                qkv_step(s + 1)
        value_step(s, 2 * chunks - 1, probs_b)
    for part in range(5):
        embed_step(batch - 1, part)


def atom_stage(part, batch, feats, near, next_, mask, counts, single, w_qkv, w_out, w_embed):
    atoms = feats.shape[1]
    tok_rows = single.shape[0]
    padded = atoms + 2 * HALO
    return pl.pallas_call(
        functools.partial(atom_kernel, first=part * batch),
        in_specs=[pl.BlockSpec(memory_space=pl.ANY)] * 9,
        out_specs=[pl.BlockSpec(memory_space=pltpu.VMEM)] * 2,
        out_shape=[
            jax.ShapeDtypeStruct((batch, tok_rows, C_TOK), f32),
            jax.ShapeDtypeStruct((batch, tok_rows, C_TOK), bf16),
        ],
        scratch_shapes=[
            pltpu.VMEM(mask.shape, jnp.int32),
            pltpu.VMEM(counts.shape, jnp.int32),
            pltpu.VMEM(single.shape, bf16),
            pltpu.VMEM(w_qkv.shape, bf16),
            pltpu.VMEM(w_out.shape, bf16),
            pltpu.VMEM(w_embed.shape, bf16),
            pltpu.SemaphoreType.DMA((6 + 3 * batch,)),
            pltpu.VMEM((2, batch, HALO, C_ATOM), bf16),
            pltpu.VMEM((batch, padded, C_ATOM), bf16),
            pltpu.VMEM((padded, C_ATOM), bf16),
            pltpu.VMEM((padded, 3 * C_ATOM), bf16),
            pltpu.VMEM((padded, 3 * C_ATOM), bf16),
            pltpu.VMEM((2, 160, 256), f32),
            pltpu.VMEM((2, 160, 256), f32),
            pltpu.VMEM((4, 128, 128), bf16),
            pltpu.VMEM((4, 128, 128), bf16),
            pltpu.VMEM((atoms, C_ATOM), bf16),
            pltpu.VMEM((atoms, C_ATOM), bf16),
            pltpu.VMEM((atoms, C_ATOM), bf16),
            pltpu.VMEM((2 * atoms, C_TOK), bf16),
            pltpu.VMEM((padded, 128), f32),
            pltpu.VMEM((tok_rows, 2 * atoms), bf16),
        ],
        compiler_params=pltpu.CompilerParams(vmem_limit_bytes=GRANT),
        cost_estimate=pl.CostEstimate(
            flops=10**10, bytes_accessed=4 * 10**6, transcendentals=3 * 10**6
        ),
        name="atoms",
    )(feats, near, next_, mask, counts, single, w_qkv, w_out, w_embed)


def head_masks(rows):
    masks = []
    for pair in range(4):
        low, high = WINDOWS[pair]
        lane = iota((rows, high - low), 1) + low
        first = 2 * pair * HD
        masks.append(
            [(lane >= first + HD * k) & (lane < first + HD * (k + 1)) for k in range(2)]
        )
    return masks


def two_heads(block, masks):
    blank = jnp.zeros_like(block)
    return jnp.concatenate([jnp.where(mask, block, blank) for mask in masks], axis=0)


def project_moves(piece_hbms, w_qkv_hbm, w_kv_ref, all_ref):
    tok_rows = piece_hbms[0].shape[1]
    here = lax.axis_index("tok")
    moves = []
    for k, piece in enumerate(piece_hbms):
        at = pl.multiple_of((here ^ k) * tok_rows, tok_rows)
        moves.append((piece, all_ref.at[:, pl.ds(at, tok_rows), :]))
    for i in range(2):
        moves.append((w_qkv_hbm.at[:, pl.ds(C_TOK * (i + 1), C_TOK)], w_kv_ref.at[i]))
    return moves


def project(copies, w_kv_ref, all_ref, keys_ref, values_ref):
    batch = all_ref.shape[0]
    for copy in copies[:-1]:
        copy.wait()
    for which, to_ref in enumerate((keys_ref, values_ref)):
        if which == 1:
            copies[-1].wait()
        for n in range(0, C_TOK, 256):
            for s in range(batch):
                to_ref[s, :, n : n + 256] = nn(
                    all_ref[s], w_kv_ref[which, :, n : n + 256]
                ).astype(bf16)


def windows(pair):
    low, high = WINDOWS[pair % 4]
    return 384 * (pair // 4) + low, 384 * (pair // 4) + high


def attend(bias_ref, queries_ref, keys_ref, values_ref, probs_ref, att_ref, done=None):
    batch, keys_all = keys_ref.shape[0], keys_ref.shape[1]
    tok_rows = queries_ref.shape[0] // batch
    masks = head_masks(tok_rows)
    factor = HD ** (-0.5)

    for s in range(batch):
        at = s * tok_rows
        for pair in range(PAIRS):
            low, high = windows(pair)
            queries = two_heads(queries_ref[pl.ds(at, tok_rows), low:high], masks[pair % 4])
            probs_ref[s, pair] = nt(keys_ref[s, :, low:high], queries)
        for pair in range(PAIRS):
            scores = probs_ref[s, pair] * factor
            bias = [bias_ref[k, pair].astype(f32) for k in range(bias_ref.shape[0])]
            scores = scores + jnp.concatenate(bias, axis=0)
            expo = jnp.exp(scores - jnp.max(scores, axis=0, keepdims=True))
            probs_ref[s, pair] = expo * (1.0 / jnp.sum(expo, axis=0, keepdims=True))
        lanes = [jnp.zeros((tok_rows, 128), f32) for _ in range(C_TOK // 128)]
        for pair in range(PAIRS):
            low, high = windows(pair)
            part = tn(probs_ref[s, pair].astype(bf16), values_ref[s, :, low:high])
            first, second = masks[pair % 4]
            mix = jnp.where(first, part[0:tok_rows], 0.0)
            mix = jnp.where(second, part[tok_rows : 2 * tok_rows], mix)
            for t in range((high - low) // 128):
                lanes[low // 128 + t] = lanes[low // 128 + t] + mix[:, 128 * t : 128 * t + 128]
        for t in range(C_TOK // 128):
            att_ref[pl.ds(at, tok_rows), 128 * t : 128 * t + 128] = lanes[t].astype(bf16)
        if done is not None:
            done(s)


def attend_kernel(*refs, count):
    (
        later_hbm, bias_hbm, w_qkv_hbm, cot_hbm, w_down_hbm, att_ref, probs_hbm, values_hbm,
        d_hidden_hbm, later_queries_ref, w_q_ref, w_kv_ref, own_ref, bias_ref, cot_ref, w_down_ref,
        probs_ref, values_ref, d_hidden_ref, sems, all_ref, queries_ref, keys_ref,
    ) = refs[count:]
    batch, tok_rows = all_ref.shape[0], refs[0].shape[1]
    moves = [
        (refs[0], own_ref.at[pl.ds(0, batch)]),
        (later_hbm, own_ref.at[pl.ds(batch, own_ref.shape[0] - batch)]),
        (w_qkv_hbm.at[:, pl.ds(0, C_TOK)], w_q_ref),
    ]
    moves += project_moves(refs[:count], w_qkv_hbm, w_kv_ref, all_ref)
    moves += [(bias_hbm, bias_ref), (cot_hbm, cot_ref), (w_down_hbm, w_down_ref)]
    copies = start_all(moves, sems)
    for copy in copies[0:3]:
        copy.wait()
    own = own_ref[...].reshape(-1, C_TOK)
    split = batch * tok_rows
    for n in range(0, C_TOK, 256):
        queries = nn(own, w_q_ref[:, n : n + 256]).astype(bf16)
        queries_ref[:, n : n + 256] = queries[0:split]
        later_queries_ref[:, n : n + 256] = queries[split:]
    project(copies[3:-3], w_kv_ref, all_ref, keys_ref, values_ref)
    for copy in copies[-3:]:
        copy.wait()
    back = [
        pltpu.make_async_copy(probs_ref.at[s], probs_hbm.at[s], sems.at[s]) for s in range(batch)
    ] + [
        pltpu.make_async_copy(values_ref, values_hbm, sems.at[batch]),
        pltpu.make_async_copy(d_hidden_ref, d_hidden_hbm, sems.at[batch + 1]),
    ]
    back[batch].start()
    cot = cot_ref[...].reshape(-1, C_TOK)
    for n in range(0, w_down_ref.shape[0], 256):
        d_hidden_ref[:, n : n + 256] = nt(cot, w_down_ref[n : n + 256, :])
    back[batch + 1].start()
    attend(
        bias_ref, queries_ref, keys_ref, values_ref, probs_ref, att_ref, lambda s: back[s].start()
    )
    for copy in back:
        copy.wait()


def attend_scratch(batch, tok_rows, keys_all):
    return [
        pltpu.VMEM((batch, keys_all, C_TOK), bf16),
        pltpu.VMEM((batch * tok_rows, C_TOK), bf16),
        pltpu.VMEM((batch, keys_all, C_TOK), bf16),
    ]


def attend_stage(pieces, later, bias, w_qkv, cot, w_down):
    batch, tok_rows, _ = pieces[0].shape
    keys_all = tok_rows * len(pieces)
    vmem = pl.BlockSpec(memory_space=pltpu.VMEM)
    hbm = pl.BlockSpec(memory_space=pl.ANY)
    d_hidden = jax.ShapeDtypeStruct((cot.shape[0] * tok_rows, w_down.shape[0]), f32)
    return pl.pallas_call(
        functools.partial(attend_kernel, count=len(pieces)),
        in_specs=[hbm] * (len(pieces) + 5),
        out_specs=[vmem, hbm, hbm, hbm, vmem],
        out_shape=[
            jax.ShapeDtypeStruct((batch * tok_rows, C_TOK), bf16),
            jax.ShapeDtypeStruct((batch, PAIRS, keys_all, 2 * tok_rows), f32),
            jax.ShapeDtypeStruct((batch, keys_all, C_TOK), bf16),
            d_hidden,
            jax.ShapeDtypeStruct((later.shape[0] * tok_rows, C_TOK), bf16),
        ],
        scratch_shapes=[
            pltpu.VMEM((C_TOK, C_TOK), bf16),
            pltpu.VMEM((2, C_TOK, C_TOK), bf16),
            pltpu.VMEM(cot.shape, bf16),
            pltpu.VMEM(bias.shape, bf16),
            pltpu.VMEM(cot.shape, bf16),
            pltpu.VMEM(w_down.shape, bf16),
            pltpu.VMEM((batch, PAIRS, keys_all, 2 * tok_rows), f32),
            pltpu.VMEM((batch, keys_all, C_TOK), bf16),
            pltpu.VMEM(d_hidden.shape, f32),
            pltpu.SemaphoreType.DMA((8 + len(pieces),)),
        ]
        + attend_scratch(batch, tok_rows, keys_all),
        compiler_params=pltpu.CompilerParams(vmem_limit_bytes=GRANT),
        cost_estimate=pl.CostEstimate(
            flops=4 * 10**9, bytes_accessed=10**7, transcendentals=10**6
        ),
        name="attend",
    )(*pieces, later, bias, w_qkv, cot, w_down)


def token_kernel(*refs, count):
    (
        queries_hbm, bias_hbm, tokens_a_hbm, tokens_b_hbm, att_a_hbm, cot_hbm, probs_a_hbm, values_a_hbm,
        w_qkv_hbm, w_out_hbm, w_gate_hbm, w_up_hbm, d_hidden_hbm,
        resid_hbm, hidden_hbm, d_bias_hbm,
        d_bias_ref, bias_ref, tokens_ref, att_a_ref, cot_ref, resid_ref, hidden_ref,
        w_kv_ref, w_out_ref, w_gate_ref, w_up_ref, d_hidden_ref, probs_ref, values_ref, sems,
        all_ref, queries_ref, keys_ref, grads_ref, d_gate_ref, d_up_ref, hat_ref,
    ) = refs[count:]
    batch, tok_rows = cot_ref.shape[0], cot_ref.shape[1]
    keys_all = values_ref.shape[1]
    rows = batch * tok_rows
    ahead = values_a_hbm.shape[0]
    lead = ahead * tok_rows
    moves = project_moves(refs[:count], w_qkv_hbm, w_kv_ref, all_ref)
    projecting = len(moves)
    moves += [
        (queries_hbm, queries_ref), (bias_hbm, bias_ref), (w_out_hbm, w_out_ref), (att_a_hbm, att_a_ref),
        (tokens_a_hbm, tokens_ref.at[pl.ds(0, ahead)]),
        (tokens_b_hbm, tokens_ref.at[pl.ds(ahead, batch - ahead)]), (cot_hbm, cot_ref),
        (d_hidden_hbm, d_hidden_ref), (w_gate_hbm, w_gate_ref), (w_up_hbm, w_up_ref),
        (values_a_hbm, values_ref.at[pl.ds(0, ahead)]), (probs_a_hbm, probs_ref.at[pl.ds(0, ahead)]),
    ]
    copies = start_all(moves, sems)
    own_values = values_ref.at[pl.ds(ahead, batch - ahead)]
    own_probs = probs_ref.at[pl.ds(ahead, batch - ahead)]
    project(copies[:projecting], w_kv_ref, all_ref, keys_ref, own_values)
    copies[projecting].wait()
    copies = copies[projecting + 1 :]
    copies[0].wait()
    attend(bias_ref, queries_ref, keys_ref, own_values, own_probs, queries_ref)

    for copy in copies[1:5]:
        copy.wait()
    tokens = tokens_ref[...].reshape(rows, C_TOK)
    resid_ref[0:lead, :] = tokens[0:lead] + nn(att_a_ref[...], w_out_ref[...])
    resid_ref[lead:rows, :] = tokens[lead:rows] + nn(queries_ref[...], w_out_ref[...])
    back = [
        pltpu.make_async_copy(resid_ref, resid_hbm, sems.at[0]),
        pltpu.make_async_copy(hidden_ref, hidden_hbm, sems.at[1]),
    ]
    back[0].start()
    hat, rstd = norm_rows(resid_ref[...])
    hat_ref[...] = hat
    grads_ref[...] = hat.astype(bf16)
    for copy in copies[5:9]:
        copy.wait()

    for n in range(0, w_gate_ref.shape[1], 256):
        shaped = grads_ref[...]
        gate = nn(shaped, w_gate_ref[:, n : n + 256])
        up = nn(shaped, w_up_ref[:, n : n + 256])
        d_hidden = d_hidden_ref[:, n : n + 256]
        sig = 1.0 / (1.0 + jnp.exp(-gate))
        act = gate * sig
        hidden_ref[:, n : n + 256] = (act * up).astype(bf16)
        d_gate_ref[:, n : n + 256] = (
            d_hidden * up * sig * (1.0 + gate * (1.0 - sig))
        ).astype(bf16)
        d_up_ref[:, n : n + 256] = (d_hidden * act).astype(bf16)

    back[1].start()
    parts = []
    for n in range(0, C_TOK, 256):
        parts.append(
            nt(d_gate_ref[...], w_gate_ref[n : n + 256, :])
            + nt(d_up_ref[...], w_up_ref[n : n + 256, :])
        )
    d_normed = jnp.concatenate(parts, axis=1)
    hat = hat_ref[...]
    first = jnp.mean(d_normed, axis=-1, keepdims=True)
    second = jnp.mean(d_normed * hat, axis=-1, keepdims=True)
    d_resid = cot_ref[...].reshape(rows, C_TOK).astype(f32) + rstd * (
        d_normed - first - hat * second
    )
    grads_ref[...] = nt(d_resid.astype(bf16), w_out_ref[...]).astype(bf16)
    for copy in copies[9:]:
        copy.wait()
    masks = head_masks(tok_rows)
    for pair in range(PAIRS):
        low, high = windows(pair)
        total = jnp.zeros((keys_all, 2 * tok_rows), f32)
        for s in range(batch):
            grads = two_heads(
                grads_ref[s * tok_rows : (s + 1) * tok_rows, low:high], masks[pair % 4]
            )
            d_probs = nt(values_ref[s, :, low:high], grads)
            probs = probs_ref[s, pair]
            delta = jnp.sum(probs * d_probs, axis=0, keepdims=True)
            total = total + probs * (d_probs - delta)
        size = d_bias_ref.shape[2]
        for k in range(d_bias_ref.shape[0]):
            d_bias_ref[k, pair] = total[size * k : size * (k + 1)].astype(bf16)
        back.append(
            pltpu.make_async_copy(
                d_bias_ref.at[:, pair], d_bias_hbm.at[:, pair], sems.at[2 + pair]
            )
        )
        back[-1].start()
    for copy in back:
        copy.wait()


def token_stage(
    pieces, queries, bias, tokens_a, tokens_b, att_a, cot, probs_a, values_a, w_qkv, w_out, w_gate, w_up,
    d_hidden,
):
    batch, tok_rows, _ = cot.shape
    keys_all = tok_rows * len(pieces)
    rows = batch * tok_rows
    hidden = w_gate.shape[1]
    vmem = pl.BlockSpec(memory_space=pltpu.VMEM)
    hbm = pl.BlockSpec(memory_space=pl.ANY)
    return pl.pallas_call(
        functools.partial(token_kernel, count=len(pieces)),
        in_specs=[hbm] * (len(pieces) + 13),
        out_specs=[hbm, hbm, hbm],
        out_shape=[
            jax.ShapeDtypeStruct((rows, C_TOK), f32),
            jax.ShapeDtypeStruct((rows, hidden), bf16),
            jax.ShapeDtypeStruct(bias.shape, bf16),
        ],
        scratch_shapes=[
            pltpu.VMEM(bias.shape, bf16),
            pltpu.VMEM(bias.shape, bf16),
            pltpu.VMEM(cot.shape, f32),
            pltpu.VMEM(att_a.shape, bf16),
            pltpu.VMEM(cot.shape, bf16),
            pltpu.VMEM((rows, C_TOK), f32),
            pltpu.VMEM((rows, hidden), bf16),
            pltpu.VMEM((2, C_TOK, C_TOK), bf16),
            pltpu.VMEM(w_out.shape, bf16),
            pltpu.VMEM(w_gate.shape, bf16),
            pltpu.VMEM(w_up.shape, bf16),
            pltpu.VMEM(d_hidden.shape, f32),
            pltpu.VMEM((batch, PAIRS, keys_all, 2 * tok_rows), f32),
            pltpu.VMEM((batch, keys_all, C_TOK), bf16),
            pltpu.SemaphoreType.DMA((16 + len(pieces),)),
        ]
        + attend_scratch(pieces[0].shape[0], tok_rows, keys_all)
        + [
            pltpu.VMEM((rows, C_TOK), bf16),
            pltpu.VMEM((rows, hidden), bf16),
            pltpu.VMEM((rows, hidden), bf16),
            pltpu.VMEM((rows, C_TOK), f32),
        ],
        compiler_params=pltpu.CompilerParams(vmem_limit_bytes=GRANT),
        cost_estimate=pl.CostEstimate(
            flops=10**10, bytes_accessed=2 * 10**7, transcendentals=10**6
        ),
        name="tokens",
    )(
        *pieces, queries, bias, tokens_a, tokens_b, att_a, cot, probs_a, values_a, w_qkv, w_out, w_gate,
        w_up, d_hidden,
    )


def output_kernel(
    resid_ref, hidden_ref, w_down_ref, pair_ref, out_ref, hat_ref, rstd_ref, pairf_ref
):
    out_ref[...] = (resid_ref[...] + nn(hidden_ref[...], w_down_ref[...])).astype(bf16)
    rows, keys = pair_ref.shape[0], pair_ref.shape[1]
    for i in range(rows // 8):
        pairf_ref[8 * keys * i : 8 * keys * (i + 1), :] = (
            pair_ref[8 * i : 8 * i + 8].astype(f32).reshape(8 * keys, CZ)
        )

    def norm_step(j, carry):
        hat, rstd = norm_rows(pairf_ref[pl.ds(j, rows, stride=keys), :])
        at = pl.multiple_of(j * rows, rows)
        hat_ref[pl.ds(at, rows), :] = hat
        rstd = jnp.broadcast_to(rstd, (rows, CZ)).T[0:1]
        rstd_ref[pl.ds(j, 1), :] = jnp.concatenate([rstd, rstd], axis=1)
        return carry

    lax.fori_loop(0, keys, norm_step, 0, unroll=4)


def output_stage(resid, hidden, w_down, pair):
    rows, keys = pair.shape[0], pair.shape[1]
    return pl.pallas_call(
        output_kernel,
        out_shape=[jax.ShapeDtypeStruct(resid.shape, bf16)]
        + [
            jax.ShapeDtypeStruct((rows * keys, CZ), f32),
            jax.ShapeDtypeStruct((keys, 2 * rows), f32),
        ],
        scratch_shapes=[pltpu.VMEM((rows * keys, CZ), f32)],
        compiler_params=pltpu.CompilerParams(vmem_limit_bytes=GRANT),
        cost_estimate=pl.CostEstimate(
            flops=10**9, bytes_accessed=8 * 10**6, transcendentals=0
        ),
        name="output",
    )(resid, hidden, w_down, pair)


def grad_kernel(
    parts_hbm, hat_hbm, rstd_hbm, gain_hbm, w_bias_hbm, out_hbm, parts_ref, hat_ref, rstd_ref,
    gain_ref, w_bias_ref, total_ref, out_ref, sems,
):
    keys = parts_ref.shape[2]
    rows = hat_ref.shape[0] // keys
    size = 8 * rows
    moves = [
        (gain_hbm, gain_ref), (w_bias_hbm, w_bias_ref), (parts_hbm, parts_ref),
        (rstd_hbm, rstd_ref),
    ]
    for c in range(keys // 8):
        moves.append((hat_hbm.at[pl.ds(size * c, size)], hat_ref.at[pl.ds(size * c, size)]))
    copies = start_all(moves, sems)
    for copy in copies[0:2]:
        copy.wait()
    weights = jnp.concatenate(split_heads(w_bias_ref[...]), axis=0) * gain_ref[...]
    weights = weights - jnp.mean(weights, axis=-1, keepdims=True)
    weights = jnp.concatenate([weights[0:PAIRS], weights[PAIRS:HEADS]], axis=1)
    w_high = weights.astype(bf16).astype(f32)
    w_middle = (weights - w_high).astype(bf16).astype(f32)
    w_low = weights - w_high - w_middle
    weights = jnp.concatenate([w_high, w_middle, w_low, w_high, w_middle, w_high], axis=0)
    weights = weights.astype(bf16)
    for copy in copies[2:4]:
        copy.wait()
    for pair in range(PAIRS):
        total = parts_ref[0, pair].astype(f32)
        for k in range(1, parts_ref.shape[0]):
            total = total + parts_ref[k, pair].astype(f32)
        total_ref[pair * keys : (pair + 1) * keys, :] = total * rstd_ref[...]
    back = []
    for c in range(keys // 8):
        copies[4 + c].wait()
        for j in range(8 * c, 8 * c + 8):
            total = total_ref[pl.ds(j, PAIRS, stride=keys), :]
            high = total.astype(bf16).astype(f32)
            middle = (total - high).astype(bf16).astype(f32)
            low = total - high - middle
            stack = jnp.concatenate([high, high, high, middle, middle, low], axis=0)
            both = nn(stack.T.astype(bf16), weights)
            scaled = both[0:rows, 0:CZ] + both[rows : 2 * rows, CZ : 2 * CZ]
            hat = hat_ref[rows * j : rows * (j + 1), :]
            second = jnp.mean(scaled * hat, axis=-1, keepdims=True)
            out_ref[pl.ds(size * c + j % 8, rows, stride=8), :] = scaled - hat * second
        back.append(
            pltpu.make_async_copy(
                out_ref.at[pl.ds(size * c, size)].reshape(rows, 8, CZ),
                out_hbm.at[:, pl.ds(8 * c, 8), :],
                sems.at[c],
            )
        )
        back[c].start()
    for copy in back:
        copy.wait()


def pair_back(parts, hat, rstd, pair_gain, w_bias_t):
    keys = parts.shape[2]
    rows = hat.shape[0] // keys
    hbm = pl.BlockSpec(memory_space=pl.ANY)
    return pl.pallas_call(
        grad_kernel,
        in_specs=[hbm] * 5,
        out_specs=hbm,
        out_shape=jax.ShapeDtypeStruct((rows, keys, CZ), f32),
        scratch_shapes=[
            pltpu.VMEM(parts.shape, bf16),
            pltpu.VMEM(hat.shape, f32),
            pltpu.VMEM(rstd.shape, f32),
            pltpu.VMEM((1, CZ), f32),
            pltpu.VMEM(w_bias_t.shape, bf16),
            pltpu.VMEM((keys * PAIRS, 2 * rows), f32),
            pltpu.VMEM((rows * keys, CZ), f32),
            pltpu.SemaphoreType.DMA((4 + keys // 8,)),
        ],
        compiler_params=pltpu.CompilerParams(vmem_limit_bytes=GRANT),
        cost_estimate=pl.CostEstimate(flops=10**8, bytes_accessed=4 * 10**6, transcendentals=0),
        name="pair_grad",
    )(parts, hat, rstd, pair_gain.reshape(1, CZ), w_bias_t)


def swap(values, axis, k):
    return lax.ppermute(values, axis, [(i, i ^ k) for i in range(lax.axis_size(axis))])


def gather(values, axis):
    far = range(lax.axis_size(axis) - 1, 0, -1)
    return [values] + [swap(values, axis, k) for k in far][::-1]


def body(
    atom_feats, atom_counts, atom_mask, token_single, pair, pair_gain, w_bias, w_atom_qkv,
    w_atom_out, w_embed, w_qkv, w_out, w_gate, w_up, w_down, cotangent,
):
    batch, atom_rows, _ = atom_feats.shape
    tok_rows = token_single.shape[0]
    shards = lax.axis_size("tok")
    groups = lax.axis_size("samp")

    w_bias_t = w_bias.T
    local_bias, near, next_ = pair_bias(pair, pair_gain, w_bias_t, atom_feats, groups)
    near = swap(near, "tok", 1)
    steps = [(i, i + 1) for i in range(1, shards - 1, 2)]
    next_ = lax.ppermute(next_, "tok", steps + [(j, i) for i, j in steps])

    bias = lax.all_to_all(local_bias, "samp", 0, 0).reshape(groups, PAIRS, -1, 2 * tok_rows)

    mask = atom_mask.reshape(-1, 128)
    mask, local_bias = lax.optimization_barrier((mask, local_bias))

    each = batch // 2
    tokens, gathered = [], []
    for part in range(2):
        tok, normed = atom_stage(
            part, each, atom_feats, near, next_, mask, atom_counts, token_single, w_atom_qkv,
            w_atom_out, w_embed,
        )
        tokens.append(tok)
        gathered.append(gather(normed, "tok"))
    att_a, probs_a, values_a, d_hidden, queries_b = attend_stage(
        gathered[0], gathered[1][0], bias, w_qkv, cotangent, w_down
    )
    resid, hidden, d_bias = token_stage(
        gathered[1], queries_b, bias, *tokens, att_a, cotangent, probs_a, values_a, w_qkv, w_out, w_gate,
        w_up, d_hidden,
    )
    parts = lax.all_to_all(d_bias, "samp", 0, 0)
    token_out, hat, rstd = output_stage(resid, hidden, w_down, pair)
    pair_grad = pair_back(parts, hat, rstd, pair_gain, w_bias_t)
    token_out = token_out.reshape(batch, tok_rows, C_TOK)
    return (token_out, pair_grad)


def solution(mesh):
    in_specs = (
        P("samp", "tok", None),
        P("tok", None),
        P(),
        P("tok", None),
        P("tok", "samp", None),
        P(), P(), P(), P(), P(), P(), P(), P(), P(), P(),
        P("samp", "tok", None),
    )
    out_specs = (P("samp", "tok", None), P("tok", "samp", None))
    return jax.shard_map(body, mesh=mesh, in_specs=in_specs, out_specs=out_specs, check_vma=False)
```

```python
import functools

import jax
import jax.numpy as jnp
from jax import lax
from jax.experimental import pallas as pl
from jax.experimental.pallas import tpu as pltpu
from jax.sharding import PartitionSpec as P

C_ATOM = 128
ATOM_HEADS = 4
C_TOK = 768
HEADS = 16
ATOM_HD = 32
HD = 48
CZ = 128
HALO = 48
PAIRS = HEADS // 2
GRANT = 64 << 20
LOG2E = 1.4426950408889634

epsilon = 1e-05
f32 = jnp.float32
bf16 = jnp.bfloat16

WINDOWS = ((0, 128), (0, 256), (128, 384), (256, 384))


def nn(a, b):
    return lax.dot_general(a, b, (((1,), (0,)), ((), ())), preferred_element_type=f32)


def nt(a, b):
    return lax.dot_general(a, b, (((1,), (1,)), ((), ())), preferred_element_type=f32)


def tn(a, b):
    return lax.dot_general(a, b, (((0,), (0,)), ((), ())), preferred_element_type=f32)


def start_all(moves, sems):
    copies = [pltpu.make_async_copy(src, dst, sems.at[i]) for i, (src, dst) in enumerate(moves)]
    for copy in copies:
        copy.start()
    return copies


def norm_rows(values):
    center = values - jnp.mean(values, axis=-1, keepdims=True)
    scale_inv = lax.rsqrt(jnp.mean(center * center, axis=-1, keepdims=True) + epsilon)
    return (center * scale_inv, scale_inv)


def iota(shape, dim):
    return lax.broadcasted_iota(jnp.int32, shape, dim)


def pick_heads(parity):
    row, col = iota((PAIRS, HEADS), 0), iota((PAIRS, HEADS), 1)
    return (col == 2 * row + parity).astype(f32).astype(bf16)


def split_heads(w_bias_t):
    return [nn(pick_heads(parity), w_bias_t) for parity in range(2)]


def bias_kernel(
    pair_hbm, gain_hbm, w_bias_hbm, feats_hbm, out_hbm, near_hbm, next_hbm, pair_ref, gain_ref,
    w_bias_ref, scaled_ref, stage_ref, local_ref, head_ref, tail_ref, sems,
):
    rows, keys = pair_ref.shape[0], pair_ref.shape[1]
    atoms = feats_hbm.shape[1]
    part = rows // 4
    stride = scaled_ref.shape[0] // rows
    moves = [
        (gain_hbm, gain_ref), (w_bias_hbm, w_bias_ref),
        (feats_hbm.at[:, pl.ds(0, HALO), :], head_ref),
        (feats_hbm.at[:, pl.ds(atoms - HALO, HALO), :], tail_ref),
    ]
    for i in range(4):
        moves.append((pair_hbm.at[pl.ds(part * i, part)], pair_ref.at[pl.ds(part * i, part)]))
    copies = start_all(moves, sems)
    for copy in copies[0:2]:
        copy.wait()
    gain = gain_ref[...]
    weights = jnp.concatenate(split_heads(w_bias_ref[...]), axis=1).astype(bf16)
    for i in range(rows // 8):
        if 8 * i % part == 0:
            copies[4 + 8 * i // part].wait()
        block = pair_ref[8 * i : 8 * i + 8].astype(f32).reshape(8 * keys, CZ)
        scaled = norm_rows(block)[0] * gain
        for k in range(8):
            at = (8 * i + k) * stride
            scaled_ref[at : at + keys, :] = scaled[keys * k : keys * (k + 1)]
    for copy in copies[2:4]:
        copy.wait()
    even = jnp.where(lax.axis_index("tok") % 2 == 0, 1.0, 0.0)
    head, tail = head_ref[...].astype(f32), tail_ref[...].astype(f32)
    head_ref[...] = (tail * even + head * (1.0 - even)).astype(bf16)
    tail_ref[...] = (head * even + tail * (1.0 - even)).astype(bf16)
    edges = start_all([(head_ref, near_hbm), (tail_ref, next_hbm)], sems)
    blank = jnp.zeros((rows, CZ), bf16)
    for j in range(keys):
        block = scaled_ref[pl.ds(j, rows, stride=stride), :].astype(bf16)
        both = jnp.concatenate(
            [jnp.concatenate([block, blank], axis=1), jnp.concatenate([blank, block], axis=1)],
            axis=0,
        )
        stage_ref[pl.ds(j, PAIRS, stride=keys), :] = nt(weights, both)
    local_ref[...] = stage_ref[...].astype(bf16)
    back = [
        pltpu.make_async_copy(local_ref, out_hbm.at[k], sems.at[2 + k])
        for k in range(out_hbm.shape[0])
    ]
    for copy in back:
        copy.start()
    for copy in edges + back:
        copy.wait()


def pair_bias(pair, pair_gain, w_bias_t, feats, copies):
    rows, keys = pair.shape[0], pair.shape[1]
    edge = jax.ShapeDtypeStruct((feats.shape[0], HALO, C_ATOM), bf16)
    hbm = pl.BlockSpec(memory_space=pl.ANY)
    return pl.pallas_call(
        bias_kernel,
        in_specs=[hbm] * 4,
        out_specs=[hbm] * 3,
        out_shape=[
            jax.ShapeDtypeStruct((copies, keys * PAIRS, 2 * rows), bf16), edge, edge,
        ],
        scratch_shapes=[
            pltpu.VMEM(pair.shape, bf16),
            pltpu.VMEM((1, CZ), f32),
            pltpu.VMEM(w_bias_t.shape, bf16),
            pltpu.VMEM((rows * (keys + 8), CZ), f32),
            pltpu.VMEM((keys * PAIRS, 2 * rows), f32),
            pltpu.VMEM((keys * PAIRS, 2 * rows), bf16),
            pltpu.VMEM(edge.shape, bf16),
            pltpu.VMEM(edge.shape, bf16),
            pltpu.SemaphoreType.DMA((8 + copies,)),
        ],
        compiler_params=pltpu.CompilerParams(vmem_limit_bytes=GRANT),
        cost_estimate=pl.CostEstimate(flops=10**7, bytes_accessed=10**7, transcendentals=0),
        name="pair_bias",
    )(pair, pair_gain.reshape(1, CZ), w_bias_t, feats)


def atom_kernel(
    feats_hbm, near_hbm, next_hbm, mask_hbm, counts_hbm, single_hbm, w_qkv_hbm, w_out_hbm,
    w_embed_hbm, tokens_ref, normed_ref, mask_ref, counts_ref, single_ref, w_qkv_ref, w_out_ref,
    w_embed_ref, sems, halos_ref, padded_ref, normed_atoms_ref, qkv_a, qkv_b, scores_a, scores_b,
    probs_a, probs_b, mixed_a, mixed_b,
    updated_ref, split_ref, last_ref, keybias_ref, onehot_ref, *, first,
):
    batch, atoms = tokens_ref.shape[0], feats_hbm.shape[1]
    padded = atoms + 2 * HALO
    moves = [(counts_hbm, counts_ref), (mask_hbm, mask_ref), (w_qkv_hbm, w_qkv_ref)]
    for s in range(batch):
        moves.append((near_hbm.at[first + s], halos_ref.at[0, s]))
        moves.append((feats_hbm.at[first + s], padded_ref.at[s, pl.ds(HALO, atoms)]))
        moves.append((next_hbm.at[first + s], halos_ref.at[1, s]))
    moves += [(w_out_hbm, w_out_ref), (w_embed_hbm, w_embed_ref), (single_hbm, single_ref)]
    copies = start_all(moves, sems)
    for copy in copies[0:2]:
        copy.wait()
    tok_rows = single_ref.shape[0]
    blocks = atoms // 128
    chunks = atoms // 256
    qkv_refs, mixed_refs = (qkv_a, qkv_b), (mixed_a, mixed_b)

    eye = iota((128, 128), 0) == iota((128, 128), 1)
    for b in range(-1, blocks + 1):
        at = lax.axis_index("tok") * blocks + b
        inside = jnp.where((at >= 0) & (at < mask_ref.shape[0]), 1, 0)
        row = mask_ref[pl.ds(jnp.clip(at, 0, mask_ref.shape[0] - 1), 1), :] * inside
        row = jnp.broadcast_to(row.astype(f32), (128, 128))
        col = jnp.sum(jnp.where(eye, row, 0.0), axis=1, keepdims=True)
        col = jnp.broadcast_to((col - 1.0) * 1e30, (128, 128))
        if b < 0:
            keybias_ref[0:HALO, :] = col[128 - HALO : 128]
        elif b < blocks:
            keybias_ref[HALO + 128 * b : HALO + 128 * b + 128, :] = col
        else:
            keybias_ref[HALO + atoms : padded, :] = col[0:HALO]
    counts = jnp.broadcast_to(counts_ref[...].astype(f32), (tok_rows, tok_rows))
    sub, lane = iota((tok_rows, tok_rows), 0), iota((tok_rows, tok_rows), 1)
    start = jnp.sum(jnp.where(lane < sub, counts, 0.0), axis=1, keepdims=True)
    own = jnp.sum(jnp.where(lane == sub, counts, 0.0), axis=1, keepdims=True)
    pos = iota((tok_rows, 256), 1).astype(f32)
    for g in range(chunks):
        at = pos + float(g * 256)
        hit = jnp.where((at >= start) & (at < start + own), 1.0, 0.0).astype(bf16)
        onehot_ref[:, 256 * g : 256 * g + 256] = hit
        onehot_ref[:, atoms + 256 * g : atoms + 256 * g + 256] = hit
    head_of = iota((32, 128), 1) // ATOM_HD
    head_mask = [(head_of == h).astype(f32).astype(bf16) for h in range(ATOM_HEADS)]
    own_atom = (iota((32, 128), 1) % 32) == iota((32, 128), 0)
    factor = ATOM_HD ** (-0.5) * LOG2E
    def qkv_step(s):
        for low in range(0, padded, padded // 4):
            part = slice(low, low + padded // 4)
            normed, unused = norm_rows(padded_ref[s, part, :].astype(f32))
            normed_atoms_ref[part, :] = normed.astype(bf16)
        qkv_refs[s % 2][...] = nn(normed_atoms_ref[...], w_qkv_ref[...]).astype(bf16)

    def score_step(s, group, to_ref):
        qkv_ref = qkv_refs[s % 2]
        for k in range(2):
            base = group * 128 + 64 * k
            queries = qkv_ref[pl.ds(base + HALO, 64), 0:C_ATOM]
            spread = jnp.concatenate(
                [
                    queries[32 * w : 32 * w + 32] * head_mask[h]
                    for w in range(2)
                    for h in range(ATOM_HEADS)
                ],
                axis=0,
            )
            to_ref[k] = nt(qkv_ref[pl.ds(base, 160), C_ATOM : 2 * C_ATOM], spread)

    def softmax_step(group, from_ref, to_ref):
        for k in range(2):
            base = group * 128 + 64 * k
            for w in range(2):
                keybias = keybias_ref[pl.ds(base + 32 * w, 128), :]
                keybias = jnp.concatenate(
                    [keybias[0:48], jnp.where(own_atom, 0.0, keybias[48:80]), keybias[80:128]],
                    axis=0,
                )
                scores = from_ref[k, 32 * w : 32 * w + 128, 128 * w : 128 * w + 128] + keybias
                expo = jnp.exp2((scores - jnp.max(scores, axis=0, keepdims=True)) * factor)
                weights = expo * (1.0 / jnp.sum(expo, axis=0, keepdims=True))
                to_ref[2 * k + w] = weights.astype(bf16)

    def value_step(s, group, from_ref):
        qkv_ref = qkv_refs[s % 2]
        for k in range(2):
            base = group * 128 + 64 * k
            mixes = []
            for w in range(2):
                values = qkv_ref[pl.ds(base + 32 * w, 128), 2 * C_ATOM : 3 * C_ATOM]
                part = tn(from_ref[2 * k + w], values)
                mix = part[0:32]
                for h in range(1, ATOM_HEADS):
                    mix = jnp.where(head_of == h, part[32 * h : 32 * h + 32], mix)
                mixes.append(mix.astype(bf16))
            mixed_refs[s % 2][pl.ds(base, 64), :] = jnp.concatenate(mixes, axis=0)

    def embed_step(s, part):
        if part == 0:
            feats = padded_ref[s, HALO : HALO + atoms, :].astype(f32)
            mixed = mixed_refs[s % 2][...]
            updated_ref[...] = (feats + nn(mixed, w_out_ref[...])).astype(bf16)
        elif part < 4:
            cols = slice(256 * (part - 1), 256 * part)
            embedded = jnp.maximum(nn(updated_ref[...], w_embed_ref[:, cols]), 0.0)
            high = embedded.astype(bf16)
            split_ref[0:atoms, cols] = high
            split_ref[atoms : 2 * atoms, cols] = (embedded - high.astype(f32)).astype(bf16)
        else:
            pooled = nn(onehot_ref[...], (last_ref if s + 1 == batch else split_ref)[...])
            tokens = pooled / own + single_ref[...].astype(f32)
            tokens_ref[s] = tokens
            normed_ref[s] = norm_rows(tokens)[0].astype(bf16)

    def embed_rows(s, g):
        rows = slice(256 * g, 256 * g + 256)
        feats = padded_ref[s, HALO + 256 * g : HALO + 256 * g + 256, :].astype(f32)
        updated = (feats + nn(mixed_refs[s % 2][rows, :], w_out_ref[...])).astype(bf16)
        embedded = jnp.maximum(nn(updated, w_embed_ref[...]), 0.0)
        high = embedded.astype(bf16)
        last_ref[rows, :] = high
        last_ref[atoms + 256 * g : atoms + 256 * g + 256, :] = (
            embedded - high.astype(f32)
        ).astype(bf16)

    for copy in copies[2:]:
        copy.wait()
    even = jnp.where(lax.axis_index("tok") % 2 == 0, 1.0, 0.0)
    near, after = halos_ref[0].astype(f32), halos_ref[1].astype(f32)
    padded_ref[:, 0:HALO, :] = (after * even + near * (1.0 - even)).astype(bf16)
    padded_ref[:, HALO + atoms : padded, :] = (near * even + after * (1.0 - even)).astype(bf16)
    qkv_step(0)
    for s in range(batch):
        score_step(s, 0, scores_a)

        for i in range(chunks):
            even, odd = 2 * i, 2 * i + 1
            score_step(s, odd, scores_b)
            softmax_step(even, scores_a, probs_a)
            if even > 0:
                value_step(s, even - 1, probs_b)
            if odd + 1 < 2 * chunks:
                score_step(s, odd + 1, scores_a)
            softmax_step(odd, scores_b, probs_b)
            value_step(s, even, probs_a)
            if s > 0:
                embed_step(s - 1, i)
            if s + 1 < batch and i == chunks // 2:
                qkv_step(s + 1)
            if s + 1 == batch and i > 0:
                embed_rows(s, i - 1)
        value_step(s, 2 * chunks - 1, probs_b)
    embed_rows(batch - 1, chunks - 1)
    embed_step(batch - 1, 4)


def atom_stage(part, batch, feats, near, next_, mask, counts, single, w_qkv, w_out, w_embed):
    atoms = feats.shape[1]
    tok_rows = single.shape[0]
    padded = atoms + 2 * HALO
    return pl.pallas_call(
        functools.partial(atom_kernel, first=part * batch),
        in_specs=[pl.BlockSpec(memory_space=pl.ANY)] * 9,
        out_specs=[pl.BlockSpec(memory_space=pltpu.VMEM)] * 2,
        out_shape=[
            jax.ShapeDtypeStruct((batch, tok_rows, C_TOK), f32),
            jax.ShapeDtypeStruct((batch, tok_rows, C_TOK), bf16),
        ],
        scratch_shapes=[
            pltpu.VMEM(mask.shape, jnp.int32),
            pltpu.VMEM(counts.shape, jnp.int32),
            pltpu.VMEM(single.shape, bf16),
            pltpu.VMEM(w_qkv.shape, bf16),
            pltpu.VMEM(w_out.shape, bf16),
            pltpu.VMEM(w_embed.shape, bf16),
            pltpu.SemaphoreType.DMA((6 + 3 * batch,)),
            pltpu.VMEM((2, batch, HALO, C_ATOM), bf16),
            pltpu.VMEM((batch, padded, C_ATOM), bf16),
            pltpu.VMEM((padded, C_ATOM), bf16),
            pltpu.VMEM((padded, 3 * C_ATOM), bf16),
            pltpu.VMEM((padded, 3 * C_ATOM), bf16),
            pltpu.VMEM((2, 160, 256), f32),
            pltpu.VMEM((2, 160, 256), f32),
            pltpu.VMEM((4, 128, 128), bf16),
            pltpu.VMEM((4, 128, 128), bf16),
            pltpu.VMEM((atoms, C_ATOM), bf16),
            pltpu.VMEM((atoms, C_ATOM), bf16),
            pltpu.VMEM((atoms, C_ATOM), bf16),
            pltpu.VMEM((2 * atoms, C_TOK), bf16),
            pltpu.VMEM((2 * atoms, C_TOK), bf16),
            pltpu.VMEM((padded, 128), f32),
            pltpu.VMEM((tok_rows, 2 * atoms), bf16),
        ],
        compiler_params=pltpu.CompilerParams(vmem_limit_bytes=GRANT),
        cost_estimate=pl.CostEstimate(
            flops=10**10, bytes_accessed=4 * 10**6, transcendentals=3 * 10**6
        ),
        name="atoms",
    )(feats, near, next_, mask, counts, single, w_qkv, w_out, w_embed)


def head_masks(rows):
    masks = []
    for pair in range(4):
        low, high = WINDOWS[pair]
        lane = iota((rows, high - low), 1) + low
        first = 2 * pair * HD
        masks.append(
            [(lane >= first + HD * k) & (lane < first + HD * (k + 1)) for k in range(2)]
        )
    return masks


def two_heads(block, masks):
    blank = jnp.zeros_like(block)
    return jnp.concatenate([jnp.where(mask, block, blank) for mask in masks], axis=0)


def project_moves(piece_hbms, w_qkv_hbm, w_kv_ref, all_ref):
    tok_rows = piece_hbms[0].shape[1]
    here = lax.axis_index("tok")
    moves = []
    for k, piece in enumerate(piece_hbms):
        at = pl.multiple_of((here ^ k) * tok_rows, tok_rows)
        moves.append((piece, all_ref.at[:, pl.ds(at, tok_rows), :]))
    for i in range(2):
        moves.append((w_qkv_hbm.at[:, pl.ds(C_TOK * (i + 1), C_TOK)], w_kv_ref.at[i]))
    return moves


def project(copies, w_kv_ref, all_ref, keys_ref, values_ref):
    batch = all_ref.shape[0]
    for copy in copies[:-1]:
        copy.wait()
    for which, to_ref in enumerate((keys_ref, values_ref)):
        if which == 1:
            copies[-1].wait()
        for n in range(0, C_TOK, 256):
            for s in range(batch):
                to_ref[s, :, n : n + 256] = nn(
                    all_ref[s], w_kv_ref[which, :, n : n + 256]
                ).astype(bf16)


def windows(pair):
    low, high = WINDOWS[pair % 4]
    return 384 * (pair // 4) + low, 384 * (pair // 4) + high


def attend(bias_ref, queries_ref, keys_ref, values_ref, probs_ref, att_ref, done=None):
    batch, keys_all = keys_ref.shape[0], keys_ref.shape[1]
    tok_rows = queries_ref.shape[0] // batch
    masks = head_masks(tok_rows)
    factor = HD ** (-0.5)

    for s in range(batch):
        at = s * tok_rows
        for pair in range(PAIRS):
            low, high = windows(pair)
            queries = two_heads(queries_ref[pl.ds(at, tok_rows), low:high], masks[pair % 4])
            probs_ref[s, pair] = nt(keys_ref[s, :, low:high], queries)
        for pair in range(PAIRS):
            scores = probs_ref[s, pair] * factor
            bias = [bias_ref[k, pair].astype(f32) for k in range(bias_ref.shape[0])]
            scores = scores + jnp.concatenate(bias, axis=0)
            expo = jnp.exp(scores - jnp.max(scores, axis=0, keepdims=True))
            probs_ref[s, pair] = expo * (1.0 / jnp.sum(expo, axis=0, keepdims=True))
        lanes = [jnp.zeros((tok_rows, 128), f32) for _ in range(C_TOK // 128)]
        for pair in range(PAIRS):
            low, high = windows(pair)
            part = tn(probs_ref[s, pair].astype(bf16), values_ref[s, :, low:high])
            first, second = masks[pair % 4]
            mix = jnp.where(first, part[0:tok_rows], 0.0)
            mix = jnp.where(second, part[tok_rows : 2 * tok_rows], mix)
            for t in range((high - low) // 128):
                lanes[low // 128 + t] = lanes[low // 128 + t] + mix[:, 128 * t : 128 * t + 128]
        for t in range(C_TOK // 128):
            att_ref[pl.ds(at, tok_rows), 128 * t : 128 * t + 128] = lanes[t].astype(bf16)
        if done is not None:
            done(s)


def attend_kernel(*refs, count):
    (
        later_hbm, bias_hbm, w_qkv_hbm, cot_hbm, w_down_hbm, att_ref, probs_hbm, values_hbm,
        d_hidden_hbm, later_queries_ref, w_q_ref, w_kv_ref, own_ref, bias_ref, cot_ref, w_down_ref,
        probs_ref, values_ref, d_hidden_ref, sems, all_ref, queries_ref, keys_ref,
    ) = refs[count:]
    batch, tok_rows = all_ref.shape[0], refs[0].shape[1]
    moves = [
        (refs[0], own_ref.at[pl.ds(0, batch)]),
        (later_hbm, own_ref.at[pl.ds(batch, own_ref.shape[0] - batch)]),
        (w_qkv_hbm.at[:, pl.ds(0, C_TOK)], w_q_ref),
    ]
    moves += project_moves(refs[:count], w_qkv_hbm, w_kv_ref, all_ref)
    moves += [(bias_hbm, bias_ref), (cot_hbm, cot_ref), (w_down_hbm, w_down_ref)]
    copies = start_all(moves, sems)
    for copy in copies[0:3]:
        copy.wait()
    own = own_ref[...].reshape(-1, C_TOK)
    split = batch * tok_rows
    for n in range(0, C_TOK, 256):
        queries = nn(own, w_q_ref[:, n : n + 256]).astype(bf16)
        queries_ref[:, n : n + 256] = queries[0:split]
        later_queries_ref[:, n : n + 256] = queries[split:]
    project(copies[3:-3], w_kv_ref, all_ref, keys_ref, values_ref)
    for copy in copies[-3:]:
        copy.wait()
    back = [
        pltpu.make_async_copy(probs_ref.at[s], probs_hbm.at[s], sems.at[s]) for s in range(batch)
    ] + [
        pltpu.make_async_copy(values_ref, values_hbm, sems.at[batch]),
        pltpu.make_async_copy(d_hidden_ref, d_hidden_hbm, sems.at[batch + 1]),
    ]
    back[batch].start()
    cot = cot_ref[...].reshape(-1, C_TOK)
    for n in range(0, w_down_ref.shape[0], 256):
        d_hidden_ref[:, n : n + 256] = nt(cot, w_down_ref[n : n + 256, :])
    back[batch + 1].start()
    attend(
        bias_ref, queries_ref, keys_ref, values_ref, probs_ref, att_ref, lambda s: back[s].start()
    )
    for copy in back:
        copy.wait()


def attend_scratch(batch, tok_rows, keys_all):
    return [
        pltpu.VMEM((batch, keys_all, C_TOK), bf16),
        pltpu.VMEM((batch * tok_rows, C_TOK), bf16),
        pltpu.VMEM((batch, keys_all, C_TOK), bf16),
    ]


def attend_stage(pieces, later, bias, w_qkv, cot, w_down):
    batch, tok_rows, _ = pieces[0].shape
    keys_all = tok_rows * len(pieces)
    vmem = pl.BlockSpec(memory_space=pltpu.VMEM)
    hbm = pl.BlockSpec(memory_space=pl.ANY)
    d_hidden = jax.ShapeDtypeStruct((cot.shape[0] * tok_rows, w_down.shape[0]), f32)
    return pl.pallas_call(
        functools.partial(attend_kernel, count=len(pieces)),
        in_specs=[hbm] * (len(pieces) + 5),
        out_specs=[vmem, hbm, hbm, hbm, vmem],
        out_shape=[
            jax.ShapeDtypeStruct((batch * tok_rows, C_TOK), bf16),
            jax.ShapeDtypeStruct((batch, PAIRS, keys_all, 2 * tok_rows), f32),
            jax.ShapeDtypeStruct((batch, keys_all, C_TOK), bf16),
            d_hidden,
            jax.ShapeDtypeStruct((later.shape[0] * tok_rows, C_TOK), bf16),
        ],
        scratch_shapes=[
            pltpu.VMEM((C_TOK, C_TOK), bf16),
            pltpu.VMEM((2, C_TOK, C_TOK), bf16),
            pltpu.VMEM(cot.shape, bf16),
            pltpu.VMEM(bias.shape, bf16),
            pltpu.VMEM(cot.shape, bf16),
            pltpu.VMEM(w_down.shape, bf16),
            pltpu.VMEM((batch, PAIRS, keys_all, 2 * tok_rows), f32),
            pltpu.VMEM((batch, keys_all, C_TOK), bf16),
            pltpu.VMEM(d_hidden.shape, f32),
            pltpu.SemaphoreType.DMA((8 + len(pieces),)),
        ]
        + attend_scratch(batch, tok_rows, keys_all),
        compiler_params=pltpu.CompilerParams(vmem_limit_bytes=GRANT),
        cost_estimate=pl.CostEstimate(
            flops=4 * 10**9, bytes_accessed=10**7, transcendentals=10**6
        ),
        name="attend",
    )(*pieces, later, bias, w_qkv, cot, w_down)


def token_kernel(*refs, count):
    (
        queries_hbm, bias_hbm, tokens_a_hbm, tokens_b_hbm, att_a_hbm, cot_hbm, probs_a_hbm, values_a_hbm,
        w_qkv_hbm, w_out_hbm, w_gate_hbm, w_up_hbm, d_hidden_hbm,
        resid_hbm, hidden_hbm, d_bias_hbm,
        d_bias_ref, bias_ref, tokens_ref, att_a_ref, cot_ref, resid_ref, hidden_ref,
        w_kv_ref, w_out_ref, w_gate_ref, w_up_ref, d_hidden_ref, probs_ref, values_ref, sems,
        all_ref, queries_ref, keys_ref, grads_ref, d_gate_ref, d_up_ref, hat_ref,
    ) = refs[count:]
    batch, tok_rows = cot_ref.shape[0], cot_ref.shape[1]
    keys_all = values_ref.shape[1]
    rows = batch * tok_rows
    ahead = values_a_hbm.shape[0]
    lead = ahead * tok_rows
    moves = project_moves(refs[:count], w_qkv_hbm, w_kv_ref, all_ref)
    projecting = len(moves)
    moves += [
        (queries_hbm, queries_ref), (bias_hbm, bias_ref), (w_out_hbm, w_out_ref), (att_a_hbm, att_a_ref),
        (tokens_a_hbm, tokens_ref.at[pl.ds(0, ahead)]),
        (tokens_b_hbm, tokens_ref.at[pl.ds(ahead, batch - ahead)]), (cot_hbm, cot_ref),
        (d_hidden_hbm, d_hidden_ref), (w_gate_hbm, w_gate_ref), (w_up_hbm, w_up_ref),
        (values_a_hbm, values_ref.at[pl.ds(0, ahead)]), (probs_a_hbm, probs_ref.at[pl.ds(0, ahead)]),
    ]
    copies = start_all(moves, sems)
    own_values = values_ref.at[pl.ds(ahead, batch - ahead)]
    own_probs = probs_ref.at[pl.ds(ahead, batch - ahead)]
    project(copies[:projecting], w_kv_ref, all_ref, keys_ref, own_values)
    copies[projecting].wait()
    copies = copies[projecting + 1 :]
    copies[0].wait()
    attend(bias_ref, queries_ref, keys_ref, own_values, own_probs, queries_ref)

    for copy in copies[1:5]:
        copy.wait()
    tokens = tokens_ref[...].reshape(rows, C_TOK)
    resid_ref[0:lead, :] = tokens[0:lead] + nn(att_a_ref[...], w_out_ref[...])
    resid_ref[lead:rows, :] = tokens[lead:rows] + nn(queries_ref[...], w_out_ref[...])
    back = [
        pltpu.make_async_copy(resid_ref, resid_hbm, sems.at[0]),
        pltpu.make_async_copy(hidden_ref, hidden_hbm, sems.at[1]),
    ]
    back[0].start()
    hat, rstd = norm_rows(resid_ref[...])
    hat_ref[...] = hat
    grads_ref[...] = hat.astype(bf16)
    for copy in copies[5:9]:
        copy.wait()

    for n in range(0, w_gate_ref.shape[1], 256):
        shaped = grads_ref[...]
        gate = nn(shaped, w_gate_ref[:, n : n + 256])
        up = nn(shaped, w_up_ref[:, n : n + 256])
        d_hidden = d_hidden_ref[:, n : n + 256]
        sig = 1.0 / (1.0 + jnp.exp(-gate))
        act = gate * sig
        hidden_ref[:, n : n + 256] = (act * up).astype(bf16)
        d_gate_ref[:, n : n + 256] = (
            d_hidden * up * sig * (1.0 + gate * (1.0 - sig))
        ).astype(bf16)
        d_up_ref[:, n : n + 256] = (d_hidden * act).astype(bf16)

    back[1].start()
    parts = []
    for n in range(0, C_TOK, 256):
        parts.append(
            nt(d_gate_ref[...], w_gate_ref[n : n + 256, :])
            + nt(d_up_ref[...], w_up_ref[n : n + 256, :])
        )
    d_normed = jnp.concatenate(parts, axis=1)
    hat = hat_ref[...]
    first = jnp.mean(d_normed, axis=-1, keepdims=True)
    second = jnp.mean(d_normed * hat, axis=-1, keepdims=True)
    d_resid = cot_ref[...].reshape(rows, C_TOK).astype(f32) + rstd * (
        d_normed - first - hat * second
    )
    grads_ref[...] = nt(d_resid.astype(bf16), w_out_ref[...]).astype(bf16)
    for copy in copies[9:]:
        copy.wait()
    masks = head_masks(tok_rows)
    for pair in range(PAIRS):
        low, high = windows(pair)
        total = jnp.zeros((keys_all, 2 * tok_rows), f32)
        for s in range(batch):
            grads = two_heads(
                grads_ref[s * tok_rows : (s + 1) * tok_rows, low:high], masks[pair % 4]
            )
            d_probs = nt(values_ref[s, :, low:high], grads)
            probs = probs_ref[s, pair]
            delta = jnp.sum(probs * d_probs, axis=0, keepdims=True)
            total = total + probs * (d_probs - delta)
        size = d_bias_ref.shape[2]
        for k in range(d_bias_ref.shape[0]):
            d_bias_ref[k, pair] = total[size * k : size * (k + 1)].astype(bf16)
        back.append(
            pltpu.make_async_copy(
                d_bias_ref.at[:, pair], d_bias_hbm.at[:, pair], sems.at[2 + pair]
            )
        )
        back[-1].start()
    for copy in back:
        copy.wait()


def token_stage(
    pieces, queries, bias, tokens_a, tokens_b, att_a, cot, probs_a, values_a, w_qkv, w_out, w_gate, w_up,
    d_hidden,
):
    batch, tok_rows, _ = cot.shape
    keys_all = tok_rows * len(pieces)
    rows = batch * tok_rows
    hidden = w_gate.shape[1]
    vmem = pl.BlockSpec(memory_space=pltpu.VMEM)
    hbm = pl.BlockSpec(memory_space=pl.ANY)
    return pl.pallas_call(
        functools.partial(token_kernel, count=len(pieces)),
        in_specs=[hbm] * (len(pieces) + 13),
        out_specs=[hbm, hbm, hbm],
        out_shape=[
            jax.ShapeDtypeStruct((rows, C_TOK), f32),
            jax.ShapeDtypeStruct((rows, hidden), bf16),
            jax.ShapeDtypeStruct(bias.shape, bf16),
        ],
        scratch_shapes=[
            pltpu.VMEM(bias.shape, bf16),
            pltpu.VMEM(bias.shape, bf16),
            pltpu.VMEM(cot.shape, f32),
            pltpu.VMEM(att_a.shape, bf16),
            pltpu.VMEM(cot.shape, bf16),
            pltpu.VMEM((rows, C_TOK), f32),
            pltpu.VMEM((rows, hidden), bf16),
            pltpu.VMEM((2, C_TOK, C_TOK), bf16),
            pltpu.VMEM(w_out.shape, bf16),
            pltpu.VMEM(w_gate.shape, bf16),
            pltpu.VMEM(w_up.shape, bf16),
            pltpu.VMEM(d_hidden.shape, f32),
            pltpu.VMEM((batch, PAIRS, keys_all, 2 * tok_rows), f32),
            pltpu.VMEM((batch, keys_all, C_TOK), bf16),
            pltpu.SemaphoreType.DMA((16 + len(pieces),)),
        ]
        + attend_scratch(pieces[0].shape[0], tok_rows, keys_all)
        + [
            pltpu.VMEM((rows, C_TOK), bf16),
            pltpu.VMEM((rows, hidden), bf16),
            pltpu.VMEM((rows, hidden), bf16),
            pltpu.VMEM((rows, C_TOK), f32),
        ],
        compiler_params=pltpu.CompilerParams(vmem_limit_bytes=GRANT),
        cost_estimate=pl.CostEstimate(
            flops=10**10, bytes_accessed=2 * 10**7, transcendentals=10**6
        ),
        name="tokens",
    )(
        *pieces, queries, bias, tokens_a, tokens_b, att_a, cot, probs_a, values_a, w_qkv, w_out, w_gate,
        w_up, d_hidden,
    )


def output_kernel(
    resid_ref, hidden_ref, w_down_ref, pair_ref, out_ref, hat_ref, rstd_ref, pairf_ref
):
    out_ref[...] = (resid_ref[...] + nn(hidden_ref[...], w_down_ref[...])).astype(bf16)
    rows, keys = pair_ref.shape[0], pair_ref.shape[1]
    for i in range(rows // 8):
        pairf_ref[8 * keys * i : 8 * keys * (i + 1), :] = (
            pair_ref[8 * i : 8 * i + 8].astype(f32).reshape(8 * keys, CZ)
        )

    def norm_step(j, carry):
        hat, rstd = norm_rows(pairf_ref[pl.ds(j, rows, stride=keys), :])
        at = pl.multiple_of(j * rows, rows)
        hat_ref[pl.ds(at, rows), :] = hat
        rstd = jnp.broadcast_to(rstd, (rows, CZ)).T[0:1]
        rstd_ref[pl.ds(j, 1), :] = jnp.concatenate([rstd, rstd], axis=1)
        return carry

    lax.fori_loop(0, keys, norm_step, 0, unroll=4)


def output_stage(resid, hidden, w_down, pair):
    rows, keys = pair.shape[0], pair.shape[1]
    return pl.pallas_call(
        output_kernel,
        out_shape=[jax.ShapeDtypeStruct(resid.shape, bf16)]
        + [
            jax.ShapeDtypeStruct((rows * keys, CZ), f32),
            jax.ShapeDtypeStruct((keys, 2 * rows), f32),
        ],
        scratch_shapes=[pltpu.VMEM((rows * keys, CZ), f32)],
        compiler_params=pltpu.CompilerParams(vmem_limit_bytes=GRANT),
        cost_estimate=pl.CostEstimate(
            flops=10**9, bytes_accessed=8 * 10**6, transcendentals=0
        ),
        name="output",
    )(resid, hidden, w_down, pair)


def grad_kernel(
    parts_hbm, hat_hbm, rstd_hbm, gain_hbm, w_bias_hbm, out_hbm, parts_ref, hat_ref, rstd_ref,
    gain_ref, w_bias_ref, total_ref, out_ref, sems,
):
    keys = parts_ref.shape[2]
    rows = hat_ref.shape[0] // keys
    size = 8 * rows
    moves = [
        (gain_hbm, gain_ref), (w_bias_hbm, w_bias_ref), (parts_hbm, parts_ref),
        (rstd_hbm, rstd_ref),
    ]
    for c in range(keys // 8):
        moves.append((hat_hbm.at[pl.ds(size * c, size)], hat_ref.at[pl.ds(size * c, size)]))
    copies = start_all(moves, sems)
    for copy in copies[0:2]:
        copy.wait()
    weights = jnp.concatenate(split_heads(w_bias_ref[...]), axis=0) * gain_ref[...]
    weights = weights - jnp.mean(weights, axis=-1, keepdims=True)
    weights = jnp.concatenate([weights[0:PAIRS], weights[PAIRS:HEADS]], axis=1)
    w_high = weights.astype(bf16).astype(f32)
    w_middle = (weights - w_high).astype(bf16).astype(f32)
    w_low = weights - w_high - w_middle
    weights = jnp.concatenate([w_high, w_middle, w_low, w_high, w_middle, w_high], axis=0)
    weights = weights.astype(bf16)
    for copy in copies[2:4]:
        copy.wait()
    for pair in range(PAIRS):
        total = parts_ref[0, pair].astype(f32)
        for k in range(1, parts_ref.shape[0]):
            total = total + parts_ref[k, pair].astype(f32)
        total_ref[pair * keys : (pair + 1) * keys, :] = total * rstd_ref[...]
    back = []
    for c in range(keys // 8):
        copies[4 + c].wait()
        for j in range(8 * c, 8 * c + 8):
            total = total_ref[pl.ds(j, PAIRS, stride=keys), :]
            high = total.astype(bf16).astype(f32)
            middle = (total - high).astype(bf16).astype(f32)
            low = total - high - middle
            stack = jnp.concatenate([high, high, high, middle, middle, low], axis=0)
            both = nn(stack.T.astype(bf16), weights)
            scaled = both[0:rows, 0:CZ] + both[rows : 2 * rows, CZ : 2 * CZ]
            hat = hat_ref[rows * j : rows * (j + 1), :]
            second = jnp.mean(scaled * hat, axis=-1, keepdims=True)
            out_ref[pl.ds(size * c + j % 8, rows, stride=8), :] = scaled - hat * second
        back.append(
            pltpu.make_async_copy(
                out_ref.at[pl.ds(size * c, size)].reshape(rows, 8, CZ),
                out_hbm.at[:, pl.ds(8 * c, 8), :],
                sems.at[c],
            )
        )
        back[c].start()
    for copy in back:
        copy.wait()


def pair_back(parts, hat, rstd, pair_gain, w_bias_t):
    keys = parts.shape[2]
    rows = hat.shape[0] // keys
    hbm = pl.BlockSpec(memory_space=pl.ANY)
    return pl.pallas_call(
        grad_kernel,
        in_specs=[hbm] * 5,
        out_specs=hbm,
        out_shape=jax.ShapeDtypeStruct((rows, keys, CZ), f32),
        scratch_shapes=[
            pltpu.VMEM(parts.shape, bf16),
            pltpu.VMEM(hat.shape, f32),
            pltpu.VMEM(rstd.shape, f32),
            pltpu.VMEM((1, CZ), f32),
            pltpu.VMEM(w_bias_t.shape, bf16),
            pltpu.VMEM((keys * PAIRS, 2 * rows), f32),
            pltpu.VMEM((rows * keys, CZ), f32),
            pltpu.SemaphoreType.DMA((4 + keys // 8,)),
        ],
        compiler_params=pltpu.CompilerParams(vmem_limit_bytes=GRANT),
        cost_estimate=pl.CostEstimate(flops=10**8, bytes_accessed=4 * 10**6, transcendentals=0),
        name="pair_grad",
    )(parts, hat, rstd, pair_gain.reshape(1, CZ), w_bias_t)


def swap(values, axis, k):
    return lax.ppermute(values, axis, [(i, i ^ k) for i in range(lax.axis_size(axis))])


def gather(values, axis):
    far = range(lax.axis_size(axis) - 1, 0, -1)
    return [values] + [swap(values, axis, k) for k in far][::-1]


def body(
    atom_feats, atom_counts, atom_mask, token_single, pair, pair_gain, w_bias, w_atom_qkv,
    w_atom_out, w_embed, w_qkv, w_out, w_gate, w_up, w_down, cotangent,
):
    batch, atom_rows, _ = atom_feats.shape
    tok_rows = token_single.shape[0]
    shards = lax.axis_size("tok")
    groups = lax.axis_size("samp")

    w_bias_t = w_bias.T
    local_bias, near, next_ = pair_bias(pair, pair_gain, w_bias_t, atom_feats, groups)
    near = swap(near, "tok", 1)
    steps = [(i, i + 1) for i in range(1, shards - 1, 2)]
    next_ = lax.ppermute(next_, "tok", steps + [(j, i) for i, j in steps])

    bias = lax.all_to_all(local_bias, "samp", 0, 0).reshape(groups, PAIRS, -1, 2 * tok_rows)

    mask = atom_mask.reshape(-1, 128)
    mask, local_bias = lax.optimization_barrier((mask, local_bias))

    each = batch // 2
    tokens, gathered = [], []
    for part in range(2):
        tok, normed = atom_stage(
            part, each, atom_feats, near, next_, mask, atom_counts, token_single, w_atom_qkv,
            w_atom_out, w_embed,
        )
        tokens.append(tok)
        gathered.append(gather(normed, "tok"))
    att_a, probs_a, values_a, d_hidden, queries_b = attend_stage(
        gathered[0], gathered[1][0], bias, w_qkv, cotangent, w_down
    )
    resid, hidden, d_bias = token_stage(
        gathered[1], queries_b, bias, *tokens, att_a, cotangent, probs_a, values_a, w_qkv, w_out, w_gate,
        w_up, d_hidden,
    )
    parts = lax.all_to_all(d_bias, "samp", 0, 0)
    token_out, hat, rstd = output_stage(resid, hidden, w_down, pair)
    pair_grad = pair_back(parts, hat, rstd, pair_gain, w_bias_t)
    token_out = token_out.reshape(batch, tok_rows, C_TOK)
    return (token_out, pair_grad)


def solution(mesh):
    in_specs = (
        P("samp", "tok", None),
        P("tok", None),
        P(),
        P("tok", None),
        P("tok", "samp", None),
        P(), P(), P(), P(), P(), P(), P(), P(), P(), P(),
        P("samp", "tok", None),
    )
    out_specs = (P("samp", "tok", None), P("tok", "samp", None))
    return jax.shard_map(body, mesh=mesh, in_specs=in_specs, out_specs=out_specs, check_vma=False)
```
